32 devices in a mesh: row: 8 (over y, x, core), col: 4 (over z).
Axes of the slice: x: 2, y: 2, z: 4, core: 2. Of those that a mesh axis runs over, the one named last changes fastest.
Arguments:
- object_field: float32 [2, 3072, 1536], P(None, 'row', 'col'), may hold values from -6 to 6
- probe: float32 [2, 128, 128], replicated, may hold values from -6 to 6
- amplitudes: float32 [8, 4, 12, 128, 128], P('row', 'col'), may hold values from 0.2 to 4
- offsets: int32 [8, 4, 12, 2], P('row', 'col'), may hold values from -64 to 319
- counts: int32 [8, 4], P('row', 'col'), may hold values from 1 to 12, as said below
Outputs:
- updated_object: float32 [2, 3072, 1536], P(None, 'row', 'col')
The draws below stay inside these ranges and needn't reach their ends.
Inputs may be any that keep to these rules, and one draw needn't show every extreme that they name: `counts`: some tile has exactly 12 live positions in every draw.
All inputs are finite; a program needn't handle non-finite values.
Results may differ from the reference program's by a relative error of at most 0.0001.
Values sent between devices are 32-bit elements; how exact they have to be, the bound alone decides.
No kernel may reach another device: no remote copies, remote signals or barrier semaphores. Data moves between devices by JAX's collectives and lax.ppermute only.
A program may use at most 64 MiB of HBM per device.

```python
import math
import jax
import jax.numpy as jnp
from jax import lax

PROBE = 128
TILE = 384
MAXPOS = 12
ITERS = 2
BLOCK_ROWS = 8
BLOCK_COLS = 4
NY = 3072
NX = 1536


def draw_counts(key, part):
    first, second, third = jax.random.split(jax.random.fold_in(key, 11), 3)
    shape = (BLOCK_ROWS, BLOCK_COLS)
    small = jax.random.randint(first, shape, 1, MAXPOS // 4 + 1)
    full = jax.random.randint(second, shape, 0, 4) == 0
    values = jnp.where(full, MAXPOS, small).reshape(-1)
    chosen = jax.random.randint(third, (), 0, BLOCK_ROWS * BLOCK_COLS)
    values = values.at[chosen].set(MAXPOS)
    return values.reshape(shape).astype(jnp.int32)


def with_ends(array, key, smallest, top_value):
    spot = [jax.random.randint(jax.random.fold_in(key, axis), (), 0, length) for axis, length in enumerate(array.shape)]
    longest = array.shape.index(max(array.shape))
    next_to = spot[:longest] + [(spot[longest] + 1) % array.shape[longest]] + spot[longest + 1:]
    return array.at[tuple(spot)].set(smallest).at[tuple(next_to)].set(top_value)


def level_of(own_key, extent, cuts, low, largest):
    def one(position, blocks):
        steps = jax.random.uniform(jax.random.fold_in(jax.random.fold_in(own_key, 6), position), (blocks,), jnp.float32, low / len(cuts), largest / len(cuts))
        return jnp.repeat(jnp.exp(steps), extent[position] // blocks).reshape((-1,) + (1,) * (len(extent) - position - 1))

    gain = one(*cuts[0])
    for cut in cuts[1:]:
        gain = gain * one(*cut)
    return gain


def centred(stream_key, extent, spread, limit, shards=(), kind=jnp.bfloat16):
    result = jax.random.normal(stream_key, extent, jnp.float32) * spread
    if len(shards) > 0:
        result = level_of(stream_key, extent, shards, -0.22, 0.18) * result
    return jnp.clip(result, min=-limit, max=limit).astype(kind)


def setup_inputs(seed: int = 0) -> dict:
    key_list = jax.random.split(jax.random.key(seed), 6)
    object_field = centred(key_list[0], (2, NY, NX), 1.0, 6.0, ((1, 8), (2, 4)), jnp.float32)
    probe = centred(key_list[1], (2, PROBE, PROBE), 1.0, 6.0, (), jnp.float32)
    amplitudes = jnp.clip(jnp.exp(math.log(4.0) - 2.9957323 * jax.random.uniform(key_list[2], (BLOCK_ROWS, BLOCK_COLS, MAXPOS, PROBE, PROBE), jnp.float32) ** level_of(key_list[2], (BLOCK_ROWS, BLOCK_COLS, MAXPOS, PROBE, PROBE), ((0, 8), (1, 4)), -0.2, 0.2)), 0.2, 4.0)
    offsets = with_ends(jax.random.randint(key_list[3], (BLOCK_ROWS, BLOCK_COLS, MAXPOS, 2), -(PROBE // 2), TILE - PROBE // 2), jax.random.fold_in(key_list[3], 1), -(PROBE // 2), (TILE - PROBE // 2) - 1).astype(jnp.int32)
    counts = draw_counts(jax.random.fold_in(key_list[5], 71), 0)
    return {"object_field": object_field, "probe": probe, "amplitudes": amplitudes, "offsets": offsets, "counts": counts}


def reference(object_field, probe, amplitudes, offsets, counts):
    half = PROBE // 2
    blocks = BLOCK_ROWS * BLOCK_COLS
    row_base = (jnp.arange(BLOCK_ROWS, dtype=jnp.int32) * TILE)[:, None, None]
    col_base = (jnp.arange(BLOCK_COLS, dtype=jnp.int32) * TILE)[None, :, None]
    start_rows = (row_base + offsets[..., 0] + half).reshape(blocks, MAXPOS).astype(jnp.int32)
    start_cols = (col_base + offsets[..., 1] + half).reshape(blocks, MAXPOS).astype(jnp.int32)
    live = (jnp.arange(MAXPOS, dtype=jnp.int32)[None, None, :] < counts[..., None]).astype(jnp.float32)
    live = live.reshape(blocks, MAXPOS)
    measured = amplitudes.reshape(blocks, MAXPOS, PROBE, PROBE)
    probe_c = lax.complex(probe[0], probe[1])
    power = probe[0] * probe[0] + probe[1] * probe[1]
    zero_i = jnp.int32(0)

    def add_light(index, total):
        block = index // MAXPOS
        slot = index % MAXPOS
        srow = start_rows[block, slot]
        scol = start_cols[block, slot]
        old = lax.dynamic_slice(total, (srow, scol), (PROBE, PROBE))
        return lax.dynamic_update_slice(total, old + power * live[block, slot], (srow, scol))
    light = lax.fori_loop(0, blocks * MAXPOS, add_light, jnp.zeros((NY + PROBE, NX + PROBE), jnp.float32))
    light = light[half:half + NY, half:half + NX]
    field = object_field
    for step in range(ITERS):
        padded = jnp.pad(field, ((0, 0), (half, half), (half, half)))

        def per_block(block, total):

            def window(srow, scol):
                return lax.dynamic_slice(padded, (zero_i, srow, scol), (2, PROBE, PROBE))
            wins = jax.vmap(window)(start_rows[block], start_cols[block])
            exit_wave = probe_c[None] * lax.complex(wins[:, 0], wins[:, 1])
            far = jnp.fft.fft2(exit_wave, norm='ortho')
            mag2 = jnp.real(far) ** 2 + jnp.imag(far) ** 2
            ratio = measured[block] / jnp.sqrt(mag2 + 0.25) - 1.0
            back = jnp.fft.ifft2(far * ratio, norm='ortho')
            grad = jnp.conj(probe_c)[None] * back * live[block][:, None, None]
            grads = jnp.stack([jnp.real(grad), jnp.imag(grad)], axis=1)

            def place(slot, acc):
                srow = start_rows[block, slot]
                scol = start_cols[block, slot]
                old = lax.dynamic_slice(acc, (zero_i, srow, scol), (2, PROBE, PROBE))
                return lax.dynamic_update_slice(acc, old + grads[slot], (zero_i, srow, scol))
            return lax.fori_loop(0, MAXPOS, place, total)
        update = lax.fori_loop(0, blocks, per_block, jnp.zeros((2, NY + PROBE, NX + PROBE), jnp.float32))
        update = update[:, half:half + NY, half:half + NX]
        field = field + update / (light[None] + 1.0)
    return field
```

```python
import math

import jax
import jax.numpy as jnp
import numpy as np
from jax import lax
from jax.experimental import pallas as pl
from jax.experimental.pallas import tpu as pltpu
from jax.sharding import PartitionSpec as P

ITERS = 2
FLOOR = 0.25
VMEM_BYTES = 40 * 1024 * 1024


def split(value):
    high = value.astype(jnp.bfloat16)
    low = (value - high.astype(jnp.float32)).astype(jnp.bfloat16)
    return high, low


def dft_tables(length):
    index = np.arange(length)
    angle = (index[:, None] * index[None, :] % length) * (2.0 * math.pi / length)
    cosine = np.cos(angle) / math.sqrt(length)
    sine = np.sin(angle) / math.sqrt(length)
    ahead = np.block([[cosine, -sine], [sine, cosine]])
    parts = []
    for table in (ahead, ahead.T):
        high = table.astype(jnp.bfloat16)
        low = (table - high.astype(np.float64)).astype(jnp.bfloat16)
        parts += [high, low]
    return np.stack(parts)


def lanes(shape):
    return lax.broadcasted_iota(jnp.int32, shape, len(shape) - 1)


def swap(value, half):
    return pltpu.roll(value, half, value.ndim - 1)


def times_right(rows, high, low):
    top, rest = split(rows)
    left = jnp.concatenate([top, top, rest], axis=1)
    right = jnp.concatenate([high, low, high], axis=0)
    return jnp.dot(left, right, preferred_element_type=jnp.float32)


def times_left(high, low, columns):
    top, rest = split(columns)
    left = jnp.concatenate([high, low, high], axis=1)
    right = jnp.concatenate([top, top, rest], axis=0)
    return jnp.dot(left, right, preferred_element_type=jnp.float32)


def beside(left, right):
    return jnp.concatenate([left, right], axis=1)


def above(top, bottom):
    return jnp.concatenate([top, bottom], axis=0)


def add_gradients(frame, acc, probe_ref, amps, offsets, counts, tables):
    length = probe_ref.shape[-1]
    half = length // 2
    npos = amps.shape[2]
    group = 4 if npos % 4 == 0 else 2 if npos % 2 == 0 else 1
    acc[...] = jnp.zeros_like(acc)
    count = counts[0, 0]
    lane = lanes((length, length))

    def place(slot):
        row = offsets[0, 0, slot, 0] + half
        col = offsets[0, 0, slot, 1] + length
        return row, col // length, col % length

    def exit_wave(slot):
        row, block, shift = place(slot)
        inside = lane >= shift
        window = [
            jnp.where(inside, frame[part, block, pl.ds(row, length), :],
                      frame[part, block + 1, pl.ds(row, length), :])
            for part in (0, 1)
        ]
        real = pltpu.roll(probe_ref[0], shift, 1)
        imag = pltpu.roll(probe_ref[1], shift, 1)
        return (real * window[0] - imag * window[1], real * window[1] + imag * window[0])

    def shrink(real, imag, slot):
        ratio = amps[0, 0, slot] * lax.rsqrt(real * real + imag * imag + FLOOR) - 1.0
        return real * ratio, imag * ratio

    def put(slot, back_r, back_i):
        row, block, shift = place(slot)
        weight = jnp.where(slot < count, 1.0, 0.0).astype(jnp.float32)
        real = pltpu.roll(probe_ref[0], shift, 1) * weight
        imag = pltpu.roll(probe_ref[1], shift, 1) * weight
        grads = (real * back_r + imag * back_i, real * back_i - imag * back_r)
        inside = lane >= shift
        for part in (0, 1):
            acc[part, block, pl.ds(row, length), :] += jnp.where(inside, grads[part], 0.0)
            acc[part, block + 1, pl.ds(row, length), :] += jnp.where(inside, 0.0, grads[part])

    def work(slots):
        waves = [exit_wave(slot) for slot in slots]
        rows = jnp.concatenate([beside(*wave) for wave in waves], axis=0)
        mid = times_right(rows, tables[0], tables[1])
        mids = [mid[k * length:(k + 1) * length] for k in range(len(slots))]
        columns = above(
            jnp.concatenate([m[:, :length] for m in mids], axis=1),
            jnp.concatenate([m[:, length:] for m in mids], axis=1),
        )
        far = times_left(tables[2], tables[3], columns)
        changes = [
            shrink(far[:length, k * length:(k + 1) * length],
                   far[length:, k * length:(k + 1) * length], slot)
            for k, slot in enumerate(slots)
        ]
        columns = above(
            jnp.concatenate([c[0] for c in changes], axis=1),
            jnp.concatenate([c[1] for c in changes], axis=1),
        )
        mid = times_left(tables[0], tables[1], columns)
        rows = jnp.concatenate(
            [
                beside(mid[:length, k * length:(k + 1) * length],
                       mid[length:, k * length:(k + 1) * length])
                for k in range(len(slots))
            ],
            axis=0,
        )
        back = times_right(rows, tables[2], tables[3])
        return [
            (back[k * length:(k + 1) * length, :length], back[k * length:(k + 1) * length, length:])
            for k in range(len(slots))
        ]

    def step(index, carry):
        slots = [index * group + k for k in range(group)]
        found = work(slots)
        for slot, (back_r, back_i) in zip(slots, found):
            put(slot, back_r, back_i)
        return carry

    lax.fori_loop(0, (count + group - 1) // group, step, 0)


def pack_start(offsets, counts, first, last, to_left, to_right):
    tile, length = first.shape[1:]
    half = length // 2
    npos = offsets.shape[2]
    low = lanes((tile, length)) < half
    to_left[:tile] = jnp.where(low, first[0], swap(first[1], half))
    to_right[:tile] = jnp.where(low, swap(last[1], half), last[0])
    spot = lanes((8, length))
    info = jnp.where(spot == 2 * npos, counts[0, 0], 0)
    for k in range(npos):
        info = jnp.where(spot == k, offsets[0, 0, k, 0], info)
        info = jnp.where(spot == npos + k, offsets[0, 0, k, 1], info)
    info = info.astype(jnp.float32)
    to_left[tile:] = info
    to_right[tile:] = info


def pack_rows_start(field, from_left, from_right, own, to_up, to_down):
    tile = field.shape[1]
    length = from_left.shape[1]
    half = length // 2
    nb = tile // length
    low = lanes((half, length)) < half
    for strip, start in ((to_up, 0), (to_down, tile - half)):
        at = pl.ds(start, half)
        for part in (0, 1):
            for b in range(nb):
                strip[pl.ds((part * (nb + 1) + b) * half, half), :] = field[
                    part, at, b * length:(b + 1) * length]
            right = from_right[at, :]
            left = from_left[at, :]
            if part:
                right, left = swap(right, half), swap(left, half)
            strip[pl.ds((part * (nb + 1) + nb) * half, half), :] = jnp.where(low, right, left)
        base = 2 * (nb + 1) * half
        row = lax.broadcasted_iota(jnp.int32, (8, length), 0)
        info = jnp.where(row == 0, own[tile:, :],
                         jnp.where(row == 1, from_left[tile:, :],
                                   jnp.where(row == 2, from_right[tile:, :], 0.0)))
        strip[base:, :] = info


def first_pass(offsets, counts, field, from_left, from_right, from_up, from_down,
               probe, amps, tables, frame, acc, to_left, to_right):
    tile = field.shape[1]
    length = probe.shape[-1]
    half = length // 2
    nb = tile // length
    own = pl.ds(half, tile)
    for part in (0, 1):
        for b in range(nb):
            frame[part, b + 1, own, :] = field[part, :, b * length:(b + 1) * length]
        for block, source in ((0, from_left), (nb + 1, from_right)):
            value = source[:tile, :]
            frame[part, block, own, :] = swap(value, half) if part else value
        for source, start in ((from_up, 0), (from_down, half + tile)):
            at = pl.ds(start, half)
            for b in range(nb):
                frame[part, b + 1, at, :] = source[
                    pl.ds((part * (nb + 1) + b) * half, half), :]
            ends = source[pl.ds((part * (nb + 1) + nb) * half, half), :]
            frame[part, 0, at, :] = ends
            frame[part, nb + 1, at, :] = ends
    add_gradients(frame, acc, probe, amps, offsets, counts, tables)
    low = lanes(to_left.shape[1:]) < half
    for part in (0, 1):
        to_left[part] = jnp.where(low, acc[part, 1], acc[part, 0])
        to_right[part] = jnp.where(low, acc[part, nb + 1], acc[part, nb])


def pack_rows_mid(acc_top, acc_bottom, from_left, from_right, to_up, to_down):
    _, blocks, length, _ = acc_top.shape
    half = length // 2
    nb = blocks - 2
    rows = from_left.shape[1]
    low = lanes((length, length)) < half
    for strip, acc, start in ((to_up, acc_top, 0), (to_down, acc_bottom, rows - length)):
        at = pl.ds(start, length)
        for part in (0, 1):
            left = from_left[part, at, :]
            right = from_right[part, at, :]
            for b in range(nb):
                value = acc[part, b + 1]
                if b == 0:
                    value = value + jnp.where(low, left, 0.0)
                if b == nb - 1:
                    value = value + jnp.where(low, 0.0, right)
                strip[part, b] = value
            strip[part, nb] = jnp.where(low, acc[part, nb + 1] + right, acc[part, 0] + left)


def light_pass(info, probe, inverse, light):
    length = probe.shape[-1]
    half = length // 2
    blocks, rows, _ = inverse.shape
    nb = blocks - 2
    tile = nb * length
    npos = info.shape[1] // 2
    light[...] = jnp.zeros_like(light)
    lane = lanes((length, length))
    for tile_index in range(9):
        down = tile_index // 3 - 1
        across = tile_index % 3 - 1

        def one(slot, carry):
            row = info[tile_index, slot] + half + down * tile
            col = info[tile_index, npos + slot] + length + across * tile

            @pl.when((row > -length) & (row < rows) & (col > half - length)
                     & (col < length + tile + half))
            def _():
                start = row + length
                block = (col + length) // length
                shift = (col + length) % length
                real = pltpu.roll(probe[0], shift, 1)
                imag = pltpu.roll(probe[1], shift, 1)
                power = real * real + imag * imag
                inside = lane >= shift
                light[block, pl.ds(start, length), :] += jnp.where(inside, power, 0.0)
                light[block + 1, pl.ds(start, length), :] += jnp.where(inside, 0.0, power)

            return carry

        lax.fori_loop(0, info[tile_index, 2 * npos], one, 0)
    have = [info[k, 2 * npos] > 0 for k in range(9)]
    spot = lax.broadcasted_iota(jnp.int32, (rows, length), 0)
    keep_up = jnp.where(have[1], 0, half)
    keep_down = jnp.where(have[7], rows, rows - half)
    kept = (spot >= keep_up) & (spot < keep_down)
    for b in range(blocks):
        value = 1.0 / (light[b + 1, pl.ds(length, rows), :] + 1.0)
        keep = kept
        if b == 0:
            keep = keep & have[3]
        if b == nb + 1:
            keep = keep & have[5]
        inverse[b] = jnp.where(keep, value, 0.0)


def second_pass(offsets, counts, frame, acc, inverse, from_left, from_right, from_up, from_down,
                probe, amps, tables, field, sums, to_up, to_down, work, total):
    length = probe.shape[-1]
    half = length // 2
    _, blocks, rows, _ = frame.shape
    nb = blocks - 2
    tile = nb * length
    low = lanes((rows, length)) < half
    for part in (0, 1):
        left = from_left[part]
        right = from_right[part]
        for b in range(blocks):
            value = acc[part, b]
            if b == 0:
                value = value + left
            if b == 1:
                value = value + jnp.where(low, left, 0.0)
            if b == nb:
                value = value + jnp.where(low, 0.0, right)
            if b == nb + 1:
                value = value + right
            where = b - 1 if 0 < b <= nb else nb
            extra = jnp.concatenate(
                [
                    from_up[part, where],
                    jnp.zeros((rows - 2 * length, length), jnp.float32),
                    from_down[part, where],
                ],
                axis=0,
            )
            work[part, b] = frame[part, b] + (value + extra) * inverse[b]
    add_gradients(work, total, probe, amps, offsets, counts, tables)
    own = pl.ds(half, tile)
    low = lanes((half, length)) < half
    for part in (0, 1):
        for b in range(nb):
            field[part, b] = work[part, b + 1, own, :]
        for b in range(blocks):
            sums[part, b] = total[part, b, own, :]
        for strip, start in ((to_up, 0), (to_down, half + tile)):
            at = pl.ds(start, half)
            for b in range(nb):
                strip[part, b] = total[part, b + 1, at, :]
            strip[part, nb] = jnp.where(low, total[part, nb + 1, at, :], total[part, 0, at, :])


def pack_columns_end(ends, from_up, from_down, to_left, to_right):
    _, _, tile, length = ends.shape
    half = length // 2
    low = lanes((tile, length)) < half
    gap = jnp.zeros((tile - 2 * half, length), jnp.float32)
    values = []
    for part in (0, 1):
        extra = jnp.concatenate([from_up[part, 0], gap, from_down[part, 0]], axis=0)
        values.append([ends[part, 0] + extra, ends[part, 1] + extra])
    to_left[...] = jnp.where(low, swap(values[1][0], half), values[0][0])
    to_right[...] = jnp.where(low, values[0][1], swap(values[1][1], half))


def last_pass(field, sums, inverse, from_up, from_down, from_left, from_right, out):
    _, nb, tile, length = field.shape
    half = length // 2
    low = lanes((tile, length)) < half
    gap = jnp.zeros((tile - 2 * half, length), jnp.float32)
    for part in (0, 1):
        left = from_left[...]
        right = from_right[...]
        if part:
            left, right = swap(left, half), swap(right, half)
        for b in range(nb):
            value = sums[part, b + 1] + jnp.concatenate(
                [from_up[part, b], gap, from_down[part, b]], axis=0)
            if b == 0:
                value = value + jnp.where(low, left, 0.0)
            if b == nb - 1:
                value = value + jnp.where(low, 0.0, right)
            out[part, :, b * length:(b + 1) * length] = (
                field[part, b] + value * inverse[b + 1, pl.ds(half, tile), :])


def whole(memory_space=pltpu.VMEM):
    return pl.BlockSpec(memory_space=memory_space)


def call(body, shapes, n_scalar, n_array, scratch=(), cost=None):
    return pl.pallas_call(
        body,
        out_shape=[jax.ShapeDtypeStruct(shape, jnp.float32) for shape in shapes],
        in_specs=[whole(pltpu.SMEM)] * n_scalar + [whole()] * n_array,
        out_specs=[whole()] * len(shapes),
        scratch_shapes=[pltpu.VMEM(shape, jnp.float32) for shape in scratch],
        compiler_params=pltpu.CompilerParams(vmem_limit_bytes=VMEM_BYTES),
        cost_estimate=cost,
    )


def swap_ends(low, high, axis):
    count = lax.axis_size(axis)
    forward = [(i, i + 1) for i in range(count - 1)]
    backward = [(i + 1, i) for i in range(count - 1)]
    return lax.ppermute(high, axis, forward), lax.ppermute(low, axis, backward)


def shards(object_field, probe, amplitudes, offsets, counts):
    length = probe.shape[-1]
    half = length // 2
    tile = object_field.shape[1]
    npos = offsets.shape[2]
    nb = tile // length
    blocks = nb + 2
    rows = tile + 2 * half
    tables = jnp.asarray(dft_tables(length))

    column = pl.BlockSpec((2, tile, length), lambda i: (0, 0, 0))
    column_end = pl.BlockSpec((2, tile, length), lambda i: (0, 0, nb - 1))
    strip = (tile + 8, length)
    to_left, to_right = pl.pallas_call(
        pack_start,
        grid=(1,),
        out_shape=[jax.ShapeDtypeStruct(strip, jnp.float32)] * 2,
        in_specs=[whole(pltpu.SMEM)] * 2 + [column, column_end],
        out_specs=[pl.BlockSpec(strip, lambda i: (0, 0))] * 2,
    )(offsets, counts, object_field, object_field)
    from_left, from_right = swap_ends(to_left, to_right, "col")
    strip = (2 * (nb + 1) * half + 8, length)
    to_up, to_down = call(pack_rows_start, [strip] * 2, 0, 4)(
        object_field, from_left, from_right, to_left)
    from_up, from_down = swap_ends(to_up, to_down, "row")

    base = strip[0] - 8
    info = jnp.concatenate(
        [from_up[base + 1], from_up[base], from_up[base + 2],
         from_left[tile], to_left[tile], from_right[tile],
         from_down[base + 1], from_down[base], from_down[base + 2]]
    ).reshape(9, length)[:, :2 * npos + 1].astype(jnp.int32)

    full = (2, blocks, rows, length)
    frame, acc, to_left, to_right = call(
        first_pass, [full, full, (2, rows, length), (2, rows, length)], 2, 8,
    )(offsets, counts, object_field, from_left, from_right, from_up, from_down,
      probe, amplitudes, tables)
    from_left, from_right = swap_ends(to_left, to_right, "col")
    (inverse,) = call(
        light_pass, [(blocks, rows, length)], 1, 1,
        scratch=[(blocks + 2, rows + 2 * length, length)],
        cost=pl.CostEstimate(flops=40_000_000, bytes_accessed=4_000_000, transcendentals=0),
    )(info, probe)
    edge = (2, nb + 1, length, length)
    acc_block = (2, blocks, length, length)
    to_up, to_down = pl.pallas_call(
        pack_rows_mid,
        grid=(1,),
        out_shape=[jax.ShapeDtypeStruct(edge, jnp.float32)] * 2,
        in_specs=[
            pl.BlockSpec(acc_block, lambda i: (0, 0, 0, 0)),
            pl.BlockSpec(acc_block, lambda i: (0, 0, rows // length - 1, 0)),
            whole(), whole(),
        ],
        out_specs=[whole(), whole()],
        compiler_params=pltpu.CompilerParams(vmem_limit_bytes=VMEM_BYTES),
    )(acc, acc, from_left, from_right)
    from_up, from_down = swap_ends(to_up, to_down, "row")
    edge = (2, nb + 1, half, length)
    field, sums, to_up, to_down = call(
        second_pass, [(2, nb, tile, length), (2, blocks, tile, length), edge, edge], 2, 10,
        scratch=[full, full],
    )(offsets, counts, frame, acc, inverse, from_left, from_right, from_up, from_down,
      probe, amplitudes, tables)
    from_up, from_down = swap_ends(to_up, to_down, "row")
    ends = jnp.stack([sums[:, 0], sums[:, nb + 1]], axis=1)
    to_left, to_right = call(pack_columns_end, [(tile, length)] * 2, 0, 3)(
        ends, from_up[:, nb:], from_down[:, nb:])
    from_left, from_right = swap_ends(to_left, to_right, "col")
    (out,) = call(last_pass, [(2, tile, tile)], 0, 7)(
        field, sums, inverse, from_up, from_down, from_left, from_right)
    return out


def solution(mesh):
    placed = (
        P(None, "row", "col"),
        P(),
        P("row", "col", None, None, None),
        P("row", "col", None, None),
        P("row", "col"),
    )
    return jax.shard_map(
        shards, mesh=mesh, in_specs=placed, out_specs=P(None, "row", "col"), check_vma=False
    )
```

```python
import math

import jax
import jax.numpy as jnp
import numpy as np
from jax import lax
from jax.experimental import pallas as pl
from jax.experimental.pallas import tpu as pltpu
from jax.sharding import PartitionSpec as P

ITERS = 2
FLOOR = 0.25
VMEM_BYTES = 40 * 1024 * 1024


def split(value):
    high = value.astype(jnp.bfloat16)
    low = (value - high.astype(jnp.float32)).astype(jnp.bfloat16)
    return high, low


def dft_tables(length):
    index = np.arange(length)
    angle = (index[:, None] * index[None, :] % length) * (2.0 * math.pi / length)
    cosine = np.cos(angle) / math.sqrt(length)
    sine = np.sin(angle) / math.sqrt(length)
    ahead = np.block([[cosine, -sine], [sine, cosine]])
    parts = []
    for table in (ahead, ahead.T):
        high = table.astype(jnp.bfloat16)
        low = (table - high.astype(np.float64)).astype(jnp.bfloat16)
        parts += [high, low]
    return np.stack(parts)


def lanes(shape):
    return lax.broadcasted_iota(jnp.int32, shape, len(shape) - 1)


def swap(value, half):
    return pltpu.roll(value, half, value.ndim - 1)


def odd_place(axis):
    return lax.axis_index(axis) % 2 == 1


def by_pairs(axis, low, high):
    odd = odd_place(axis)
    return jnp.where(odd, high, low), jnp.where(odd, low, high)


def by_side(axis, first, second):
    odd = odd_place(axis)
    return jnp.where(odd, second, first), jnp.where(odd, first, second)


def times_right(rows, high, low):
    top, rest = split(rows)
    left = jnp.concatenate([top, top, rest], axis=1)
    right = jnp.concatenate([high, low, high], axis=0)
    return jnp.dot(left, right, preferred_element_type=jnp.float32)


def times_left(high, low, columns):
    top, rest = split(columns)
    left = jnp.concatenate([high, low, high], axis=1)
    right = jnp.concatenate([top, top, rest], axis=0)
    return jnp.dot(left, right, preferred_element_type=jnp.float32)


def beside(left, right):
    return jnp.concatenate([left, right], axis=1)


def above(top, bottom):
    return jnp.concatenate([top, bottom], axis=0)


def add_gradients(frame, acc, probe_ref, amps, offsets, counts, tables):
    length = probe_ref.shape[-1]
    half = length // 2
    npos = amps.shape[2]
    group = 4 if npos % 4 == 0 else 2 if npos % 2 == 0 else 1
    acc[...] = jnp.zeros_like(acc)
    count = counts[0, 0]
    lane = lanes((length, length))

    def place(slot):
        row = offsets[0, 0, 0, slot] + half
        col = offsets[0, 0, 1, slot] + length
        return row, col // length, col % length

    def exit_wave(slot):
        row, block, shift = place(slot)
        inside = lane >= shift
        window = [
            jnp.where(inside, frame[part, block, pl.ds(row, length), :],
                      frame[part, block + 1, pl.ds(row, length), :])
            for part in (0, 1)
        ]
        real = pltpu.roll(probe_ref[0], shift, 1)
        imag = pltpu.roll(probe_ref[1], shift, 1)
        return (real * window[0] - imag * window[1], real * window[1] + imag * window[0])

    def shrink(real, imag, slot):
        ratio = amps[0, 0, slot] * lax.rsqrt(real * real + imag * imag + FLOOR) - 1.0
        return real * ratio, imag * ratio

    def put(slot, back_r, back_i):
        row, block, shift = place(slot)
        weight = jnp.where(slot < count, 1.0, 0.0).astype(jnp.float32)
        real = pltpu.roll(probe_ref[0], shift, 1) * weight
        imag = pltpu.roll(probe_ref[1], shift, 1) * weight
        grads = (real * back_r + imag * back_i, real * back_i - imag * back_r)
        inside = lane >= shift
        for part in (0, 1):
            acc[part, block, pl.ds(row, length), :] += jnp.where(inside, grads[part], 0.0)
            acc[part, block + 1, pl.ds(row, length), :] += jnp.where(inside, 0.0, grads[part])

    def work(slots):
        waves = [exit_wave(slot) for slot in slots]
        rows = jnp.concatenate([beside(*wave) for wave in waves], axis=0)
        mid = times_right(rows, tables[0], tables[1])
        mids = [mid[k * length:(k + 1) * length] for k in range(len(slots))]
        columns = above(
            jnp.concatenate([m[:, :length] for m in mids], axis=1),
            jnp.concatenate([m[:, length:] for m in mids], axis=1),
        )
        far = times_left(tables[2], tables[3], columns)
        changes = [
            shrink(far[:length, k * length:(k + 1) * length],
                   far[length:, k * length:(k + 1) * length], slot)
            for k, slot in enumerate(slots)
        ]
        columns = above(
            jnp.concatenate([c[0] for c in changes], axis=1),
            jnp.concatenate([c[1] for c in changes], axis=1),
        )
        mid = times_left(tables[0], tables[1], columns)
        rows = jnp.concatenate(
            [
                beside(mid[:length, k * length:(k + 1) * length],
                       mid[length:, k * length:(k + 1) * length])
                for k in range(len(slots))
            ],
            axis=0,
        )
        back = times_right(rows, tables[2], tables[3])
        return [
            (back[k * length:(k + 1) * length, :length], back[k * length:(k + 1) * length, length:])
            for k in range(len(slots))
        ]

    def step(index, carry):
        slots = [index * group + k for k in range(group)]
        found = work(slots)
        for slot, (back_r, back_i) in zip(slots, found):
            put(slot, back_r, back_i)
        return carry

    lax.fori_loop(0, (count + group - 1) // group, step, 0)


def start_pass(offsets, counts, field, tile_out, cols_a, cols_b, rows_a, rows_b):
    _, nb, tile, length = tile_out.shape
    half = length // 2
    npos = offsets.shape[3]
    low = lanes((tile, length)) < half
    last = (nb - 1) * length
    to_left = jnp.where(low, field[0, :, :length], swap(field[1, :, :length], half))
    to_right = jnp.where(low, swap(field[1, :, last:], half), field[0, :, last:])
    cols_a[:tile], cols_b[:tile] = by_pairs("col", to_left, to_right)
    spot = lanes((8, length))
    info = jnp.where(spot == 2 * npos, counts[0, 0], 0)
    info = jnp.where(spot == 2 * npos + 1, lax.axis_index("row"), info)
    info = jnp.where(spot == 2 * npos + 2, lax.axis_index("col"), info)
    for k in range(npos):
        info = jnp.where(spot == k, offsets[0, 0, 0, k], info)
        info = jnp.where(spot == npos + k, offsets[0, 0, 1, k], info)
    info = info.astype(jnp.float32)
    cols_a[tile:] = info
    cols_b[tile:] = info
    for part in (0, 1):
        for b in range(nb):
            value = field[part, :, b * length:(b + 1) * length]
            tile_out[part, b] = value
            at = pl.ds((part * nb + b) * half, half)
            rows_a[at, :], rows_b[at, :] = by_pairs("row", value[:half], value[tile - half:])
    rows_a[2 * nb * half:] = info
    rows_b[2 * nb * half:] = info


def start_corners(cols_a, cols_b, corners_a, corners_b):
    length = cols_a.shape[1]
    half = length // 2
    tile = cols_a.shape[0] - 8
    low = lanes((tile, length)) < half
    left, right = by_side("col", cols_a[:tile], cols_b[:tile])
    for part in (0, 1):
        if part:
            left, right = swap(left, half), swap(right, half)
        value = jnp.where(low, right, left)
        at = pl.ds(part * half, half)
        corners_a[at, :], corners_b[at, :] = by_pairs("row", value[:half], value[tile - half:])
    first = lax.broadcasted_iota(jnp.int32, (8, length), 0) == 0
    info = jnp.where(first, cols_a[tile:], cols_b[tile:])
    corners_a[2 * half:] = info
    corners_b[2 * half:] = info


def first_pass(offsets, counts, field, cols_a, cols_b, rows_a, rows_b, corners_a, corners_b,
               probe, amps, tables, frame, acc, sums_a, sums_b, edges_a, edges_b):
    _, nb, tile, length = field.shape
    half = length // 2
    rows = tile + 2 * half
    own = pl.ds(half, tile)
    left, right = by_side("col", cols_a[:tile], cols_b[:tile])
    top = pl.ds(0, half)
    bottom = pl.ds(half + tile, half)
    for part in (0, 1):
        for b in range(nb):
            frame[part, b + 1, own, :] = field[part, b]
            at = pl.ds((part * nb + b) * half, half)
            frame[part, b + 1, top, :], frame[part, b + 1, bottom, :] = by_side(
                "row", rows_a[at, :], rows_b[at, :])
        frame[part, 0, own, :] = swap(left, half) if part else left
        frame[part, nb + 1, own, :] = swap(right, half) if part else right
        at = pl.ds(part * half, half)
        ends = by_side("row", corners_a[at, :], corners_b[at, :])
        for block in (0, nb + 1):
            frame[part, block, top, :], frame[part, block, bottom, :] = ends
    add_gradients(frame, acc, probe, amps, offsets, counts, tables)
    low = lanes((rows, length)) < half
    for part in (0, 1):
        sums_a[part], sums_b[part] = by_pairs(
            "col",
            jnp.where(low, acc[part, 1], acc[part, 0]),
            jnp.where(low, acc[part, nb + 1], acc[part, nb]),
        )
        for b in range(nb + 1):
            value = acc[part, b + 1] if b < nb else jnp.where(low, acc[part, nb + 1], acc[part, 0])
            edges_a[part, b], edges_b[part, b] = by_pairs(
                "row", value[:length], value[rows - length:])


def middle_corners(sums_a, sums_b, corners_a, corners_b):
    _, rows, length = sums_a.shape
    for part in (0, 1):
        sides = by_side("col", sums_a[part], sums_b[part])
        for side in (0, 1):
            corners_a[part, side], corners_b[part, side] = by_pairs(
                "row", sides[side][:length], sides[side][rows - length:])


def light_pass(info, probe, inverse, light):
    length = probe.shape[-1]
    half = length // 2
    blocks, rows, _ = inverse.shape
    nb = blocks - 2
    tile = nb * length
    npos = (info.shape[1] - 3) // 2
    light[...] = jnp.zeros_like(light)
    lane = lanes((length, length))
    my_row = lax.axis_index("row")
    my_col = lax.axis_index("col")

    def one_tile(index, carry):
        down = (info[index, 2 * npos + 1] - my_row) * tile
        across = (info[index, 2 * npos + 2] - my_col) * tile

        def one(slot, carry):
            row = info[index, slot] + half + down
            col = info[index, npos + slot] + length + across

            @pl.when((row > -length) & (row < rows) & (col > half - length)
                     & (col < length + tile + half))
            def _():
                start = row + length
                block = (col + length) // length
                shift = (col + length) % length
                real = pltpu.roll(probe[0], shift, 1)
                imag = pltpu.roll(probe[1], shift, 1)
                power = real * real + imag * imag
                inside = lane >= shift
                light[block, pl.ds(start, length), :] += jnp.where(inside, power, 0.0)
                light[block + 1, pl.ds(start, length), :] += jnp.where(inside, 0.0, power)

            return carry

        return lax.fori_loop(0, info[index, 2 * npos], one, carry)

    lax.fori_loop(0, info.shape[0], one_tile, 0)
    spot = lax.broadcasted_iota(jnp.int32, (rows, length), 0)
    keep_from = jnp.where(my_row > 0, 0, half)
    keep_to = jnp.where(my_row < lax.axis_size("row") - 1, rows, rows - half)
    kept = (spot >= keep_from) & (spot < keep_to)
    for b in range(blocks):
        value = 1.0 / (light[b + 1, pl.ds(length, rows), :] + 1.0)
        keep = kept
        if b == 0:
            keep = keep & (my_col > 0)
        if b == nb + 1:
            keep = keep & (my_col < lax.axis_size("col") - 1)
        inverse[b] = jnp.where(keep, value, 0.0)


def second_pass(offsets, counts, frame, acc, inverse, sums_a, sums_b, edges_a, edges_b,
                corners_a, corners_b, probe, amps, tables,
                field, sums, rows_a, rows_b, work, total):
    length = probe.shape[-1]
    half = length // 2
    _, blocks, rows, _ = frame.shape
    nb = blocks - 2
    tile = nb * length
    low = lanes((rows, length)) < half
    near = lanes((length, length)) < half
    gap = jnp.zeros((rows - 2 * length, length), jnp.float32)
    for part in (0, 1):
        left, right = by_side("col", sums_a[part], sums_b[part])
        edges = [by_side("row", edges_a[part, b], edges_b[part, b]) for b in range(nb + 1)]
        corners = [by_side("row", corners_a[part, side], corners_b[part, side]) for side in (0, 1)]
        ends = []
        for k in (0, 1):
            add = edges[:nb]
            add = [pair[k] for pair in add]
            add[0] = add[0] + jnp.where(near, corners[0][k], 0.0)
            add[nb - 1] = add[nb - 1] + jnp.where(near, 0.0, corners[1][k])
            add = [edges[nb][k] + corners[0][k]] + add + [edges[nb][k] + corners[1][k]]
            ends.append(add)
        for b in range(blocks):
            value = acc[part, b] + above(above(ends[0][b], gap), ends[1][b])
            if b == 0:
                value = value + left
            if b == 1:
                value = value + jnp.where(low, left, 0.0)
            if b == nb:
                value = value + jnp.where(low, 0.0, right)
            if b == nb + 1:
                value = value + right
            work[part, b] = frame[part, b] + value * inverse[b]
    add_gradients(work, total, probe, amps, offsets, counts, tables)
    own = pl.ds(half, tile)
    near = lanes((half, length)) < half
    top = pl.ds(0, half)
    bottom = pl.ds(half + tile, half)
    for part in (0, 1):
        for b in range(nb):
            field[part, b] = work[part, b + 1, own, :]
        for b in range(blocks):
            sums[part, b] = total[part, b, own, :]
        for b in range(nb + 1):
            ends = [
                total[part, b + 1, at, :] if b < nb
                else jnp.where(near, total[part, nb + 1, at, :], total[part, 0, at, :])
                for at in (top, bottom)
            ]
            rows_a[part, b], rows_b[part, b] = by_pairs("row", *ends)


def end_columns(sums, rows_a, rows_b, cols_a, cols_b):
    _, blocks, tile, length = sums.shape
    half = length // 2
    nb = blocks - 2
    low = lanes((tile, length)) < half
    gap = jnp.zeros((tile - 2 * half, length), jnp.float32)
    values = []
    for part in (0, 1):
        up, down = by_side("row", rows_a[part, nb], rows_b[part, nb])
        extra = above(above(up, gap), down)
        values.append((sums[part, 0] + extra, sums[part, nb + 1] + extra))
    cols_a[...], cols_b[...] = by_pairs(
        "col",
        jnp.where(low, swap(values[1][0], half), values[0][0]),
        jnp.where(low, values[0][1], swap(values[1][1], half)),
    )


def last_pass(field, sums, inverse, rows_a, rows_b, cols_a, cols_b, out):
    _, nb, tile, length = field.shape
    half = length // 2
    low = lanes((tile, length)) < half
    gap = jnp.zeros((tile - 2 * half, length), jnp.float32)
    left, right = by_side("col", cols_a[...], cols_b[...])
    for part in (0, 1):
        if part:
            left, right = swap(left, half), swap(right, half)
        for b in range(nb):
            up, down = by_side("row", rows_a[part, b], rows_b[part, b])
            value = sums[part, b + 1] + above(above(up, gap), down)
            if b == 0:
                value = value + jnp.where(low, left, 0.0)
            if b == nb - 1:
                value = value + jnp.where(low, 0.0, right)
            out[part, :, b * length:(b + 1) * length] = (
                field[part, b] + value * inverse[b + 1, pl.ds(half, tile), :])


def whole(memory_space=pltpu.VMEM):
    return pl.BlockSpec(memory_space=memory_space)


def call(body, shapes, n_scalar, n_array, scratch=(), cost=None):
    return pl.pallas_call(
        body,
        out_shape=[jax.ShapeDtypeStruct(shape, jnp.float32) for shape in shapes],
        in_specs=[whole(pltpu.SMEM)] * n_scalar + [whole()] * n_array,
        out_specs=[whole()] * len(shapes),
        scratch_shapes=[pltpu.VMEM(shape, jnp.float32) for shape in scratch],
        compiler_params=pltpu.CompilerParams(vmem_limit_bytes=VMEM_BYTES),
        cost_estimate=cost,
    )


def swap_pairs(first, second, axis):
    count = lax.axis_size(axis)
    got = []
    for value, start in ((first, 1), (second, 0)):
        pairs = [(i, i + 1) for i in range(start, count - 1, 2)]
        got.append(lax.ppermute(value, axis, pairs + [(b, a) for a, b in pairs]))
    return got


def shards(object_field, probe, amplitudes, offsets, counts):
    length = probe.shape[-1]
    half = length // 2
    tile = object_field.shape[1]
    npos = offsets.shape[2]
    nb = tile // length
    blocks = nb + 2
    rows = tile + 2 * half
    tables = jnp.asarray(dft_tables(length))
    offsets = jnp.swapaxes(offsets, 2, 3)

    strip = (tile + 8, length)
    edge = (2 * nb * half + 8, length)
    field, cols_a, cols_b, rows_a, rows_b = call(
        start_pass, [(2, nb, tile, length), strip, strip, edge, edge], 2, 1,
    )(offsets, counts, object_field)
    mine = cols_a
    cols_a, cols_b = swap_pairs(cols_a, cols_b, "col")
    rows_a, rows_b = swap_pairs(rows_a, rows_b, "row")
    corner = (2 * half + 8, length)
    corners_a, corners_b = call(start_corners, [corner, corner], 0, 2)(cols_a, cols_b)
    corners_a, corners_b = swap_pairs(corners_a, corners_b, "row")
    info = jnp.stack(
        [mine[tile], cols_a[tile], cols_b[tile], rows_a[-8], rows_b[-8],
         corners_a[-8], corners_a[-7], corners_b[-8], corners_b[-7]]
    )[:, :2 * npos + 3].astype(jnp.int32)

    full = (2, blocks, rows, length)
    strip = (2, rows, length)
    edge = (2, nb + 1, length, length)
    frame, acc, sums_a, sums_b, edges_a, edges_b = call(
        first_pass, [full, full, strip, strip, edge, edge], 2, 10,
    )(offsets, counts, field, cols_a, cols_b, rows_a, rows_b, corners_a, corners_b,
      probe, amplitudes, tables)
    sums_a, sums_b = swap_pairs(sums_a, sums_b, "col")
    edges_a, edges_b = swap_pairs(edges_a, edges_b, "row")
    (inverse,) = call(
        light_pass, [(blocks, rows, length)], 1, 1,
        scratch=[(blocks + 2, rows + 2 * length, length)],
        cost=pl.CostEstimate(flops=40_000_000, bytes_accessed=4_000_000, transcendentals=0),
    )(info, probe)
    corner = (2, 2, length, length)
    corners_a, corners_b = call(middle_corners, [corner, corner], 0, 2)(sums_a, sums_b)
    corners_a, corners_b = swap_pairs(corners_a, corners_b, "row")

    edge = (2, nb + 1, half, length)
    field, sums, rows_a, rows_b = call(
        second_pass, [(2, nb, tile, length), (2, blocks, tile, length), edge, edge], 2, 12,
        scratch=[full, full],
    )(offsets, counts, frame, acc, inverse, sums_a, sums_b, edges_a, edges_b,
      corners_a, corners_b, probe, amplitudes, tables)
    rows_a, rows_b = swap_pairs(rows_a, rows_b, "row")
    strip = (tile, length)
    cols_a, cols_b = call(end_columns, [strip, strip], 0, 3)(sums, rows_a, rows_b)
    cols_a, cols_b = swap_pairs(cols_a, cols_b, "col")
    (out,) = call(last_pass, [(2, tile, tile)], 0, 7)(
        field, sums, inverse, rows_a, rows_b, cols_a, cols_b)
    return out


def solution(mesh):
    placed = (
        P(None, "row", "col"),
        P(),
        P("row", "col", None, None, None),
        P("row", "col", None, None),
        P("row", "col"),
    )
    return jax.shard_map(
        shards, mesh=mesh, in_specs=placed, out_specs=P(None, "row", "col"), check_vma=False
    )
```

```python
import math

import jax
import jax.numpy as jnp
import numpy as np
from jax import lax
from jax.experimental import pallas as pl
from jax.experimental.pallas import tpu as pltpu
from jax.sharding import PartitionSpec as P

ITERS = 2
FLOOR = 0.25
VMEM_BYTES = 16 * 1024 * 1024
GROUP = 4


def split(value):
    high = value.astype(jnp.bfloat16)
    low = (value - high.astype(jnp.float32)).astype(jnp.bfloat16)
    return high, low


def dft_tables(length):
    index = np.arange(length)
    angle = (index[:, None] * index[None, :] % length) * (2.0 * math.pi / length)
    cosine = np.cos(angle) / math.sqrt(length)
    sine = np.sin(angle) / math.sqrt(length)
    ahead = np.block([[cosine, -sine], [sine, cosine]])
    parts = []
    for table in (ahead, ahead.T):
        high = table.astype(jnp.bfloat16)
        low = (table - high.astype(np.float64)).astype(jnp.bfloat16)
        parts += [high, low]
    return np.stack(parts)


def lanes(shape):
    return lax.broadcasted_iota(jnp.int32, shape, len(shape) - 1)


def swap(value, half):
    return pltpu.roll(value, half, value.ndim - 1)


def odd_place(axis):
    return lax.axis_index(axis) % 2 == 1


def by_pairs(axis, low, high):
    odd = odd_place(axis)
    return jnp.where(odd, high, low), jnp.where(odd, low, high)


def by_side(axis, first, second):
    odd = odd_place(axis)
    return jnp.where(odd, second, first), jnp.where(odd, first, second)


def times_right(rows, high, low):
    top, rest = split(rows)
    left = jnp.concatenate([top, top, rest], axis=1)
    right = jnp.concatenate([high, low, high], axis=0)
    return jnp.dot(left, right, preferred_element_type=jnp.float32)


def times_left(high, low, columns):
    top, rest = split(columns)
    left = jnp.concatenate([high, low, high], axis=1)
    right = jnp.concatenate([top, top, rest], axis=0)
    return jnp.dot(left, right, preferred_element_type=jnp.float32)


def beside(left, right):
    return jnp.concatenate([left, right], axis=1)


def above(top, bottom):
    return jnp.concatenate([top, bottom], axis=0)


def choose(chosen, offsets, counts, tile, length, inner):
    def look(slot, found):
        row = offsets[0, 0, 0, slot]
        col = offsets[0, 0, 1, slot]
        last = tile - length
        inside = (row >= 0) & (row <= last) & (col >= 0) & (col <= last)
        chosen[found] = slot
        return found + jnp.where(inside == inner, 1, 0)

    found = lax.fori_loop(0, counts[0, 0], look, 0)
    filler = chosen[0]
    for k in range(GROUP):
        chosen[found + k] = filler
    return found


def add_gradients(frame, acc, probe_ref, amps, offsets, tables, chosen, found, first_row, first_col):
    length = probe_ref.shape[-1]
    blocks = frame.shape[1]
    lane = lanes((length, length))

    def place(slot):
        row = offsets[0, 0, 0, slot] - first_row
        col = offsets[0, 0, 1, slot] - first_col
        block = col // length
        return row, block, jnp.minimum(block + 1, blocks - 1), col % length

    def exit_wave(slot):
        row, block, after, shift = place(slot)
        inside = lane >= shift
        window = [
            jnp.where(inside, frame[part, block, pl.ds(row, length), :],
                      frame[part, after, pl.ds(row, length), :])
            for part in (0, 1)
        ]
        real = pltpu.roll(probe_ref[0], shift, 1)
        imag = pltpu.roll(probe_ref[1], shift, 1)
        return (real * window[0] - imag * window[1], real * window[1] + imag * window[0])

    def shrink(real, imag, slot):
        ratio = amps[0, 0, slot] * lax.rsqrt(real * real + imag * imag + FLOOR) - 1.0
        return real * ratio, imag * ratio

    def put(slot, live, back_r, back_i):
        row, block, after, shift = place(slot)
        weight = jnp.where(live, 1.0, 0.0).astype(jnp.float32)
        real = pltpu.roll(probe_ref[0], shift, 1) * weight
        imag = pltpu.roll(probe_ref[1], shift, 1) * weight
        grads = (real * back_r + imag * back_i, real * back_i - imag * back_r)
        inside = lane >= shift
        for part in (0, 1):
            acc[part, block, pl.ds(row, length), :] += jnp.where(inside, grads[part], 0.0)
            acc[part, after, pl.ds(row, length), :] += jnp.where(inside, 0.0, grads[part])

    def work(slots):
        waves = [exit_wave(slot) for slot in slots]
        rows = jnp.concatenate([beside(*wave) for wave in waves], axis=0)
        mid = times_right(rows, tables[0], tables[1])
        mids = [mid[k * length:(k + 1) * length] for k in range(len(slots))]
        columns = above(
            jnp.concatenate([m[:, :length] for m in mids], axis=1),
            jnp.concatenate([m[:, length:] for m in mids], axis=1),
        )
        far = times_left(tables[2], tables[3], columns)
        changes = [
            shrink(far[:length, k * length:(k + 1) * length],
                   far[length:, k * length:(k + 1) * length], slot)
            for k, slot in enumerate(slots)
        ]
        columns = above(
            jnp.concatenate([c[0] for c in changes], axis=1),
            jnp.concatenate([c[1] for c in changes], axis=1),
        )
        mid = times_left(tables[0], tables[1], columns)
        rows = jnp.concatenate(
            [
                beside(mid[:length, k * length:(k + 1) * length],
                       mid[length:, k * length:(k + 1) * length])
                for k in range(len(slots))
            ],
            axis=0,
        )
        back = times_right(rows, tables[2], tables[3])
        return [
            (back[k * length:(k + 1) * length, :length], back[k * length:(k + 1) * length, length:])
            for k in range(len(slots))
        ]

    def step(index, carry):
        places = [index * GROUP + k for k in range(GROUP)]
        slots = [chosen[at] for at in places]
        gradients = work(slots)
        for at, slot, (back_r, back_i) in zip(places, slots, gradients):
            put(slot, at < found, back_r, back_i)
        return carry

    lax.fori_loop(0, (found + GROUP - 1) // GROUP, step, 0)


def start_pass(offsets_from, counts, field, tile_out, cols_a, cols_b, rows_a, rows_b, offsets, sems):
    _, nb, tile, length = tile_out.shape
    half = length // 2
    npos = offsets.shape[3]
    copies = {
        b: pltpu.make_async_copy(
            field.at[:, :, b * length:(b + 1) * length], tile_out.at[:, b], sems.at[b])
        for b in range(nb)
    }
    listed = pltpu.make_async_copy(offsets_from, offsets, sems.at[nb])
    listed.start()
    order = sorted(range(nb), key=lambda b: 0 < b < nb - 1)
    for b in order:
        copies[b].start()
    listed.wait()
    spot = lanes((8, length))
    info = jnp.where(spot == 2 * npos, counts[0, 0], 0)
    info = jnp.where(spot == 2 * npos + 1, lax.axis_index("row"), info)
    info = jnp.where(spot == 2 * npos + 2, lax.axis_index("col"), info)
    for k in range(npos):
        info = jnp.where(spot == k, offsets[0, 0, 0, k], info)
        info = jnp.where(spot == npos + k, offsets[0, 0, 1, k], info)
    info = info.astype(jnp.float32)
    cols_a[tile:] = info
    cols_b[tile:] = info
    rows_a[2 * nb * half:] = info
    rows_b[2 * nb * half:] = info
    for b in order:
        copies[b].wait()
    low = lanes((tile, length)) < half
    first = (tile_out[0, 0], tile_out[1, 0])
    last = (tile_out[0, nb - 1], tile_out[1, nb - 1])
    to_left = jnp.where(low, first[0], swap(first[1], half))
    to_right = jnp.where(low, swap(last[1], half), last[0])
    cols_a[:tile], cols_b[:tile] = by_pairs("col", to_left, to_right)
    for part in (0, 1):
        for b in range(nb):
            at = pl.ds((part * nb + b) * half, half)
            rows_a[at, :], rows_b[at, :] = by_pairs(
                "row", tile_out[part, b, :half], tile_out[part, b, tile - half:])


def inner_pass(offsets, counts, field, probe, amps, tables, acc, chosen):
    tile, length = field.shape[2:]
    acc[...] = jnp.zeros_like(acc)
    found = choose(chosen, offsets, counts, tile, length, True)
    add_gradients(field, acc, probe, amps, offsets, tables, chosen, found, 0, 0)


def start_corners(cols_a, cols_b, after, corners_a, corners_b):
    length = cols_a.shape[1]
    half = length // 2
    tile = cols_a.shape[0] - 8
    low = lanes((tile, length)) < half
    left, right = by_side("col", cols_a[:tile], cols_b[:tile])
    for part in (0, 1):
        if part:
            left, right = swap(left, half), swap(right, half)
        value = jnp.where(low, right, left)
        at = pl.ds(part * half, half)
        corners_a[at, :], corners_b[at, :] = by_pairs("row", value[:half], value[tile - half:])
    first = lax.broadcasted_iota(jnp.int32, (8, length), 0) == 0
    info = jnp.where(first, cols_a[tile:], cols_b[tile:])
    corners_a[2 * half:] = info
    corners_b[2 * half:] = info


def first_pass(offsets, counts, field, inner, cols_a, cols_b, rows_a, rows_b, corners_a, corners_b,
               probe, amps, tables, frame, acc, sums_a, sums_b, edges_a, edges_b, chosen):
    _, nb, tile, length = field.shape
    half = length // 2
    rows = tile + 2 * half
    own = pl.ds(half, tile)
    left, right = by_side("col", cols_a[:tile], cols_b[:tile])
    top = pl.ds(0, half)
    bottom = pl.ds(half + tile, half)
    for part in (0, 1):
        for b in range(nb):
            frame[part, b + 1, own, :] = field[part, b]
            at = pl.ds((part * nb + b) * half, half)
            frame[part, b + 1, top, :], frame[part, b + 1, bottom, :] = by_side(
                "row", rows_a[at, :], rows_b[at, :])
        frame[part, 0, own, :] = swap(left, half) if part else left
        frame[part, nb + 1, own, :] = swap(right, half) if part else right
        at = pl.ds(part * half, half)
        ends = by_side("row", corners_a[at, :], corners_b[at, :])
        for block in (0, nb + 1):
            frame[part, block, top, :], frame[part, block, bottom, :] = ends
    empty = jnp.zeros((half, length), jnp.float32)
    for part in (0, 1):
        for b in range(nb + 2):
            acc[part, b, top, :] = empty
            acc[part, b, bottom, :] = empty
            acc[part, b, own, :] = (
                inner[part, b - 1] if 0 < b <= nb else jnp.zeros((tile, length), jnp.float32))
    found = choose(chosen, offsets, counts, tile, length, False)
    add_gradients(frame, acc, probe, amps, offsets, tables, chosen, found, -half, -length)
    low = lanes((rows, length)) < half
    for part in (0, 1):
        sums_a[part], sums_b[part] = by_pairs(
            "col",
            jnp.where(low, acc[part, 1], acc[part, 0]),
            jnp.where(low, acc[part, nb + 1], acc[part, nb]),
        )
        for b in range(nb + 1):
            value = acc[part, b + 1] if b < nb else jnp.where(low, acc[part, nb + 1], acc[part, 0])
            edges_a[part, b], edges_b[part, b] = by_pairs(
                "row", value[:length], value[rows - length:])


def middle_corners(sums_a, sums_b, after, corners_a, corners_b):
    _, rows, length = sums_a.shape
    for part in (0, 1):
        sides = by_side("col", sums_a[part], sums_b[part])
        for side in (0, 1):
            corners_a[part, side], corners_b[part, side] = by_pairs(
                "row", sides[side][:length], sides[side][rows - length:])


def light_pass(info, probe, after, inverse, light):
    length = probe.shape[-1]
    half = length // 2
    blocks, rows, _ = inverse.shape
    nb = blocks - 2
    tile = nb * length
    npos = (info.shape[1] - 3) // 2
    light[...] = jnp.zeros_like(light)
    lane = lanes((length, length))
    my_row = lax.axis_index("row")
    my_col = lax.axis_index("col")

    def one_tile(index, carry):
        down = (info[index, 2 * npos + 1] - my_row) * tile
        across = (info[index, 2 * npos + 2] - my_col) * tile

        def one(slot, carry):
            row = info[index, slot] + half + down
            col = info[index, npos + slot] + length + across

            @pl.when((row > -length) & (row < rows) & (col > half - length)
                     & (col < length + tile + half))
            def _():
                start = row + length
                block = (col + length) // length
                shift = (col + length) % length
                real = pltpu.roll(probe[0], shift, 1)
                imag = pltpu.roll(probe[1], shift, 1)
                power = real * real + imag * imag
                inside = lane >= shift
                light[block, pl.ds(start, length), :] += jnp.where(inside, power, 0.0)
                light[block + 1, pl.ds(start, length), :] += jnp.where(inside, 0.0, power)

            return carry

        return lax.fori_loop(0, info[index, 2 * npos], one, carry)

    lax.fori_loop(0, info.shape[0], one_tile, 0)
    spot = lax.broadcasted_iota(jnp.int32, (rows, length), 0)
    keep_from = jnp.where(my_row > 0, 0, half)
    keep_to = jnp.where(my_row < lax.axis_size("row") - 1, rows, rows - half)
    kept = (spot >= keep_from) & (spot < keep_to)
    for b in range(blocks):
        value = 1.0 / (light[b + 1, pl.ds(length, rows), :] + 1.0)
        keep = kept
        if b == 0:
            keep = keep & (my_col > 0)
        if b == nb + 1:
            keep = keep & (my_col < lax.axis_size("col") - 1)
        inverse[b] = jnp.where(keep, value, 0.0)


def second_pass(offsets, counts, frame, acc, inverse, sums_a, sums_b, edges_a, edges_b,
                corners_a, corners_b, probe, amps, tables,
                field, sums, rows_a, rows_b, work, total, chosen):
    length = probe.shape[-1]
    half = length // 2
    _, blocks, rows, _ = frame.shape
    nb = blocks - 2
    tile = nb * length
    low = lanes((rows, length)) < half
    near = lanes((length, length)) < half
    gap = jnp.zeros((rows - 2 * length, length), jnp.float32)
    for part in (0, 1):
        left, right = by_side("col", sums_a[part], sums_b[part])
        edges = [by_side("row", edges_a[part, b], edges_b[part, b]) for b in range(nb + 1)]
        corners = [by_side("row", corners_a[part, side], corners_b[part, side]) for side in (0, 1)]
        ends = []
        for k in (0, 1):
            add = edges[:nb]
            add = [pair[k] for pair in add]
            add[0] = add[0] + jnp.where(near, corners[0][k], 0.0)
            add[nb - 1] = add[nb - 1] + jnp.where(near, 0.0, corners[1][k])
            add = [edges[nb][k] + corners[0][k]] + add + [edges[nb][k] + corners[1][k]]
            ends.append(add)
        for b in range(blocks):
            value = acc[part, b] + above(above(ends[0][b], gap), ends[1][b])
            if b == 0:
                value = value + left
            if b == 1:
                value = value + jnp.where(low, left, 0.0)
            if b == nb:
                value = value + jnp.where(low, 0.0, right)
            if b == nb + 1:
                value = value + right
            work[part, b] = frame[part, b] + value * inverse[b]
    total[...] = jnp.zeros_like(total)
    found = choose(chosen, offsets, counts, tile, length, False)
    add_gradients(work, total, probe, amps, offsets, tables, chosen, found, -half, -length)
    own = pl.ds(half, tile)
    near = lanes((half, length)) < half
    top = pl.ds(0, half)
    bottom = pl.ds(half + tile, half)
    for part in (0, 1):
        for b in range(nb):
            field[part, b] = work[part, b + 1, own, :]
        for b in range(blocks):
            sums[part, b] = total[part, b, own, :]
        for b in range(nb + 1):
            ends = [
                total[part, b + 1, at, :] if b < nb
                else jnp.where(near, total[part, nb + 1, at, :], total[part, 0, at, :])
                for at in (top, bottom)
            ]
            rows_a[part, b], rows_b[part, b] = by_pairs("row", *ends)


def end_columns(sums, rows_a, rows_b, cols_a, cols_b):
    _, blocks, tile, length = sums.shape
    half = length // 2
    nb = blocks - 2
    low = lanes((tile, length)) < half
    gap = jnp.zeros((tile - 2 * half, length), jnp.float32)
    values = []
    for part in (0, 1):
        up, down = by_side("row", rows_a[part, nb], rows_b[part, nb])
        extra = above(above(up, gap), down)
        values.append((sums[part, 0] + extra, sums[part, nb + 1] + extra))
    cols_a[...], cols_b[...] = by_pairs(
        "col",
        jnp.where(low, swap(values[1][0], half), values[0][0]),
        jnp.where(low, values[0][1], swap(values[1][1], half)),
    )


def last_pass(field, sums, inner, inverse, rows_a, rows_b, cols_a, cols_b, out):
    _, nb, tile, length = field.shape
    half = length // 2
    low = lanes((tile, length)) < half
    gap = jnp.zeros((tile - 2 * half, length), jnp.float32)
    left, right = by_side("col", cols_a[...], cols_b[...])
    for part in (0, 1):
        if part:
            left, right = swap(left, half), swap(right, half)
        for b in range(nb):
            up, down = by_side("row", rows_a[part, b], rows_b[part, b])
            value = sums[part, b + 1] + inner[part, b] + above(above(up, gap), down)
            if b == 0:
                value = value + jnp.where(low, left, 0.0)
            if b == nb - 1:
                value = value + jnp.where(low, 0.0, right)
            out[part, :, b * length:(b + 1) * length] = (
                field[part, b] + value * inverse[b + 1, pl.ds(half, tile), :])


def whole(memory_space=pltpu.VMEM):
    return pl.BlockSpec(memory_space=memory_space)


def call(body, shapes, places, scratch=(), cost=None):
    return pl.pallas_call(
        body,
        out_shape=[jax.ShapeDtypeStruct(shape, jnp.float32) for shape in shapes],
        in_specs=[whole({"s": pltpu.SMEM, "v": pltpu.VMEM, "a": pl.ANY, "h": pltpu.HBM}[p]) for p in places],
        out_specs=[whole()] * len(shapes),
        scratch_shapes=list(scratch),
        compiler_params=pltpu.CompilerParams(vmem_limit_bytes=VMEM_BYTES),
        cost_estimate=cost,
    )


def swap_pairs(first, second, axis):
    count = lax.axis_size(axis)
    got = []
    for value, start in ((first, 1), (second, 0)):
        pairs = [(i, i + 1) for i in range(start, count - 1, 2)]
        got.append(lax.ppermute(value, axis, pairs + [(b, a) for a, b in pairs]))
    return got


def shards(object_field, probe, amplitudes, offsets, counts):
    length = probe.shape[-1]
    half = length // 2
    tile = object_field.shape[1]
    npos = offsets.shape[2]
    nb = tile // length
    blocks = nb + 2
    rows = tile + 2 * half
    tables = jnp.asarray(dft_tables(length))
    offsets = jnp.swapaxes(offsets, 2, 3)

    def cost(positions):
        steps = 4 * 3 * 2 * length * (2 * length) ** 2
        return pl.CostEstimate(
            flops=positions * steps, bytes_accessed=8_000_000,
            transcendentals=positions * length * length)

    memory = pltpu.VMEM
    listed = pltpu.SMEM((npos + GROUP,), jnp.int32)
    own = (2, nb, tile, length)
    strip = (tile + 8, length)
    edge = (2 * nb * half + 8, length)
    field, cols_a, cols_b, rows_a, rows_b = call(
        start_pass, [own, strip, strip, edge, edge], "hsh",
        [pltpu.SMEM((1, 1, 2, npos), jnp.int32), pltpu.SemaphoreType.DMA((nb + 1,))],
    )(offsets, counts, object_field)
    mine = cols_a
    cols_a, cols_b = swap_pairs(cols_a, cols_b, "col")
    rows_a, rows_b = swap_pairs(rows_a, rows_b, "row")
    (inner,) = call(inner_pass, [own], "ssvvvv", [listed], cost(npos))(
        offsets, counts, field, probe, amplitudes, tables)
    corner = (2 * half + 8, length)
    corners_a, corners_b = call(start_corners, [corner, corner], "vva")(cols_a, cols_b, inner)
    corners_a, corners_b = swap_pairs(corners_a, corners_b, "row")
    info = jnp.stack(
        [mine[tile], cols_a[tile], cols_b[tile], rows_a[-8], rows_b[-8],
         corners_a[-8], corners_a[-7], corners_b[-8], corners_b[-7]]
    )[:, :2 * npos + 3].astype(jnp.int32)

    full = (2, blocks, rows, length)
    strip = (2, rows, length)
    edge = (2, nb + 1, length, length)
    frame, acc, sums_a, sums_b, edges_a, edges_b = call(
        first_pass, [full, full, strip, strip, edge, edge], "ss" + 11 * "v", [listed], cost(npos),
    )(offsets, counts, field, inner, cols_a, cols_b, rows_a, rows_b, corners_a, corners_b,
      probe, amplitudes, tables)
    light = memory((blocks + 2, rows + 2 * length, length), jnp.float32)
    (inverse,) = call(
        light_pass, [(blocks, rows, length)], "sva", [light], cost(npos // 2),
    )(info, probe, acc)
    sums_a, sums_b = swap_pairs(sums_a, sums_b, "col")
    edges_a, edges_b = swap_pairs(edges_a, edges_b, "row")
    corner = (2, 2, length, length)
    corners_a, corners_b = call(middle_corners, [corner, corner], "vva")(sums_a, sums_b, inverse)
    corners_a, corners_b = swap_pairs(corners_a, corners_b, "row")

    edge = (2, nb + 1, half, length)
    field, sums, rows_a, rows_b = call(
        second_pass, [own, (2, blocks, tile, length), edge, edge], "ss" + 12 * "v",
        [memory(full, jnp.float32), memory(full, jnp.float32), listed], cost(npos),
    )(offsets, counts, frame, acc, inverse, sums_a, sums_b, edges_a, edges_b,
      corners_a, corners_b, probe, amplitudes, tables)
    rows_a, rows_b = swap_pairs(rows_a, rows_b, "row")
    (inner,) = call(inner_pass, [own], "ssvvvv", [listed], cost(npos))(
        offsets, counts, field, probe, amplitudes, tables)
    strip = (tile, length)
    cols_a, cols_b = call(end_columns, [strip, strip], "vvv")(sums, rows_a, rows_b)
    cols_a, cols_b = swap_pairs(cols_a, cols_b, "col")
    (out,) = call(last_pass, [(2, tile, tile)], 8 * "v")(
        field, sums, inner, inverse, rows_a, rows_b, cols_a, cols_b)
    return out


def solution(mesh):
    placed = (
        P(None, "row", "col"),
        P(),
        P("row", "col", None, None, None),
        P("row", "col", None, None),
        P("row", "col"),
    )
    return jax.shard_map(
        shards, mesh=mesh, in_specs=placed, out_specs=P(None, "row", "col"), check_vma=False
    )
```

```python
import functools
import math

import jax
import jax.numpy as jnp
import numpy as np
from jax import lax
from jax.experimental import pallas as pl
from jax.experimental.pallas import tpu as pltpu
from jax.sharding import PartitionSpec as P

ITERS = 2
FLOOR = 0.25
VMEM_BYTES = 16 * 1024 * 1024
GROUP = 4


def split(value):
    high = value.astype(jnp.bfloat16)
    low = (value - high.astype(jnp.float32)).astype(jnp.bfloat16)
    return high, low


def dft_tables(length):
    index = np.arange(length)
    angle = (index[:, None] * index[None, :] % length) * (2.0 * math.pi / length)
    cosine = np.cos(angle) / math.sqrt(length)
    sine = np.sin(angle) / math.sqrt(length)
    ahead = np.block([[cosine, -sine], [sine, cosine]])
    parts = []
    for table in (ahead, ahead.T):
        high = table.astype(jnp.bfloat16)
        low = (table - high.astype(np.float64)).astype(jnp.bfloat16)
        parts += [high, low]
    return np.stack(parts)


def lanes(shape):
    return lax.broadcasted_iota(jnp.int32, shape, len(shape) - 1)


def swap(value, half):
    return pltpu.roll(value, half, value.ndim - 1)


def odd_place(axis):
    return lax.axis_index(axis) % 2 == 1


def by_pairs(axis, low, high):
    odd = odd_place(axis)
    return jnp.where(odd, high, low), jnp.where(odd, low, high)


def by_side(axis, first, second):
    odd = odd_place(axis)
    return jnp.where(odd, second, first), jnp.where(odd, first, second)


def times_right(rows, high, low):
    top, rest = split(rows)
    left = jnp.concatenate([top, top, rest], axis=1)
    right = jnp.concatenate([high, low, high], axis=0)
    return jnp.dot(left, right, preferred_element_type=jnp.float32)


def times_left(high, low, columns):
    top, rest = split(columns)
    left = jnp.concatenate([high, low, high], axis=1)
    right = jnp.concatenate([top, top, rest], axis=0)
    return jnp.dot(left, right, preferred_element_type=jnp.float32)


def beside(left, right):
    return jnp.concatenate([left, right], axis=1)


def above(top, bottom):
    return jnp.concatenate([top, bottom], axis=0)


def choose(chosen, offsets, counts, tile, length, wanted):
    last = tile - length
    half = length // 2

    def look(slot, found):
        row = offsets[0, 0, 0, slot]
        col = offsets[0, 0, 1, slot]
        taken = wanted(
            mid_row=(row >= half) & (row <= last - half),
            mid_col=(col >= half) & (col <= last - half),
            cross_row=(row < 0) | (row > last),
            cross_col=(col < 0) | (col > last),
        )
        chosen[found] = slot
        return found + jnp.where(taken, 1, 0)

    found = lax.fori_loop(0, counts[0, 0], look, 0)
    filler = chosen[0]
    for k in range(GROUP):
        chosen[found + k] = filler
    return found


def add_gradients(frame, acc, probe_ref, amps, offsets, tables, chosen, found, first_row, first_col,
                  skip=0):
    length = probe_ref.shape[-1]
    blocks = frame.shape[1]
    lane = lanes((length, length))

    def place(slot):
        row = offsets[0, 0, 0, slot] - first_row
        col = offsets[0, 0, 1, slot] - first_col
        block = col // length
        return row, block, jnp.minimum(block + 1, blocks - 1), col % length

    def exit_wave(slot):
        row, block, after, shift = place(slot)
        inside = lane >= shift
        window = [
            jnp.where(inside, frame[part, block, pl.ds(row + skip, length), :],
                      frame[part, after, pl.ds(row + skip, length), :])
            for part in (0, 1)
        ]
        real = pltpu.roll(probe_ref[0], shift, 1)
        imag = pltpu.roll(probe_ref[1], shift, 1)
        return (real * window[0] - imag * window[1], real * window[1] + imag * window[0])

    def shrink(real, imag, slot):
        ratio = amps[0, 0, slot] * lax.rsqrt(real * real + imag * imag + FLOOR) - 1.0
        return real * ratio, imag * ratio

    def put(slot, live, back_r, back_i):
        row, block, after, shift = place(slot)
        weight = jnp.where(live, 1.0, 0.0).astype(jnp.float32)
        real = pltpu.roll(probe_ref[0], shift, 1) * weight
        imag = pltpu.roll(probe_ref[1], shift, 1) * weight
        grads = (real * back_r + imag * back_i, real * back_i - imag * back_r)
        inside = lane >= shift
        for part in (0, 1):
            acc[part, block, pl.ds(row, length), :] += jnp.where(inside, grads[part], 0.0)
            acc[part, after, pl.ds(row, length), :] += jnp.where(inside, 0.0, grads[part])

    def work(slots):
        waves = [exit_wave(slot) for slot in slots]
        rows = jnp.concatenate([beside(*wave) for wave in waves], axis=0)
        mid = times_right(rows, tables[0], tables[1])
        mids = [mid[k * length:(k + 1) * length] for k in range(len(slots))]
        columns = above(
            jnp.concatenate([m[:, :length] for m in mids], axis=1),
            jnp.concatenate([m[:, length:] for m in mids], axis=1),
        )
        far = times_left(tables[2], tables[3], columns)
        changes = [
            shrink(far[:length, k * length:(k + 1) * length],
                   far[length:, k * length:(k + 1) * length], slot)
            for k, slot in enumerate(slots)
        ]
        columns = above(
            jnp.concatenate([c[0] for c in changes], axis=1),
            jnp.concatenate([c[1] for c in changes], axis=1),
        )
        mid = times_left(tables[0], tables[1], columns)
        rows = jnp.concatenate(
            [
                beside(mid[:length, k * length:(k + 1) * length],
                       mid[length:, k * length:(k + 1) * length])
                for k in range(len(slots))
            ],
            axis=0,
        )
        back = times_right(rows, tables[2], tables[3])
        return [
            (back[k * length:(k + 1) * length, :length], back[k * length:(k + 1) * length, length:])
            for k in range(len(slots))
        ]

    def step(index, carry):
        places = [index * GROUP + k for k in range(GROUP)]
        slots = [chosen[at] for at in places]
        gradients = work(slots)
        for at, slot, (back_r, back_i) in zip(places, slots, gradients):
            put(slot, at < found, back_r, back_i)
        return carry

    lax.fori_loop(0, (found + GROUP - 1) // GROUP, step, 0)


def start_pass(offsets_from, counts, field, tile_out, cols_a, cols_b, rows_a, rows_b, offsets, sems):
    _, nb, tile, length = tile_out.shape
    half = length // 2
    npos = offsets.shape[3]
    copies = {
        b: pltpu.make_async_copy(
            field.at[:, :, b * length:(b + 1) * length], tile_out.at[:, b], sems.at[b])
        for b in range(nb)
    }
    listed = pltpu.make_async_copy(offsets_from, offsets, sems.at[nb])
    listed.start()
    order = sorted(range(nb), key=lambda b: 0 < b < nb - 1)
    for b in order:
        copies[b].start()
    listed.wait()
    spot = lanes((8, length))
    info = jnp.where(spot == 2 * npos, counts[0, 0], 0)
    info = jnp.where(spot == 2 * npos + 1, lax.axis_index("row"), info)
    info = jnp.where(spot == 2 * npos + 2, lax.axis_index("col"), info)
    for k in range(npos):
        info = jnp.where(spot == k, offsets[0, 0, 0, k], info)
        info = jnp.where(spot == npos + k, offsets[0, 0, 1, k], info)
    info = info.astype(jnp.float32)
    cols_a[tile:] = info
    cols_b[tile:] = info
    rows_a[2 * nb * half:] = info
    rows_b[2 * nb * half:] = info
    for b in order:
        copies[b].wait()
    low = lanes((tile, length)) < half
    first = (tile_out[0, 0], tile_out[1, 0])
    last = (tile_out[0, nb - 1], tile_out[1, nb - 1])
    to_left = jnp.where(low, first[0], swap(first[1], half))
    to_right = jnp.where(low, swap(last[1], half), last[0])
    cols_a[:tile], cols_b[:tile] = by_pairs("col", to_left, to_right)
    for part in (0, 1):
        for b in range(nb):
            at = pl.ds((part * nb + b) * half, half)
            rows_a[at, :], rows_b[at, :] = by_pairs(
                "row", tile_out[part, b, :half], tile_out[part, b, tile - half:])


def start_corners(cols_a, cols_b, corners_a, corners_b):
    length = cols_a.shape[1]
    half = length // 2
    tile = cols_a.shape[0] - 8
    low = lanes((tile, length)) < half
    left, right = by_side("col", cols_a[:tile], cols_b[:tile])
    for part in (0, 1):
        if part:
            left, right = swap(left, half), swap(right, half)
        value = jnp.where(low, right, left)
        at = pl.ds(part * half, half)
        corners_a[at, :], corners_b[at, :] = by_pairs("row", value[:half], value[tile - half:])
    first = lax.broadcasted_iota(jnp.int32, (8, length), 0) == 0
    info = jnp.where(first, cols_a[tile:], cols_b[tile:])
    corners_a[2 * half:] = info
    corners_b[2 * half:] = info


def first_pass(offsets, counts, field, cols_a, cols_b, rows_a, rows_b, corners_a, corners_b,
               probe, amps, tables, frame, acc, sums_a, sums_b, chosen):
    _, nb, tile, length = field.shape
    half = length // 2
    rows = tile + 2 * half
    own = pl.ds(half, tile)
    left, right = by_side("col", cols_a[:tile], cols_b[:tile])
    top = pl.ds(0, half)
    bottom = pl.ds(half + tile, half)
    for part in (0, 1):
        for b in range(nb):
            frame[part, b + 1, own, :] = field[part, b]
            at = pl.ds((part * nb + b) * half, half)
            frame[part, b + 1, top, :], frame[part, b + 1, bottom, :] = by_side(
                "row", rows_a[at, :], rows_b[at, :])
        frame[part, 0, own, :] = swap(left, half) if part else left
        frame[part, nb + 1, own, :] = swap(right, half) if part else right
        at = pl.ds(part * half, half)
        ends = by_side("row", corners_a[at, :], corners_b[at, :])
        for block in (0, nb + 1):
            frame[part, block, top, :], frame[part, block, bottom, :] = ends
    acc[...] = jnp.zeros_like(acc)
    found = choose(chosen, offsets, counts, tile, length, lambda mid_col, **_: ~mid_col)
    add_gradients(frame, acc, probe, amps, offsets, tables, chosen, found, -half, -length)
    low = lanes((rows, length)) < half
    for part in (0, 1):
        sums_a[part], sums_b[part] = by_pairs(
            "col",
            jnp.where(low, acc[part, 1], acc[part, 0]),
            jnp.where(low, acc[part, nb + 1], acc[part, nb]),
        )


def first_rest(offsets, counts, frame, acc_from, probe, amps, tables,
               acc, edges_a, edges_b, chosen):
    _, blocks, rows, length = frame.shape
    half = length // 2
    nb = blocks - 2
    acc[...] = acc_from[...]
    found = choose(chosen, offsets, counts, nb * length, length, lambda mid_col, **_: mid_col)
    add_gradients(frame, acc, probe, amps, offsets, tables, chosen, found, -half, -length)
    low = lanes((length, length)) < half
    for part in (0, 1):
        for b in range(nb + 1):
            ends = [
                acc[part, b + 1, at, :] if b < nb
                else jnp.where(low, acc[part, nb + 1, at, :], acc[part, 0, at, :])
                for at in (pl.ds(0, length), pl.ds(rows - length, length))
            ]
            edges_a[part, b], edges_b[part, b] = by_pairs("row", *ends)


def middle_corners(sums_a, sums_b, after, corners_a, corners_b):
    _, rows, length = sums_a.shape
    for part in (0, 1):
        sides = by_side("col", sums_a[part], sums_b[part])
        for side in (0, 1):
            corners_a[part, side], corners_b[part, side] = by_pairs(
                "row", sides[side][:length], sides[side][rows - length:])


def light_pass(mine, cols_a, cols_b, rows_a, rows_b, corners_a, corners_b, probe, after,
               inverse, light, listed, sems, *, npos):
    length = probe.shape[-1]
    half = length // 2
    blocks, rows, _ = inverse.shape
    nb = blocks - 2
    tile = nb * length
    sources = (mine, cols_a, cols_b, rows_a, rows_b, corners_a, corners_b)
    copies = [
        pltpu.make_async_copy(
            source.at[pl.ds(source.shape[0] - 8, 8), :], listed.at[pl.ds(8 * k, 8), :], sems.at[k])
        for k, source in enumerate(sources)
    ]
    for copy in copies:
        copy.start()
    light[...] = jnp.zeros_like(light)
    for copy in copies:
        copy.wait()
    lane = lanes((length, length))
    my_row = lax.axis_index("row")
    my_col = lax.axis_index("col")

    def number(line, place):
        return listed[line, place].astype(jnp.int32)

    def one_tile(index, carry):
        line = jnp.where(index < len(sources), 8 * index, 8 * (index - 2) + 1)
        down = (number(line, 2 * npos + 1) - my_row) * tile
        across = (number(line, 2 * npos + 2) - my_col) * tile

        def one(slot, carry):
            row = number(line, slot) + half + down
            col = number(line, npos + slot) + length + across

            @pl.when((row > -length) & (row < rows) & (col > half - length)
                     & (col < length + tile + half))
            def _():
                start = row + length
                block = (col + length) // length
                shift = (col + length) % length
                real = pltpu.roll(probe[0], shift, 1)
                imag = pltpu.roll(probe[1], shift, 1)
                power = real * real + imag * imag
                inside = lane >= shift
                light[block, pl.ds(start, length), :] += jnp.where(inside, power, 0.0)
                light[block + 1, pl.ds(start, length), :] += jnp.where(inside, 0.0, power)

            return carry

        return lax.fori_loop(0, number(line, 2 * npos), one, carry)

    lax.fori_loop(0, len(sources) + 2, one_tile, 0)
    spot = lax.broadcasted_iota(jnp.int32, (rows, length), 0)
    keep_from = jnp.where(my_row > 0, 0, half)
    keep_to = jnp.where(my_row < lax.axis_size("row") - 1, rows, rows - half)
    kept = (spot >= keep_from) & (spot < keep_to)
    for b in range(blocks):
        value = 1.0 / (light[b + 1, pl.ds(length, rows), :] + 1.0)
        keep = kept
        if b == 0:
            keep = keep & (my_col > 0)
        if b == nb + 1:
            keep = keep & (my_col < lax.axis_size("col") - 1)
        inverse[b] = jnp.where(keep, value, 0.0)


def update_pass(offsets, counts, frame, acc, inverse, sums_a, sums_b, probe, amps, tables,
                work, total, chosen):
    _, blocks, rows, length = frame.shape
    half = length // 2
    nb = blocks - 2
    low = lanes((rows, length)) < half
    for part in (0, 1):
        left, right = by_side("col", sums_a[part], sums_b[part])
        for b in range(blocks):
            value = acc[part, b]
            if b == 0:
                value = value + left
            if b == 1:
                value = value + jnp.where(low, left, 0.0)
            if b == nb:
                value = value + jnp.where(low, 0.0, right)
            if b == nb + 1:
                value = value + right
            work[part, b] = frame[part, b] + value * inverse[b]
    total[...] = jnp.zeros_like(total)
    found = choose(chosen, offsets, counts, nb * length, length, lambda mid_row, **_: mid_row)
    add_gradients(work, total, probe, amps, offsets, tables, chosen, found, -half, -length)


def second_pass(offsets, counts, work_from, total_from, inverse, edges_a, edges_b,
                corners_a, corners_b, probe, amps, tables,
                work, sums, rows_a, rows_b, total, chosen):
    _, blocks, rows, length = work.shape
    half = length // 2
    nb = blocks - 2
    tile = nb * length
    near = lanes((length, length)) < half
    top = pl.ds(0, length)
    bottom = pl.ds(rows - length, length)
    middle = pl.ds(length, rows - 2 * length)
    for part in (0, 1):
        edges = [by_side("row", edges_a[part, b], edges_b[part, b]) for b in range(nb + 1)]
        corners = [by_side("row", corners_a[part, side], corners_b[part, side]) for side in (0, 1)]
        for k, at in enumerate((top, bottom)):
            add = [edges[nb][k] + corners[0][k]]
            add += [edges[b][k] for b in range(nb)]
            add += [edges[nb][k] + corners[1][k]]
            add[1] = add[1] + jnp.where(near, corners[0][k], 0.0)
            add[nb] = add[nb] + jnp.where(near, 0.0, corners[1][k])
            for b in range(blocks):
                work[part, b, at, :] = work_from[part, b, at, :] + add[b] * inverse[b, at, :]
        for b in range(blocks):
            work[part, b, middle, :] = work_from[part, b, middle, :]
    total[...] = total_from[...]
    found = choose(chosen, offsets, counts, tile, length, lambda cross_row, **_: cross_row)
    add_gradients(work, total, probe, amps, offsets, tables, chosen, found, -half, -length)
    own = pl.ds(half, tile)
    near = lanes((half, length)) < half
    top = pl.ds(0, half)
    bottom = pl.ds(half + tile, half)
    for part in (0, 1):
        for b in range(blocks):
            sums[part, b] = total[part, b, own, :]
        for b in range(nb + 1):
            ends = [
                total[part, b + 1, at, :] if b < nb
                else jnp.where(near, total[part, nb + 1, at, :], total[part, 0, at, :])
                for at in (top, bottom)
            ]
            rows_a[part, b], rows_b[part, b] = by_pairs("row", *ends)


def sides_pass(offsets, counts, work, sums_from, probe, amps, tables, sums, chosen):
    _, blocks, tile, length = sums.shape
    sums[...] = sums_from[...]
    found = choose(
        chosen, offsets, counts, tile, length,
        lambda mid_row, cross_row, cross_col, **_: ~mid_row & ~cross_row & cross_col)
    add_gradients(work, sums, probe, amps, offsets, tables, chosen, found, 0, -length, length // 2)


def inner_pass(offsets, counts, work, probe, amps, tables, sums, chosen):
    _, blocks, tile, length = sums.shape
    sums[...] = jnp.zeros_like(sums)
    found = choose(
        chosen, offsets, counts, tile, length,
        lambda mid_row, cross_row, cross_col, **_: ~mid_row & ~cross_row & ~cross_col)
    add_gradients(work, sums, probe, amps, offsets, tables, chosen, found, 0, -length, length // 2)


def end_columns(sums, rows_a, rows_b, cols_a, cols_b):
    _, blocks, tile, length = sums.shape
    half = length // 2
    nb = blocks - 2
    low = lanes((tile, length)) < half
    gap = jnp.zeros((tile - 2 * half, length), jnp.float32)
    values = []
    for part in (0, 1):
        up, down = by_side("row", rows_a[part, nb], rows_b[part, nb])
        extra = above(above(up, gap), down)
        values.append((sums[part, 0] + extra, sums[part, nb + 1] + extra))
    cols_a[...], cols_b[...] = by_pairs(
        "col",
        jnp.where(low, swap(values[1][0], half), values[0][0]),
        jnp.where(low, values[0][1], swap(values[1][1], half)),
    )


def last_pass(work, sums, inner, inverse, rows_a, rows_b, cols_a, cols_b, out):
    _, blocks, tile, length = sums.shape
    half = length // 2
    nb = blocks - 2
    low = lanes((tile, length)) < half
    own = pl.ds(half, tile)
    gap = jnp.zeros((tile - 2 * half, length), jnp.float32)
    left, right = by_side("col", cols_a[...], cols_b[...])
    for part in (0, 1):
        if part:
            left, right = swap(left, half), swap(right, half)
        for b in range(nb):
            up, down = by_side("row", rows_a[part, b], rows_b[part, b])
            value = sums[part, b + 1] + inner[part, b + 1] + above(above(up, gap), down)
            if b == 0:
                value = value + jnp.where(low, left, 0.0)
            if b == nb - 1:
                value = value + jnp.where(low, 0.0, right)
            out[part, :, b * length:(b + 1) * length] = (
                work[part, b + 1, own, :] + value * inverse[b + 1, own, :])


def whole(memory_space=pltpu.VMEM):
    return pl.BlockSpec(memory_space=memory_space)


def call(body, shapes, places, scratch=(), cost=None):
    return pl.pallas_call(
        body,
        out_shape=[jax.ShapeDtypeStruct(shape, jnp.float32) for shape in shapes],
        in_specs=[whole({"s": pltpu.SMEM, "v": pltpu.VMEM, "a": pl.ANY, "h": pltpu.HBM}[p]) for p in places],
        out_specs=[whole()] * len(shapes),
        scratch_shapes=list(scratch),
        compiler_params=pltpu.CompilerParams(vmem_limit_bytes=VMEM_BYTES),
        cost_estimate=cost,
    )


def swap_pairs(first, second, axis):
    count = lax.axis_size(axis)
    got = []
    for value, start in ((first, 1), (second, 0)):
        pairs = [(i, i + 1) for i in range(start, count - 1, 2)]
        got.append(lax.ppermute(value, axis, pairs + [(b, a) for a, b in pairs]))
    return got


def shards(object_field, probe, amplitudes, offsets, counts):
    length = probe.shape[-1]
    half = length // 2
    tile = object_field.shape[1]
    npos = offsets.shape[2]
    nb = tile // length
    blocks = nb + 2
    rows = tile + 2 * half
    tables = jnp.asarray(dft_tables(length))
    offsets = jnp.swapaxes(offsets, 2, 3)

    def cost(positions):
        steps = 4 * 3 * 2 * length * (2 * length) ** 2
        return pl.CostEstimate(
            flops=positions * steps, bytes_accessed=8_000_000,
            transcendentals=positions * length * length)

    memory = pltpu.VMEM
    chosen = pltpu.SMEM((npos + GROUP,), jnp.int32)
    strip = (tile + 8, length)
    edge = (2 * nb * half + 8, length)
    field, cols_a, cols_b, rows_a, rows_b = call(
        start_pass, [(2, nb, tile, length), strip, strip, edge, edge], "asa",
        [pltpu.SMEM((1, 1, 2, npos), jnp.int32), pltpu.SemaphoreType.DMA((nb + 1,))],
    )(offsets, counts, object_field)
    mine = cols_a
    cols_a, cols_b = swap_pairs(cols_a, cols_b, "col")
    rows_a, rows_b = swap_pairs(rows_a, rows_b, "row")
    corner = (2 * half + 8, length)
    corners_a, corners_b = call(start_corners, [corner, corner], "vv")(cols_a, cols_b)
    corners_a, corners_b = swap_pairs(corners_a, corners_b, "row")

    full = (2, blocks, rows, length)
    strip = (2, rows, length)
    frame, acc, sums_a, sums_b = call(
        first_pass, [full, full, strip, strip], "ss" + 10 * "v", [chosen], cost(npos),
    )(offsets, counts, field, cols_a, cols_b, rows_a, rows_b, corners_a, corners_b,
      probe, amplitudes, tables)
    sums_a, sums_b = swap_pairs(sums_a, sums_b, "col")
    edge = (2, nb + 1, length, length)
    acc, edges_a, edges_b = call(
        first_rest, [full, edge, edge], "ss" + 5 * "v", [chosen], cost(npos // 2),
    )(offsets, counts, frame, acc, probe, amplitudes, tables)
    edges_a, edges_b = swap_pairs(edges_a, edges_b, "row")
    (inverse,) = call(
        functools.partial(light_pass, npos=npos), [(blocks, rows, length)], 8 * "v" + "a",
        [memory((blocks + 2, rows + 2 * length, length), jnp.float32),
         pltpu.SMEM((7 * 8, length), jnp.float32), pltpu.SemaphoreType.DMA((7,))],
        cost(npos // 2),
    )(mine, cols_a, cols_b, rows_a, rows_b, corners_a, corners_b, probe, acc)
    corner = (2, 2, length, length)
    corners_a, corners_b = call(middle_corners, [corner, corner], "vva")(sums_a, sums_b, inverse)
    corners_a, corners_b = swap_pairs(corners_a, corners_b, "row")

    work, total = call(update_pass, [full, full], "ss" + 8 * "v", [chosen], cost(npos // 2))(
        offsets, counts, frame, acc, inverse, sums_a, sums_b, probe, amplitudes, tables)
    edge = (2, nb + 1, half, length)
    tall = (2, blocks, tile, length)
    work, sums, rows_a, rows_b = call(
        second_pass, [full, tall, edge, edge], "ss" + 10 * "v",
        [memory(full, jnp.float32), chosen], cost(npos // 2),
    )(offsets, counts, work, total, inverse, edges_a, edges_b, corners_a, corners_b,
      probe, amplitudes, tables)
    rows_a, rows_b = swap_pairs(rows_a, rows_b, "row")
    (sums,) = call(sides_pass, [tall], "ss" + 5 * "v", [chosen], cost(npos // 4))(
        offsets, counts, work, sums, probe, amplitudes, tables)
    strip = (tile, length)
    cols_a, cols_b = call(end_columns, [strip, strip], "vvv")(sums, rows_a, rows_b)
    cols_a, cols_b = swap_pairs(cols_a, cols_b, "col")
    (inner,) = call(inner_pass, [tall], "ss" + 4 * "v", [chosen], cost(npos // 2))(
        offsets, counts, work, probe, amplitudes, tables)
    (out,) = call(last_pass, [(2, tile, tile)], 8 * "v")(
        work, sums, inner, inverse, rows_a, rows_b, cols_a, cols_b)
    return out


def solution(mesh):
    placed = (
        P(None, "row", "col"),
        P(),
        P("row", "col", None, None, None),
        P("row", "col", None, None),
        P("row", "col"),
    )
    return jax.shard_map(
        shards, mesh=mesh, in_specs=placed, out_specs=P(None, "row", "col"), check_vma=False
    )
```

```python
import functools
import math

import jax
import jax.numpy as jnp
import numpy as np
from jax import lax
from jax.experimental import pallas as pl
from jax.experimental.pallas import tpu as pltpu
from jax.sharding import PartitionSpec as P

ITERS = 2
FLOOR = 0.25
VMEM_BYTES = 16 * 1024 * 1024
GROUP = 4


def split(value):
    high = value.astype(jnp.bfloat16)
    low = (value - high.astype(jnp.float32)).astype(jnp.bfloat16)
    return high, low


def dft_tables(length):
    index = np.arange(length)
    angle = (index[:, None] * index[None, :] % length) * (2.0 * math.pi / length)
    cosine = np.cos(angle) / math.sqrt(length)
    sine = np.sin(angle) / math.sqrt(length)
    ahead = np.block([[cosine, -sine], [sine, cosine]])
    parts = []
    for table in (ahead, ahead.T):
        high = table.astype(jnp.bfloat16)
        low = (table - high.astype(np.float64)).astype(jnp.bfloat16)
        parts += [high, low]
    return np.stack(parts)


def lanes(shape):
    return lax.broadcasted_iota(jnp.int32, shape, len(shape) - 1)


def swap(value, half):
    return pltpu.roll(value, half, value.ndim - 1)


def odd_place(axis):
    return lax.axis_index(axis) % 2 == 1


def by_pairs(axis, low, high):
    odd = odd_place(axis)
    return jnp.where(odd, high, low), jnp.where(odd, low, high)


def by_side(axis, first, second):
    odd = odd_place(axis)
    return jnp.where(odd, second, first), jnp.where(odd, first, second)


def times_right(rows, high, low):
    top, rest = split(rows)
    left = jnp.concatenate([top, top, rest], axis=1)
    right = jnp.concatenate([high, low, high], axis=0)
    return jnp.dot(left, right, preferred_element_type=jnp.float32)


def times_left(high, low, columns):
    top, rest = split(columns)
    left = jnp.concatenate([high, low, high], axis=1)
    right = jnp.concatenate([top, top, rest], axis=0)
    return jnp.dot(left, right, preferred_element_type=jnp.float32)


def beside(left, right):
    return jnp.concatenate([left, right], axis=1)


def above(top, bottom):
    return jnp.concatenate([top, bottom], axis=0)


def choose(chosen, offsets, counts, tile, length, wanted):
    last = tile - length
    half = length // 2

    def look(slot, found):
        row = offsets[0, 0, 0, slot]
        col = offsets[0, 0, 1, slot]
        taken = wanted(
            mid_row=(row >= half) & (row <= last - half),
            mid_col=(col >= half) & (col <= last - half),
            cross_row=(row < 0) | (row > last),
            cross_col=(col < 0) | (col > last),
        )
        chosen[found] = slot
        return found + jnp.where(taken, 1, 0)

    found = lax.fori_loop(0, counts[0, 0], look, 0)
    filler = chosen[0]
    for k in range(GROUP):
        chosen[found + k] = filler
    return found


def add_gradients(frame, acc, probe_ref, amps, offsets, tables, chosen, found, first_row, first_col,
                  skip=0):
    length = probe_ref.shape[-1]
    blocks = frame.shape[1]
    lane = lanes((length, length))

    def place(slot):
        row = offsets[0, 0, 0, slot] - first_row
        col = offsets[0, 0, 1, slot] - first_col
        block = col // length
        return row, block, jnp.minimum(block + 1, blocks - 1), col % length

    def exit_wave(slot):
        row, block, after, shift = place(slot)
        inside = lane >= shift
        window = [
            jnp.where(inside, frame[part, block, pl.ds(row + skip, length), :],
                      frame[part, after, pl.ds(row + skip, length), :])
            for part in (0, 1)
        ]
        real = pltpu.roll(probe_ref[0], shift, 1)
        imag = pltpu.roll(probe_ref[1], shift, 1)
        return (real * window[0] - imag * window[1], real * window[1] + imag * window[0])

    def shrink(real, imag, slot):
        ratio = amps[0, 0, slot] * lax.rsqrt(real * real + imag * imag + FLOOR) - 1.0
        return real * ratio, imag * ratio

    def put(slot, live, back_r, back_i):
        row, block, after, shift = place(slot)
        weight = jnp.where(live, 1.0, 0.0).astype(jnp.float32)
        real = pltpu.roll(probe_ref[0], shift, 1) * weight
        imag = pltpu.roll(probe_ref[1], shift, 1) * weight
        grads = (real * back_r + imag * back_i, real * back_i - imag * back_r)
        inside = lane >= shift
        for part in (0, 1):
            acc[part, block, pl.ds(row, length), :] += jnp.where(inside, grads[part], 0.0)
            acc[part, after, pl.ds(row, length), :] += jnp.where(inside, 0.0, grads[part])

    def work(slots):
        waves = [exit_wave(slot) for slot in slots]
        rows = jnp.concatenate([beside(*wave) for wave in waves], axis=0)
        mid = times_right(rows, tables[0], tables[1])
        mids = [mid[k * length:(k + 1) * length] for k in range(len(slots))]
        columns = above(
            jnp.concatenate([m[:, :length] for m in mids], axis=1),
            jnp.concatenate([m[:, length:] for m in mids], axis=1),
        )
        far = times_left(tables[2], tables[3], columns)
        changes = [
            shrink(far[:length, k * length:(k + 1) * length],
                   far[length:, k * length:(k + 1) * length], slot)
            for k, slot in enumerate(slots)
        ]
        columns = above(
            jnp.concatenate([c[0] for c in changes], axis=1),
            jnp.concatenate([c[1] for c in changes], axis=1),
        )
        mid = times_left(tables[0], tables[1], columns)
        rows = jnp.concatenate(
            [
                beside(mid[:length, k * length:(k + 1) * length],
                       mid[length:, k * length:(k + 1) * length])
                for k in range(len(slots))
            ],
            axis=0,
        )
        back = times_right(rows, tables[2], tables[3])
        return [
            (back[k * length:(k + 1) * length, :length], back[k * length:(k + 1) * length, length:])
            for k in range(len(slots))
        ]

    def pairs(slots):
        return [slots[k:k + 2] for k in range(0, len(slots), 2)]

    def step(index, carry):
        places = [index * GROUP + k for k in range(GROUP)]
        slots = [chosen[at] for at in places]
        gradients = [found for pair in pairs(slots) for found in work(pair)]
        for at, slot, (back_r, back_i) in zip(places, slots, gradients):
            put(slot, at < found, back_r, back_i)
        return carry

    lax.fori_loop(0, (found + GROUP - 1) // GROUP, step, 0)


def start_pass(offsets_from, counts, field, tile_out, cols_a, cols_b, rows_a, rows_b, offsets, sems):
    _, nb, tile, length = tile_out.shape
    half = length // 2
    npos = offsets.shape[3]
    copies = {
        b: pltpu.make_async_copy(
            field.at[:, :, b * length:(b + 1) * length], tile_out.at[:, b], sems.at[b])
        for b in range(nb)
    }
    listed = pltpu.make_async_copy(offsets_from, offsets, sems.at[nb])
    listed.start()
    order = sorted(range(nb), key=lambda b: 0 < b < nb - 1)
    for b in order:
        copies[b].start()
    listed.wait()
    spot = lanes((8, length))
    info = jnp.zeros((8, length), jnp.int32)
    down = (lax.axis_index("row") + 1) * tile
    across = (lax.axis_index("col") + 1) * tile
    for k in range(npos):
        live = k < counts[0, 0]
        info = jnp.where(spot == k, jnp.where(live, offsets[0, 0, 0, k] + down, 0), info)
        info = jnp.where(spot == npos + k, jnp.where(live, offsets[0, 0, 1, k] + across, 0), info)
    info = info.astype(jnp.float32)
    cols_a[tile:] = info
    cols_b[tile:] = info
    rows_a[2 * nb * half:] = info
    rows_b[2 * nb * half:] = info
    for b in order:
        copies[b].wait()
    low = lanes((tile, length)) < half
    first = (tile_out[0, 0], tile_out[1, 0])
    last = (tile_out[0, nb - 1], tile_out[1, nb - 1])
    to_left = jnp.where(low, first[0], swap(first[1], half))
    to_right = jnp.where(low, swap(last[1], half), last[0])
    cols_a[:tile], cols_b[:tile] = by_pairs("col", to_left, to_right)
    for part in (0, 1):
        for b in range(nb):
            at = pl.ds((part * nb + b) * half, half)
            rows_a[at, :], rows_b[at, :] = by_pairs(
                "row", tile_out[part, b, :half], tile_out[part, b, tile - half:])


def start_corners(cols_a, cols_b, corners_a, corners_b):
    length = cols_a.shape[1]
    half = length // 2
    tile = cols_a.shape[0] - 8
    low = lanes((tile, length)) < half
    left, right = by_side("col", cols_a[:tile], cols_b[:tile])
    for part in (0, 1):
        if part:
            left, right = swap(left, half), swap(right, half)
        value = jnp.where(low, right, left)
        at = pl.ds(part * half, half)
        corners_a[at, :], corners_b[at, :] = by_pairs("row", value[:half], value[tile - half:])
    first = lax.broadcasted_iota(jnp.int32, (8, length), 0) == 0
    info = jnp.where(first, cols_a[tile:], cols_b[tile:])
    corners_a[2 * half:] = info
    corners_b[2 * half:] = info


def first_pass(offsets, counts, field, cols_a, cols_b, rows_a, rows_b, corners_a, corners_b,
               probe, amps, tables, frame, acc, sums_a, sums_b, chosen):
    _, nb, tile, length = field.shape
    half = length // 2
    rows = tile + 2 * half
    own = pl.ds(half, tile)
    left, right = by_side("col", cols_a[:tile], cols_b[:tile])
    top = pl.ds(0, half)
    bottom = pl.ds(half + tile, half)
    for part in (0, 1):
        for b in range(nb):
            frame[part, b + 1, own, :] = field[part, b]
            at = pl.ds((part * nb + b) * half, half)
            frame[part, b + 1, top, :], frame[part, b + 1, bottom, :] = by_side(
                "row", rows_a[at, :], rows_b[at, :])
        frame[part, 0, own, :] = swap(left, half) if part else left
        frame[part, nb + 1, own, :] = swap(right, half) if part else right
        at = pl.ds(part * half, half)
        ends = by_side("row", corners_a[at, :], corners_b[at, :])
        for block in (0, nb + 1):
            frame[part, block, top, :], frame[part, block, bottom, :] = ends
    acc[...] = jnp.zeros_like(acc)
    found = choose(chosen, offsets, counts, tile, length, lambda mid_col, **_: ~mid_col)
    add_gradients(frame, acc, probe, amps, offsets, tables, chosen, found, -half, -length)
    low = lanes((rows, length)) < half
    for part in (0, 1):
        sums_a[part], sums_b[part] = by_pairs(
            "col",
            jnp.where(low, acc[part, 1], acc[part, 0]),
            jnp.where(low, acc[part, nb + 1], acc[part, nb]),
        )


def first_rest(offsets, counts, frame, acc_from, probe, amps, tables,
               acc, edges_a, edges_b, chosen):
    _, blocks, rows, length = frame.shape
    half = length // 2
    nb = blocks - 2
    acc[...] = acc_from[...]
    found = choose(
        chosen, offsets, counts, nb * length, length,
        lambda mid_row, mid_col, **_: mid_col & ~mid_row)
    add_gradients(frame, acc, probe, amps, offsets, tables, chosen, found, -half, -length)
    low = lanes((length, length)) < half
    for part in (0, 1):
        for b in range(nb + 1):
            ends = [
                acc[part, b + 1, at, :] if b < nb
                else jnp.where(low, acc[part, nb + 1, at, :], acc[part, 0, at, :])
                for at in (pl.ds(0, length), pl.ds(rows - length, length))
            ]
            edges_a[part, b], edges_b[part, b] = by_pairs("row", *ends)


def middle_corners(sums_a, sums_b, after, corners_a, corners_b):
    _, rows, length = sums_a.shape
    for part in (0, 1):
        sides = by_side("col", sums_a[part], sums_b[part])
        for side in (0, 1):
            corners_a[part, side], corners_b[part, side] = by_pairs(
                "row", sides[side][:length], sides[side][rows - length:])


def light_pass(mine, cols_a, cols_b, rows_a, rows_b, corners_a, corners_b, probe, after,
               inverse, light, power, places, listed, sem, *, npos):
    length = probe.shape[-1]
    half = length // 2
    blocks, rows, _ = inverse.shape
    nb = blocks - 2
    tile = nb * length
    my_row = lax.axis_index("row")
    my_col = lax.axis_index("col")
    sources = (mine, cols_a, cols_b, rows_a, rows_b, corners_a, corners_b)
    for k, source in enumerate(sources):
        given = source[source.shape[0] - 8:, :].astype(jnp.int32)
        col = pltpu.roll(given, length - npos, 1) - (my_col + 1) * tile + 2 * length
        row = given - (my_row + 1) * tile + half + length
        near = (given > 0) & (row > 0) & (row < rows + length)
        near = near & (col > length - half) & (col < 2 * length + tile + half)
        places[pl.ds(8 * k, 8), :] = jnp.where(near, row * 4 * tile + col, 0)
    copy = pltpu.make_async_copy(places, listed, sem)
    copy.start()
    light[...] = jnp.zeros_like(light)
    power[...] = probe[0] * probe[0] + probe[1] * probe[1]
    lane = lanes((length, length))
    copy.wait()

    def one_tile(index, carry):
        line = jnp.where(index < len(sources), 8 * index, 8 * (index - 2) + 1)

        def one(slot, carry):
            place = listed[line, slot]

            @pl.when(place > 0)
            def _():
                start = place // (4 * tile)
                col = place % (4 * tile)
                block = col // length
                shift = col % length
                value = pltpu.roll(power[...], shift, 1)
                inside = lane >= shift
                light[block, pl.ds(start, length), :] += jnp.where(inside, value, 0.0)
                light[block + 1, pl.ds(start, length), :] += jnp.where(inside, 0.0, value)

            return carry

        return lax.fori_loop(0, npos, one, carry)

    lax.fori_loop(0, len(sources) + 2, one_tile, 0)
    spot = lax.broadcasted_iota(jnp.int32, (rows, length), 0)
    keep_from = jnp.where(my_row > 0, 0, half)
    keep_to = jnp.where(my_row < lax.axis_size("row") - 1, rows, rows - half)
    kept = (spot >= keep_from) & (spot < keep_to)
    for b in range(blocks):
        value = 1.0 / (light[b + 1, pl.ds(length, rows), :] + 1.0)
        keep = kept
        if b == 0:
            keep = keep & (my_col > 0)
        if b == nb + 1:
            keep = keep & (my_col < lax.axis_size("col") - 1)
        inverse[b] = jnp.where(keep, value, 0.0)


def update_pass(offsets, counts, frame, acc, inverse, sums_a, sums_b, probe, amps, tables,
                work, total, chosen):
    _, blocks, rows, length = frame.shape
    half = length // 2
    nb = blocks - 2
    work[...] = acc[...]
    found = choose(
        chosen, offsets, counts, nb * length, length,
        lambda mid_row, mid_col, **_: mid_col & mid_row)
    add_gradients(frame, work, probe, amps, offsets, tables, chosen, found, -half, -length)
    low = lanes((rows, length)) < half
    for part in (0, 1):
        left, right = by_side("col", sums_a[part], sums_b[part])
        for b in range(blocks):
            value = work[part, b]
            if b == 0:
                value = value + left
            if b == 1:
                value = value + jnp.where(low, left, 0.0)
            if b == nb:
                value = value + jnp.where(low, 0.0, right)
            if b == nb + 1:
                value = value + right
            work[part, b] = frame[part, b] + value * inverse[b]
    total[...] = jnp.zeros_like(total)
    found = choose(chosen, offsets, counts, nb * length, length, lambda mid_row, **_: mid_row)
    add_gradients(work, total, probe, amps, offsets, tables, chosen, found, -half, -length)


def second_pass(offsets, counts, work_from, total_from, inverse, edges_a, edges_b,
                corners_a, corners_b, probe, amps, tables,
                work, sums, rows_a, rows_b, total, chosen):
    _, blocks, rows, length = work.shape
    half = length // 2
    nb = blocks - 2
    tile = nb * length
    near = lanes((length, length)) < half
    top = pl.ds(0, length)
    bottom = pl.ds(rows - length, length)
    middle = pl.ds(length, rows - 2 * length)
    for part in (0, 1):
        edges = [by_side("row", edges_a[part, b], edges_b[part, b]) for b in range(nb + 1)]
        corners = [by_side("row", corners_a[part, side], corners_b[part, side]) for side in (0, 1)]
        for k, at in enumerate((top, bottom)):
            add = [edges[nb][k] + corners[0][k]]
            add += [edges[b][k] for b in range(nb)]
            add += [edges[nb][k] + corners[1][k]]
            add[1] = add[1] + jnp.where(near, corners[0][k], 0.0)
            add[nb] = add[nb] + jnp.where(near, 0.0, corners[1][k])
            for b in range(blocks):
                work[part, b, at, :] = work_from[part, b, at, :] + add[b] * inverse[b, at, :]
        for b in range(blocks):
            work[part, b, middle, :] = work_from[part, b, middle, :]
    total[...] = total_from[...]
    found = choose(chosen, offsets, counts, tile, length, lambda cross_row, **_: cross_row)
    add_gradients(work, total, probe, amps, offsets, tables, chosen, found, -half, -length)
    own = pl.ds(half, tile)
    near = lanes((half, length)) < half
    top = pl.ds(0, half)
    bottom = pl.ds(half + tile, half)
    for part in (0, 1):
        for b in range(blocks):
            sums[part, b] = total[part, b, own, :]
        for b in range(nb + 1):
            ends = [
                total[part, b + 1, at, :] if b < nb
                else jnp.where(near, total[part, nb + 1, at, :], total[part, 0, at, :])
                for at in (top, bottom)
            ]
            rows_a[part, b], rows_b[part, b] = by_pairs("row", *ends)


def sides_pass(offsets, counts, work, sums_from, probe, amps, tables, sums, chosen):
    _, blocks, tile, length = sums.shape
    sums[...] = sums_from[...]
    found = choose(
        chosen, offsets, counts, tile, length,
        lambda mid_row, cross_row, cross_col, **_: ~mid_row & ~cross_row & cross_col)
    add_gradients(work, sums, probe, amps, offsets, tables, chosen, found, 0, -length, length // 2)


def inner_pass(offsets, counts, work, probe, amps, tables, sums, chosen):
    _, blocks, tile, length = sums.shape
    sums[...] = jnp.zeros_like(sums)
    found = choose(
        chosen, offsets, counts, tile, length,
        lambda mid_row, cross_row, cross_col, **_: ~mid_row & ~cross_row & ~cross_col)
    add_gradients(work, sums, probe, amps, offsets, tables, chosen, found, 0, -length, length // 2)


def end_columns(sums, rows_a, rows_b, cols_a, cols_b):
    _, blocks, tile, length = sums.shape
    half = length // 2
    nb = blocks - 2
    low = lanes((tile, length)) < half
    gap = jnp.zeros((tile - 2 * half, length), jnp.float32)
    values = []
    for part in (0, 1):
        up, down = by_side("row", rows_a[part, nb], rows_b[part, nb])
        extra = above(above(up, gap), down)
        values.append((sums[part, 0] + extra, sums[part, nb + 1] + extra))
    cols_a[...], cols_b[...] = by_pairs(
        "col",
        jnp.where(low, swap(values[1][0], half), values[0][0]),
        jnp.where(low, values[0][1], swap(values[1][1], half)),
    )


def last_pass(work, sums, inner, inverse, rows_a, rows_b, cols_a, cols_b, out):
    _, blocks, tile, length = sums.shape
    half = length // 2
    nb = blocks - 2
    low = lanes((tile, length)) < half
    own = pl.ds(half, tile)
    gap = jnp.zeros((tile - 2 * half, length), jnp.float32)
    left, right = by_side("col", cols_a[...], cols_b[...])
    for part in (0, 1):
        if part:
            left, right = swap(left, half), swap(right, half)
        for b in range(nb):
            up, down = by_side("row", rows_a[part, b], rows_b[part, b])
            value = sums[part, b + 1] + inner[part, b + 1] + above(above(up, gap), down)
            if b == 0:
                value = value + jnp.where(low, left, 0.0)
            if b == nb - 1:
                value = value + jnp.where(low, 0.0, right)
            out[part, :, b * length:(b + 1) * length] = (
                work[part, b + 1, own, :] + value * inverse[b + 1, own, :])


def whole(memory_space=pltpu.VMEM):
    return pl.BlockSpec(memory_space=memory_space)


def call(body, shapes, places, scratch=(), cost=None):
    return pl.pallas_call(
        body,
        out_shape=[jax.ShapeDtypeStruct(shape, jnp.float32) for shape in shapes],
        in_specs=[whole({"s": pltpu.SMEM, "v": pltpu.VMEM, "a": pl.ANY, "h": pltpu.HBM}[p]) for p in places],
        out_specs=[whole()] * len(shapes),
        scratch_shapes=list(scratch),
        compiler_params=pltpu.CompilerParams(vmem_limit_bytes=VMEM_BYTES),
        cost_estimate=cost,
    )


def swap_pairs(first, second, axis):
    count = lax.axis_size(axis)
    got = []
    for value, start in ((first, 1), (second, 0)):
        pairs = [(i, i + 1) for i in range(start, count - 1, 2)]
        got.append(lax.ppermute(value, axis, pairs + [(b, a) for a, b in pairs]))
    return got


def shards(object_field, probe, amplitudes, offsets, counts):
    length = probe.shape[-1]
    half = length // 2
    tile = object_field.shape[1]
    npos = offsets.shape[2]
    nb = tile // length
    blocks = nb + 2
    rows = tile + 2 * half
    tables = jnp.asarray(dft_tables(length))
    offsets = jnp.swapaxes(offsets, 2, 3)

    def cost(positions):
        steps = 4 * 3 * 2 * length * (2 * length) ** 2
        return pl.CostEstimate(
            flops=positions * steps, bytes_accessed=8_000_000,
            transcendentals=positions * length * length)

    memory = pltpu.VMEM
    chosen = pltpu.SMEM((npos + GROUP,), jnp.int32)
    strip = (tile + 8, length)
    edge = (2 * nb * half + 8, length)
    field, cols_a, cols_b, rows_a, rows_b = call(
        start_pass, [(2, nb, tile, length), strip, strip, edge, edge], "asa",
        [pltpu.SMEM((1, 1, 2, npos), jnp.int32), pltpu.SemaphoreType.DMA((nb + 1,))],
    )(offsets, counts, object_field)
    mine = cols_a
    cols_a, cols_b = swap_pairs(cols_a, cols_b, "col")
    rows_a, rows_b = swap_pairs(rows_a, rows_b, "row")
    corner = (2 * half + 8, length)
    corners_a, corners_b = call(start_corners, [corner, corner], "vv")(cols_a, cols_b)
    corners_a, corners_b = swap_pairs(corners_a, corners_b, "row")

    full = (2, blocks, rows, length)
    strip = (2, rows, length)
    frame, acc, sums_a, sums_b = call(
        first_pass, [full, full, strip, strip], "ss" + 10 * "v", [chosen],
    )(offsets, counts, field, cols_a, cols_b, rows_a, rows_b, corners_a, corners_b,
      probe, amplitudes, tables)
    sums_a, sums_b = swap_pairs(sums_a, sums_b, "col")
    edge = (2, nb + 1, length, length)
    acc, edges_a, edges_b = call(
        first_rest, [full, edge, edge], "ss" + 5 * "v", [chosen], cost(npos // 2),
    )(offsets, counts, frame, acc, probe, amplitudes, tables)
    edges_a, edges_b = swap_pairs(edges_a, edges_b, "row")
    (inverse,) = call(
        functools.partial(light_pass, npos=npos), [(blocks, rows, length)], 8 * "v" + "a",
        [memory((blocks + 2, rows + 2 * length, length), jnp.float32),
         memory((length, length), jnp.float32), memory((7 * 8, length), jnp.int32),
         pltpu.SMEM((7 * 8, length), jnp.int32), pltpu.SemaphoreType.DMA],
        cost(npos // 2),
    )(mine, cols_a, cols_b, rows_a, rows_b, corners_a, corners_b, probe, acc)
    corner = (2, 2, length, length)
    corners_a, corners_b = call(middle_corners, [corner, corner], "vva")(sums_a, sums_b, inverse)
    corners_a, corners_b = swap_pairs(corners_a, corners_b, "row")

    work, total = call(update_pass, [full, full], "ss" + 8 * "v", [chosen], cost(npos // 2))(
        offsets, counts, frame, acc, inverse, sums_a, sums_b, probe, amplitudes, tables)
    edge = (2, nb + 1, half, length)
    tall = (2, blocks, tile, length)
    work, sums, rows_a, rows_b = call(
        second_pass, [full, tall, edge, edge], "ss" + 10 * "v",
        [memory(full, jnp.float32), chosen], cost(npos // 2),
    )(offsets, counts, work, total, inverse, edges_a, edges_b, corners_a, corners_b,
      probe, amplitudes, tables)
    rows_a, rows_b = swap_pairs(rows_a, rows_b, "row")
    (sums,) = call(sides_pass, [tall], "ss" + 5 * "v", [chosen], cost(npos // 4))(
        offsets, counts, work, sums, probe, amplitudes, tables)
    strip = (tile, length)
    cols_a, cols_b = call(end_columns, [strip, strip], "vvv")(sums, rows_a, rows_b)
    cols_a, cols_b = swap_pairs(cols_a, cols_b, "col")
    (inner,) = call(inner_pass, [tall], "ss" + 4 * "v", [chosen], cost(npos // 2))(
        offsets, counts, work, probe, amplitudes, tables)
    (out,) = call(last_pass, [(2, tile, tile)], 8 * "v")(
        work, sums, inner, inverse, rows_a, rows_b, cols_a, cols_b)
    return out


def solution(mesh):
    placed = (
        P(None, "row", "col"),
        P(),
        P("row", "col", None, None, None),
        P("row", "col", None, None),
        P("row", "col"),
    )
    return jax.shard_map(
        shards, mesh=mesh, in_specs=placed, out_specs=P(None, "row", "col"), check_vma=False
    )
```

```python
import functools
import math

import jax
import jax.numpy as jnp
import numpy as np
from jax import lax
from jax.experimental import pallas as pl
from jax.experimental.pallas import tpu as pltpu
from jax.sharding import PartitionSpec as P

ITERS = 2
FLOOR = 0.25
VMEM_BYTES = 16 * 1024 * 1024
GROUP = 4


def split(value):
    high = value.astype(jnp.bfloat16)
    low = (value - high.astype(jnp.float32)).astype(jnp.bfloat16)
    return high, low


def dft_tables(length):
    index = np.arange(length)
    angle = (index[:, None] * index[None, :] % length) * (2.0 * math.pi / length)
    cosine = np.cos(angle) / math.sqrt(length)
    sine = np.sin(angle) / math.sqrt(length)
    ahead = np.block([[cosine, -sine], [sine, cosine]])
    parts = []
    for table in (ahead, ahead.T):
        high = table.astype(jnp.bfloat16)
        low = (table - high.astype(np.float64)).astype(jnp.bfloat16)
        parts += [high, low]
    return np.stack(parts)


def lanes(shape):
    return lax.broadcasted_iota(jnp.int32, shape, len(shape) - 1)


def swap(value, half):
    return pltpu.roll(value, half, value.ndim - 1)


def odd_place(axis):
    return lax.axis_index(axis) % 2 == 1


def by_pairs(axis, low, high):
    odd = odd_place(axis)
    return jnp.where(odd, high, low), jnp.where(odd, low, high)


def by_side(axis, first, second):
    odd = odd_place(axis)
    return jnp.where(odd, second, first), jnp.where(odd, first, second)


def product(left, right):
    return jnp.dot(left, right, preferred_element_type=jnp.float32)


def times_right(rows, high, low):
    top, rest = split(rows)
    return product(top, high) + (product(top, low) + product(rest, high))


def times_left(high, low, columns):
    top, rest = split(columns)
    return product(high, top) + (product(low, top) + product(high, rest))


def beside(left, right):
    return jnp.concatenate([left, right], axis=1)


def above(top, bottom):
    return jnp.concatenate([top, bottom], axis=0)


def choose(chosen, offsets, counts, tile, length, wanted):
    last = tile - length
    half = length // 2

    def look(slot, found):
        row = offsets[0, 0, 0, slot]
        col = offsets[0, 0, 1, slot]
        taken = wanted(
            mid_row=(row >= half) & (row <= last - half),
            mid_col=(col >= half) & (col <= last - half),
            cross_row=(row < 0) | (row > last),
            cross_col=(col < 0) | (col > last),
        )
        chosen[found] = slot
        return found + jnp.where(taken, 1, 0)

    found = lax.fori_loop(0, counts[0, 0], look, 0)
    filler = chosen[0]
    for k in range(GROUP):
        chosen[found + k] = filler
    return found


def add_gradients(frame, acc, probe_ref, amps, offsets, tables, chosen, found, first_row, first_col,
                  skip=0):
    length = probe_ref.shape[-1]
    blocks = frame.shape[1]
    lane = lanes((length, length))

    def place(slot):
        row = offsets[0, 0, 0, slot] - first_row
        col = offsets[0, 0, 1, slot] - first_col
        block = col // length
        return row, block, jnp.minimum(block + 1, blocks - 1), col % length

    def exit_wave(slot):
        row, block, after, shift = place(slot)
        inside = lane >= shift
        window = [
            jnp.where(inside, frame[part, block, pl.ds(row + skip, length), :],
                      frame[part, after, pl.ds(row + skip, length), :])
            for part in (0, 1)
        ]
        real = pltpu.roll(probe_ref[0], shift, 1)
        imag = pltpu.roll(probe_ref[1], shift, 1)
        return (real * window[0] - imag * window[1], real * window[1] + imag * window[0])

    def shrink(real, imag, slot):
        ratio = amps[0, 0, slot] * lax.rsqrt(real * real + imag * imag + FLOOR) - 1.0
        return real * ratio, imag * ratio

    def put(slot, live, back_r, back_i):
        row, block, after, shift = place(slot)
        weight = jnp.where(live, 1.0, 0.0).astype(jnp.float32)
        real = pltpu.roll(probe_ref[0], shift, 1) * weight
        imag = pltpu.roll(probe_ref[1], shift, 1) * weight
        grads = (real * back_r + imag * back_i, real * back_i - imag * back_r)
        inside = lane >= shift
        for part in (0, 1):
            acc[part, block, pl.ds(row, length), :] += jnp.where(inside, grads[part], 0.0)
            acc[part, after, pl.ds(row, length), :] += jnp.where(inside, 0.0, grads[part])

    def work(slots):
        waves = [exit_wave(slot) for slot in slots]
        rows = jnp.concatenate([beside(*wave) for wave in waves], axis=0)
        mid = times_right(rows, tables[0], tables[1])
        mids = [mid[k * length:(k + 1) * length] for k in range(len(slots))]
        columns = above(
            jnp.concatenate([m[:, :length] for m in mids], axis=1),
            jnp.concatenate([m[:, length:] for m in mids], axis=1),
        )
        far = times_left(tables[2], tables[3], columns)
        changes = [
            shrink(far[:length, k * length:(k + 1) * length],
                   far[length:, k * length:(k + 1) * length], slot)
            for k, slot in enumerate(slots)
        ]
        columns = above(
            jnp.concatenate([c[0] for c in changes], axis=1),
            jnp.concatenate([c[1] for c in changes], axis=1),
        )
        mid = times_left(tables[0], tables[1], columns)
        rows = jnp.concatenate(
            [
                beside(mid[:length, k * length:(k + 1) * length],
                       mid[length:, k * length:(k + 1) * length])
                for k in range(len(slots))
            ],
            axis=0,
        )
        back = times_right(rows, tables[2], tables[3])
        return [
            (back[k * length:(k + 1) * length, :length], back[k * length:(k + 1) * length, length:])
            for k in range(len(slots))
        ]

    def step(index, carry):
        places = [index * GROUP + k for k in range(GROUP)]
        slots = [chosen[at] for at in places]
        gradients = work(slots)
        for at, slot, (back_r, back_i) in zip(places, slots, gradients):
            put(slot, at < found, back_r, back_i)
        return carry

    lax.fori_loop(0, (found + GROUP - 1) // GROUP, step, 0)


def start_pass(offsets_from, counts, field, tile_out, cols_a, cols_b, rows_a, rows_b, offsets, sems):
    _, nb, tile, length = tile_out.shape
    half = length // 2
    npos = offsets.shape[3]
    copies = {
        b: pltpu.make_async_copy(
            field.at[:, :, b * length:(b + 1) * length], tile_out.at[:, b], sems.at[b])
        for b in range(nb)
    }
    listed = pltpu.make_async_copy(offsets_from, offsets, sems.at[nb])
    listed.start()
    order = sorted(range(nb), key=lambda b: 0 < b < nb - 1)
    for b in order:
        copies[b].start()
    listed.wait()
    spot = lanes((8, length))
    info = jnp.zeros((8, length), jnp.int32)
    down = (lax.axis_index("row") + 1) * tile
    across = (lax.axis_index("col") + 1) * tile
    for k in range(npos):
        live = k < counts[0, 0]
        info = jnp.where(spot == k, jnp.where(live, offsets[0, 0, 0, k] + down, 0), info)
        info = jnp.where(spot == npos + k, jnp.where(live, offsets[0, 0, 1, k] + across, 0), info)
    info = info.astype(jnp.float32)
    cols_a[tile:] = info
    cols_b[tile:] = info
    rows_a[2 * nb * half:] = info
    rows_b[2 * nb * half:] = info
    for b in order:
        copies[b].wait()
    low = lanes((tile, length)) < half
    first = (tile_out[0, 0], tile_out[1, 0])
    last = (tile_out[0, nb - 1], tile_out[1, nb - 1])
    to_left = jnp.where(low, first[0], swap(first[1], half))
    to_right = jnp.where(low, swap(last[1], half), last[0])
    cols_a[:tile], cols_b[:tile] = by_pairs("col", to_left, to_right)
    for part in (0, 1):
        for b in range(nb):
            at = pl.ds((part * nb + b) * half, half)
            rows_a[at, :], rows_b[at, :] = by_pairs(
                "row", tile_out[part, b, :half], tile_out[part, b, tile - half:])


def start_corners(cols_a, cols_b, corners_a, corners_b):
    length = cols_a.shape[1]
    half = length // 2
    tile = cols_a.shape[0] - 8
    low = lanes((tile, length)) < half
    left, right = by_side("col", cols_a[:tile], cols_b[:tile])
    for part in (0, 1):
        if part:
            left, right = swap(left, half), swap(right, half)
        value = jnp.where(low, right, left)
        at = pl.ds(part * half, half)
        corners_a[at, :], corners_b[at, :] = by_pairs("row", value[:half], value[tile - half:])
    first = lax.broadcasted_iota(jnp.int32, (8, length), 0) == 0
    info = jnp.where(first, cols_a[tile:], cols_b[tile:])
    corners_a[2 * half:] = info
    corners_b[2 * half:] = info


def fetch_pass(after, probe, amps, tables, out):
    out[...] = jnp.zeros_like(out)


def first_pass(offsets, counts, ready, field, cols_a, cols_b, rows_a, rows_b, corners_a, corners_b,
               probe, amps, tables, frame, acc, sums_a, sums_b, chosen):
    _, nb, tile, length = field.shape
    half = length // 2
    rows = tile + 2 * half
    own = pl.ds(half, tile)
    left, right = by_side("col", cols_a[:tile], cols_b[:tile])
    top = pl.ds(0, half)
    bottom = pl.ds(half + tile, half)
    for part in (0, 1):
        for b in range(nb):
            frame[part, b + 1, own, :] = field[part, b]
            at = pl.ds((part * nb + b) * half, half)
            frame[part, b + 1, top, :], frame[part, b + 1, bottom, :] = by_side(
                "row", rows_a[at, :], rows_b[at, :])
        frame[part, 0, own, :] = swap(left, half) if part else left
        frame[part, nb + 1, own, :] = swap(right, half) if part else right
        at = pl.ds(part * half, half)
        ends = by_side("row", corners_a[at, :], corners_b[at, :])
        for block in (0, nb + 1):
            frame[part, block, top, :], frame[part, block, bottom, :] = ends
    acc[...] = jnp.zeros_like(acc)
    found = choose(chosen, offsets, counts, tile, length, lambda mid_col, **_: ~mid_col)
    add_gradients(frame, acc, probe, amps, offsets, tables, chosen, found, -half, -length)
    low = lanes((rows, length)) < half
    for part in (0, 1):
        sums_a[part], sums_b[part] = by_pairs(
            "col",
            jnp.where(low, acc[part, 1], acc[part, 0]),
            jnp.where(low, acc[part, nb + 1], acc[part, nb]),
        )


def first_rest(offsets, counts, frame, acc_from, probe, amps, tables,
               acc, edges_a, edges_b, chosen):
    _, blocks, rows, length = frame.shape
    half = length // 2
    nb = blocks - 2
    acc[...] = acc_from[...]
    found = choose(
        chosen, offsets, counts, nb * length, length,
        lambda mid_row, mid_col, **_: mid_col & ~mid_row)
    add_gradients(frame, acc, probe, amps, offsets, tables, chosen, found, -half, -length)
    low = lanes((length, length)) < half
    for part in (0, 1):
        for b in range(nb + 1):
            ends = [
                acc[part, b + 1, at, :] if b < nb
                else jnp.where(low, acc[part, nb + 1, at, :], acc[part, 0, at, :])
                for at in (pl.ds(0, length), pl.ds(rows - length, length))
            ]
            edges_a[part, b], edges_b[part, b] = by_pairs("row", *ends)


def middle_corners(sums_a, sums_b, after, corners_a, corners_b):
    _, rows, length = sums_a.shape
    for part in (0, 1):
        sides = by_side("col", sums_a[part], sums_b[part])
        for side in (0, 1):
            corners_a[part, side], corners_b[part, side] = by_pairs(
                "row", sides[side][:length], sides[side][rows - length:])


def light_pass(mine, cols_a, cols_b, rows_a, rows_b, corners_a, corners_b, probe, after,
               inverse, light, power, places, listed, chosen, sem, *, npos):
    length = probe.shape[-1]
    half = length // 2
    blocks, rows, _ = inverse.shape
    nb = blocks - 2
    tile = nb * length
    my_row = lax.axis_index("row")
    my_col = lax.axis_index("col")
    sources = (mine, cols_a, cols_b, rows_a, rows_b, corners_a, corners_b)
    for k, source in enumerate(sources):
        given = source[source.shape[0] - 8:, :].astype(jnp.int32)
        col = pltpu.roll(given, length - npos, 1) - (my_col + 1) * tile + 2 * length
        row = given - (my_row + 1) * tile + half + length
        near = (given > 0) & (row > 0) & (row < rows + length)
        near = near & (col > length - half) & (col < 2 * length + tile + half)
        places[pl.ds(8 * k, 8), :] = jnp.where(near, row * 4 * tile + col, 0)
    copy = pltpu.make_async_copy(places, listed, sem)
    copy.start()
    light[...] = jnp.zeros_like(light)
    power[...] = probe[0] * probe[0] + probe[1] * probe[1]
    lane = lanes((length, length))
    copy.wait()

    def look(index, found):
        line = jnp.where(index < len(sources), 8 * index, 8 * (index - 2) + 1)
        for slot in range(npos):
            place = listed[line, slot]
            chosen[found] = place
            found = found + jnp.where(place > 0, 1, 0)
        return found

    found = lax.fori_loop(0, len(sources) + 2, look, 0)

    def put(index, carry):
        place = chosen[index]
        start = lax.div(place, 4 * tile)
        col = lax.rem(place, 4 * tile)
        block = lax.div(col, length)
        shift = lax.rem(col, length)
        value = pltpu.roll(power[...], shift, 1)
        inside = lane >= shift
        light[block, pl.ds(start, length), :] += jnp.where(inside, value, 0.0)
        light[block + 1, pl.ds(start, length), :] += jnp.where(inside, 0.0, value)
        return carry

    lax.fori_loop(0, found, put, 0)
    spot = lax.broadcasted_iota(jnp.int32, (rows, length), 0)
    keep_from = jnp.where(my_row > 0, 0, half)
    keep_to = jnp.where(my_row < lax.axis_size("row") - 1, rows, rows - half)
    kept = (spot >= keep_from) & (spot < keep_to)
    for b in range(blocks):
        value = 1.0 / (light[b + 1, pl.ds(length, rows), :] + 1.0)
        keep = kept
        if b == 0:
            keep = keep & (my_col > 0)
        if b == nb + 1:
            keep = keep & (my_col < lax.axis_size("col") - 1)
        inverse[b] = jnp.where(keep, value, 0.0)


def update_pass(offsets, counts, frame, acc, inverse, sums_a, sums_b, probe, amps, tables,
                work, total, chosen):
    _, blocks, rows, length = frame.shape
    half = length // 2
    nb = blocks - 2
    work[...] = acc[...]
    found = choose(
        chosen, offsets, counts, nb * length, length,
        lambda mid_row, mid_col, **_: mid_col & mid_row)
    add_gradients(frame, work, probe, amps, offsets, tables, chosen, found, -half, -length)
    low = lanes((rows, length)) < half
    for part in (0, 1):
        left, right = by_side("col", sums_a[part], sums_b[part])
        for b in range(blocks):
            value = work[part, b]
            if b == 0:
                value = value + left
            if b == 1:
                value = value + jnp.where(low, left, 0.0)
            if b == nb:
                value = value + jnp.where(low, 0.0, right)
            if b == nb + 1:
                value = value + right
            work[part, b] = frame[part, b] + value * inverse[b]
    total[...] = jnp.zeros_like(total)
    found = choose(chosen, offsets, counts, nb * length, length, lambda mid_row, **_: mid_row)
    add_gradients(work, total, probe, amps, offsets, tables, chosen, found, -half, -length)


def second_pass(offsets, counts, work_from, total_from, inverse, edges_a, edges_b,
                corners_a, corners_b, probe, amps, tables,
                work, sums, rows_a, rows_b, total, chosen):
    _, blocks, rows, length = work.shape
    half = length // 2
    nb = blocks - 2
    tile = nb * length
    near = lanes((length, length)) < half
    top = pl.ds(0, length)
    bottom = pl.ds(rows - length, length)
    middle = pl.ds(length, rows - 2 * length)
    for part in (0, 1):
        edges = [by_side("row", edges_a[part, b], edges_b[part, b]) for b in range(nb + 1)]
        corners = [by_side("row", corners_a[part, side], corners_b[part, side]) for side in (0, 1)]
        for k, at in enumerate((top, bottom)):
            add = [edges[nb][k] + corners[0][k]]
            add += [edges[b][k] for b in range(nb)]
            add += [edges[nb][k] + corners[1][k]]
            add[1] = add[1] + jnp.where(near, corners[0][k], 0.0)
            add[nb] = add[nb] + jnp.where(near, 0.0, corners[1][k])
            for b in range(blocks):
                work[part, b, at, :] = work_from[part, b, at, :] + add[b] * inverse[b, at, :]
        for b in range(blocks):
            work[part, b, middle, :] = work_from[part, b, middle, :]
    total[...] = total_from[...]
    found = choose(chosen, offsets, counts, tile, length, lambda cross_row, **_: cross_row)
    add_gradients(work, total, probe, amps, offsets, tables, chosen, found, -half, -length)
    own = pl.ds(half, tile)
    near = lanes((half, length)) < half
    top = pl.ds(0, half)
    bottom = pl.ds(half + tile, half)
    for part in (0, 1):
        for b in range(blocks):
            sums[part, b] = total[part, b, own, :]
        for b in range(nb + 1):
            ends = [
                total[part, b + 1, at, :] if b < nb
                else jnp.where(near, total[part, nb + 1, at, :], total[part, 0, at, :])
                for at in (top, bottom)
            ]
            rows_a[part, b], rows_b[part, b] = by_pairs("row", *ends)


def sides_pass(offsets, counts, work, sums_from, probe, amps, tables, sums, chosen):
    _, blocks, tile, length = sums.shape
    sums[...] = sums_from[...]
    found = choose(
        chosen, offsets, counts, tile, length,
        lambda mid_row, cross_row, cross_col, **_: ~mid_row & ~cross_row & cross_col)
    add_gradients(work, sums, probe, amps, offsets, tables, chosen, found, 0, -length, length // 2)


def inner_pass(offsets, counts, work, probe, amps, tables, sums, chosen):
    _, blocks, tile, length = sums.shape
    sums[...] = jnp.zeros_like(sums)
    found = choose(
        chosen, offsets, counts, tile, length,
        lambda mid_row, cross_row, cross_col, **_: ~mid_row & ~cross_row & ~cross_col)
    add_gradients(work, sums, probe, amps, offsets, tables, chosen, found, 0, -length, length // 2)


def end_columns(sums, rows_a, rows_b, cols_a, cols_b):
    _, blocks, tile, length = sums.shape
    half = length // 2
    nb = blocks - 2
    low = lanes((tile, length)) < half
    gap = jnp.zeros((tile - 2 * half, length), jnp.float32)
    values = []
    for part in (0, 1):
        up, down = by_side("row", rows_a[part, nb], rows_b[part, nb])
        extra = above(above(up, gap), down)
        values.append((sums[part, 0] + extra, sums[part, nb + 1] + extra))
    cols_a[...], cols_b[...] = by_pairs(
        "col",
        jnp.where(low, swap(values[1][0], half), values[0][0]),
        jnp.where(low, values[0][1], swap(values[1][1], half)),
    )


def last_pass(work, sums, inner, inverse, rows_a, rows_b, cols_a, cols_b, out):
    _, blocks, tile, length = sums.shape
    half = length // 2
    nb = blocks - 2
    low = lanes((tile, length)) < half
    own = pl.ds(half, tile)
    gap = jnp.zeros((tile - 2 * half, length), jnp.float32)
    left, right = by_side("col", cols_a[...], cols_b[...])
    for part in (0, 1):
        if part:
            left, right = swap(left, half), swap(right, half)
        for b in range(nb):
            up, down = by_side("row", rows_a[part, b], rows_b[part, b])
            value = sums[part, b + 1] + inner[part, b + 1] + above(above(up, gap), down)
            if b == 0:
                value = value + jnp.where(low, left, 0.0)
            if b == nb - 1:
                value = value + jnp.where(low, 0.0, right)
            out[part, :, b * length:(b + 1) * length] = (
                work[part, b + 1, own, :] + value * inverse[b + 1, own, :])


def whole(memory_space=pltpu.VMEM):
    return pl.BlockSpec(memory_space=memory_space)


def call(body, shapes, places, scratch=(), cost=None):
    return pl.pallas_call(
        body,
        out_shape=[jax.ShapeDtypeStruct(shape, jnp.float32) for shape in shapes],
        in_specs=[whole({"s": pltpu.SMEM, "v": pltpu.VMEM, "a": pl.ANY, "h": pltpu.HBM}[p]) for p in places],
        out_specs=[whole()] * len(shapes),
        scratch_shapes=list(scratch),
        compiler_params=pltpu.CompilerParams(vmem_limit_bytes=VMEM_BYTES),
        cost_estimate=cost,
    )


def swap_pairs(first, second, axis):
    count = lax.axis_size(axis)
    got = []
    for value, start in ((first, 1), (second, 0)):
        pairs = [(i, i + 1) for i in range(start, count - 1, 2)]
        got.append(lax.ppermute(value, axis, pairs + [(b, a) for a, b in pairs]))
    return got


def shards(object_field, probe, amplitudes, offsets, counts):
    length = probe.shape[-1]
    half = length // 2
    tile = object_field.shape[1]
    npos = offsets.shape[2]
    nb = tile // length
    blocks = nb + 2
    rows = tile + 2 * half
    tables = jnp.asarray(dft_tables(length))
    offsets = jnp.swapaxes(offsets, 2, 3)

    def cost(positions):
        steps = 4 * 3 * 2 * length * (2 * length) ** 2
        return pl.CostEstimate(
            flops=positions * steps, bytes_accessed=8_000_000,
            transcendentals=positions * length * length)

    memory = pltpu.VMEM
    chosen = pltpu.SMEM((npos + GROUP,), jnp.int32)
    strip = (tile + 8, length)
    edge = (2 * nb * half + 8, length)
    field, cols_a, cols_b, rows_a, rows_b = call(
        start_pass, [(2, nb, tile, length), strip, strip, edge, edge], "asa",
        [pltpu.SMEM((1, 1, 2, npos), jnp.int32), pltpu.SemaphoreType.DMA((nb + 1,))],
    )(offsets, counts, object_field)
    mine = cols_a
    cols_a, cols_b = swap_pairs(cols_a, cols_b, "col")
    rows_a, rows_b = swap_pairs(rows_a, rows_b, "row")
    corner = (2 * half + 8, length)
    corners_a, corners_b = call(start_corners, [corner, corner], "vv")(cols_a, cols_b)
    (ready,) = call(fetch_pass, [(8, length)], "avvv", cost=cost(1))(
        corners_a, probe, amplitudes, tables)
    corners_a, corners_b = swap_pairs(corners_a, corners_b, "row")

    full = (2, blocks, rows, length)
    strip = (2, rows, length)
    frame, acc, sums_a, sums_b = call(
        first_pass, [full, full, strip, strip], "ssa" + 10 * "v", [chosen],
    )(offsets, counts, ready, field, cols_a, cols_b, rows_a, rows_b, corners_a, corners_b,
      probe, amplitudes, tables)
    sums_a, sums_b = swap_pairs(sums_a, sums_b, "col")
    edge = (2, nb + 1, length, length)
    acc, edges_a, edges_b = call(
        first_rest, [full, edge, edge], "ss" + 5 * "v", [chosen], cost(npos // 2),
    )(offsets, counts, frame, acc, probe, amplitudes, tables)
    edges_a, edges_b = swap_pairs(edges_a, edges_b, "row")
    (inverse,) = call(
        functools.partial(light_pass, npos=npos), [(blocks, rows, length)], 8 * "v" + "a",
        [memory((blocks + 2, rows + 2 * length, length), jnp.float32),
         memory((length, length), jnp.float32), memory((7 * 8, length), jnp.int32),
         pltpu.SMEM((7 * 8, length), jnp.int32), pltpu.SMEM((9 * npos + 1,), jnp.int32),
         pltpu.SemaphoreType.DMA],
        cost(npos // 2),
    )(mine, cols_a, cols_b, rows_a, rows_b, corners_a, corners_b, probe, acc)
    corner = (2, 2, length, length)
    corners_a, corners_b = call(middle_corners, [corner, corner], "vva")(sums_a, sums_b, inverse)
    corners_a, corners_b = swap_pairs(corners_a, corners_b, "row")

    work, total = call(update_pass, [full, full], "ss" + 8 * "v", [chosen], cost(npos // 2))(
        offsets, counts, frame, acc, inverse, sums_a, sums_b, probe, amplitudes, tables)
    edge = (2, nb + 1, half, length)
    tall = (2, blocks, tile, length)
    work, sums, rows_a, rows_b = call(
        second_pass, [full, tall, edge, edge], "ss" + 10 * "v",
        [memory(full, jnp.float32), chosen], cost(npos // 2),
    )(offsets, counts, work, total, inverse, edges_a, edges_b, corners_a, corners_b,
      probe, amplitudes, tables)
    rows_a, rows_b = swap_pairs(rows_a, rows_b, "row")
    (sums,) = call(sides_pass, [tall], "ss" + 5 * "v", [chosen], cost(npos // 4))(
        offsets, counts, work, sums, probe, amplitudes, tables)
    strip = (tile, length)
    cols_a, cols_b = call(end_columns, [strip, strip], "vvv")(sums, rows_a, rows_b)
    cols_a, cols_b = swap_pairs(cols_a, cols_b, "col")
    (inner,) = call(inner_pass, [tall], "ss" + 4 * "v", [chosen], cost(npos // 2))(
        offsets, counts, work, probe, amplitudes, tables)
    (out,) = call(last_pass, [(2, tile, tile)], 8 * "v")(
        work, sums, inner, inverse, rows_a, rows_b, cols_a, cols_b)
    return out


def solution(mesh):
    placed = (
        P(None, "row", "col"),
        P(),
        P("row", "col", None, None, None),
        P("row", "col", None, None),
        P("row", "col"),
    )
    return jax.shard_map(
        shards, mesh=mesh, in_specs=placed, out_specs=P(None, "row", "col"), check_vma=False
    )
```

```python
import functools
import math

import jax
import jax.numpy as jnp
import numpy as np
from jax import lax
from jax.experimental import pallas as pl
from jax.experimental.pallas import tpu as pltpu
from jax.sharding import PartitionSpec as P

ITERS = 2
FLOOR = 0.25
VMEM_BYTES = 16 * 1024 * 1024
GROUP = 4


def split(value):
    high = value.astype(jnp.bfloat16)
    low = (value - high.astype(jnp.float32)).astype(jnp.bfloat16)
    return high, low


def dft_tables(length):
    index = np.arange(length)
    angle = (index[:, None] * index[None, :] % length) * (2.0 * math.pi / length)
    cosine = np.cos(angle) / math.sqrt(length)
    sine = np.sin(angle) / math.sqrt(length)
    ahead = np.block([[cosine, -sine], [sine, cosine]])
    parts = []
    for table in (ahead, ahead.T):
        high = table.astype(jnp.bfloat16)
        low = (table - high.astype(np.float64)).astype(jnp.bfloat16)
        parts += [high, low]
    return np.stack(parts)


def lanes(shape):
    return lax.broadcasted_iota(jnp.int32, shape, len(shape) - 1)


def swap(value, half):
    return pltpu.roll(value, half, value.ndim - 1)


def odd_place(axis):
    return lax.axis_index(axis) % 2 == 1


def by_pairs(axis, low, high):
    odd = odd_place(axis)
    return jnp.where(odd, high, low), jnp.where(odd, low, high)


def by_side(axis, first, second):
    odd = odd_place(axis)
    return jnp.where(odd, second, first), jnp.where(odd, first, second)


def product(left, right):
    return jnp.dot(left, right, preferred_element_type=jnp.float32)


def times_right(rows, high, low):
    top, rest = split(rows)
    count = rows.shape[0]
    both = product(above(top, rest), high)
    return both[:count] + (both[count:] + product(top, low))


def times_left(high, low, columns):
    top, rest = split(columns)
    count = high.shape[0]
    both = product(above(high, low), top)
    return both[:count] + (both[count:] + product(high, rest))


def beside(left, right):
    return jnp.concatenate([left, right], axis=1)


def above(top, bottom):
    return jnp.concatenate([top, bottom], axis=0)


def choose(chosen, offsets, counts, tile, length, wanted):
    last = tile - length
    half = length // 2

    def look(slot, found):
        row = offsets[0, 0, 0, slot]
        col = offsets[0, 0, 1, slot]
        taken = wanted(
            mid_row=(row >= half) & (row <= last - half),
            mid_col=(col >= half) & (col <= last - half),
            cross_row=(row < 0) | (row > last),
            cross_col=(col < 0) | (col > last),
        )
        chosen[found] = slot
        return found + jnp.where(taken, 1, 0)

    found = lax.fori_loop(0, counts[0, 0], look, 0)
    filler = chosen[0]
    for k in range(GROUP):
        chosen[found + k] = filler
    return found


def add_gradients(frame, acc, probe_ref, amps, offsets, tables, chosen, found, first_row=None, skip=0):
    length = probe_ref.shape[-1]
    half = length // 2
    last = acc.shape[1] - 1
    begin = -half if first_row is None else first_row
    lane = lanes((length, length))

    def place(slot):
        col = offsets[0, 0, 1, slot] + length
        return offsets[0, 0, 0, slot], lax.div(col, length), lax.rem(col, length)

    def exit_wave(slot):
        row, block, shift = place(slot)
        inside = lane >= shift
        at = pl.ds(row + half, length)
        window = [
            jnp.where(inside, frame[part, block, at, :], frame[part, block + 1, at, :])
            for part in (0, 1)
        ]
        probe = (pltpu.roll(probe_ref[0], shift, 1), pltpu.roll(probe_ref[1], shift, 1))
        wave = (probe[0] * window[0] - probe[1] * window[1],
                probe[0] * window[1] + probe[1] * window[0])
        return probe, wave

    def shrink(real, imag, slot):
        ratio = amps[0, 0, slot] * lax.rsqrt(real * real + imag * imag + FLOOR) - 1.0
        return real * ratio, imag * ratio

    def put(slot, live, probe, back_r, back_i):
        row, block, shift = place(slot)
        at = pl.ds(row - begin, length)
        block = block - skip
        after = jnp.minimum(block + 1, last)
        grads = (probe[0] * back_r + probe[1] * back_i, probe[0] * back_i - probe[1] * back_r)
        bound = jnp.where(live, shift, length)
        inside = lane >= bound
        beyond = lane < jnp.where(live, shift, 0)
        for part in (0, 1):
            acc[part, block, at, :] += jnp.where(inside, grads[part], 0.0)
            acc[part, after, at, :] += jnp.where(beyond, grads[part], 0.0)

    def work(slots):
        probes, waves = zip(*[exit_wave(slot) for slot in slots])
        rows = jnp.concatenate([beside(*wave) for wave in waves], axis=0)
        mid = times_right(rows, tables[0], tables[1])
        mids = [mid[k * length:(k + 1) * length] for k in range(len(slots))]
        columns = above(
            jnp.concatenate([m[:, :length] for m in mids], axis=1),
            jnp.concatenate([m[:, length:] for m in mids], axis=1),
        )
        far = times_left(tables[2], tables[3], columns)
        changes = [
            shrink(far[:length, k * length:(k + 1) * length],
                   far[length:, k * length:(k + 1) * length], slot)
            for k, slot in enumerate(slots)
        ]
        columns = above(
            jnp.concatenate([c[0] for c in changes], axis=1),
            jnp.concatenate([c[1] for c in changes], axis=1),
        )
        mid = times_left(tables[0], tables[1], columns)
        rows = jnp.concatenate(
            [
                beside(mid[:length, k * length:(k + 1) * length],
                       mid[length:, k * length:(k + 1) * length])
                for k in range(len(slots))
            ],
            axis=0,
        )
        back = times_right(rows, tables[2], tables[3])
        return [
            (probes[k], back[k * length:(k + 1) * length, :length],
             back[k * length:(k + 1) * length, length:])
            for k in range(len(slots))
        ]

    def step(index, carry):
        places = [index * GROUP + k for k in range(GROUP)]
        slots = [chosen[at] for at in places]
        gradients = work(slots)
        for at, slot, gradient in zip(places, slots, gradients):
            put(slot, at < found, *gradient)
        return carry

    lax.fori_loop(0, (found + GROUP - 1) // GROUP, step, 0)


def start_pass(offsets_from, counts, field, tile_out, cols_a, cols_b, rows_a, rows_b, offsets, sems):
    _, nb, tile, length = tile_out.shape
    half = length // 2
    npos = offsets.shape[3]
    copies = {
        b: pltpu.make_async_copy(
            field.at[:, :, b * length:(b + 1) * length], tile_out.at[:, b], sems.at[b])
        for b in range(nb)
    }
    listed = pltpu.make_async_copy(offsets_from, offsets, sems.at[nb])
    listed.start()
    order = sorted(range(nb), key=lambda b: 0 < b < nb - 1)
    for b in order:
        copies[b].start()
    listed.wait()
    spot = lanes((8, length))
    info = jnp.zeros((8, length), jnp.int32)
    down = (lax.axis_index("row") + 1) * tile
    across = (lax.axis_index("col") + 1) * tile
    for k in range(npos):
        live = k < counts[0, 0]
        info = jnp.where(spot == k, jnp.where(live, offsets[0, 0, 0, k] + down, 0), info)
        info = jnp.where(spot == npos + k, jnp.where(live, offsets[0, 0, 1, k] + across, 0), info)
    info = info.astype(jnp.float32)
    cols_a[tile:] = info
    cols_b[tile:] = info
    rows_a[2 * nb * half:] = info
    rows_b[2 * nb * half:] = info
    for b in order:
        copies[b].wait()
    low = lanes((tile, length)) < half
    first = (tile_out[0, 0], tile_out[1, 0])
    last = (tile_out[0, nb - 1], tile_out[1, nb - 1])
    to_left = jnp.where(low, first[0], swap(first[1], half))
    to_right = jnp.where(low, swap(last[1], half), last[0])
    cols_a[:tile], cols_b[:tile] = by_pairs("col", to_left, to_right)
    for part in (0, 1):
        for b in range(nb):
            at = pl.ds((part * nb + b) * half, half)
            rows_a[at, :], rows_b[at, :] = by_pairs(
                "row", tile_out[part, b, :half], tile_out[part, b, tile - half:])


def start_corners(cols_a, cols_b, corners_a, corners_b):
    length = cols_a.shape[1]
    half = length // 2
    tile = cols_a.shape[0] - 8
    low = lanes((tile, length)) < half
    left, right = by_side("col", cols_a[:tile], cols_b[:tile])
    for part in (0, 1):
        if part:
            left, right = swap(left, half), swap(right, half)
        value = jnp.where(low, right, left)
        at = pl.ds(part * half, half)
        corners_a[at, :], corners_b[at, :] = by_pairs("row", value[:half], value[tile - half:])
    first = lax.broadcasted_iota(jnp.int32, (8, length), 0) == 0
    info = jnp.where(first, cols_a[tile:], cols_b[tile:])
    corners_a[2 * half:] = info
    corners_b[2 * half:] = info


def fetch_pass(after, probe, amps, tables, out):
    out[...] = jnp.zeros_like(out)


def first_pass(offsets, counts, ready, field, cols_a, cols_b, rows_a, rows_b, corners_a, corners_b,
               probe, amps, tables, frame, acc, sums_a, sums_b, chosen):
    _, nb, tile, length = field.shape
    half = length // 2
    rows = tile + 2 * half
    own = pl.ds(half, tile)
    left, right = by_side("col", cols_a[:tile], cols_b[:tile])
    top = pl.ds(0, half)
    bottom = pl.ds(half + tile, half)
    for part in (0, 1):
        for b in range(nb):
            frame[part, b + 1, own, :] = field[part, b]
            at = pl.ds((part * nb + b) * half, half)
            frame[part, b + 1, top, :], frame[part, b + 1, bottom, :] = by_side(
                "row", rows_a[at, :], rows_b[at, :])
        frame[part, 0, own, :] = swap(left, half) if part else left
        frame[part, nb + 1, own, :] = swap(right, half) if part else right
        at = pl.ds(part * half, half)
        ends = by_side("row", corners_a[at, :], corners_b[at, :])
        for block in (0, nb + 1):
            frame[part, block, top, :], frame[part, block, bottom, :] = ends
    acc[...] = jnp.zeros_like(acc)
    found = choose(chosen, offsets, counts, tile, length, lambda mid_col, **_: ~mid_col)
    add_gradients(frame, acc, probe, amps, offsets, tables, chosen, found)
    low = lanes((rows, length)) < half
    for part in (0, 1):
        sums_a[part], sums_b[part] = by_pairs(
            "col",
            jnp.where(low, acc[part, 1], acc[part, 0]),
            jnp.where(low, acc[part, nb + 1], acc[part, nb]),
        )


def first_rest(offsets, counts, frame, acc_from, probe, amps, tables,
               acc, edges_a, edges_b, chosen):
    _, blocks, rows, length = frame.shape
    half = length // 2
    nb = blocks - 2
    acc[...] = acc_from[...]
    found = choose(
        chosen, offsets, counts, nb * length, length,
        lambda mid_row, mid_col, **_: mid_col & ~mid_row)
    add_gradients(frame, acc, probe, amps, offsets, tables, chosen, found)
    low = lanes((length, length)) < half
    for part in (0, 1):
        for b in range(nb - 1):
            ends = [
                acc[part, b + 2, at, :] if b < nb - 2
                else jnp.where(low, acc[part, nb, at, :], acc[part, 1, at, :])
                for at in (pl.ds(0, length), pl.ds(rows - length, length))
            ]
            edges_a[part, b], edges_b[part, b] = by_pairs("row", *ends)


def middle_corners(mine_a, mine_b, sums_a, sums_b, after, corners_a, corners_b):
    _, rows, length = sums_a.shape
    for part in (0, 1):
        for at, k in ((pl.ds(0, length), 0), (pl.ds(rows - length, length), 1)):
            sides = by_side(
                "col", mine_a[part, at, :] + sums_a[part, at, :],
                mine_b[part, at, :] + sums_b[part, at, :])
            for side in (0, 1):
                if k == 0:
                    up = sides
                else:
                    corners_a[part, side], corners_b[part, side] = by_pairs(
                        "row", up[side], sides[side])


def light_pass(mine, cols_a, cols_b, rows_a, rows_b, corners_a, corners_b, probe, after,
               inverse, light, power, places, listed, chosen, sem, *, npos):
    length = probe.shape[-1]
    half = length // 2
    blocks, rows, _ = inverse.shape
    nb = blocks - 2
    tile = nb * length
    my_row = lax.axis_index("row")
    my_col = lax.axis_index("col")
    sources = (mine, cols_a, cols_b, rows_a, rows_b, corners_a, corners_b)
    for k, source in enumerate(sources):
        given = source[source.shape[0] - 8:, :].astype(jnp.int32)
        col = pltpu.roll(given, length - npos, 1) - (my_col + 1) * tile + 2 * length
        row = given - (my_row + 1) * tile + half + length
        near = (given > 0) & (row > 0) & (row < rows + length)
        near = near & (col > length - half) & (col < 2 * length + tile + half)
        places[pl.ds(8 * k, 8), :] = jnp.where(near, row * 4 * tile + col, 0)
    copy = pltpu.make_async_copy(places, listed, sem)
    copy.start()
    light[...] = jnp.zeros_like(light)
    power[...] = probe[0] * probe[0] + probe[1] * probe[1]
    lane = lanes((length, length))
    copy.wait()

    def look(index, found):
        line = jnp.where(index < len(sources), 8 * index, 8 * (index - 2) + 1)
        for slot in range(npos):
            place = listed[line, slot]
            chosen[found] = place
            found = found + jnp.where(place > 0, 1, 0)
        return found

    found = lax.fori_loop(0, len(sources) + 2, look, 0)

    def put(index, carry):
        place = chosen[index]
        start = lax.div(place, 4 * tile)
        col = lax.rem(place, 4 * tile)
        block = lax.div(col, length)
        shift = lax.rem(col, length)
        value = pltpu.roll(power[...], shift, 1)
        inside = lane >= shift
        light[block, pl.ds(start, length), :] += jnp.where(inside, value, 0.0)
        light[block + 1, pl.ds(start, length), :] += jnp.where(inside, 0.0, value)
        return carry

    lax.fori_loop(0, found, put, 0)
    spot = lax.broadcasted_iota(jnp.int32, (rows, length), 0)
    keep_from = jnp.where(my_row > 0, 0, half)
    keep_to = jnp.where(my_row < lax.axis_size("row") - 1, rows, rows - half)
    kept = (spot >= keep_from) & (spot < keep_to)
    for b in range(blocks):
        value = 1.0 / (light[b + 1, pl.ds(length, rows), :] + 1.0)
        keep = kept
        if b == 0:
            keep = keep & (my_col > 0)
        if b == nb + 1:
            keep = keep & (my_col < lax.axis_size("col") - 1)
        inverse[b] = jnp.where(keep, value, 0.0)


def update_pass(offsets, counts, frame, acc, inverse, sums_a, sums_b, probe, amps, tables,
                work, total, chosen):
    _, blocks, rows, length = frame.shape
    half = length // 2
    nb = blocks - 2
    work[...] = acc[...]
    found = choose(
        chosen, offsets, counts, nb * length, length,
        lambda mid_row, mid_col, **_: mid_col & mid_row)
    add_gradients(frame, work, probe, amps, offsets, tables, chosen, found)
    low = lanes((rows, length)) < half
    for part in (0, 1):
        left, right = by_side("col", sums_a[part], sums_b[part])
        for b in range(blocks):
            value = work[part, b]
            if b == 0:
                value = value + left
            if b == 1:
                value = value + jnp.where(low, left, 0.0)
            if b == nb:
                value = value + jnp.where(low, 0.0, right)
            if b == nb + 1:
                value = value + right
            work[part, b] = frame[part, b] + value * inverse[b]
    total[...] = jnp.zeros_like(total)
    found = choose(chosen, offsets, counts, nb * length, length, lambda mid_row, **_: mid_row)
    add_gradients(work, total, probe, amps, offsets, tables, chosen, found)


def second_pass(offsets, counts, work_from, total_from, inverse, edges_a, edges_b,
                corners_a, corners_b, probe, amps, tables,
                work, total, cols_a, cols_b, chosen):
    _, blocks, rows, length = work.shape
    half = length // 2
    nb = blocks - 2
    tile = nb * length
    near = lanes((length, length)) < half
    middle = pl.ds(length, rows - 2 * length)
    for part in (0, 1):
        edges = [by_side("row", edges_a[part, b], edges_b[part, b]) for b in range(nb - 1)]
        corners = [by_side("row", corners_a[part, side], corners_b[part, side]) for side in (0, 1)]
        for k, at in enumerate((pl.ds(0, length), pl.ds(rows - length, length))):
            left, right, ends = corners[0][k], corners[1][k], edges[nb - 2][k]
            add = [left, jnp.where(near, left, ends)]
            add += [edges[b][k] for b in range(nb - 2)]
            add += [jnp.where(near, ends, right), right]
            for b in range(blocks):
                work[part, b, at, :] = work_from[part, b, at, :] + add[b] * inverse[b, at, :]
        for b in range(blocks):
            work[part, b, middle, :] = work_from[part, b, middle, :]
    total[...] = total_from[...]
    found = choose(
        chosen, offsets, counts, tile, length,
        lambda mid_row, cross_col, **_: ~mid_row & cross_col)
    add_gradients(work, total, probe, amps, offsets, tables, chosen, found)
    low = lanes((rows, length)) < half
    cols_a[...], cols_b[...] = by_pairs(
        "col",
        jnp.where(low, swap(total[1, 0], half), total[0, 0]),
        jnp.where(low, total[0, nb + 1], swap(total[1, nb + 1], half)),
    )


def rows_pass(offsets, counts, work, total, probe, amps, tables, sums, rows_a, rows_b, acc, chosen):
    _, nb, tile, length = sums.shape
    half = length // 2
    acc[...] = total[:, 1:nb + 1]
    found = choose(
        chosen, offsets, counts, tile, length,
        lambda cross_row, cross_col, **_: cross_row & ~cross_col)
    add_gradients(work, acc, probe, amps, offsets, tables, chosen, found, skip=1)
    for part in (0, 1):
        for b in range(nb):
            sums[part, b] = acc[part, b, pl.ds(half, tile), :]
            rows_a[part, b], rows_b[part, b] = by_pairs(
                "row", acc[part, b, :half, :], acc[part, b, half + tile:, :])


def inner_pass(offsets, counts, work, probe, amps, tables, sums, chosen):
    _, nb, tile, length = sums.shape
    sums[...] = jnp.zeros_like(sums)
    found = choose(
        chosen, offsets, counts, tile, length,
        lambda mid_row, cross_row, cross_col, **_: ~mid_row & ~cross_row & ~cross_col)
    add_gradients(work, sums, probe, amps, offsets, tables, chosen, found, first_row=0, skip=1)


def end_corners(cols_a, cols_b, corners_a, corners_b):
    rows, length = cols_a.shape
    half = length // 2
    for side, value in enumerate(by_side("col", cols_a[...], cols_b[...])):
        corners_a[side], corners_b[side] = by_pairs("row", value[:half], value[rows - half:])


def last_pass(work, sums, inner, inverse, cols_a, cols_b, rows_a, rows_b, corners_a, corners_b, out):
    _, nb, tile, length = sums.shape
    half = length // 2
    low = lanes((tile, length)) < half
    own = pl.ds(half, tile)
    gap = jnp.zeros((tile - 2 * half, length), jnp.float32)
    sides = []
    for side, value in enumerate(by_side("col", cols_a[own, :], cols_b[own, :])):
        up, down = by_side("row", corners_a[side], corners_b[side])
        sides.append(value + above(above(up, gap), down))
    left, right = sides
    for part in (0, 1):
        if part:
            left, right = swap(left, half), swap(right, half)
        for b in range(nb):
            up, down = by_side("row", rows_a[part, b], rows_b[part, b])
            value = sums[part, b] + inner[part, b] + above(above(up, gap), down)
            if b == 0:
                value = value + jnp.where(low, left, 0.0)
            if b == nb - 1:
                value = value + jnp.where(low, 0.0, right)
            out[part, :, b * length:(b + 1) * length] = (
                work[part, b + 1, own, :] + value * inverse[b + 1, own, :])


def whole(memory_space=pltpu.VMEM):
    return pl.BlockSpec(memory_space=memory_space)


def call(body, shapes, places, scratch=(), cost=None):
    return pl.pallas_call(
        body,
        out_shape=[jax.ShapeDtypeStruct(shape, jnp.float32) for shape in shapes],
        in_specs=[whole({"s": pltpu.SMEM, "v": pltpu.VMEM, "a": pl.ANY, "h": pltpu.HBM}[p]) for p in places],
        out_specs=[whole()] * len(shapes),
        scratch_shapes=list(scratch),
        compiler_params=pltpu.CompilerParams(vmem_limit_bytes=VMEM_BYTES),
        cost_estimate=cost,
    )


def swap_pairs(first, second, axis):
    count = lax.axis_size(axis)
    got = []
    for value, start in ((first, 1), (second, 0)):
        pairs = [(i, i + 1) for i in range(start, count - 1, 2)]
        got.append(lax.ppermute(value, axis, pairs + [(b, a) for a, b in pairs]))
    return got


def shards(object_field, probe, amplitudes, offsets, counts):
    length = probe.shape[-1]
    half = length // 2
    tile = object_field.shape[1]
    npos = offsets.shape[2]
    nb = tile // length
    blocks = nb + 2
    rows = tile + 2 * half
    tables = jnp.asarray(dft_tables(length))
    offsets = jnp.swapaxes(offsets, 2, 3)

    def cost(positions):
        steps = 4 * 3 * 2 * length * (2 * length) ** 2
        return pl.CostEstimate(
            flops=positions * steps, bytes_accessed=8_000_000,
            transcendentals=positions * length * length)

    memory = pltpu.VMEM
    chosen = pltpu.SMEM((npos + GROUP,), jnp.int32)
    strip = (tile + 8, length)
    edge = (2 * nb * half + 8, length)
    field, cols_a, cols_b, rows_a, rows_b = call(
        start_pass, [(2, nb, tile, length), strip, strip, edge, edge], "asa",
        [pltpu.SMEM((1, 1, 2, npos), jnp.int32), pltpu.SemaphoreType.DMA((nb + 1,))],
    )(offsets, counts, object_field)
    mine = cols_a
    cols_a, cols_b = swap_pairs(cols_a, cols_b, "col")
    rows_a, rows_b = swap_pairs(rows_a, rows_b, "row")
    corner = (2 * half + 8, length)
    corners_a, corners_b = call(start_corners, [corner, corner], "vv")(cols_a, cols_b)
    (ready,) = call(fetch_pass, [(8, length)], "avvv", cost=cost(1))(
        corners_a, probe, amplitudes, tables)
    corners_a, corners_b = swap_pairs(corners_a, corners_b, "row")

    full = (2, blocks, rows, length)
    strip = (2, rows, length)
    frame, acc, sums_a, sums_b = call(
        first_pass, [full, full, strip, strip], "ssa" + 10 * "v", [chosen],
    )(offsets, counts, ready, field, cols_a, cols_b, rows_a, rows_b, corners_a, corners_b,
      probe, amplitudes, tables)
    mine_a, mine_b = sums_a, sums_b
    sums_a, sums_b = swap_pairs(sums_a, sums_b, "col")
    edge = (2, nb - 1, length, length)
    acc, edges_a, edges_b = call(
        first_rest, [full, edge, edge], "ss" + 5 * "v", [chosen], cost(npos // 2),
    )(offsets, counts, frame, acc, probe, amplitudes, tables)
    edges_a, edges_b = swap_pairs(edges_a, edges_b, "row")
    (inverse,) = call(
        functools.partial(light_pass, npos=npos), [(blocks, rows, length)], 8 * "v" + "a",
        [memory((blocks + 2, rows + 2 * length, length), jnp.float32),
         memory((length, length), jnp.float32), memory((7 * 8, length), jnp.int32),
         pltpu.SMEM((7 * 8, length), jnp.int32), pltpu.SMEM((9 * npos + 1,), jnp.int32),
         pltpu.SemaphoreType.DMA],
        cost(npos // 2),
    )(mine, cols_a, cols_b, rows_a, rows_b, corners_a, corners_b, probe, acc)
    corner = (2, 2, length, length)
    corners_a, corners_b = call(middle_corners, [corner, corner], "vvvva")(
        mine_a, mine_b, sums_a, sums_b, inverse)
    corners_a, corners_b = swap_pairs(corners_a, corners_b, "row")

    work, total = call(update_pass, [full, full], "ss" + 8 * "v", [chosen], cost(npos // 2))(
        offsets, counts, frame, acc, inverse, sums_a, sums_b, probe, amplitudes, tables)
    strip = (rows, length)
    work, total, cols_a, cols_b = call(
        second_pass, [full, full, strip, strip], "ss" + 10 * "v", [chosen], cost(npos // 4),
    )(offsets, counts, work, total, inverse, edges_a, edges_b, corners_a, corners_b,
      probe, amplitudes, tables)
    cols_a, cols_b = swap_pairs(cols_a, cols_b, "col")
    own = (2, nb, tile, length)
    edge = (2, nb, half, length)
    sums, rows_a, rows_b = call(
        rows_pass, [own, edge, edge], "ss" + 5 * "v",
        [memory((2, nb, rows, length), jnp.float32), chosen], cost(npos // 4),
    )(offsets, counts, work, total, probe, amplitudes, tables)
    rows_a, rows_b = swap_pairs(rows_a, rows_b, "row")
    (inner,) = call(inner_pass, [own], "ss" + 4 * "v", [chosen], cost(npos // 4))(
        offsets, counts, work, probe, amplitudes, tables)
    corner = (2, half, length)
    corners_a, corners_b = call(end_corners, [corner, corner], "vv")(cols_a, cols_b)
    corners_a, corners_b = swap_pairs(corners_a, corners_b, "row")
    (out,) = call(last_pass, [(2, tile, tile)], 10 * "v")(
        work, sums, inner, inverse, cols_a, cols_b, rows_a, rows_b, corners_a, corners_b)
    return out


def solution(mesh):
    placed = (
        P(None, "row", "col"),
        P(),
        P("row", "col", None, None, None),
        P("row", "col", None, None),
        P("row", "col"),
    )
    return jax.shard_map(
        shards, mesh=mesh, in_specs=placed, out_specs=P(None, "row", "col"), check_vma=False
    )
```

```python
import functools
import math

import jax
import jax.numpy as jnp
import numpy as np
from jax import lax
from jax.experimental import pallas as pl
from jax.experimental.pallas import tpu as pltpu
from jax.sharding import PartitionSpec as P

ITERS = 2
FLOOR = 0.25
VMEM_BYTES = 16 * 1024 * 1024
GROUP = 4
ROWS = 8


def split(value):
    high = value.astype(jnp.bfloat16)
    low = (value - high.astype(jnp.float32)).astype(jnp.bfloat16)
    return high, low


def dft_tables(length):
    index = np.arange(length)
    angle = (index[:, None] * index[None, :] % length) * (2.0 * math.pi / length)
    cosine = np.cos(angle) / math.sqrt(length)
    sine = np.sin(angle) / math.sqrt(length)
    ahead = np.block([[cosine, -sine], [sine, cosine]])
    parts = []
    for table in (ahead, ahead.T):
        high = table.astype(jnp.bfloat16)
        low = (table - high.astype(np.float64)).astype(jnp.bfloat16)
        parts += [high, low]
    return np.stack(parts)


def lanes(shape):
    return lax.broadcasted_iota(jnp.int32, shape, len(shape) - 1)


def swap(value, half):
    return pltpu.roll(value, half, value.ndim - 1)


def odd_place(axis):
    return lax.axis_index(axis) % 2 == 1


def by_pairs(axis, low, high):
    odd = odd_place(axis)
    return jnp.where(odd, high, low), jnp.where(odd, low, high)


def by_side(axis, first, second):
    odd = odd_place(axis)
    return jnp.where(odd, second, first), jnp.where(odd, first, second)


def product(left, right):
    return jnp.dot(left, right, preferred_element_type=jnp.float32)


def times_right(rows, high, low):
    top, rest = split(rows)
    count = rows.shape[0]
    both = product(above(top, rest), high)
    return both[:count] + (both[count:] + product(top, low))


def times_left(high, low, columns):
    top, rest = split(columns)
    count = high.shape[0]
    both = product(above(high, low), top)
    return both[:count] + (both[count:] + product(high, rest))


def beside(left, right):
    return jnp.concatenate([left, right], axis=1)


def above(top, bottom):
    return jnp.concatenate([top, bottom], axis=0)


def choose(chosen, offsets, counts, tile, length, wanted):
    last = tile - length
    half = length // 2

    def look(slot, found):
        row = offsets[0, 0, 0, slot]
        col = offsets[0, 0, 1, slot]
        taken = wanted(
            mid_row=(row >= half) & (row <= last - half),
            mid_col=(col >= half) & (col <= last - half),
            cross_row=(row < 0) | (row > last),
            cross_col=(col < 0) | (col > last),
        )
        chosen[found] = slot
        return found + jnp.where(taken, 1, 0)

    found = lax.fori_loop(0, counts[0, 0], look, 0)
    filler = chosen[0]
    for k in range(GROUP):
        chosen[found + k] = filler
    return found


def read_turned(ref, lead, start, turn, length):
    body = ref[(*lead, pl.ds(start, length), slice(None))]
    tail = ref[(*lead, pl.ds(start + length, ROWS), slice(None))]
    own = lax.broadcasted_iota(jnp.int32, tail.shape, 0) >= turn
    return above(jnp.where(own, body[:ROWS], tail), body[ROWS:])


def add_turned(ref, lead, start, turn, value, taken):
    length = value.shape[0]
    value = jnp.where(taken, value, 0.0)
    first = value[:ROWS]
    own = lax.broadcasted_iota(jnp.int32, first.shape, 0) >= turn
    ref[(*lead, pl.ds(start, length), slice(None))] += above(
        jnp.where(own, first, 0.0), value[ROWS:])
    after = jnp.minimum(start + length, ref.shape[-2] - ROWS)
    after = pl.multiple_of(after, ROWS)
    ref[(*lead, pl.ds(after, ROWS), slice(None))] += jnp.where(own, 0.0, first)


def turned_start(row):
    turn = lax.rem(row, ROWS)
    return pl.multiple_of(row - turn, ROWS), turn


def add_gradients(frame, acc, probes, amps, offsets, tables, chosen, found, first_row=None, skip=0):
    length = probes.shape[-1]
    half = length // 2
    last = acc.shape[1] - 1
    begin = -half if first_row is None else first_row
    lane = lanes((length, length))

    def place(slot):
        col = offsets[0, 0, 1, slot] + length
        row, turn = turned_start(offsets[0, 0, 0, slot] + half)
        return row, turn, lax.div(col, length), lax.rem(col, length)

    def exit_wave(slot):
        row, turn, block, shift = place(slot)
        inside = lane >= shift
        window = [
            jnp.where(inside, read_turned(frame, (part, block), row, turn, length),
                      read_turned(frame, (part, block + 1), row, turn, length))
            for part in (0, 1)
        ]
        probe = (pltpu.roll(probes[turn, 0], shift, 1), pltpu.roll(probes[turn, 1], shift, 1))
        wave = (probe[0] * window[0] - probe[1] * window[1],
                probe[0] * window[1] + probe[1] * window[0])
        return probe, wave

    def shrink(real, imag, slot):
        ratio = amps[0, 0, slot] * lax.rsqrt(real * real + imag * imag + FLOOR) - 1.0
        return real * ratio, imag * ratio

    def put(slot, live, probe, back_r, back_i):
        row, turn, block, shift = place(slot)
        row = pl.multiple_of(row - half - begin, ROWS)
        block = block - skip
        after = jnp.minimum(block + 1, last)
        grads = (probe[0] * back_r + probe[1] * back_i, probe[0] * back_i - probe[1] * back_r)
        inside = lane >= jnp.where(live, shift, length)
        beyond = lane < jnp.where(live, shift, 0)
        for part in (0, 1):
            add_turned(acc, (part, block), row, turn, grads[part], inside)
            add_turned(acc, (part, after), row, turn, grads[part], beyond)

    def work(slots):
        probes, waves = zip(*[exit_wave(slot) for slot in slots])
        rows = jnp.concatenate([beside(*wave) for wave in waves], axis=0)
        mid = times_right(rows, tables[0], tables[1])
        mids = [mid[k * length:(k + 1) * length] for k in range(len(slots))]
        columns = above(
            jnp.concatenate([m[:, :length] for m in mids], axis=1),
            jnp.concatenate([m[:, length:] for m in mids], axis=1),
        )
        far = times_left(tables[2], tables[3], columns)
        changes = [
            shrink(far[:length, k * length:(k + 1) * length],
                   far[length:, k * length:(k + 1) * length], slot)
            for k, slot in enumerate(slots)
        ]
        columns = above(
            jnp.concatenate([c[0] for c in changes], axis=1),
            jnp.concatenate([c[1] for c in changes], axis=1),
        )
        mid = times_left(tables[0], tables[1], columns)
        rows = jnp.concatenate(
            [
                beside(mid[:length, k * length:(k + 1) * length],
                       mid[length:, k * length:(k + 1) * length])
                for k in range(len(slots))
            ],
            axis=0,
        )
        back = times_right(rows, tables[2], tables[3])
        return [
            (probes[k], back[k * length:(k + 1) * length, :length],
             back[k * length:(k + 1) * length, length:])
            for k in range(len(slots))
        ]

    def step(index, carry):
        places = [index * GROUP + k for k in range(GROUP)]
        slots = [chosen[at] for at in places]
        gradients = work(slots)
        for at, slot, gradient in zip(places, slots, gradients):
            put(slot, at < found, *gradient)
        return carry

    lax.fori_loop(0, (found + GROUP - 1) // GROUP, step, 0)


def start_pass(offsets_from, counts, field, tile_out, cols_a, cols_b, rows_a, rows_b, offsets, sems):
    _, nb, tile, length = tile_out.shape
    half = length // 2
    npos = offsets.shape[3]
    copies = {
        b: pltpu.make_async_copy(
            field.at[:, :, b * length:(b + 1) * length], tile_out.at[:, b], sems.at[b])
        for b in range(nb)
    }
    listed = pltpu.make_async_copy(offsets_from, offsets, sems.at[nb])
    listed.start()
    order = sorted(range(nb), key=lambda b: 0 < b < nb - 1)
    for b in order:
        copies[b].start()
    listed.wait()
    spot = lanes((8, length))
    info = jnp.zeros((8, length), jnp.int32)
    down = (lax.axis_index("row") + 1) * tile
    across = (lax.axis_index("col") + 1) * tile
    for k in range(npos):
        live = k < counts[0, 0]
        info = jnp.where(spot == k, jnp.where(live, offsets[0, 0, 0, k] + down, 0), info)
        info = jnp.where(spot == npos + k, jnp.where(live, offsets[0, 0, 1, k] + across, 0), info)
    info = info.astype(jnp.float32)
    cols_a[tile:] = info
    cols_b[tile:] = info
    rows_a[2 * nb * half:] = info
    rows_b[2 * nb * half:] = info
    for b in order:
        copies[b].wait()
    low = lanes((tile, length)) < half
    first = (tile_out[0, 0], tile_out[1, 0])
    last = (tile_out[0, nb - 1], tile_out[1, nb - 1])
    to_left = jnp.where(low, first[0], swap(first[1], half))
    to_right = jnp.where(low, swap(last[1], half), last[0])
    cols_a[:tile], cols_b[:tile] = by_pairs("col", to_left, to_right)
    for part in (0, 1):
        for b in range(nb):
            at = pl.ds((part * nb + b) * half, half)
            rows_a[at, :], rows_b[at, :] = by_pairs(
                "row", tile_out[part, b, :half], tile_out[part, b, tile - half:])


def start_corners(cols_a, cols_b, corners_a, corners_b):
    length = cols_a.shape[1]
    half = length // 2
    tile = cols_a.shape[0] - 8
    low = lanes((tile, length)) < half
    left, right = by_side("col", cols_a[:tile], cols_b[:tile])
    for part in (0, 1):
        if part:
            left, right = swap(left, half), swap(right, half)
        value = jnp.where(low, right, left)
        at = pl.ds(part * half, half)
        corners_a[at, :], corners_b[at, :] = by_pairs("row", value[:half], value[tile - half:])
    first = lax.broadcasted_iota(jnp.int32, (8, length), 0) == 0
    info = jnp.where(first, cols_a[tile:], cols_b[tile:])
    corners_a[2 * half:] = info
    corners_b[2 * half:] = info


def turn_pass(after, probe, amps, tables, probes):
    for turn in range(ROWS):
        for part in (0, 1):
            probes[turn, part] = pltpu.roll(probe[part], turn, 0) if turn else probe[part]


def first_pass(offsets, counts, field, cols_a, cols_b, rows_a, rows_b, corners_a, corners_b,
               probes, amps, tables, frame, acc, sums_a, sums_b, chosen):
    _, nb, tile, length = field.shape
    half = length // 2
    rows = tile + 2 * half
    own = pl.ds(half, tile)
    left, right = by_side("col", cols_a[:tile], cols_b[:tile])
    top = pl.ds(0, half)
    bottom = pl.ds(half + tile, half)
    for part in (0, 1):
        for b in range(nb):
            frame[part, b + 1, own, :] = field[part, b]
            at = pl.ds((part * nb + b) * half, half)
            frame[part, b + 1, top, :], frame[part, b + 1, bottom, :] = by_side(
                "row", rows_a[at, :], rows_b[at, :])
        frame[part, 0, own, :] = swap(left, half) if part else left
        frame[part, nb + 1, own, :] = swap(right, half) if part else right
        at = pl.ds(part * half, half)
        ends = by_side("row", corners_a[at, :], corners_b[at, :])
        for block in (0, nb + 1):
            frame[part, block, top, :], frame[part, block, bottom, :] = ends
    acc[...] = jnp.zeros_like(acc)
    found = choose(chosen, offsets, counts, tile, length, lambda mid_col, **_: ~mid_col)
    add_gradients(frame, acc, probes, amps, offsets, tables, chosen, found)
    low = lanes((rows, length)) < half
    for part in (0, 1):
        sums_a[part], sums_b[part] = by_pairs(
            "col",
            jnp.where(low, acc[part, 1], acc[part, 0]),
            jnp.where(low, acc[part, nb + 1], acc[part, nb]),
        )


def first_rest(offsets, counts, frame, acc_from, probes, amps, tables,
               acc, edges_a, edges_b, chosen):
    _, blocks, rows, length = frame.shape
    half = length // 2
    nb = blocks - 2
    acc[...] = acc_from[...]
    found = choose(
        chosen, offsets, counts, nb * length, length,
        lambda mid_row, mid_col, **_: mid_col & ~mid_row)
    add_gradients(frame, acc, probes, amps, offsets, tables, chosen, found)
    low = lanes((length, length)) < half
    for part in (0, 1):
        for b in range(nb - 1):
            ends = [
                acc[part, b + 2, at, :] if b < nb - 2
                else jnp.where(low, acc[part, nb, at, :], acc[part, 1, at, :])
                for at in (pl.ds(0, length), pl.ds(rows - length, length))
            ]
            edges_a[part, b], edges_b[part, b] = by_pairs("row", *ends)


def middle_corners(mine_a, mine_b, sums_a, sums_b, after, corners_a, corners_b):
    _, rows, length = sums_a.shape
    for part in (0, 1):
        for at, k in ((pl.ds(0, length), 0), (pl.ds(rows - length, length), 1)):
            sides = by_side(
                "col", mine_a[part, at, :] + sums_a[part, at, :],
                mine_b[part, at, :] + sums_b[part, at, :])
            for side in (0, 1):
                if k == 0:
                    up = sides
                else:
                    corners_a[part, side], corners_b[part, side] = by_pairs(
                        "row", up[side], sides[side])


def light_pass(mine, cols_a, cols_b, rows_a, rows_b, corners_a, corners_b, probes, after,
               inverse, light, places, listed, chosen, sem, *, npos):
    length = probes.shape[-1]
    half = length // 2
    blocks, rows, _ = inverse.shape
    nb = blocks - 2
    tile = nb * length
    my_row = lax.axis_index("row")
    my_col = lax.axis_index("col")
    sources = (mine, cols_a, cols_b, rows_a, rows_b, corners_a, corners_b)
    for k, source in enumerate(sources):
        given = source[source.shape[0] - 8:, :].astype(jnp.int32)
        col = pltpu.roll(given, length - npos, 1) - (my_col + 1) * tile + 2 * length
        row = given - (my_row + 1) * tile + half + length
        near = (given > 0) & (row > 0) & (row < rows + length)
        near = near & (col > length - half) & (col < 2 * length + tile + half)
        places[pl.ds(8 * k, 8), :] = jnp.where(near, row * 4 * tile + col, 0)
    copy = pltpu.make_async_copy(places, listed, sem)
    copy.start()
    light[...] = jnp.zeros_like(light)
    lane = lanes((length, length))
    copy.wait()

    def look(index, found):
        line = jnp.where(index < len(sources), 8 * index, 8 * (index - 2) + 1)
        for slot in range(npos):
            place = listed[line, slot]
            chosen[found] = place
            found = found + jnp.where(place > 0, 1, 0)
        return found

    found = lax.fori_loop(0, len(sources) + 2, look, 0)

    def put(index, carry):
        place = chosen[index]
        start, turn = turned_start(lax.div(place, 4 * tile))
        col = lax.rem(place, 4 * tile)
        block = lax.div(col, length)
        shift = lax.rem(col, length)
        real, imag = probes[turn, 0], probes[turn, 1]
        value = pltpu.roll(real * real + imag * imag, shift, 1)
        add_turned(light, (block,), start, turn, value, lane >= shift)
        add_turned(light, (block + 1,), start, turn, value, lane < shift)
        return carry

    lax.fori_loop(0, found, put, 0)
    spot = lax.broadcasted_iota(jnp.int32, (rows, length), 0)
    keep_from = jnp.where(my_row > 0, 0, half)
    keep_to = jnp.where(my_row < lax.axis_size("row") - 1, rows, rows - half)
    kept = (spot >= keep_from) & (spot < keep_to)
    for b in range(blocks):
        value = 1.0 / (light[b + 1, pl.ds(length, rows), :] + 1.0)
        keep = kept
        if b == 0:
            keep = keep & (my_col > 0)
        if b == nb + 1:
            keep = keep & (my_col < lax.axis_size("col") - 1)
        inverse[b] = jnp.where(keep, value, 0.0)


def update_pass(offsets, counts, frame, acc, inverse, sums_a, sums_b, probes, amps, tables,
                work, total, chosen):
    _, blocks, rows, length = frame.shape
    half = length // 2
    nb = blocks - 2
    work[...] = acc[...]
    found = choose(
        chosen, offsets, counts, nb * length, length,
        lambda mid_row, mid_col, **_: mid_col & mid_row)
    add_gradients(frame, work, probes, amps, offsets, tables, chosen, found)
    low = lanes((rows, length)) < half
    for part in (0, 1):
        left, right = by_side("col", sums_a[part], sums_b[part])
        for b in range(blocks):
            value = work[part, b]
            if b == 0:
                value = value + left
            if b == 1:
                value = value + jnp.where(low, left, 0.0)
            if b == nb:
                value = value + jnp.where(low, 0.0, right)
            if b == nb + 1:
                value = value + right
            work[part, b] = frame[part, b] + value * inverse[b]
    total[...] = jnp.zeros_like(total)
    found = choose(chosen, offsets, counts, nb * length, length, lambda mid_row, **_: mid_row)
    add_gradients(work, total, probes, amps, offsets, tables, chosen, found)


def second_pass(offsets, counts, work_from, total_from, inverse, edges_a, edges_b,
                corners_a, corners_b, probes, amps, tables,
                work, total, cols_a, cols_b, chosen):
    _, blocks, rows, length = work.shape
    half = length // 2
    nb = blocks - 2
    tile = nb * length
    near = lanes((length, length)) < half
    middle = pl.ds(length, rows - 2 * length)
    for part in (0, 1):
        edges = [by_side("row", edges_a[part, b], edges_b[part, b]) for b in range(nb - 1)]
        corners = [by_side("row", corners_a[part, side], corners_b[part, side]) for side in (0, 1)]
        for k, at in enumerate((pl.ds(0, length), pl.ds(rows - length, length))):
            left, right, ends = corners[0][k], corners[1][k], edges[nb - 2][k]
            add = [left, jnp.where(near, left, ends)]
            add += [edges[b][k] for b in range(nb - 2)]
            add += [jnp.where(near, ends, right), right]
            for b in range(blocks):
                work[part, b, at, :] = work_from[part, b, at, :] + add[b] * inverse[b, at, :]
        for b in range(blocks):
            work[part, b, middle, :] = work_from[part, b, middle, :]
    total[...] = total_from[...]
    found = choose(
        chosen, offsets, counts, tile, length,
        lambda mid_row, cross_col, **_: ~mid_row & cross_col)
    add_gradients(work, total, probes, amps, offsets, tables, chosen, found)
    low = lanes((rows, length)) < half
    cols_a[...], cols_b[...] = by_pairs(
        "col",
        jnp.where(low, swap(total[1, 0], half), total[0, 0]),
        jnp.where(low, total[0, nb + 1], swap(total[1, nb + 1], half)),
    )


def rows_pass(offsets, counts, work, total, probes, amps, tables, sums, rows_a, rows_b, acc, chosen):
    _, nb, tile, length = sums.shape
    half = length // 2
    acc[...] = total[:, 1:nb + 1]
    found = choose(
        chosen, offsets, counts, tile, length,
        lambda cross_row, cross_col, **_: cross_row & ~cross_col)
    add_gradients(work, acc, probes, amps, offsets, tables, chosen, found, skip=1)
    for part in (0, 1):
        for b in range(nb):
            sums[part, b] = acc[part, b, pl.ds(half, tile), :]
            rows_a[part, b], rows_b[part, b] = by_pairs(
                "row", acc[part, b, :half, :], acc[part, b, half + tile:, :])


def inner_pass(offsets, counts, work, probes, amps, tables, sums, chosen):
    _, nb, tile, length = sums.shape
    sums[...] = jnp.zeros_like(sums)
    found = choose(
        chosen, offsets, counts, tile, length,
        lambda mid_row, cross_row, cross_col, **_: ~mid_row & ~cross_row & ~cross_col)
    add_gradients(work, sums, probes, amps, offsets, tables, chosen, found, first_row=0, skip=1)


def end_corners(cols_a, cols_b, corners_a, corners_b):
    rows, length = cols_a.shape
    half = length // 2
    for side, value in enumerate(by_side("col", cols_a[...], cols_b[...])):
        corners_a[side], corners_b[side] = by_pairs("row", value[:half], value[rows - half:])


def last_pass(work, sums, inner, inverse, cols_a, cols_b, rows_a, rows_b, corners_a, corners_b, out):
    _, nb, tile, length = sums.shape
    half = length // 2
    low = lanes((tile, length)) < half
    own = pl.ds(half, tile)
    gap = jnp.zeros((tile - 2 * half, length), jnp.float32)
    sides = []
    for side, value in enumerate(by_side("col", cols_a[own, :], cols_b[own, :])):
        up, down = by_side("row", corners_a[side], corners_b[side])
        sides.append(value + above(above(up, gap), down))
    left, right = sides
    for part in (0, 1):
        if part:
            left, right = swap(left, half), swap(right, half)
        for b in range(nb):
            up, down = by_side("row", rows_a[part, b], rows_b[part, b])
            value = sums[part, b] + inner[part, b] + above(above(up, gap), down)
            if b == 0:
                value = value + jnp.where(low, left, 0.0)
            if b == nb - 1:
                value = value + jnp.where(low, 0.0, right)
            out[part, :, b * length:(b + 1) * length] = (
                work[part, b + 1, own, :] + value * inverse[b + 1, own, :])


def whole(memory_space=pltpu.VMEM):
    return pl.BlockSpec(memory_space=memory_space)


def call(body, shapes, places, scratch=(), cost=None):
    return pl.pallas_call(
        body,
        out_shape=[jax.ShapeDtypeStruct(shape, jnp.float32) for shape in shapes],
        in_specs=[whole({"s": pltpu.SMEM, "v": pltpu.VMEM, "a": pl.ANY, "h": pltpu.HBM}[p]) for p in places],
        out_specs=[whole()] * len(shapes),
        scratch_shapes=list(scratch),
        compiler_params=pltpu.CompilerParams(vmem_limit_bytes=VMEM_BYTES),
        cost_estimate=cost,
    )


def swap_pairs(first, second, axis):
    count = lax.axis_size(axis)
    got = []
    for value, start in ((first, 1), (second, 0)):
        pairs = [(i, i + 1) for i in range(start, count - 1, 2)]
        got.append(lax.ppermute(value, axis, pairs + [(b, a) for a, b in pairs]))
    return got


def shards(object_field, probe, amplitudes, offsets, counts):
    length = probe.shape[-1]
    half = length // 2
    tile = object_field.shape[1]
    npos = offsets.shape[2]
    nb = tile // length
    blocks = nb + 2
    rows = tile + 2 * half
    tables = jnp.asarray(dft_tables(length))
    offsets = jnp.swapaxes(offsets, 2, 3)

    def cost(positions):
        steps = 4 * 3 * 2 * length * (2 * length) ** 2
        return pl.CostEstimate(
            flops=positions * steps, bytes_accessed=8_000_000,
            transcendentals=positions * length * length)

    memory = pltpu.VMEM
    chosen = pltpu.SMEM((npos + GROUP,), jnp.int32)
    strip = (tile + 8, length)
    edge = (2 * nb * half + 8, length)
    field, cols_a, cols_b, rows_a, rows_b = call(
        start_pass, [(2, nb, tile, length), strip, strip, edge, edge], "asa",
        [pltpu.SMEM((1, 1, 2, npos), jnp.int32), pltpu.SemaphoreType.DMA((nb + 1,))],
    )(offsets, counts, object_field)
    mine = cols_a
    cols_a, cols_b = swap_pairs(cols_a, cols_b, "col")
    rows_a, rows_b = swap_pairs(rows_a, rows_b, "row")
    corner = (2 * half + 8, length)
    corners_a, corners_b = call(start_corners, [corner, corner], "vv")(cols_a, cols_b)
    (probes,) = call(turn_pass, [(ROWS, 2, length, length)], "avvv", cost=cost(1))(
        corners_a, probe, amplitudes, tables)
    corners_a, corners_b = swap_pairs(corners_a, corners_b, "row")

    full = (2, blocks, rows, length)
    strip = (2, rows, length)
    frame, acc, sums_a, sums_b = call(
        first_pass, [full, full, strip, strip], "ss" + 10 * "v", [chosen],
    )(offsets, counts, field, cols_a, cols_b, rows_a, rows_b, corners_a, corners_b,
      probes, amplitudes, tables)
    mine_a, mine_b = sums_a, sums_b
    sums_a, sums_b = swap_pairs(sums_a, sums_b, "col")
    edge = (2, nb - 1, length, length)
    acc, edges_a, edges_b = call(
        first_rest, [full, edge, edge], "ss" + 5 * "v", [chosen], cost(npos // 2),
    )(offsets, counts, frame, acc, probes, amplitudes, tables)
    edges_a, edges_b = swap_pairs(edges_a, edges_b, "row")
    (inverse,) = call(
        functools.partial(light_pass, npos=npos), [(blocks, rows, length)], 8 * "v" + "a",
        [memory((blocks + 2, rows + 2 * length, length), jnp.float32),
         memory((7 * 8, length), jnp.int32),
         pltpu.SMEM((7 * 8, length), jnp.int32), pltpu.SMEM((9 * npos + 1,), jnp.int32),
         pltpu.SemaphoreType.DMA],
        cost(npos // 2),
    )(mine, cols_a, cols_b, rows_a, rows_b, corners_a, corners_b, probes, acc)
    corner = (2, 2, length, length)
    corners_a, corners_b = call(middle_corners, [corner, corner], "vvvva")(
        mine_a, mine_b, sums_a, sums_b, inverse)
    corners_a, corners_b = swap_pairs(corners_a, corners_b, "row")

    work, total = call(update_pass, [full, full], "ss" + 8 * "v", [chosen], cost(npos // 2))(
        offsets, counts, frame, acc, inverse, sums_a, sums_b, probes, amplitudes, tables)
    strip = (rows, length)
    work, total, cols_a, cols_b = call(
        second_pass, [full, full, strip, strip], "ss" + 10 * "v", [chosen], cost(npos // 4),
    )(offsets, counts, work, total, inverse, edges_a, edges_b, corners_a, corners_b,
      probes, amplitudes, tables)
    cols_a, cols_b = swap_pairs(cols_a, cols_b, "col")
    own = (2, nb, tile, length)
    edge = (2, nb, half, length)
    sums, rows_a, rows_b = call(
        rows_pass, [own, edge, edge], "ss" + 5 * "v",
        [memory((2, nb, rows, length), jnp.float32), chosen], cost(npos // 4),
    )(offsets, counts, work, total, probes, amplitudes, tables)
    rows_a, rows_b = swap_pairs(rows_a, rows_b, "row")
    (inner,) = call(inner_pass, [own], "ss" + 4 * "v", [chosen], cost(npos // 4))(
        offsets, counts, work, probes, amplitudes, tables)
    corner = (2, half, length)
    corners_a, corners_b = call(end_corners, [corner, corner], "vv")(cols_a, cols_b)
    corners_a, corners_b = swap_pairs(corners_a, corners_b, "row")
    (out,) = call(last_pass, [(2, tile, tile)], 10 * "v")(
        work, sums, inner, inverse, cols_a, cols_b, rows_a, rows_b, corners_a, corners_b)
    return out


def solution(mesh):
    placed = (
        P(None, "row", "col"),
        P(),
        P("row", "col", None, None, None),
        P("row", "col", None, None),
        P("row", "col"),
    )
    return jax.shard_map(
        shards, mesh=mesh, in_specs=placed, out_specs=P(None, "row", "col"), check_vma=False
    )
```

```python
import functools
import math

import jax
import jax.numpy as jnp
import numpy as np
from jax import lax
from jax.experimental import pallas as pl
from jax.experimental.pallas import tpu as pltpu
from jax.sharding import PartitionSpec as P

ITERS = 2
FLOOR = 0.25
VMEM_BYTES = 16 * 1024 * 1024
GROUP = 4
CHAIN = 2


def split(value):
    high = value.astype(jnp.bfloat16)
    low = (value - high.astype(jnp.float32)).astype(jnp.bfloat16)
    return high, low


def dft_tables(length):
    index = np.arange(length)
    angle = (index[:, None] * index[None, :] % length) * (2.0 * math.pi / length)
    cosine = np.cos(angle) / math.sqrt(length)
    sine = np.sin(angle) / math.sqrt(length)
    ahead = np.block([[cosine, -sine], [sine, cosine]])
    parts = []
    for table in (ahead, ahead.T):
        high = table.astype(jnp.bfloat16)
        low = (table - high.astype(np.float64)).astype(jnp.bfloat16)
        parts += [high, low]
    return np.stack(parts)


def lanes(shape):
    return lax.broadcasted_iota(jnp.int32, shape, len(shape) - 1)


def swap(value, half):
    return pltpu.roll(value, half, value.ndim - 1)


def odd_place(axis):
    return lax.axis_index(axis) % 2 == 1


def by_pairs(axis, low, high):
    odd = odd_place(axis)
    return jnp.where(odd, high, low), jnp.where(odd, low, high)


def by_side(axis, first, second):
    odd = odd_place(axis)
    return jnp.where(odd, second, first), jnp.where(odd, first, second)


def times_right(rows, high, low):
    top, rest = split(rows)
    left = jnp.concatenate([top, top, rest], axis=1)
    right = jnp.concatenate([high, low, high], axis=0)
    return jnp.dot(left, right, preferred_element_type=jnp.float32)


def times_left(high, low, columns):
    top, rest = split(columns)
    left = jnp.concatenate([high, low, high], axis=1)
    right = jnp.concatenate([top, top, rest], axis=0)
    return jnp.dot(left, right, preferred_element_type=jnp.float32)


def beside(left, right):
    return jnp.concatenate([left, right], axis=1)


def above(top, bottom):
    return jnp.concatenate([top, bottom], axis=0)


def choose(chosen, offsets, counts, tile, length, wanted):
    last = tile - length
    half = length // 2

    def look(slot, found):
        row = offsets[0, 0, 0, slot]
        col = offsets[0, 0, 1, slot]
        taken = wanted(
            mid_row=(row >= half) & (row <= last - half),
            mid_col=(col >= half) & (col <= last - half),
            cross_row=(row < 0) | (row > last),
            cross_col=(col < 0) | (col > last),
        )
        chosen[found] = slot
        return found + jnp.where(taken, 1, 0)

    found = lax.fori_loop(0, counts[0, 0], look, 0)
    filler = chosen[0]
    for k in range(GROUP):
        chosen[found + k] = filler
    return found


def add_gradients(frame, acc, probe_ref, amps, offsets, tables, chosen, found, first_row=None, skip=0):
    length = probe_ref.shape[-1]
    half = length // 2
    last = acc.shape[1] - 1
    begin = -half if first_row is None else first_row
    lane = lanes((length, length))

    def place(slot):
        col = offsets[0, 0, 1, slot] + length
        return offsets[0, 0, 0, slot], lax.div(col, length), lax.rem(col, length)

    def exit_wave(slot):
        row, block, shift = place(slot)
        inside = lane >= shift
        at = pl.ds(row + half, length)
        window = [
            jnp.where(inside, frame[part, block, at, :], frame[part, block + 1, at, :])
            for part in (0, 1)
        ]
        probe = (pltpu.roll(probe_ref[0], shift, 1), pltpu.roll(probe_ref[1], shift, 1))
        wave = (probe[0] * window[0] - probe[1] * window[1],
                probe[0] * window[1] + probe[1] * window[0])
        return probe, wave

    def shrink(real, imag, slot):
        ratio = amps[0, 0, slot] * lax.rsqrt(real * real + imag * imag + FLOOR) - 1.0
        return real * ratio, imag * ratio

    def put(slot, live, probe, back_r, back_i):
        row, block, shift = place(slot)
        at = pl.ds(row - begin, length)
        block = block - skip
        after = jnp.minimum(block + 1, last)
        grads = (probe[0] * back_r + probe[1] * back_i, probe[0] * back_i - probe[1] * back_r)
        bound = jnp.where(live, shift, length)
        inside = lane >= bound
        beyond = lane < jnp.where(live, shift, 0)
        for part in (0, 1):
            acc[part, block, at, :] += jnp.where(inside, grads[part], 0.0)
            acc[part, after, at, :] += jnp.where(beyond, grads[part], 0.0)

    def work(slots):
        probes, waves = zip(*[exit_wave(slot) for slot in slots])
        rows = jnp.concatenate([beside(*wave) for wave in waves], axis=0)
        mid = times_right(rows, tables[0], tables[1])
        yield None
        mids = [mid[k * length:(k + 1) * length] for k in range(len(slots))]
        columns = above(
            jnp.concatenate([m[:, :length] for m in mids], axis=1),
            jnp.concatenate([m[:, length:] for m in mids], axis=1),
        )
        far = times_left(tables[2], tables[3], columns)
        yield None
        changes = [
            shrink(far[:length, k * length:(k + 1) * length],
                   far[length:, k * length:(k + 1) * length], slot)
            for k, slot in enumerate(slots)
        ]
        columns = above(
            jnp.concatenate([c[0] for c in changes], axis=1),
            jnp.concatenate([c[1] for c in changes], axis=1),
        )
        mid = times_left(tables[0], tables[1], columns)
        yield None
        rows = jnp.concatenate(
            [
                beside(mid[:length, k * length:(k + 1) * length],
                       mid[length:, k * length:(k + 1) * length])
                for k in range(len(slots))
            ],
            axis=0,
        )
        back = times_right(rows, tables[2], tables[3])
        yield None
        yield [
            (probes[k], back[k * length:(k + 1) * length, :length],
             back[k * length:(k + 1) * length, length:])
            for k in range(len(slots))
        ]

    def step(index, carry):
        places = [index * GROUP + k for k in range(GROUP)]
        slots = [chosen[at] for at in places]
        chains = [work(slots[k:k + CHAIN]) for k in range(0, GROUP, CHAIN)]
        gradients = [None]
        while gradients[0] is None:
            gradients = [next(chain) for chain in chains]
        gradients = [gradient for chain in gradients for gradient in chain]
        for at, slot, gradient in zip(places, slots, gradients):
            put(slot, at < found, *gradient)
        return carry

    lax.fori_loop(0, (found + GROUP - 1) // GROUP, step, 0)


def start_pass(offsets_from, counts, field, tile_out, cols_a, cols_b, rows_a, rows_b, offsets, sems):
    _, nb, tile, length = tile_out.shape
    half = length // 2
    npos = offsets.shape[3]
    copies = {
        b: pltpu.make_async_copy(
            field.at[:, :, b * length:(b + 1) * length], tile_out.at[:, b], sems.at[b])
        for b in range(nb)
    }
    listed = pltpu.make_async_copy(offsets_from, offsets, sems.at[nb])
    listed.start()
    order = sorted(range(nb), key=lambda b: 0 < b < nb - 1)
    for b in order:
        copies[b].start()
    listed.wait()
    spot = lanes((8, length))
    info = jnp.zeros((8, length), jnp.int32)
    down = (lax.axis_index("row") + 1) * tile
    across = (lax.axis_index("col") + 1) * tile
    for k in range(npos):
        live = k < counts[0, 0]
        info = jnp.where(spot == k, jnp.where(live, offsets[0, 0, 0, k] + down, 0), info)
        info = jnp.where(spot == npos + k, jnp.where(live, offsets[0, 0, 1, k] + across, 0), info)
    info = info.astype(jnp.float32)
    cols_a[tile:] = info
    cols_b[tile:] = info
    rows_a[2 * nb * half:] = info
    rows_b[2 * nb * half:] = info
    for b in order:
        copies[b].wait()
    low = lanes((tile, length)) < half
    first = (tile_out[0, 0], tile_out[1, 0])
    last = (tile_out[0, nb - 1], tile_out[1, nb - 1])
    to_left = jnp.where(low, first[0], swap(first[1], half))
    to_right = jnp.where(low, swap(last[1], half), last[0])
    cols_a[:tile], cols_b[:tile] = by_pairs("col", to_left, to_right)
    for part in (0, 1):
        for b in range(nb):
            at = pl.ds((part * nb + b) * half, half)
            rows_a[at, :], rows_b[at, :] = by_pairs(
                "row", tile_out[part, b, :half], tile_out[part, b, tile - half:])


def start_corners(cols_a, cols_b, corners_a, corners_b):
    length = cols_a.shape[1]
    half = length // 2
    tile = cols_a.shape[0] - 8
    low = lanes((tile, length)) < half
    left, right = by_side("col", cols_a[:tile], cols_b[:tile])
    for part in (0, 1):
        if part:
            left, right = swap(left, half), swap(right, half)
        value = jnp.where(low, right, left)
        at = pl.ds(part * half, half)
        corners_a[at, :], corners_b[at, :] = by_pairs("row", value[:half], value[tile - half:])
    first = lax.broadcasted_iota(jnp.int32, (8, length), 0) == 0
    info = jnp.where(first, cols_a[tile:], cols_b[tile:])
    corners_a[2 * half:] = info
    corners_b[2 * half:] = info


def fetch_pass(after, probe, amps, tables, out):
    out[...] = jnp.zeros_like(out)


def first_pass(offsets, counts, ready, field, cols_a, cols_b, rows_a, rows_b, corners_a, corners_b,
               probe, amps, tables, frame, acc, sums_a, sums_b, chosen):
    _, nb, tile, length = field.shape
    half = length // 2
    rows = tile + 2 * half
    own = pl.ds(half, tile)
    left, right = by_side("col", cols_a[:tile], cols_b[:tile])
    top = pl.ds(0, half)
    bottom = pl.ds(half + tile, half)
    for part in (0, 1):
        for b in range(nb):
            frame[part, b + 1, own, :] = field[part, b]
            at = pl.ds((part * nb + b) * half, half)
            frame[part, b + 1, top, :], frame[part, b + 1, bottom, :] = by_side(
                "row", rows_a[at, :], rows_b[at, :])
        frame[part, 0, own, :] = swap(left, half) if part else left
        frame[part, nb + 1, own, :] = swap(right, half) if part else right
        at = pl.ds(part * half, half)
        ends = by_side("row", corners_a[at, :], corners_b[at, :])
        for block in (0, nb + 1):
            frame[part, block, top, :], frame[part, block, bottom, :] = ends
    acc[...] = jnp.zeros_like(acc)
    found = choose(chosen, offsets, counts, tile, length, lambda mid_col, **_: ~mid_col)
    add_gradients(frame, acc, probe, amps, offsets, tables, chosen, found)
    low = lanes((rows, length)) < half
    for part in (0, 1):
        sums_a[part], sums_b[part] = by_pairs(
            "col",
            jnp.where(low, acc[part, 1], acc[part, 0]),
            jnp.where(low, acc[part, nb + 1], acc[part, nb]),
        )


def first_rest(offsets, counts, frame, acc_from, probe, amps, tables,
               acc, edges_a, edges_b, chosen):
    _, blocks, rows, length = frame.shape
    half = length // 2
    nb = blocks - 2
    acc[...] = acc_from[...]
    found = choose(
        chosen, offsets, counts, nb * length, length,
        lambda mid_row, mid_col, **_: mid_col & ~mid_row)
    add_gradients(frame, acc, probe, amps, offsets, tables, chosen, found)
    low = lanes((length, length)) < half
    for part in (0, 1):
        for b in range(nb - 1):
            ends = [
                acc[part, b + 2, at, :] if b < nb - 2
                else jnp.where(low, acc[part, nb, at, :], acc[part, 1, at, :])
                for at in (pl.ds(0, length), pl.ds(rows - length, length))
            ]
            edges_a[part, b], edges_b[part, b] = by_pairs("row", *ends)


def middle_corners(mine_a, mine_b, sums_a, sums_b, after, corners_a, corners_b):
    _, rows, length = sums_a.shape
    for part in (0, 1):
        for at, k in ((pl.ds(0, length), 0), (pl.ds(rows - length, length), 1)):
            sides = by_side(
                "col", mine_a[part, at, :] + sums_a[part, at, :],
                mine_b[part, at, :] + sums_b[part, at, :])
            for side in (0, 1):
                if k == 0:
                    up = sides
                else:
                    corners_a[part, side], corners_b[part, side] = by_pairs(
                        "row", up[side], sides[side])


def light_pass(mine, cols_a, cols_b, rows_a, rows_b, corners_a, corners_b, probe, after,
               inverse, light, power, places, listed, chosen, sem, *, npos):
    length = probe.shape[-1]
    half = length // 2
    blocks, rows, _ = inverse.shape
    nb = blocks - 2
    tile = nb * length
    my_row = lax.axis_index("row")
    my_col = lax.axis_index("col")
    sources = (mine, cols_a, cols_b, rows_a, rows_b, corners_a, corners_b)
    for k, source in enumerate(sources):
        given = source[source.shape[0] - 8:, :].astype(jnp.int32)
        col = pltpu.roll(given, length - npos, 1) - (my_col + 1) * tile + 2 * length
        row = given - (my_row + 1) * tile + half + length
        near = (given > 0) & (row > 0) & (row < rows + length)
        near = near & (col > length - half) & (col < 2 * length + tile + half)
        places[pl.ds(8 * k, 8), :] = jnp.where(near, row * 4 * tile + col, 0)
    copy = pltpu.make_async_copy(places, listed, sem)
    copy.start()
    light[...] = jnp.zeros_like(light)
    power[...] = probe[0] * probe[0] + probe[1] * probe[1]
    lane = lanes((length, length))
    copy.wait()

    def look(index, found):
        line = jnp.where(index < len(sources), 8 * index, 8 * (index - 2) + 1)
        for slot in range(npos):
            place = listed[line, slot]
            chosen[found] = place
            found = found + jnp.where(place > 0, 1, 0)
        return found

    found = lax.fori_loop(0, len(sources) + 2, look, 0)

    def put(index, carry):
        place = chosen[index]
        start = lax.div(place, 4 * tile)
        col = lax.rem(place, 4 * tile)
        block = lax.div(col, length)
        shift = lax.rem(col, length)
        value = pltpu.roll(power[...], shift, 1)
        inside = lane >= shift
        light[block, pl.ds(start, length), :] += jnp.where(inside, value, 0.0)
        light[block + 1, pl.ds(start, length), :] += jnp.where(inside, 0.0, value)
        return carry

    lax.fori_loop(0, found, put, 0)
    spot = lax.broadcasted_iota(jnp.int32, (rows, length), 0)
    keep_from = jnp.where(my_row > 0, 0, half)
    keep_to = jnp.where(my_row < lax.axis_size("row") - 1, rows, rows - half)
    kept = (spot >= keep_from) & (spot < keep_to)
    for b in range(blocks):
        value = 1.0 / (light[b + 1, pl.ds(length, rows), :] + 1.0)
        keep = kept
        if b == 0:
            keep = keep & (my_col > 0)
        if b == nb + 1:
            keep = keep & (my_col < lax.axis_size("col") - 1)
        inverse[b] = jnp.where(keep, value, 0.0)


def update_pass(offsets, counts, frame, acc, inverse, sums_a, sums_b, probe, amps, tables,
                work, total, chosen):
    _, blocks, rows, length = frame.shape
    half = length // 2
    nb = blocks - 2
    work[...] = acc[...]
    found = choose(
        chosen, offsets, counts, nb * length, length,
        lambda mid_row, mid_col, **_: mid_col & mid_row)
    add_gradients(frame, work, probe, amps, offsets, tables, chosen, found)
    low = lanes((rows, length)) < half
    for part in (0, 1):
        left, right = by_side("col", sums_a[part], sums_b[part])
        for b in range(blocks):
            value = work[part, b]
            if b == 0:
                value = value + left
            if b == 1:
                value = value + jnp.where(low, left, 0.0)
            if b == nb:
                value = value + jnp.where(low, 0.0, right)
            if b == nb + 1:
                value = value + right
            work[part, b] = frame[part, b] + value * inverse[b]
    total[...] = jnp.zeros_like(total)
    found = choose(chosen, offsets, counts, nb * length, length, lambda mid_row, **_: mid_row)
    add_gradients(work, total, probe, amps, offsets, tables, chosen, found)


def second_pass(offsets, counts, work_from, total_from, inverse, edges_a, edges_b,
                corners_a, corners_b, probe, amps, tables,
                work, total, cols_a, cols_b, chosen):
    _, blocks, rows, length = work.shape
    half = length // 2
    nb = blocks - 2
    tile = nb * length
    near = lanes((length, length)) < half
    middle = pl.ds(length, rows - 2 * length)
    for part in (0, 1):
        edges = [by_side("row", edges_a[part, b], edges_b[part, b]) for b in range(nb - 1)]
        corners = [by_side("row", corners_a[part, side], corners_b[part, side]) for side in (0, 1)]
        for k, at in enumerate((pl.ds(0, length), pl.ds(rows - length, length))):
            left, right, ends = corners[0][k], corners[1][k], edges[nb - 2][k]
            add = [left, jnp.where(near, left, ends)]
            add += [edges[b][k] for b in range(nb - 2)]
            add += [jnp.where(near, ends, right), right]
            for b in range(blocks):
                work[part, b, at, :] = work_from[part, b, at, :] + add[b] * inverse[b, at, :]
        for b in range(blocks):
            work[part, b, middle, :] = work_from[part, b, middle, :]
    total[...] = total_from[...]
    found = choose(
        chosen, offsets, counts, tile, length,
        lambda mid_row, cross_col, **_: ~mid_row & cross_col)
    add_gradients(work, total, probe, amps, offsets, tables, chosen, found)
    low = lanes((rows, length)) < half
    cols_a[...], cols_b[...] = by_pairs(
        "col",
        jnp.where(low, swap(total[1, 0], half), total[0, 0]),
        jnp.where(low, total[0, nb + 1], swap(total[1, nb + 1], half)),
    )


def rows_pass(offsets, counts, work, total, probe, amps, tables, sums, rows_a, rows_b, acc, chosen):
    _, nb, tile, length = sums.shape
    half = length // 2
    acc[...] = total[:, 1:nb + 1]
    found = choose(
        chosen, offsets, counts, tile, length,
        lambda cross_row, cross_col, **_: cross_row & ~cross_col)
    add_gradients(work, acc, probe, amps, offsets, tables, chosen, found, skip=1)
    for part in (0, 1):
        for b in range(nb):
            sums[part, b] = acc[part, b, pl.ds(half, tile), :]
            rows_a[part, b], rows_b[part, b] = by_pairs(
                "row", acc[part, b, :half, :], acc[part, b, half + tile:, :])


def inner_pass(offsets, counts, work, probe, amps, tables, sums, chosen):
    _, nb, tile, length = sums.shape
    sums[...] = jnp.zeros_like(sums)
    found = choose(
        chosen, offsets, counts, tile, length,
        lambda mid_row, cross_row, cross_col, **_: ~mid_row & ~cross_row & ~cross_col)
    add_gradients(work, sums, probe, amps, offsets, tables, chosen, found, first_row=0, skip=1)


def end_corners(cols_a, cols_b, corners_a, corners_b):
    rows, length = cols_a.shape
    half = length // 2
    for side, value in enumerate(by_side("col", cols_a[...], cols_b[...])):
        corners_a[side], corners_b[side] = by_pairs("row", value[:half], value[rows - half:])


def last_pass(work, sums, inner, inverse, cols_a, cols_b, rows_a, rows_b, corners_a, corners_b, out):
    _, nb, tile, length = sums.shape
    half = length // 2
    low = lanes((tile, length)) < half
    own = pl.ds(half, tile)
    gap = jnp.zeros((tile - 2 * half, length), jnp.float32)
    sides = []
    for side, value in enumerate(by_side("col", cols_a[own, :], cols_b[own, :])):
        up, down = by_side("row", corners_a[side], corners_b[side])
        sides.append(value + above(above(up, gap), down))
    left, right = sides
    for part in (0, 1):
        if part:
            left, right = swap(left, half), swap(right, half)
        for b in range(nb):
            up, down = by_side("row", rows_a[part, b], rows_b[part, b])
            value = sums[part, b] + inner[part, b] + above(above(up, gap), down)
            if b == 0:
                value = value + jnp.where(low, left, 0.0)
            if b == nb - 1:
                value = value + jnp.where(low, 0.0, right)
            out[part, :, b * length:(b + 1) * length] = (
                work[part, b + 1, own, :] + value * inverse[b + 1, own, :])


def whole(memory_space=pltpu.VMEM):
    return pl.BlockSpec(memory_space=memory_space)


def call(body, shapes, places, scratch=(), cost=None):
    return pl.pallas_call(
        body,
        out_shape=[jax.ShapeDtypeStruct(shape, jnp.float32) for shape in shapes],
        in_specs=[whole({"s": pltpu.SMEM, "v": pltpu.VMEM, "a": pl.ANY, "h": pltpu.HBM}[p]) for p in places],
        out_specs=[whole()] * len(shapes),
        scratch_shapes=list(scratch),
        compiler_params=pltpu.CompilerParams(vmem_limit_bytes=VMEM_BYTES),
        cost_estimate=cost,
    )


def swap_pairs(first, second, axis):
    count = lax.axis_size(axis)
    got = []
    for value, start in ((first, 1), (second, 0)):
        pairs = [(i, i + 1) for i in range(start, count - 1, 2)]
        got.append(lax.ppermute(value, axis, pairs + [(b, a) for a, b in pairs]))
    return got


def shards(object_field, probe, amplitudes, offsets, counts):
    length = probe.shape[-1]
    half = length // 2
    tile = object_field.shape[1]
    npos = offsets.shape[2]
    nb = tile // length
    blocks = nb + 2
    rows = tile + 2 * half
    tables = jnp.asarray(dft_tables(length))
    offsets = jnp.swapaxes(offsets, 2, 3)

    def cost(positions):
        steps = 4 * 3 * 2 * length * (2 * length) ** 2
        return pl.CostEstimate(
            flops=positions * steps, bytes_accessed=8_000_000,
            transcendentals=positions * length * length)

    memory = pltpu.VMEM
    chosen = pltpu.SMEM((npos + GROUP,), jnp.int32)
    strip = (tile + 8, length)
    edge = (2 * nb * half + 8, length)
    field, cols_a, cols_b, rows_a, rows_b = call(
        start_pass, [(2, nb, tile, length), strip, strip, edge, edge], "asa",
        [pltpu.SMEM((1, 1, 2, npos), jnp.int32), pltpu.SemaphoreType.DMA((nb + 1,))],
    )(offsets, counts, object_field)
    mine = cols_a
    cols_a, cols_b = swap_pairs(cols_a, cols_b, "col")
    rows_a, rows_b = swap_pairs(rows_a, rows_b, "row")
    corner = (2 * half + 8, length)
    corners_a, corners_b = call(start_corners, [corner, corner], "vv")(cols_a, cols_b)
    (ready,) = call(fetch_pass, [(8, length)], "avvv", cost=cost(1))(
        corners_a, probe, amplitudes, tables)
    corners_a, corners_b = swap_pairs(corners_a, corners_b, "row")

    full = (2, blocks, rows, length)
    strip = (2, rows, length)
    frame, acc, sums_a, sums_b = call(
        first_pass, [full, full, strip, strip], "ssa" + 10 * "v", [chosen],
    )(offsets, counts, ready, field, cols_a, cols_b, rows_a, rows_b, corners_a, corners_b,
      probe, amplitudes, tables)
    mine_a, mine_b = sums_a, sums_b
    sums_a, sums_b = swap_pairs(sums_a, sums_b, "col")
    edge = (2, nb - 1, length, length)
    acc, edges_a, edges_b = call(
        first_rest, [full, edge, edge], "ss" + 5 * "v", [chosen], cost(npos // 2),
    )(offsets, counts, frame, acc, probe, amplitudes, tables)
    edges_a, edges_b = swap_pairs(edges_a, edges_b, "row")
    (inverse,) = call(
        functools.partial(light_pass, npos=npos), [(blocks, rows, length)], 8 * "v" + "a",
        [memory((blocks + 2, rows + 2 * length, length), jnp.float32),
         memory((length, length), jnp.float32), memory((7 * 8, length), jnp.int32),
         pltpu.SMEM((7 * 8, length), jnp.int32), pltpu.SMEM((9 * npos + 1,), jnp.int32),
         pltpu.SemaphoreType.DMA],
        cost(npos // 2),
    )(mine, cols_a, cols_b, rows_a, rows_b, corners_a, corners_b, probe, acc)
    corner = (2, 2, length, length)
    corners_a, corners_b = call(middle_corners, [corner, corner], "vvvva")(
        mine_a, mine_b, sums_a, sums_b, inverse)
    corners_a, corners_b = swap_pairs(corners_a, corners_b, "row")

    work, total = call(update_pass, [full, full], "ss" + 8 * "v", [chosen], cost(npos // 2))(
        offsets, counts, frame, acc, inverse, sums_a, sums_b, probe, amplitudes, tables)
    strip = (rows, length)
    work, total, cols_a, cols_b = call(
        second_pass, [full, full, strip, strip], "ss" + 10 * "v", [chosen], cost(npos // 4),
    )(offsets, counts, work, total, inverse, edges_a, edges_b, corners_a, corners_b,
      probe, amplitudes, tables)
    cols_a, cols_b = swap_pairs(cols_a, cols_b, "col")
    own = (2, nb, tile, length)
    edge = (2, nb, half, length)
    sums, rows_a, rows_b = call(
        rows_pass, [own, edge, edge], "ss" + 5 * "v",
        [memory((2, nb, rows, length), jnp.float32), chosen], cost(npos // 4),
    )(offsets, counts, work, total, probe, amplitudes, tables)
    rows_a, rows_b = swap_pairs(rows_a, rows_b, "row")
    (inner,) = call(inner_pass, [own], "ss" + 4 * "v", [chosen], cost(npos // 4))(
        offsets, counts, work, probe, amplitudes, tables)
    corner = (2, half, length)
    corners_a, corners_b = call(end_corners, [corner, corner], "vv")(cols_a, cols_b)
    corners_a, corners_b = swap_pairs(corners_a, corners_b, "row")
    (out,) = call(last_pass, [(2, tile, tile)], 10 * "v")(
        work, sums, inner, inverse, cols_a, cols_b, rows_a, rows_b, corners_a, corners_b)
    return out


def solution(mesh):
    placed = (
        P(None, "row", "col"),
        P(),
        P("row", "col", None, None, None),
        P("row", "col", None, None),
        P("row", "col"),
    )
    return jax.shard_map(
        shards, mesh=mesh, in_specs=placed, out_specs=P(None, "row", "col"), check_vma=False
    )
```

```python
import functools
import math

import jax
import jax.numpy as jnp
import numpy as np
from jax import lax
from jax.experimental import pallas as pl
from jax.experimental.pallas import tpu as pltpu
from jax.sharding import PartitionSpec as P

ITERS = 2
FLOOR = 0.25
VMEM_BYTES = 16 * 1024 * 1024
GROUP = 4
CHAIN = 2


def split(value):
    high = value.astype(jnp.bfloat16)
    low = (value - high.astype(jnp.float32)).astype(jnp.bfloat16)
    return high, low


def dft_tables(length):
    index = np.arange(length)
    angle = (index[:, None] * index[None, :] % length) * (2.0 * math.pi / length)
    cosine = np.cos(angle) / math.sqrt(length)
    sine = np.sin(angle) / math.sqrt(length)
    ahead = np.block([[cosine, -sine], [sine, cosine]])
    parts = []
    for table in (ahead, ahead.T):
        high = table.astype(jnp.bfloat16)
        low = (table - high.astype(np.float64)).astype(jnp.bfloat16)
        parts += [high, low]
    return np.stack(parts)


def lanes(shape):
    return lax.broadcasted_iota(jnp.int32, shape, len(shape) - 1)


def swap(value, half):
    return pltpu.roll(value, half, value.ndim - 1)


def odd_place(axis):
    return lax.axis_index(axis) % 2 == 1


def by_pairs(axis, low, high):
    odd = odd_place(axis)
    return jnp.where(odd, high, low), jnp.where(odd, low, high)


def by_side(axis, first, second):
    odd = odd_place(axis)
    return jnp.where(odd, second, first), jnp.where(odd, first, second)


def times_right(rows, high, low):
    top, rest = split(rows)
    left = jnp.concatenate([top, top, rest], axis=1)
    right = jnp.concatenate([high, low, high], axis=0)
    return jnp.dot(left, right, preferred_element_type=jnp.float32)


def times_left(high, low, columns):
    top, rest = split(columns)
    left = jnp.concatenate([high, low, high], axis=1)
    right = jnp.concatenate([top, top, rest], axis=0)
    return jnp.dot(left, right, preferred_element_type=jnp.float32)


def beside(left, right):
    return jnp.concatenate([left, right], axis=1)


def above(top, bottom):
    return jnp.concatenate([top, bottom], axis=0)


def early(mid_col, cross_row, cross_col, **_):
    return ~mid_col & ~cross_row & ~cross_col


def choose(chosen, offsets, counts, tile, length, wanted, done_early=False):
    last = tile - length
    half = length // 2

    def look(slot, carry):
        found, seen = carry
        row = offsets[0, 0, 0, slot]
        col = offsets[0, 0, 1, slot]
        spot = dict(
            mid_row=(row >= half) & (row <= last - half),
            mid_col=(col >= half) & (col <= last - half),
            cross_row=(row < 0) | (row > last),
            cross_col=(col < 0) | (col > last),
        )
        taken = wanted(**spot)
        if done_early:
            soon = early(**spot)
            taken = taken & ~(soon & (seen < GROUP))
            seen = seen + jnp.where(soon, 1, 0)
        chosen[found] = slot
        return found + jnp.where(taken, 1, 0), seen

    found, _ = lax.fori_loop(0, counts[0, 0], look, (0, 0))
    filler = chosen[0]
    for k in range(GROUP):
        chosen[found + k] = filler
    return found


def add_gradients(frame, acc, probe_ref, amps, offsets, tables, chosen, found, own_frame=False, own_acc=False):
    length = probe_ref.shape[-1]
    half = length // 2
    lane = lanes((length, length))

    def place(slot, ref, own):
        col = offsets[0, 0, 1, slot] + length
        block = lax.div(col, length)
        row = offsets[0, 0, 0, slot]
        if own:
            block = block - 1
        else:
            row = row + half
        after = jnp.minimum(block + 1, ref.shape[1] - 1)
        return pl.ds(row, length), block, after, lax.rem(col, length)

    def exit_wave(slot):
        at, block, after, shift = place(slot, frame, own_frame)
        inside = lane >= shift
        window = [
            jnp.where(inside, frame[part, block, at, :], frame[part, after, at, :])
            for part in (0, 1)
        ]
        probe = (pltpu.roll(probe_ref[0], shift, 1), pltpu.roll(probe_ref[1], shift, 1))
        wave = (probe[0] * window[0] - probe[1] * window[1],
                probe[0] * window[1] + probe[1] * window[0])
        return probe, wave

    def shrink(real, imag, slot):
        ratio = amps[0, 0, slot] * lax.rsqrt(real * real + imag * imag + FLOOR) - 1.0
        return real * ratio, imag * ratio

    def put(slot, live, probe, back_r, back_i):
        at, block, after, shift = place(slot, acc, own_acc)
        grads = (probe[0] * back_r + probe[1] * back_i, probe[0] * back_i - probe[1] * back_r)
        bound = jnp.where(live, shift, length)
        inside = lane >= bound
        beyond = lane < jnp.where(live, shift, 0)
        for part in (0, 1):
            acc[part, block, at, :] += jnp.where(inside, grads[part], 0.0)
            acc[part, after, at, :] += jnp.where(beyond, grads[part], 0.0)

    def work(slots):
        probes, waves = zip(*[exit_wave(slot) for slot in slots])
        rows = jnp.concatenate([beside(*wave) for wave in waves], axis=0)
        mid = times_right(rows, tables[0], tables[1])
        yield None
        mids = [mid[k * length:(k + 1) * length] for k in range(len(slots))]
        columns = above(
            jnp.concatenate([m[:, :length] for m in mids], axis=1),
            jnp.concatenate([m[:, length:] for m in mids], axis=1),
        )
        far = times_left(tables[2], tables[3], columns)
        yield None
        changes = [
            shrink(far[:length, k * length:(k + 1) * length],
                   far[length:, k * length:(k + 1) * length], slot)
            for k, slot in enumerate(slots)
        ]
        columns = above(
            jnp.concatenate([c[0] for c in changes], axis=1),
            jnp.concatenate([c[1] for c in changes], axis=1),
        )
        mid = times_left(tables[0], tables[1], columns)
        yield None
        rows = jnp.concatenate(
            [
                beside(mid[:length, k * length:(k + 1) * length],
                       mid[length:, k * length:(k + 1) * length])
                for k in range(len(slots))
            ],
            axis=0,
        )
        back = times_right(rows, tables[2], tables[3])
        yield None
        yield [
            (probes[k], back[k * length:(k + 1) * length, :length],
             back[k * length:(k + 1) * length, length:])
            for k in range(len(slots))
        ]

    def step(index, carry):
        places = [index * GROUP + k for k in range(GROUP)]
        slots = [chosen[at] for at in places]
        chains = [work(slots[k:k + CHAIN]) for k in range(0, GROUP, CHAIN)]
        gradients = [None]
        while gradients[0] is None:
            gradients = [next(chain) for chain in chains]
        gradients = [gradient for chain in gradients for gradient in chain]
        for at, slot, gradient in zip(places, slots, gradients):
            put(slot, at < found, *gradient)
        return carry

    lax.fori_loop(0, (found + GROUP - 1) // GROUP, step, 0)


def list_pass(offsets, counts, info, *, tile):
    npos = offsets.shape[3]
    spot = lanes(info.shape)
    rows = jnp.zeros(info.shape, jnp.int32)
    down = (lax.axis_index("row") + 1) * tile
    across = (lax.axis_index("col") + 1) * tile
    for k in range(npos):
        live = k < counts[0, 0]
        rows = jnp.where(spot == k, jnp.where(live, offsets[0, 0, 0, k] + down, 0), rows)
        rows = jnp.where(spot == npos + k, jnp.where(live, offsets[0, 0, 1, k] + across, 0), rows)
    info[...] = rows.astype(jnp.float32)


def start_pass(field, listed, tile_out, cols_a, cols_b, rows_a, rows_b):
    _, nb, tile, length = tile_out.shape
    half = length // 2
    low = lanes((tile, length)) < half
    last = (nb - 1) * length
    to_left = jnp.where(low, field[0, :, :length], swap(field[1, :, :length], half))
    to_right = jnp.where(low, swap(field[1, :, last:], half), field[0, :, last:])
    cols_a[:tile], cols_b[:tile] = by_pairs("col", to_left, to_right)
    for part in (0, 1):
        for b in range(nb):
            value = field[part, :, b * length:(b + 1) * length]
            tile_out[part, b] = value
            at = pl.ds((part * nb + b) * half, half)
            rows_a[at, :], rows_b[at, :] = by_pairs("row", value[:half], value[tile - half:])
    info = listed[...]
    cols_a[tile:] = info
    cols_b[tile:] = info
    rows_a[2 * nb * half:] = info
    rows_b[2 * nb * half:] = info


def start_corners(cols_a, cols_b, after, corners_a, corners_b):
    length = cols_a.shape[1]
    half = length // 2
    tile = cols_a.shape[0] - 8
    low = lanes((tile, length)) < half
    left, right = by_side("col", cols_a[:tile], cols_b[:tile])
    for part in (0, 1):
        if part:
            left, right = swap(left, half), swap(right, half)
        value = jnp.where(low, right, left)
        at = pl.ds(part * half, half)
        corners_a[at, :], corners_b[at, :] = by_pairs("row", value[:half], value[tile - half:])
    first = lax.broadcasted_iota(jnp.int32, (8, length), 0) == 0
    info = jnp.where(first, cols_a[tile:], cols_b[tile:])
    corners_a[2 * half:] = info
    corners_b[2 * half:] = info


def fetch_pass(after, probe, amps, tables, out):
    out[...] = jnp.zeros_like(out)


def early_pass(offsets, counts, after, ready, field, probe, amps, tables, acc, chosen):
    _, nb, tile, length = field.shape
    acc[...] = jnp.zeros_like(acc)
    found = jnp.minimum(choose(chosen, offsets, counts, tile, length, early), GROUP)
    add_gradients(field, acc, probe, amps, offsets, tables, chosen, found,
                  own_frame=True, own_acc=True)


def first_pass(offsets, counts, field, done, cols_a, cols_b, rows_a, rows_b, corners_a, corners_b,
               probe, amps, tables, frame, acc, sums_a, sums_b, chosen):
    _, nb, tile, length = field.shape
    half = length // 2
    rows = tile + 2 * half
    own = pl.ds(half, tile)
    left, right = by_side("col", cols_a[:tile], cols_b[:tile])
    top = pl.ds(0, half)
    bottom = pl.ds(half + tile, half)
    for part in (0, 1):
        for b in range(nb):
            frame[part, b + 1, own, :] = field[part, b]
            at = pl.ds((part * nb + b) * half, half)
            frame[part, b + 1, top, :], frame[part, b + 1, bottom, :] = by_side(
                "row", rows_a[at, :], rows_b[at, :])
        frame[part, 0, own, :] = swap(left, half) if part else left
        frame[part, nb + 1, own, :] = swap(right, half) if part else right
        at = pl.ds(part * half, half)
        ends = by_side("row", corners_a[at, :], corners_b[at, :])
        for block in (0, nb + 1):
            frame[part, block, top, :], frame[part, block, bottom, :] = ends
    empty = jnp.zeros((half, length), jnp.float32)
    for part in (0, 1):
        for b in range(nb + 2):
            acc[part, b, top, :] = empty
            acc[part, b, bottom, :] = empty
            acc[part, b, own, :] = (
                done[part, b - 1] if 0 < b <= nb else jnp.zeros((tile, length), jnp.float32))
    found = choose(
        chosen, offsets, counts, tile, length, lambda mid_col, **_: ~mid_col, done_early=True)
    add_gradients(frame, acc, probe, amps, offsets, tables, chosen, found)
    low = lanes((rows, length)) < half
    for part in (0, 1):
        sums_a[part], sums_b[part] = by_pairs(
            "col",
            jnp.where(low, acc[part, 1], acc[part, 0]),
            jnp.where(low, acc[part, nb + 1], acc[part, nb]),
        )


def first_rest(offsets, counts, frame, acc_from, probe, amps, tables,
               acc, edges_a, edges_b, chosen):
    _, blocks, rows, length = frame.shape
    half = length // 2
    nb = blocks - 2
    acc[...] = acc_from[...]
    found = choose(
        chosen, offsets, counts, nb * length, length,
        lambda mid_row, mid_col, **_: mid_col & ~mid_row)
    add_gradients(frame, acc, probe, amps, offsets, tables, chosen, found)
    low = lanes((length, length)) < half
    for part in (0, 1):
        for b in range(nb - 1):
            ends = [
                acc[part, b + 2, at, :] if b < nb - 2
                else jnp.where(low, acc[part, nb, at, :], acc[part, 1, at, :])
                for at in (pl.ds(0, length), pl.ds(rows - length, length))
            ]
            edges_a[part, b], edges_b[part, b] = by_pairs("row", *ends)


def middle_corners(mine_a, mine_b, sums_a, sums_b, after, corners_a, corners_b):
    _, rows, length = sums_a.shape
    for part in (0, 1):
        for at, k in ((pl.ds(0, length), 0), (pl.ds(rows - length, length), 1)):
            sides = by_side(
                "col", mine_a[part, at, :] + sums_a[part, at, :],
                mine_b[part, at, :] + sums_b[part, at, :])
            for side in (0, 1):
                if k == 0:
                    up = sides
                else:
                    corners_a[part, side], corners_b[part, side] = by_pairs(
                        "row", up[side], sides[side])


def light_pass(mine, cols_a, cols_b, rows_a, rows_b, corners_a, corners_b, probe, after,
               inverse, light, power, places, listed, chosen, sem, *, npos):
    length = probe.shape[-1]
    half = length // 2
    blocks, rows, _ = inverse.shape
    nb = blocks - 2
    tile = nb * length
    my_row = lax.axis_index("row")
    my_col = lax.axis_index("col")
    sources = (mine, cols_a, cols_b, rows_a, rows_b, corners_a, corners_b)
    for k, source in enumerate(sources):
        given = source[source.shape[0] - 8:, :].astype(jnp.int32)
        col = pltpu.roll(given, length - npos, 1) - (my_col + 1) * tile + 2 * length
        row = given - (my_row + 1) * tile + half + length
        near = (given > 0) & (row > 0) & (row < rows + length)
        near = near & (col > length - half) & (col < 2 * length + tile + half)
        places[pl.ds(8 * k, 8), :] = jnp.where(near, row * 4 * tile + col, 0)
    copy = pltpu.make_async_copy(places, listed, sem)
    copy.start()
    light[...] = jnp.zeros_like(light)
    power[...] = probe[0] * probe[0] + probe[1] * probe[1]
    lane = lanes((length, length))
    copy.wait()

    def look(index, found):
        line = jnp.where(index < len(sources), 8 * index, 8 * (index - 2) + 1)
        for slot in range(npos):
            place = listed[line, slot]
            chosen[found] = place
            found = found + jnp.where(place > 0, 1, 0)
        return found

    found = lax.fori_loop(0, len(sources) + 2, look, 0)

    def put(index, carry):
        place = chosen[index]
        start = lax.div(place, 4 * tile)
        col = lax.rem(place, 4 * tile)
        block = lax.div(col, length)
        shift = lax.rem(col, length)
        value = pltpu.roll(power[...], shift, 1)
        inside = lane >= shift
        light[block, pl.ds(start, length), :] += jnp.where(inside, value, 0.0)
        light[block + 1, pl.ds(start, length), :] += jnp.where(inside, 0.0, value)
        return carry

    lax.fori_loop(0, found, put, 0)
    spot = lax.broadcasted_iota(jnp.int32, (rows, length), 0)
    keep_from = jnp.where(my_row > 0, 0, half)
    keep_to = jnp.where(my_row < lax.axis_size("row") - 1, rows, rows - half)
    kept = (spot >= keep_from) & (spot < keep_to)
    for b in range(blocks):
        value = 1.0 / (light[b + 1, pl.ds(length, rows), :] + 1.0)
        keep = kept
        if b == 0:
            keep = keep & (my_col > 0)
        if b == nb + 1:
            keep = keep & (my_col < lax.axis_size("col") - 1)
        inverse[b] = jnp.where(keep, value, 0.0)


def update_pass(offsets, counts, frame, acc, inverse, sums_a, sums_b, probe, amps, tables,
                work, total, chosen):
    _, blocks, rows, length = frame.shape
    half = length // 2
    nb = blocks - 2
    work[...] = acc[...]
    found = choose(
        chosen, offsets, counts, nb * length, length,
        lambda mid_row, mid_col, **_: mid_col & mid_row)
    add_gradients(frame, work, probe, amps, offsets, tables, chosen, found)
    low = lanes((rows, length)) < half
    for part in (0, 1):
        left, right = by_side("col", sums_a[part], sums_b[part])
        for b in range(blocks):
            value = work[part, b]
            if b == 0:
                value = value + left
            if b == 1:
                value = value + jnp.where(low, left, 0.0)
            if b == nb:
                value = value + jnp.where(low, 0.0, right)
            if b == nb + 1:
                value = value + right
            work[part, b] = frame[part, b] + value * inverse[b]
    total[...] = jnp.zeros_like(total)
    found = choose(chosen, offsets, counts, nb * length, length, lambda mid_row, **_: mid_row)
    add_gradients(work, total, probe, amps, offsets, tables, chosen, found)


def second_pass(offsets, counts, work_from, total_from, inverse, edges_a, edges_b,
                corners_a, corners_b, probe, amps, tables,
                work, sums, cols_a, cols_b, rows_a, rows_b, total, chosen):
    _, blocks, rows, length = work.shape
    half = length // 2
    nb = blocks - 2
    tile = nb * length
    near = lanes((length, length)) < half
    middle = pl.ds(length, rows - 2 * length)
    for part in (0, 1):
        edges = [by_side("row", edges_a[part, b], edges_b[part, b]) for b in range(nb - 1)]
        corners = [by_side("row", corners_a[part, side], corners_b[part, side]) for side in (0, 1)]
        for k, at in enumerate((pl.ds(0, length), pl.ds(rows - length, length))):
            left, right, ends = corners[0][k], corners[1][k], edges[nb - 2][k]
            add = [left, jnp.where(near, left, ends)]
            add += [edges[b][k] for b in range(nb - 2)]
            add += [jnp.where(near, ends, right), right]
            for b in range(blocks):
                work[part, b, at, :] = work_from[part, b, at, :] + add[b] * inverse[b, at, :]
        for b in range(blocks):
            work[part, b, middle, :] = work_from[part, b, middle, :]
    total[...] = total_from[...]
    found = choose(
        chosen, offsets, counts, tile, length,
        lambda mid_row, cross_row, cross_col, **_: ~mid_row & (cross_row | cross_col))
    add_gradients(work, total, probe, amps, offsets, tables, chosen, found)
    low = lanes((rows, length)) < half
    cols_a[...], cols_b[...] = by_pairs(
        "col",
        jnp.where(low, swap(total[1, 0], half), total[0, 0]),
        jnp.where(low, total[0, nb + 1], swap(total[1, nb + 1], half)),
    )
    for part in (0, 1):
        for b in range(nb):
            sums[part, b] = total[part, b + 1, pl.ds(half, tile), :]
            rows_a[part, b], rows_b[part, b] = by_pairs(
                "row", total[part, b + 1, :half, :], total[part, b + 1, half + tile:, :])


def inner_pass(offsets, counts, work, probe, amps, tables, sums, chosen):
    _, nb, tile, length = sums.shape
    sums[...] = jnp.zeros_like(sums)
    found = choose(
        chosen, offsets, counts, tile, length,
        lambda mid_row, cross_row, cross_col, **_: ~mid_row & ~cross_row & ~cross_col)
    add_gradients(work, sums, probe, amps, offsets, tables, chosen, found, own_acc=True)


def end_corners(cols_a, cols_b, corners_a, corners_b):
    rows, length = cols_a.shape
    half = length // 2
    for side, value in enumerate(by_side("col", cols_a[...], cols_b[...])):
        corners_a[side], corners_b[side] = by_pairs("row", value[:half], value[rows - half:])


def last_pass(work, sums, inner, inverse, cols_a, cols_b, rows_a, rows_b, corners_a, corners_b, out):
    _, nb, tile, length = sums.shape
    half = length // 2
    low = lanes((tile, length)) < half
    own = pl.ds(half, tile)
    gap = jnp.zeros((tile - 2 * half, length), jnp.float32)
    sides = []
    for side, value in enumerate(by_side("col", cols_a[own, :], cols_b[own, :])):
        up, down = by_side("row", corners_a[side], corners_b[side])
        sides.append(value + above(above(up, gap), down))
    left, right = sides
    for part in (0, 1):
        if part:
            left, right = swap(left, half), swap(right, half)
        for b in range(nb):
            up, down = by_side("row", rows_a[part, b], rows_b[part, b])
            value = sums[part, b] + inner[part, b] + above(above(up, gap), down)
            if b == 0:
                value = value + jnp.where(low, left, 0.0)
            if b == nb - 1:
                value = value + jnp.where(low, 0.0, right)
            out[part, :, b * length:(b + 1) * length] = (
                work[part, b + 1, own, :] + value * inverse[b + 1, own, :])


def whole(memory_space=pltpu.VMEM):
    return pl.BlockSpec(memory_space=memory_space)


def call(body, shapes, places, scratch=(), cost=None):
    return pl.pallas_call(
        body,
        out_shape=[jax.ShapeDtypeStruct(shape, jnp.float32) for shape in shapes],
        in_specs=[whole({"s": pltpu.SMEM, "v": pltpu.VMEM, "a": pl.ANY, "h": pltpu.HBM}[p]) for p in places],
        out_specs=[whole()] * len(shapes),
        scratch_shapes=list(scratch),
        compiler_params=pltpu.CompilerParams(vmem_limit_bytes=VMEM_BYTES),
        cost_estimate=cost,
    )


def swap_pairs(first, second, axis):
    count = lax.axis_size(axis)
    got = []
    for value, start in ((first, 1), (second, 0)):
        pairs = [(i, i + 1) for i in range(start, count - 1, 2)]
        got.append(lax.ppermute(value, axis, pairs + [(b, a) for a, b in pairs]))
    return got


def shards(object_field, probe, amplitudes, offsets, counts):
    length = probe.shape[-1]
    half = length // 2
    tile = object_field.shape[1]
    npos = offsets.shape[2]
    nb = tile // length
    blocks = nb + 2
    rows = tile + 2 * half
    tables = jnp.asarray(dft_tables(length))
    offsets = jnp.swapaxes(offsets, 2, 3)

    def cost(positions):
        steps = 4 * 3 * 2 * length * (2 * length) ** 2
        return pl.CostEstimate(
            flops=positions * steps, bytes_accessed=8_000_000,
            transcendentals=positions * length * length)

    memory = pltpu.VMEM
    chosen = pltpu.SMEM((npos + GROUP,), jnp.int32)
    strip = (tile + 8, length)
    edge = (2 * nb * half + 8, length)
    (mine,) = call(functools.partial(list_pass, tile=tile), [(8, length)], "ss")(offsets, counts)
    field, cols_a, cols_b, rows_a, rows_b = call(
        start_pass, [(2, nb, tile, length), strip, strip, edge, edge], "vv",
    )(object_field, mine)
    (ready,) = call(fetch_pass, [(8, length)], "avvv", cost=cost(1))(
        cols_a, probe, amplitudes, tables)
    cols_a, cols_b = swap_pairs(cols_a, cols_b, "col")
    rows_a, rows_b = swap_pairs(rows_a, rows_b, "row")
    corner = (2 * half + 8, length)
    corners_a, corners_b = call(start_corners, [corner, corner], "vva")(cols_a, cols_b, ready)
    (done,) = call(
        early_pass, [(2, nb, tile, length)], "ssaavvvv", [chosen], cost(GROUP),
    )(offsets, counts, corners_b, ready, field, probe, amplitudes, tables)
    corners_a, corners_b = swap_pairs(corners_a, corners_b, "row")

    full = (2, blocks, rows, length)
    strip = (2, rows, length)
    frame, acc, sums_a, sums_b = call(
        first_pass, [full, full, strip, strip], "ss" + 11 * "v", [chosen],
    )(offsets, counts, field, done, cols_a, cols_b, rows_a, rows_b, corners_a, corners_b,
      probe, amplitudes, tables)
    mine_a, mine_b = sums_a, sums_b
    sums_a, sums_b = swap_pairs(sums_a, sums_b, "col")
    edge = (2, nb - 1, length, length)
    acc, edges_a, edges_b = call(
        first_rest, [full, edge, edge], "ss" + 5 * "v", [chosen], cost(npos // 2),
    )(offsets, counts, frame, acc, probe, amplitudes, tables)
    edges_a, edges_b = swap_pairs(edges_a, edges_b, "row")
    (inverse,) = call(
        functools.partial(light_pass, npos=npos), [(blocks, rows, length)], 8 * "v" + "a",
        [memory((blocks + 2, rows + 2 * length, length), jnp.float32),
         memory((length, length), jnp.float32), memory((7 * 8, length), jnp.int32),
         pltpu.SMEM((7 * 8, length), jnp.int32), pltpu.SMEM((9 * npos + 1,), jnp.int32),
         pltpu.SemaphoreType.DMA],
        cost(npos // 2),
    )(mine, cols_a, cols_b, rows_a, rows_b, corners_a, corners_b, probe, acc)
    corner = (2, 2, length, length)
    corners_a, corners_b = call(middle_corners, [corner, corner], "vvvva")(
        mine_a, mine_b, sums_a, sums_b, inverse)
    corners_a, corners_b = swap_pairs(corners_a, corners_b, "row")

    work, total = call(update_pass, [full, full], "ss" + 8 * "v", [chosen], cost(npos // 2))(
        offsets, counts, frame, acc, inverse, sums_a, sums_b, probe, amplitudes, tables)
    strip = (rows, length)
    own = (2, nb, tile, length)
    edge = (2, nb, half, length)
    work, sums, cols_a, cols_b, rows_a, rows_b = call(
        second_pass, [full, own, strip, strip, edge, edge], "ss" + 10 * "v",
        [memory(full, jnp.float32), chosen], cost(npos // 2),
    )(offsets, counts, work, total, inverse, edges_a, edges_b, corners_a, corners_b,
      probe, amplitudes, tables)
    cols_a, cols_b = swap_pairs(cols_a, cols_b, "col")
    rows_a, rows_b = swap_pairs(rows_a, rows_b, "row")
    (inner,) = call(inner_pass, [own], "ss" + 4 * "v", [chosen], cost(npos // 4))(
        offsets, counts, work, probe, amplitudes, tables)
    corner = (2, half, length)
    corners_a, corners_b = call(end_corners, [corner, corner], "vv")(cols_a, cols_b)
    corners_a, corners_b = swap_pairs(corners_a, corners_b, "row")
    (out,) = call(last_pass, [(2, tile, tile)], 10 * "v")(
        work, sums, inner, inverse, cols_a, cols_b, rows_a, rows_b, corners_a, corners_b)
    return out


def solution(mesh):
    placed = (
        P(None, "row", "col"),
        P(),
        P("row", "col", None, None, None),
        P("row", "col", None, None),
        P("row", "col"),
    )
    return jax.shard_map(
        shards, mesh=mesh, in_specs=placed, out_specs=P(None, "row", "col"), check_vma=False
    )
```

```python
import functools
import math

import jax
import jax.numpy as jnp
import numpy as np
from jax import lax
from jax.experimental import pallas as pl
from jax.experimental.pallas import tpu as pltpu
from jax.sharding import PartitionSpec as P

ITERS = 2
FLOOR = 0.25
VMEM_BYTES = 16 * 1024 * 1024
GROUP = 4
CHAIN = 2


def split(value):
    high = value.astype(jnp.bfloat16)
    low = (value - high.astype(jnp.float32)).astype(jnp.bfloat16)
    return high, low


def dft_tables(length):
    index = np.arange(length)
    angle = (index[:, None] * index[None, :] % length) * (2.0 * math.pi / length)
    cosine = np.cos(angle) / math.sqrt(length)
    sine = np.sin(angle) / math.sqrt(length)
    ahead = np.block([[cosine, -sine], [sine, cosine]])
    parts = []
    for table in (ahead, ahead.T):
        high = table.astype(jnp.bfloat16)
        low = (table - high.astype(np.float64)).astype(jnp.bfloat16)
        parts += [high, low]
    return np.stack(parts)


def lanes(shape):
    return lax.broadcasted_iota(jnp.int32, shape, len(shape) - 1)


def swap(value, half):
    return pltpu.roll(value, half, value.ndim - 1)


def odd_place(axis):
    return lax.axis_index(axis) % 2 == 1


def by_pairs(axis, low, high):
    odd = odd_place(axis)
    return jnp.where(odd, high, low), jnp.where(odd, low, high)


def by_side(axis, first, second):
    odd = odd_place(axis)
    return jnp.where(odd, second, first), jnp.where(odd, first, second)


def times_right(rows, high, low):
    top, rest = split(rows)
    left = jnp.concatenate([top, top, rest], axis=1)
    right = jnp.concatenate([high, low, high], axis=0)
    return jnp.dot(left, right, preferred_element_type=jnp.float32)


def times_left(high, low, columns):
    top, rest = split(columns)
    left = jnp.concatenate([high, low, high], axis=1)
    right = jnp.concatenate([top, top, rest], axis=0)
    return jnp.dot(left, right, preferred_element_type=jnp.float32)


def beside(left, right):
    return jnp.concatenate([left, right], axis=1)


def above(top, bottom):
    return jnp.concatenate([top, bottom], axis=0)


def touching(mid_row, mid_col, **_):
    return ~(mid_row & mid_col)


def early(cross_row, cross_col, **spot):
    return touching(**spot) & ~cross_row & ~cross_col


def choose(chosen, offsets, counts, tile, length, wanted, done_early=False):
    last = tile - length
    half = length // 2

    def look(slot, carry):
        found, seen = carry
        row = offsets[0, 0, 0, slot]
        col = offsets[0, 0, 1, slot]
        spot = dict(
            mid_row=(row >= half) & (row <= last - half),
            mid_col=(col >= half) & (col <= last - half),
            cross_row=(row < 0) | (row > last),
            cross_col=(col < 0) | (col > last),
        )
        taken = wanted(**spot)
        if done_early:
            soon = early(**spot)
            taken = taken & ~(soon & (seen < GROUP))
            seen = seen + jnp.where(soon, 1, 0)
        chosen[found] = slot
        return found + jnp.where(taken, 1, 0), seen

    found, _ = lax.fori_loop(0, counts[0, 0], look, (0, 0))
    filler = chosen[0]
    for k in range(GROUP):
        chosen[found + k] = filler
    return found


def add_gradients(frame, acc, probe_ref, amps, offsets, tables, chosen, found, own_frame=False, own_acc=False):
    length = probe_ref.shape[-1]
    half = length // 2
    lane = lanes((length, length))

    def place(slot, ref, own):
        col = offsets[0, 0, 1, slot] + length
        block = lax.div(col, length)
        row = offsets[0, 0, 0, slot]
        if own:
            block = block - 1
        else:
            row = row + half
        after = jnp.minimum(block + 1, ref.shape[1] - 1)
        return pl.ds(row, length), block, after, lax.rem(col, length)

    def exit_wave(slot):
        at, block, after, shift = place(slot, frame, own_frame)
        inside = lane >= shift
        window = [
            jnp.where(inside, frame[part, block, at, :], frame[part, after, at, :])
            for part in (0, 1)
        ]
        probe = (pltpu.roll(probe_ref[0], shift, 1), pltpu.roll(probe_ref[1], shift, 1))
        wave = (probe[0] * window[0] - probe[1] * window[1],
                probe[0] * window[1] + probe[1] * window[0])
        return probe, wave

    def shrink(real, imag, slot):
        ratio = amps[0, 0, slot] * lax.rsqrt(real * real + imag * imag + FLOOR) - 1.0
        return real * ratio, imag * ratio

    def put(slot, live, probe, back_r, back_i):
        at, block, after, shift = place(slot, acc, own_acc)
        grads = (probe[0] * back_r + probe[1] * back_i, probe[0] * back_i - probe[1] * back_r)
        bound = jnp.where(live, shift, length)
        inside = lane >= bound
        beyond = lane < jnp.where(live, shift, 0)
        for part in (0, 1):
            acc[part, block, at, :] += jnp.where(inside, grads[part], 0.0)
            acc[part, after, at, :] += jnp.where(beyond, grads[part], 0.0)

    def work(slots):
        probes, waves = zip(*[exit_wave(slot) for slot in slots])
        rows = jnp.concatenate([beside(*wave) for wave in waves], axis=0)
        mid = times_right(rows, tables[0], tables[1])
        yield None
        mids = [mid[k * length:(k + 1) * length] for k in range(len(slots))]
        columns = above(
            jnp.concatenate([m[:, :length] for m in mids], axis=1),
            jnp.concatenate([m[:, length:] for m in mids], axis=1),
        )
        far = times_left(tables[2], tables[3], columns)
        yield None
        changes = [
            shrink(far[:length, k * length:(k + 1) * length],
                   far[length:, k * length:(k + 1) * length], slot)
            for k, slot in enumerate(slots)
        ]
        columns = above(
            jnp.concatenate([c[0] for c in changes], axis=1),
            jnp.concatenate([c[1] for c in changes], axis=1),
        )
        mid = times_left(tables[0], tables[1], columns)
        yield None
        rows = jnp.concatenate(
            [
                beside(mid[:length, k * length:(k + 1) * length],
                       mid[length:, k * length:(k + 1) * length])
                for k in range(len(slots))
            ],
            axis=0,
        )
        back = times_right(rows, tables[2], tables[3])
        yield None
        yield [
            (probes[k], back[k * length:(k + 1) * length, :length],
             back[k * length:(k + 1) * length, length:])
            for k in range(len(slots))
        ]

    def step(index, carry):
        places = [index * GROUP + k for k in range(GROUP)]
        slots = [chosen[at] for at in places]
        chains = [work(slots[k:k + CHAIN]) for k in range(0, GROUP, CHAIN)]
        gradients = [None]
        while gradients[0] is None:
            gradients = [next(chain) for chain in chains]
        gradients = [gradient for chain in gradients for gradient in chain]
        for at, slot, gradient in zip(places, slots, gradients):
            put(slot, at < found, *gradient)
        return carry

    lax.fori_loop(0, (found + GROUP - 1) // GROUP, step, 0)


def start_pass(field, offsets_from, counts, tile_out, cols_a, cols_b, rows_a, rows_b, offsets, sems):
    _, nb, tile, length = tile_out.shape
    half = length // 2
    npos = offsets.shape[3]
    listed = pltpu.make_async_copy(offsets_from, offsets, sems.at[nb])
    listed.start()
    copies = [
        pltpu.make_async_copy(
            field.at[:, :, b * length:(b + 1) * length], tile_out.at[:, b], sems.at[b])
        for b in range(nb)
    ]
    for copy in copies:
        copy.start()
    listed.wait()
    spot = lanes((8, length))
    info = jnp.zeros((8, length), jnp.int32)
    down = (lax.axis_index("row") + 1) * tile
    across = (lax.axis_index("col") + 1) * tile
    for k in range(npos):
        live = k < counts[0, 0]
        info = jnp.where(spot == k, jnp.where(live, offsets[0, 0, 0, k] + down, 0), info)
        info = jnp.where(spot == npos + k, jnp.where(live, offsets[0, 0, 1, k] + across, 0), info)
    info = info.astype(jnp.float32)
    for end in (cols_a, cols_b, rows_a, rows_b):
        end[pl.ds(end.shape[0] - 8, 8), :] = info
    for copy in copies:
        copy.wait()
    low = lanes((tile, length)) < half
    to_left = jnp.where(low, tile_out[0, 0], swap(tile_out[1, 0], half))
    to_right = jnp.where(low, swap(tile_out[1, nb - 1], half), tile_out[0, nb - 1])
    cols_a[:tile], cols_b[:tile] = by_pairs("col", to_left, to_right)
    for part in (0, 1):
        for b in range(nb):
            at = pl.ds((part * nb + b) * half, half)
            rows_a[at, :], rows_b[at, :] = by_pairs(
                "row", tile_out[part, b, :half], tile_out[part, b, tile - half:])


def start_corners(cols_a, cols_b, after, corners_a, corners_b):
    length = cols_a.shape[1]
    half = length // 2
    tile = cols_a.shape[0] - 8
    low = lanes((tile, length)) < half
    left, right = by_side("col", cols_a[:tile], cols_b[:tile])
    for part in (0, 1):
        if part:
            left, right = swap(left, half), swap(right, half)
        value = jnp.where(low, right, left)
        at = pl.ds(part * half, half)
        corners_a[at, :], corners_b[at, :] = by_pairs("row", value[:half], value[tile - half:])
    first = lax.broadcasted_iota(jnp.int32, (8, length), 0) == 0
    info = jnp.where(first, cols_a[tile:], cols_b[tile:])
    corners_a[2 * half:] = info
    corners_b[2 * half:] = info


def fetch_pass(after, probe_from, amps_from, tables_from, probe, amps, tables, sems):
    copies = [
        pltpu.make_async_copy(source, target, sems.at[k])
        for k, (source, target) in enumerate(
            ((amps_from, amps), (tables_from, tables), (probe_from, probe)))
    ]
    for copy in copies:
        copy.start()
    for copy in copies:
        copy.wait()


def early_pass(offsets, counts, after, field, probe, amps, tables, acc, chosen):
    _, nb, tile, length = field.shape
    acc[...] = jnp.zeros_like(acc)
    found = jnp.minimum(choose(chosen, offsets, counts, tile, length, early), GROUP)
    add_gradients(field, acc, probe, amps, offsets, tables, chosen, found,
                  own_frame=True, own_acc=True)


def first_pass(offsets, counts, field, done, cols_a, cols_b, rows_a, rows_b, corners_a, corners_b,
               probe, amps, tables, frame, acc, sums_a, sums_b, edges_a, edges_b, chosen):
    _, nb, tile, length = field.shape
    half = length // 2
    rows = tile + 2 * half
    own = pl.ds(half, tile)
    left, right = by_side("col", cols_a[:tile], cols_b[:tile])
    top = pl.ds(0, half)
    bottom = pl.ds(half + tile, half)
    for part in (0, 1):
        for b in range(nb):
            frame[part, b + 1, own, :] = field[part, b]
            at = pl.ds((part * nb + b) * half, half)
            frame[part, b + 1, top, :], frame[part, b + 1, bottom, :] = by_side(
                "row", rows_a[at, :], rows_b[at, :])
        frame[part, 0, own, :] = swap(left, half) if part else left
        frame[part, nb + 1, own, :] = swap(right, half) if part else right
        at = pl.ds(part * half, half)
        ends = by_side("row", corners_a[at, :], corners_b[at, :])
        for block in (0, nb + 1):
            frame[part, block, top, :], frame[part, block, bottom, :] = ends
    empty = jnp.zeros((half, length), jnp.float32)
    for part in (0, 1):
        for b in range(nb + 2):
            acc[part, b, top, :] = empty
            acc[part, b, bottom, :] = empty
            acc[part, b, own, :] = (
                done[part, b - 1] if 0 < b <= nb else jnp.zeros((tile, length), jnp.float32))
    found = choose(
        chosen, offsets, counts, tile, length, touching, done_early=True)
    add_gradients(frame, acc, probe, amps, offsets, tables, chosen, found)
    low = lanes((rows, length)) < half
    for part in (0, 1):
        sums_a[part], sums_b[part] = by_pairs(
            "col",
            jnp.where(low, acc[part, 1], acc[part, 0]),
            jnp.where(low, acc[part, nb + 1], acc[part, nb]),
        )
    near = lanes((length, length)) < half
    for part in (0, 1):
        for b in range(nb - 1):
            ends = [
                acc[part, b + 2, at, :] if b < nb - 2
                else jnp.where(near, acc[part, nb, at, :], acc[part, 1, at, :])
                for at in (pl.ds(0, length), pl.ds(rows - length, length))
            ]
            edges_a[part, b], edges_b[part, b] = by_pairs("row", *ends)


def middle_corners(mine_a, mine_b, sums_a, sums_b, after, corners_a, corners_b):
    _, rows, length = sums_a.shape
    for part in (0, 1):
        for at, k in ((pl.ds(0, length), 0), (pl.ds(rows - length, length), 1)):
            sides = by_side(
                "col", mine_a[part, at, :] + sums_a[part, at, :],
                mine_b[part, at, :] + sums_b[part, at, :])
            for side in (0, 1):
                if k == 0:
                    up = sides
                else:
                    corners_a[part, side], corners_b[part, side] = by_pairs(
                        "row", up[side], sides[side])


def light_pass(mine, cols_a, cols_b, rows_a, rows_b, corners_a, corners_b, probe, after,
               inverse, light, power, places, listed, chosen, sem, *, npos):
    length = probe.shape[-1]
    half = length // 2
    blocks, rows, _ = inverse.shape
    nb = blocks - 2
    tile = nb * length
    my_row = lax.axis_index("row")
    my_col = lax.axis_index("col")
    sources = (mine, cols_a, cols_b, rows_a, rows_b, corners_a, corners_b)
    for k, source in enumerate(sources):
        given = source[source.shape[0] - 8:, :].astype(jnp.int32)
        col = pltpu.roll(given, length - npos, 1) - (my_col + 1) * tile + 2 * length
        row = given - (my_row + 1) * tile + half + length
        near = (given > 0) & (row > 0) & (row < rows + length)
        near = near & (col > length - half) & (col < 2 * length + tile + half)
        places[pl.ds(8 * k, 8), :] = jnp.where(near, row * 4 * tile + col, 0)
    copy = pltpu.make_async_copy(places, listed, sem)
    copy.start()
    light[...] = jnp.zeros_like(light)
    power[...] = probe[0] * probe[0] + probe[1] * probe[1]
    lane = lanes((length, length))
    copy.wait()

    def look(index, found):
        line = jnp.where(index < len(sources), 8 * index, 8 * (index - 2) + 1)
        for slot in range(npos):
            place = listed[line, slot]
            chosen[found] = place
            found = found + jnp.where(place > 0, 1, 0)
        return found

    found = lax.fori_loop(0, len(sources) + 2, look, 0)

    def put(index, carry):
        place = chosen[index]
        start = lax.div(place, 4 * tile)
        col = lax.rem(place, 4 * tile)
        block = lax.div(col, length)
        shift = lax.rem(col, length)
        value = pltpu.roll(power[...], shift, 1)
        inside = lane >= shift
        light[block, pl.ds(start, length), :] += jnp.where(inside, value, 0.0)
        light[block + 1, pl.ds(start, length), :] += jnp.where(inside, 0.0, value)
        return carry

    lax.fori_loop(0, found, put, 0)
    spot = lax.broadcasted_iota(jnp.int32, (rows, length), 0)
    keep_from = jnp.where(my_row > 0, 0, half)
    keep_to = jnp.where(my_row < lax.axis_size("row") - 1, rows, rows - half)
    kept = (spot >= keep_from) & (spot < keep_to)
    for b in range(blocks):
        value = 1.0 / (light[b + 1, pl.ds(length, rows), :] + 1.0)
        keep = kept
        if b == 0:
            keep = keep & (my_col > 0)
        if b == nb + 1:
            keep = keep & (my_col < lax.axis_size("col") - 1)
        inverse[b] = jnp.where(keep, value, 0.0)


def update_pass(offsets, counts, frame, acc, inverse, sums_a, sums_b, probe, amps, tables,
                work, total, chosen):
    _, blocks, rows, length = frame.shape
    half = length // 2
    nb = blocks - 2
    work[...] = acc[...]
    found = choose(
        chosen, offsets, counts, nb * length, length,
        lambda mid_row, mid_col, **_: mid_col & mid_row)
    add_gradients(frame, work, probe, amps, offsets, tables, chosen, found)
    low = lanes((rows, length)) < half
    for part in (0, 1):
        left, right = by_side("col", sums_a[part], sums_b[part])
        for b in range(blocks):
            value = work[part, b]
            if b == 0:
                value = value + left
            if b == 1:
                value = value + jnp.where(low, left, 0.0)
            if b == nb:
                value = value + jnp.where(low, 0.0, right)
            if b == nb + 1:
                value = value + right
            work[part, b] = frame[part, b] + value * inverse[b]
    total[...] = jnp.zeros_like(total)
    found = choose(chosen, offsets, counts, nb * length, length, lambda mid_row, **_: mid_row)
    add_gradients(work, total, probe, amps, offsets, tables, chosen, found)


def second_pass(offsets, counts, work_from, total_from, inverse, edges_a, edges_b,
                corners_a, corners_b, probe, amps, tables,
                work, sums, cols_a, cols_b, rows_a, rows_b, total, chosen):
    _, blocks, rows, length = work.shape
    half = length // 2
    nb = blocks - 2
    tile = nb * length
    near = lanes((length, length)) < half
    middle = pl.ds(length, rows - 2 * length)
    for part in (0, 1):
        edges = [by_side("row", edges_a[part, b], edges_b[part, b]) for b in range(nb - 1)]
        corners = [by_side("row", corners_a[part, side], corners_b[part, side]) for side in (0, 1)]
        for k, at in enumerate((pl.ds(0, length), pl.ds(rows - length, length))):
            left, right, ends = corners[0][k], corners[1][k], edges[nb - 2][k]
            add = [left, jnp.where(near, left, ends)]
            add += [edges[b][k] for b in range(nb - 2)]
            add += [jnp.where(near, ends, right), right]
            for b in range(blocks):
                work[part, b, at, :] = work_from[part, b, at, :] + add[b] * inverse[b, at, :]
        for b in range(blocks):
            work[part, b, middle, :] = work_from[part, b, middle, :]
    total[...] = total_from[...]
    found = choose(
        chosen, offsets, counts, tile, length,
        lambda mid_row, cross_row, cross_col, **_: ~mid_row & (cross_row | cross_col))
    add_gradients(work, total, probe, amps, offsets, tables, chosen, found)
    low = lanes((rows, length)) < half
    cols_a[...], cols_b[...] = by_pairs(
        "col",
        jnp.where(low, swap(total[1, 0], half), total[0, 0]),
        jnp.where(low, total[0, nb + 1], swap(total[1, nb + 1], half)),
    )
    for part in (0, 1):
        for b in range(nb):
            sums[part, b] = total[part, b + 1, pl.ds(half, tile), :]
            rows_a[part, b], rows_b[part, b] = by_pairs(
                "row", total[part, b + 1, :half, :], total[part, b + 1, half + tile:, :])


def inner_pass(offsets, counts, work, probe, amps, tables, sums, chosen):
    _, nb, tile, length = sums.shape
    sums[...] = jnp.zeros_like(sums)
    found = choose(
        chosen, offsets, counts, tile, length,
        lambda mid_row, cross_row, cross_col, **_: ~mid_row & ~cross_row & ~cross_col)
    add_gradients(work, sums, probe, amps, offsets, tables, chosen, found, own_acc=True)


def end_corners(cols_a, cols_b, corners_a, corners_b):
    rows, length = cols_a.shape
    half = length // 2
    for side, value in enumerate(by_side("col", cols_a[...], cols_b[...])):
        corners_a[side], corners_b[side] = by_pairs("row", value[:half], value[rows - half:])


def last_pass(work, sums, inner, inverse, cols_a, cols_b, rows_a, rows_b, corners_a, corners_b, out):
    _, nb, tile, length = sums.shape
    half = length // 2
    low = lanes((tile, length)) < half
    own = pl.ds(half, tile)
    gap = jnp.zeros((tile - 2 * half, length), jnp.float32)
    sides = []
    for side, value in enumerate(by_side("col", cols_a[own, :], cols_b[own, :])):
        up, down = by_side("row", corners_a[side], corners_b[side])
        sides.append(value + above(above(up, gap), down))
    left, right = sides
    for part in (0, 1):
        if part:
            left, right = swap(left, half), swap(right, half)
        for b in range(nb):
            up, down = by_side("row", rows_a[part, b], rows_b[part, b])
            value = sums[part, b] + inner[part, b] + above(above(up, gap), down)
            if b == 0:
                value = value + jnp.where(low, left, 0.0)
            if b == nb - 1:
                value = value + jnp.where(low, 0.0, right)
            out[part, :, b * length:(b + 1) * length] = (
                work[part, b + 1, own, :] + value * inverse[b + 1, own, :])


def whole(memory_space=pltpu.VMEM):
    return pl.BlockSpec(memory_space=memory_space)


def call(body, shapes, places, scratch=(), cost=None):
    return pl.pallas_call(
        body,
        out_shape=[jax.ShapeDtypeStruct(shape, jnp.float32) for shape in shapes],
        in_specs=[whole({"s": pltpu.SMEM, "v": pltpu.VMEM, "a": pl.ANY, "h": pltpu.HBM}[p]) for p in places],
        out_specs=[whole()] * len(shapes),
        scratch_shapes=list(scratch),
        compiler_params=pltpu.CompilerParams(vmem_limit_bytes=VMEM_BYTES),
        cost_estimate=cost,
    )


def swap_pairs(first, second, axis):
    count = lax.axis_size(axis)
    got = []
    for value, start in ((first, 1), (second, 0)):
        pairs = [(i, i + 1) for i in range(start, count - 1, 2)]
        got.append(lax.ppermute(value, axis, pairs + [(b, a) for a, b in pairs]))
    return got


def shards(object_field, probe, amplitudes, offsets, counts):
    length = probe.shape[-1]
    half = length // 2
    tile = object_field.shape[1]
    npos = offsets.shape[2]
    nb = tile // length
    blocks = nb + 2
    rows = tile + 2 * half
    tables = jnp.asarray(dft_tables(length))
    offsets = jnp.swapaxes(offsets, 2, 3)

    def cost(positions):
        steps = 4 * 3 * 2 * length * (2 * length) ** 2
        return pl.CostEstimate(
            flops=positions * steps, bytes_accessed=8_000_000,
            transcendentals=positions * length * length)

    memory = pltpu.VMEM
    chosen = pltpu.SMEM((npos + GROUP,), jnp.int32)
    strip = (tile + 8, length)
    edge = (2 * nb * half + 8, length)
    def kept(array):
        return pltpu.with_memory_space_constraint(array, pltpu.HBM)

    field, cols_a, cols_b, rows_a, rows_b = call(
        start_pass, [(2, nb, tile, length), strip, strip, edge, edge], "hhs",
        [pltpu.SMEM((1, 1, 2, npos), jnp.int32), pltpu.SemaphoreType.DMA((nb + 1,))],
    )(kept(object_field), kept(offsets), counts)
    mine = cols_a
    probe, amplitudes, tables = pl.pallas_call(
        fetch_pass,
        out_shape=[
            jax.ShapeDtypeStruct(array.shape, array.dtype) for array in (probe, amplitudes, tables)],
        in_specs=[whole(pl.ANY)] + [whole(pltpu.HBM)] * 3,
        out_specs=[whole()] * 3,
        scratch_shapes=[pltpu.SemaphoreType.DMA((3,))],
        compiler_params=pltpu.CompilerParams(vmem_limit_bytes=VMEM_BYTES),
        cost_estimate=cost(1),
    )(cols_a, kept(probe), kept(amplitudes), kept(tables))
    cols_a, cols_b = swap_pairs(cols_a, cols_b, "col")
    rows_a, rows_b = swap_pairs(rows_a, rows_b, "row")
    corner = (2 * half + 8, length)
    corners_a, corners_b = call(start_corners, [corner, corner], "vva")(cols_a, cols_b, probe)
    (done,) = call(
        early_pass, [(2, nb, tile, length)], "ssavvvv", [chosen], cost(GROUP),
    )(offsets, counts, corners_b, field, probe, amplitudes, tables)
    corners_a, corners_b = swap_pairs(corners_a, corners_b, "row")

    full = (2, blocks, rows, length)
    strip = (2, rows, length)
    edge = (2, nb - 1, length, length)
    frame, acc, sums_a, sums_b, edges_a, edges_b = call(
        first_pass, [full, full, strip, strip, edge, edge], "ss" + 11 * "v", [chosen],
    )(offsets, counts, field, done, cols_a, cols_b, rows_a, rows_b, corners_a, corners_b,
      probe, amplitudes, tables)
    info = (mine, cols_a, cols_b, rows_a, rows_b, corners_a, corners_b)
    mine_a, mine_b = sums_a, sums_b
    sums_a, sums_b = swap_pairs(sums_a, sums_b, "col")
    edges_a, edges_b = swap_pairs(edges_a, edges_b, "row")
    (inverse,) = call(
        functools.partial(light_pass, npos=npos), [(blocks, rows, length)], 8 * "v" + "a",
        [memory((blocks + 2, rows + 2 * length, length), jnp.float32),
         memory((length, length), jnp.float32), memory((7 * 8, length), jnp.int32),
         pltpu.SMEM((7 * 8, length), jnp.int32), pltpu.SMEM((9 * npos + 1,), jnp.int32),
         pltpu.SemaphoreType.DMA],
        cost(npos // 2),
    )(*info, probe, acc)
    corner = (2, 2, length, length)
    corners_a, corners_b = call(middle_corners, [corner, corner], "vvvva")(
        mine_a, mine_b, sums_a, sums_b, inverse)
    corners_a, corners_b = swap_pairs(corners_a, corners_b, "row")

    work, total = call(update_pass, [full, full], "ss" + 8 * "v", [chosen], cost(npos // 2))(
        offsets, counts, frame, acc, inverse, sums_a, sums_b, probe, amplitudes, tables)
    strip = (rows, length)
    own = (2, nb, tile, length)
    edge = (2, nb, half, length)
    work, sums, cols_a, cols_b, rows_a, rows_b = call(
        second_pass, [full, own, strip, strip, edge, edge], "ss" + 10 * "v",
        [memory(full, jnp.float32), chosen], cost(npos // 2),
    )(offsets, counts, work, total, inverse, edges_a, edges_b, corners_a, corners_b,
      probe, amplitudes, tables)
    cols_a, cols_b = swap_pairs(cols_a, cols_b, "col")
    rows_a, rows_b = swap_pairs(rows_a, rows_b, "row")
    (inner,) = call(inner_pass, [own], "ss" + 4 * "v", [chosen], cost(npos // 4))(
        offsets, counts, work, probe, amplitudes, tables)
    corner = (2, half, length)
    corners_a, corners_b = call(end_corners, [corner, corner], "vv")(cols_a, cols_b)
    corners_a, corners_b = swap_pairs(corners_a, corners_b, "row")
    (out,) = call(last_pass, [(2, tile, tile)], 10 * "v")(
        work, sums, inner, inverse, cols_a, cols_b, rows_a, rows_b, corners_a, corners_b)
    return out


def solution(mesh):
    placed = (
        P(None, "row", "col"),
        P(),
        P("row", "col", None, None, None),
        P("row", "col", None, None),
        P("row", "col"),
    )
    return jax.shard_map(
        shards, mesh=mesh, in_specs=placed, out_specs=P(None, "row", "col"), check_vma=False
    )
```

```python
import functools
import math

import jax
import jax.numpy as jnp
import numpy as np
from jax import lax
from jax.experimental import pallas as pl
from jax.experimental.pallas import tpu as pltpu
from jax.sharding import PartitionSpec as P

ITERS = 2
FLOOR = 0.25
VMEM_BYTES = 16 * 1024 * 1024
GROUP = 4
CHAIN = 2


def split(value):
    high = value.astype(jnp.bfloat16)
    low = (value - high.astype(jnp.float32)).astype(jnp.bfloat16)
    return high, low


def dft_tables(length):
    index = np.arange(length)
    angle = (index[:, None] * index[None, :] % length) * (2.0 * math.pi / length)
    cosine = np.cos(angle) / math.sqrt(length)
    sine = np.sin(angle) / math.sqrt(length)
    ahead = np.block([[cosine, -sine], [sine, cosine]])
    parts = []
    for table in (ahead, ahead.T):
        high = table.astype(jnp.bfloat16)
        low = (table - high.astype(np.float64)).astype(jnp.bfloat16)
        parts += [high, low]
    return np.stack(parts)


def lanes(shape):
    return lax.broadcasted_iota(jnp.int32, shape, len(shape) - 1)


def swap(value, half):
    return pltpu.roll(value, half, value.ndim - 1)


def odd_place(axis):
    return lax.axis_index(axis) % 2 == 1


def by_pairs(axis, low, high):
    odd = odd_place(axis)
    return jnp.where(odd, high, low), jnp.where(odd, low, high)


def by_side(axis, first, second):
    odd = odd_place(axis)
    return jnp.where(odd, second, first), jnp.where(odd, first, second)


def times_right(rows, high, low):
    top, rest = split(rows)
    left = jnp.concatenate([top, top, rest], axis=1)
    right = jnp.concatenate([high, low, high], axis=0)
    return jnp.dot(left, right, preferred_element_type=jnp.float32)


def times_left(high, low, columns):
    top, rest = split(columns)
    left = jnp.concatenate([high, low, high], axis=1)
    right = jnp.concatenate([top, top, rest], axis=0)
    return jnp.dot(left, right, preferred_element_type=jnp.float32)


def beside(left, right):
    return jnp.concatenate([left, right], axis=1)


def above(top, bottom):
    return jnp.concatenate([top, bottom], axis=0)


def touching(mid_row, mid_col, **_):
    return ~(mid_row & mid_col)


def early(cross_row, cross_col, **spot):
    return touching(**spot) & ~cross_row & ~cross_col


def choose(chosen, offsets, counts, tile, length, wanted, done_early=False):
    last = tile - length
    half = length // 2

    def look(slot, carry):
        found, seen = carry
        row = offsets[0, 0, 0, slot]
        col = offsets[0, 0, 1, slot]
        spot = dict(
            mid_row=(row >= half) & (row <= last - half),
            mid_col=(col >= half) & (col <= last - half),
            cross_row=(row < 0) | (row > last),
            cross_col=(col < 0) | (col > last),
        )
        taken = wanted(**spot)
        if done_early:
            soon = early(**spot)
            taken = taken & ~(soon & (seen < GROUP))
            seen = seen + jnp.where(soon, 1, 0)
        chosen[found] = slot
        return found + jnp.where(taken, 1, 0), seen

    found, _ = lax.fori_loop(0, counts[0, 0], look, (0, 0))
    filler = chosen[0]
    for k in range(GROUP):
        chosen[found + k] = filler
    return found


def add_gradients(frame, acc, probe_ref, amps, offsets, tables, chosen, found, own_frame=False, own_acc=False):
    length = probe_ref.shape[-1]
    half = length // 2
    lane = lanes((length, length))

    def place(slot, ref, own):
        col = offsets[0, 0, 1, slot] + length
        block = lax.div(col, length)
        row = offsets[0, 0, 0, slot]
        if own:
            block = block - 1
        else:
            row = row + half
        after = jnp.minimum(block + 1, ref.shape[1] - 1)
        return pl.ds(row, length), block, after, lax.rem(col, length)

    def exit_wave(slot):
        at, block, after, shift = place(slot, frame, own_frame)
        inside = lane >= shift
        window = [
            jnp.where(inside, frame[part, block, at, :], frame[part, after, at, :])
            for part in (0, 1)
        ]
        probe = (pltpu.roll(probe_ref[0], shift, 1), pltpu.roll(probe_ref[1], shift, 1))
        wave = (probe[0] * window[0] - probe[1] * window[1],
                probe[0] * window[1] + probe[1] * window[0])
        return probe, wave

    def shrink(real, imag, slot):
        ratio = amps[0, 0, slot] * lax.rsqrt(real * real + imag * imag + FLOOR) - 1.0
        return real * ratio, imag * ratio

    def put(slot, live, probe, back_r, back_i):
        at, block, after, shift = place(slot, acc, own_acc)
        grads = (probe[0] * back_r + probe[1] * back_i, probe[0] * back_i - probe[1] * back_r)
        bound = jnp.where(live, shift, length)
        inside = lane >= bound
        beyond = lane < jnp.where(live, shift, 0)
        for part in (0, 1):
            acc[part, block, at, :] += jnp.where(inside, grads[part], 0.0)
            acc[part, after, at, :] += jnp.where(beyond, grads[part], 0.0)

    def work(slots):
        probes, waves = zip(*[exit_wave(slot) for slot in slots])
        rows = jnp.concatenate([beside(*wave) for wave in waves], axis=0)
        mid = times_right(rows, tables[0], tables[1])
        yield None
        mids = [mid[k * length:(k + 1) * length] for k in range(len(slots))]
        columns = above(
            jnp.concatenate([m[:, :length] for m in mids], axis=1),
            jnp.concatenate([m[:, length:] for m in mids], axis=1),
        )
        far = times_left(tables[2], tables[3], columns)
        yield None
        changes = [
            shrink(far[:length, k * length:(k + 1) * length],
                   far[length:, k * length:(k + 1) * length], slot)
            for k, slot in enumerate(slots)
        ]
        columns = above(
            jnp.concatenate([c[0] for c in changes], axis=1),
            jnp.concatenate([c[1] for c in changes], axis=1),
        )
        mid = times_left(tables[0], tables[1], columns)
        yield None
        rows = jnp.concatenate(
            [
                beside(mid[:length, k * length:(k + 1) * length],
                       mid[length:, k * length:(k + 1) * length])
                for k in range(len(slots))
            ],
            axis=0,
        )
        back = times_right(rows, tables[2], tables[3])
        yield None
        yield [
            (probes[k], back[k * length:(k + 1) * length, :length],
             back[k * length:(k + 1) * length, length:])
            for k in range(len(slots))
        ]

    def step(index, carry):
        places = [index * GROUP + k for k in range(GROUP)]
        slots = [chosen[at] for at in places]
        chains = [work(slots[k:k + CHAIN]) for k in range(0, GROUP, CHAIN)]
        gradients = [None]
        while gradients[0] is None:
            gradients = [next(chain) for chain in chains]
        gradients = [gradient for chain in gradients for gradient in chain]
        for at, slot, gradient in zip(places, slots, gradients):
            put(slot, at < found, *gradient)
        return carry

    lax.fori_loop(0, (found + GROUP - 1) // GROUP, step, 0)


def start_pass(field, offsets_from, counts, tile_out, cols_a, cols_b, rows_a, rows_b, offsets, sems):
    _, nb, tile, length = tile_out.shape
    half = length // 2
    npos = offsets.shape[3]
    listed = pltpu.make_async_copy(offsets_from, offsets, sems.at[nb])
    listed.start()
    copies = [
        pltpu.make_async_copy(
            field.at[:, :, b * length:(b + 1) * length], tile_out.at[:, b], sems.at[b])
        for b in range(nb)
    ]
    for copy in copies:
        copy.start()
    listed.wait()
    spot = lanes((8, length))
    info = jnp.zeros((8, length), jnp.int32)
    down = (lax.axis_index("row") + 1) * tile
    across = (lax.axis_index("col") + 1) * tile
    for k in range(npos):
        live = k < counts[0, 0]
        info = jnp.where(spot == k, jnp.where(live, offsets[0, 0, 0, k] + down, 0), info)
        info = jnp.where(spot == npos + k, jnp.where(live, offsets[0, 0, 1, k] + across, 0), info)
    info = info.astype(jnp.float32)
    for end in (cols_a, cols_b, rows_a, rows_b):
        end[pl.ds(end.shape[0] - 8, 8), :] = info
    for copy in copies:
        copy.wait()
    low = lanes((tile, length)) < half
    to_left = jnp.where(low, tile_out[0, 0], swap(tile_out[1, 0], half))
    to_right = jnp.where(low, swap(tile_out[1, nb - 1], half), tile_out[0, nb - 1])
    cols_a[:tile], cols_b[:tile] = by_pairs("col", to_left, to_right)
    for part in (0, 1):
        for b in range(nb):
            at = pl.ds((part * nb + b) * half, half)
            rows_a[at, :], rows_b[at, :] = by_pairs(
                "row", tile_out[part, b, :half], tile_out[part, b, tile - half:])


def start_corners(cols_a, cols_b, after, corners_a, corners_b):
    length = cols_a.shape[1]
    half = length // 2
    tile = cols_a.shape[0] - 8
    low = lanes((tile, length)) < half
    left, right = by_side("col", cols_a[:tile], cols_b[:tile])
    for part in (0, 1):
        if part:
            left, right = swap(left, half), swap(right, half)
        value = jnp.where(low, right, left)
        at = pl.ds(part * half, half)
        corners_a[at, :], corners_b[at, :] = by_pairs("row", value[:half], value[tile - half:])
    first = lax.broadcasted_iota(jnp.int32, (8, length), 0) == 0
    info = jnp.where(first, cols_a[tile:], cols_b[tile:])
    corners_a[2 * half:] = info
    corners_b[2 * half:] = info


def fetch_pass(after, probe_from, amps_from, tables_from, probe, amps, tables, sems):
    copies = [
        pltpu.make_async_copy(source, target, sems.at[k])
        for k, (source, target) in enumerate(
            ((amps_from, amps), (tables_from, tables), (probe_from, probe)))
    ]
    for copy in copies:
        copy.start()
    for copy in copies:
        copy.wait()


def early_pass(offsets, counts, after, field, probe, amps, tables, acc, chosen):
    _, nb, tile, length = field.shape
    acc[...] = jnp.zeros_like(acc)
    found = jnp.minimum(choose(chosen, offsets, counts, tile, length, early), GROUP)
    add_gradients(field, acc, probe, amps, offsets, tables, chosen, found,
                  own_frame=True, own_acc=True)


def first_pass(offsets, counts, field, done, cols_a, cols_b, rows_a, rows_b, corners_a, corners_b,
               probe, amps, tables, frame, acc, tips_a, tips_b, sums_a, sums_b, edges_a, edges_b, chosen):
    _, nb, tile, length = field.shape
    half = length // 2
    rows = tile + 2 * half
    own = pl.ds(half, tile)
    left, right = by_side("col", cols_a[:tile], cols_b[:tile])
    top = pl.ds(0, half)
    bottom = pl.ds(half + tile, half)
    for part in (0, 1):
        for b in range(nb):
            frame[part, b + 1, own, :] = field[part, b]
            at = pl.ds((part * nb + b) * half, half)
            frame[part, b + 1, top, :], frame[part, b + 1, bottom, :] = by_side(
                "row", rows_a[at, :], rows_b[at, :])
        frame[part, 0, own, :] = swap(left, half) if part else left
        frame[part, nb + 1, own, :] = swap(right, half) if part else right
        at = pl.ds(part * half, half)
        ends = by_side("row", corners_a[at, :], corners_b[at, :])
        for block in (0, nb + 1):
            frame[part, block, top, :], frame[part, block, bottom, :] = ends
    empty = jnp.zeros((half, length), jnp.float32)
    for part in (0, 1):
        for b in range(nb + 2):
            acc[part, b, top, :] = empty
            acc[part, b, bottom, :] = empty
            acc[part, b, own, :] = (
                done[part, b - 1] if 0 < b <= nb else jnp.zeros((tile, length), jnp.float32))
    found = choose(
        chosen, offsets, counts, tile, length, touching, done_early=True)
    add_gradients(frame, acc, probe, amps, offsets, tables, chosen, found)
    low = lanes((rows, length)) < half
    for part in (0, 1):
        strip_a, strip_b = by_pairs(
            "col",
            jnp.where(low, acc[part, 1], acc[part, 0]),
            jnp.where(low, acc[part, nb + 1], acc[part, nb]),
        )
        for strip, tips, sums in ((strip_a, tips_a, sums_a), (strip_b, tips_b, sums_b)):
            tips[part, 0] = strip[:length]
            tips[part, 1] = strip[rows - length:]
            sums[part] = strip[length:rows - length]
    near = lanes((length, length)) < half
    for part in (0, 1):
        for b in range(nb - 1):
            ends = [
                acc[part, b + 2, at, :] if b < nb - 2
                else jnp.where(near, acc[part, nb, at, :], acc[part, 1, at, :])
                for at in (pl.ds(0, length), pl.ds(rows - length, length))
            ]
            edges_a[part, b], edges_b[part, b] = by_pairs("row", *ends)


def middle_corners(mine_a, mine_b, tips_a, tips_b, after, corners, *, odd_pairs):
    for part in (0, 1):
        up, down = [
            by_side("col", mine_a[part, k] + tips_a[part, k], mine_b[part, k] + tips_b[part, k])
            for k in (0, 1)
        ]
        for side in (0, 1):
            corners[part, side] = by_pairs("row", up[side], down[side])[0 if odd_pairs else 1]


def light_pass(mine, cols_a, cols_b, rows_a, rows_b, corners_a, corners_b, probe, after,
               inverse, light, power, places, listed, chosen, sem, *, npos):
    length = probe.shape[-1]
    half = length // 2
    blocks, rows, _ = inverse.shape
    nb = blocks - 2
    tile = nb * length
    my_row = lax.axis_index("row")
    my_col = lax.axis_index("col")
    sources = (mine, cols_a, cols_b, rows_a, rows_b, corners_a, corners_b)
    for k, source in enumerate(sources):
        given = source[source.shape[0] - 8:, :].astype(jnp.int32)
        col = pltpu.roll(given, length - npos, 1) - (my_col + 1) * tile + 2 * length
        row = given - (my_row + 1) * tile + half + length
        near = (given > 0) & (row > 0) & (row < rows + length)
        near = near & (col > length - half) & (col < 2 * length + tile + half)
        places[pl.ds(8 * k, 8), :] = jnp.where(near, row * 4 * tile + col, 0)
    copy = pltpu.make_async_copy(places, listed, sem)
    copy.start()
    light[...] = jnp.zeros_like(light)
    power[...] = probe[0] * probe[0] + probe[1] * probe[1]
    lane = lanes((length, length))
    copy.wait()

    def look(index, found):
        line = jnp.where(index < len(sources), 8 * index, 8 * (index - 2) + 1)
        for slot in range(npos):
            place = listed[line, slot]
            chosen[found] = place
            found = found + jnp.where(place > 0, 1, 0)
        return found

    found = lax.fori_loop(0, len(sources) + 2, look, 0)

    def put(index, carry):
        place = chosen[index]
        start = lax.div(place, 4 * tile)
        col = lax.rem(place, 4 * tile)
        block = lax.div(col, length)
        shift = lax.rem(col, length)
        value = pltpu.roll(power[...], shift, 1)
        inside = lane >= shift
        light[block, pl.ds(start, length), :] += jnp.where(inside, value, 0.0)
        light[block + 1, pl.ds(start, length), :] += jnp.where(inside, 0.0, value)
        return carry

    lax.fori_loop(0, found, put, 0)
    spot = lax.broadcasted_iota(jnp.int32, (rows, length), 0)
    keep_from = jnp.where(my_row > 0, 0, half)
    keep_to = jnp.where(my_row < lax.axis_size("row") - 1, rows, rows - half)
    kept = (spot >= keep_from) & (spot < keep_to)
    for b in range(blocks):
        value = 1.0 / (light[b + 1, pl.ds(length, rows), :] + 1.0)
        keep = kept
        if b == 0:
            keep = keep & (my_col > 0)
        if b == nb + 1:
            keep = keep & (my_col < lax.axis_size("col") - 1)
        inverse[b] = jnp.where(keep, value, 0.0)


def update_pass(offsets, counts, frame, acc, inverse, tips_a, tips_b, sums_a, sums_b, probe, amps, tables,
                work, total, chosen):
    _, blocks, rows, length = frame.shape
    half = length // 2
    nb = blocks - 2
    work[...] = acc[...]
    found = choose(
        chosen, offsets, counts, nb * length, length,
        lambda mid_row, mid_col, **_: mid_col & mid_row)
    add_gradients(frame, work, probe, amps, offsets, tables, chosen, found)
    low = lanes((rows, length)) < half
    for part in (0, 1):
        left, right = by_side("col", *[
            above(above(tips[part, 0], sums[part]), tips[part, 1])
            for tips, sums in ((tips_a, sums_a), (tips_b, sums_b))
        ])
        for b in range(blocks):
            value = work[part, b]
            if b == 0:
                value = value + left
            if b == 1:
                value = value + jnp.where(low, left, 0.0)
            if b == nb:
                value = value + jnp.where(low, 0.0, right)
            if b == nb + 1:
                value = value + right
            work[part, b] = frame[part, b] + value * inverse[b]
    total[...] = jnp.zeros_like(total)
    found = choose(chosen, offsets, counts, nb * length, length, lambda mid_row, **_: mid_row)
    add_gradients(work, total, probe, amps, offsets, tables, chosen, found)


def second_pass(offsets, counts, work_from, total_from, inverse, edges_a, edges_b,
                corners_a, corners_b, probe, amps, tables,
                work, sums, cols_a, cols_b, rows_a, rows_b, total, chosen):
    _, blocks, rows, length = work.shape
    half = length // 2
    nb = blocks - 2
    tile = nb * length
    near = lanes((length, length)) < half
    middle = pl.ds(length, rows - 2 * length)
    for part in (0, 1):
        edges = [by_side("row", edges_a[part, b], edges_b[part, b]) for b in range(nb - 1)]
        corners = [by_side("row", corners_a[part, side], corners_b[part, side]) for side in (0, 1)]
        for k, at in enumerate((pl.ds(0, length), pl.ds(rows - length, length))):
            left, right, ends = corners[0][k], corners[1][k], edges[nb - 2][k]
            add = [left, jnp.where(near, left, ends)]
            add += [edges[b][k] for b in range(nb - 2)]
            add += [jnp.where(near, ends, right), right]
            for b in range(blocks):
                work[part, b, at, :] = work_from[part, b, at, :] + add[b] * inverse[b, at, :]
        for b in range(blocks):
            work[part, b, middle, :] = work_from[part, b, middle, :]
    total[...] = total_from[...]
    found = choose(
        chosen, offsets, counts, tile, length,
        lambda mid_row, cross_row, cross_col, **_: ~mid_row & (cross_row | cross_col))
    add_gradients(work, total, probe, amps, offsets, tables, chosen, found)
    low = lanes((rows, length)) < half
    cols_a[...], cols_b[...] = by_pairs(
        "col",
        jnp.where(low, swap(total[1, 0], half), total[0, 0]),
        jnp.where(low, total[0, nb + 1], swap(total[1, nb + 1], half)),
    )
    for part in (0, 1):
        for b in range(nb):
            sums[part, b] = total[part, b + 1, pl.ds(half, tile), :]
            rows_a[part, b], rows_b[part, b] = by_pairs(
                "row", total[part, b + 1, :half, :], total[part, b + 1, half + tile:, :])


def inner_pass(offsets, counts, work, probe, amps, tables, sums, chosen):
    _, nb, tile, length = sums.shape
    sums[...] = jnp.zeros_like(sums)
    found = choose(
        chosen, offsets, counts, tile, length,
        lambda mid_row, cross_row, cross_col, **_: ~mid_row & ~cross_row & ~cross_col)
    add_gradients(work, sums, probe, amps, offsets, tables, chosen, found, own_acc=True)


def end_corners(cols_a, cols_b, corners_a, corners_b):
    rows, length = cols_a.shape
    half = length // 2
    for side, value in enumerate(by_side("col", cols_a[...], cols_b[...])):
        corners_a[side], corners_b[side] = by_pairs("row", value[:half], value[rows - half:])


def last_pass(work, sums, inner, inverse, cols_a, cols_b, rows_a, rows_b, corners_a, corners_b, out):
    _, nb, tile, length = sums.shape
    half = length // 2
    low = lanes((tile, length)) < half
    own = pl.ds(half, tile)
    gap = jnp.zeros((tile - 2 * half, length), jnp.float32)
    sides = []
    for side, value in enumerate(by_side("col", cols_a[own, :], cols_b[own, :])):
        up, down = by_side("row", corners_a[side], corners_b[side])
        sides.append(value + above(above(up, gap), down))
    left, right = sides
    for part in (0, 1):
        if part:
            left, right = swap(left, half), swap(right, half)
        for b in range(nb):
            up, down = by_side("row", rows_a[part, b], rows_b[part, b])
            value = sums[part, b] + inner[part, b] + above(above(up, gap), down)
            if b == 0:
                value = value + jnp.where(low, left, 0.0)
            if b == nb - 1:
                value = value + jnp.where(low, 0.0, right)
            out[part, :, b * length:(b + 1) * length] = (
                work[part, b + 1, own, :] + value * inverse[b + 1, own, :])


def whole(memory_space=pltpu.VMEM):
    return pl.BlockSpec(memory_space=memory_space)


def call(body, shapes, places, scratch=(), cost=None):
    return pl.pallas_call(
        body,
        out_shape=[jax.ShapeDtypeStruct(shape, jnp.float32) for shape in shapes],
        in_specs=[whole({"s": pltpu.SMEM, "v": pltpu.VMEM, "a": pl.ANY, "h": pltpu.HBM}[p]) for p in places],
        out_specs=[whole()] * len(shapes),
        scratch_shapes=list(scratch),
        compiler_params=pltpu.CompilerParams(vmem_limit_bytes=VMEM_BYTES),
        cost_estimate=cost,
    )


def swap_pairs(first, second, axis):
    count = lax.axis_size(axis)
    got = []
    for value, start in ((first, 1), (second, 0)):
        pairs = [(i, i + 1) for i in range(start, count - 1, 2)]
        got.append(lax.ppermute(value, axis, pairs + [(b, a) for a, b in pairs]))
    return got


def shards(object_field, probe, amplitudes, offsets, counts):
    length = probe.shape[-1]
    half = length // 2
    tile = object_field.shape[1]
    npos = offsets.shape[2]
    nb = tile // length
    blocks = nb + 2
    rows = tile + 2 * half
    tables = jnp.asarray(dft_tables(length))
    offsets = jnp.swapaxes(offsets, 2, 3)

    def cost(positions):
        steps = 4 * 3 * 2 * length * (2 * length) ** 2
        return pl.CostEstimate(
            flops=positions * steps, bytes_accessed=8_000_000,
            transcendentals=positions * length * length)

    memory = pltpu.VMEM
    chosen = pltpu.SMEM((npos + GROUP,), jnp.int32)
    strip = (tile + 8, length)
    edge = (2 * nb * half + 8, length)
    def kept(array):
        return pltpu.with_memory_space_constraint(array, pltpu.HBM)

    field, cols_a, cols_b, rows_a, rows_b = call(
        start_pass, [(2, nb, tile, length), strip, strip, edge, edge], "hhs",
        [pltpu.SMEM((1, 1, 2, npos), jnp.int32), pltpu.SemaphoreType.DMA((nb + 1,))],
    )(kept(object_field), kept(offsets), counts)
    mine = cols_a
    probe, amplitudes, tables = pl.pallas_call(
        fetch_pass,
        out_shape=[
            jax.ShapeDtypeStruct(array.shape, array.dtype) for array in (probe, amplitudes, tables)],
        in_specs=[whole(pl.ANY)] + [whole(pltpu.HBM)] * 3,
        out_specs=[whole()] * 3,
        scratch_shapes=[pltpu.SemaphoreType.DMA((3,))],
        compiler_params=pltpu.CompilerParams(vmem_limit_bytes=VMEM_BYTES),
        cost_estimate=cost(1),
    )(cols_a, kept(probe), kept(amplitudes), kept(tables))
    cols_a, cols_b = swap_pairs(cols_a, cols_b, "col")
    rows_a, rows_b = swap_pairs(rows_a, rows_b, "row")
    corner = (2 * half + 8, length)
    corners_a, corners_b = call(start_corners, [corner, corner], "vva")(cols_a, cols_b, probe)
    (done,) = call(
        early_pass, [(2, nb, tile, length)], "ssavvvv", [chosen], cost(GROUP),
    )(offsets, counts, corners_b, field, probe, amplitudes, tables)
    corners_a, corners_b = swap_pairs(corners_a, corners_b, "row")

    full = (2, blocks, rows, length)
    strip = (2, rows, length)
    edge = (2, nb - 1, length, length)
    tip = (2, 2, length, length)
    strip = (2, rows - 2 * length, length)
    frame, acc, tips_a, tips_b, sums_a, sums_b, edges_a, edges_b = call(
        first_pass, [full, full, tip, tip, strip, strip, edge, edge], "ss" + 11 * "v", [chosen],
    )(offsets, counts, field, done, cols_a, cols_b, rows_a, rows_b, corners_a, corners_b,
      probe, amplitudes, tables)
    info = (mine, cols_a, cols_b, rows_a, rows_b, corners_a, corners_b)
    mine_a, mine_b = tips_a, tips_b
    tips_a, tips_b = swap_pairs(tips_a, tips_b, "col")
    edges_a, edges_b = swap_pairs(edges_a, edges_b, "row")
    sums_a, sums_b = swap_pairs(sums_a, sums_b, "col")
    (inverse,) = call(
        functools.partial(light_pass, npos=npos), [(blocks, rows, length)], 8 * "v" + "a",
        [memory((blocks + 2, rows + 2 * length, length), jnp.float32),
         memory((length, length), jnp.float32), memory((7 * 8, length), jnp.int32),
         pltpu.SMEM((7 * 8, length), jnp.int32), pltpu.SMEM((9 * npos + 1,), jnp.int32),
         pltpu.SemaphoreType.DMA],
        cost(npos // 2),
    )(*info, probe, acc)
    corners_a, corners_b = [
        call(functools.partial(middle_corners, odd_pairs=odd_pairs), [tip], "vvvva")(
            mine_a, mine_b, tips_a, tips_b, after)[0]
        for odd_pairs, after in ((True, acc), (False, inverse))
    ]
    corners_a, corners_b = swap_pairs(corners_a, corners_b, "row")

    work, total = call(update_pass, [full, full], "ss" + 10 * "v", [chosen], cost(npos // 2))(
        offsets, counts, frame, acc, inverse, tips_a, tips_b, sums_a, sums_b,
        probe, amplitudes, tables)
    strip = (rows, length)
    own = (2, nb, tile, length)
    edge = (2, nb, half, length)
    work, sums, cols_a, cols_b, rows_a, rows_b = call(
        second_pass, [full, own, strip, strip, edge, edge], "ss" + 10 * "v",
        [memory(full, jnp.float32), chosen], cost(npos // 2),
    )(offsets, counts, work, total, inverse, edges_a, edges_b, corners_a, corners_b,
      probe, amplitudes, tables)
    cols_a, cols_b = swap_pairs(cols_a, cols_b, "col")
    rows_a, rows_b = swap_pairs(rows_a, rows_b, "row")
    (inner,) = call(inner_pass, [own], "ss" + 4 * "v", [chosen], cost(npos // 4))(
        offsets, counts, work, probe, amplitudes, tables)
    corner = (2, half, length)
    corners_a, corners_b = call(end_corners, [corner, corner], "vv")(cols_a, cols_b)
    corners_a, corners_b = swap_pairs(corners_a, corners_b, "row")
    (out,) = call(last_pass, [(2, tile, tile)], 10 * "v")(
        work, sums, inner, inverse, cols_a, cols_b, rows_a, rows_b, corners_a, corners_b)
    return out


def solution(mesh):
    placed = (
        P(None, "row", "col"),
        P(),
        P("row", "col", None, None, None),
        P("row", "col", None, None),
        P("row", "col"),
    )
    return jax.shard_map(
        shards, mesh=mesh, in_specs=placed, out_specs=P(None, "row", "col"), check_vma=False
    )
```

```python
import functools
import math

import jax
import jax.numpy as jnp
import numpy as np
from jax import lax
from jax.experimental import pallas as pl
from jax.experimental.pallas import tpu as pltpu
from jax.sharding import PartitionSpec as P

ITERS = 2
FLOOR = 0.25
VMEM_BYTES = 16 * 1024 * 1024
GROUP = 4
CHAIN = 2


def split(value):
    high = value.astype(jnp.bfloat16)
    low = (value - high.astype(jnp.float32)).astype(jnp.bfloat16)
    return high, low


def dft_tables(length):
    index = np.arange(length)
    angle = (index[:, None] * index[None, :] % length) * (2.0 * math.pi / length)
    cosine = np.cos(angle) / math.sqrt(length)
    sine = np.sin(angle) / math.sqrt(length)
    ahead = np.block([[cosine, -sine], [sine, cosine]])
    parts = []
    for table in (ahead, ahead.T):
        high = table.astype(jnp.bfloat16)
        low = (table - high.astype(np.float64)).astype(jnp.bfloat16)
        parts += [high, low]
    return np.stack(parts)


def lanes(shape):
    return lax.broadcasted_iota(jnp.int32, shape, len(shape) - 1)


def swap(value, half):
    return pltpu.roll(value, half, value.ndim - 1)


def odd_place(axis):
    return lax.axis_index(axis) % 2 == 1


def by_pairs(axis, low, high):
    odd = odd_place(axis)
    return jnp.where(odd, high, low), jnp.where(odd, low, high)


def by_side(axis, first, second):
    odd = odd_place(axis)
    return jnp.where(odd, second, first), jnp.where(odd, first, second)


def times_right(rows, high, low):
    top, rest = split(rows)
    left = jnp.concatenate([top, top, rest], axis=1)
    right = jnp.concatenate([high, low, high], axis=0)
    return jnp.dot(left, right, preferred_element_type=jnp.float32)


def times_left(high, low, columns):
    top, rest = split(columns)
    left = jnp.concatenate([high, low, high], axis=1)
    right = jnp.concatenate([top, top, rest], axis=0)
    return jnp.dot(left, right, preferred_element_type=jnp.float32)


def beside(left, right):
    return jnp.concatenate([left, right], axis=1)


def above(top, bottom):
    return jnp.concatenate([top, bottom], axis=0)


def touching(mid_row, mid_col, **_):
    return ~(mid_row & mid_col)


def early(cross_row, cross_col, **spot):
    return touching(**spot) & ~cross_row & ~cross_col


def choose(chosen, offsets, counts, tile, length, wanted, done_early=False):
    last = tile - length
    half = length // 2

    def look(slot, carry):
        found, seen = carry
        row = offsets[0, 0, 0, slot]
        col = offsets[0, 0, 1, slot]
        spot = dict(
            mid_row=(row >= half) & (row <= last - half),
            mid_col=(col >= half) & (col <= last - half),
            cross_row=(row < 0) | (row > last),
            cross_col=(col < 0) | (col > last),
        )
        taken = wanted(**spot)
        if done_early:
            soon = early(**spot)
            taken = taken & ~(soon & (seen < GROUP))
            seen = seen + jnp.where(soon, 1, 0)
        chosen[found] = slot
        return found + jnp.where(taken, 1, 0), seen

    found, _ = lax.fori_loop(0, counts[0, 0], look, (0, 0))
    filler = chosen[0]
    for k in range(GROUP):
        chosen[found + k] = filler
    return found


def add_gradients(frame, acc, probe_ref, amps, offsets, tables, chosen, found, own_frame=False, own_acc=False):
    length = probe_ref.shape[-1]
    half = length // 2
    lane = lanes((length, length))

    def place(slot, ref, own):
        col = offsets[0, 0, 1, slot] + length
        block = lax.div(col, length)
        row = offsets[0, 0, 0, slot]
        if own:
            block = block - 1
        else:
            row = row + half
        after = jnp.minimum(block + 1, ref.shape[1] - 1)
        return pl.ds(row, length), block, after, lax.rem(col, length)

    def exit_wave(slot):
        at, block, after, shift = place(slot, frame, own_frame)
        inside = lane >= shift
        window = [
            jnp.where(inside, frame[part, block, at, :], frame[part, after, at, :])
            for part in (0, 1)
        ]
        probe = (pltpu.roll(probe_ref[0], shift, 1), pltpu.roll(probe_ref[1], shift, 1))
        wave = (probe[0] * window[0] - probe[1] * window[1],
                probe[0] * window[1] + probe[1] * window[0])
        return probe, wave

    def shrink(real, imag, slot):
        ratio = amps[0, 0, slot] * lax.rsqrt(real * real + imag * imag + FLOOR) - 1.0
        return real * ratio, imag * ratio

    def put(slot, live, probe, back_r, back_i):
        at, block, after, shift = place(slot, acc, own_acc)
        grads = (probe[0] * back_r + probe[1] * back_i, probe[0] * back_i - probe[1] * back_r)
        bound = jnp.where(live, shift, length)
        inside = lane >= bound
        beyond = lane < jnp.where(live, shift, 0)
        for part in (0, 1):
            acc[part, block, at, :] += jnp.where(inside, grads[part], 0.0)
            acc[part, after, at, :] += jnp.where(beyond, grads[part], 0.0)

    def work(slots):
        probes, waves = zip(*[exit_wave(slot) for slot in slots])
        rows = jnp.concatenate([beside(*wave) for wave in waves], axis=0)
        mid = times_right(rows, tables[0], tables[1])
        yield None
        mids = [mid[k * length:(k + 1) * length] for k in range(len(slots))]
        columns = above(
            jnp.concatenate([m[:, :length] for m in mids], axis=1),
            jnp.concatenate([m[:, length:] for m in mids], axis=1),
        )
        far = times_left(tables[2], tables[3], columns)
        yield None
        changes = [
            shrink(far[:length, k * length:(k + 1) * length],
                   far[length:, k * length:(k + 1) * length], slot)
            for k, slot in enumerate(slots)
        ]
        columns = above(
            jnp.concatenate([c[0] for c in changes], axis=1),
            jnp.concatenate([c[1] for c in changes], axis=1),
        )
        mid = times_left(tables[0], tables[1], columns)
        yield None
        rows = jnp.concatenate(
            [
                beside(mid[:length, k * length:(k + 1) * length],
                       mid[length:, k * length:(k + 1) * length])
                for k in range(len(slots))
            ],
            axis=0,
        )
        back = times_right(rows, tables[2], tables[3])
        yield None
        yield [
            (probes[k], back[k * length:(k + 1) * length, :length],
             back[k * length:(k + 1) * length, length:])
            for k in range(len(slots))
        ]

    def step(index, carry):
        places = [index * GROUP + k for k in range(GROUP)]
        slots = [chosen[at] for at in places]
        chains = [work(slots[k:k + CHAIN]) for k in range(0, GROUP, CHAIN)]
        gradients = [None]
        while gradients[0] is None:
            gradients = [next(chain) for chain in chains]
        gradients = [gradient for chain in gradients for gradient in chain]
        for at, slot, gradient in zip(places, slots, gradients):
            put(slot, at < found, *gradient)
        return carry

    lax.fori_loop(0, (found + GROUP - 1) // GROUP, step, 0)


def start_pass(field, offsets_from, counts, tile_out, cols_a, cols_b, rows_a, rows_b, offsets, sems):
    _, nb, tile, length = tile_out.shape
    half = length // 2
    npos = offsets.shape[3]
    listed = pltpu.make_async_copy(offsets_from, offsets, sems.at[nb])
    listed.start()
    copies = [
        pltpu.make_async_copy(
            field.at[:, :, b * length:(b + 1) * length], tile_out.at[:, b], sems.at[b])
        for b in range(nb)
    ]
    for copy in copies:
        copy.start()
    listed.wait()
    spot = lanes((8, length))
    info = jnp.zeros((8, length), jnp.int32)
    down = (lax.axis_index("row") + 1) * tile
    across = (lax.axis_index("col") + 1) * tile
    for k in range(npos):
        live = k < counts[0, 0]
        info = jnp.where(spot == k, jnp.where(live, offsets[0, 0, 0, k] + down, 0), info)
        info = jnp.where(spot == npos + k, jnp.where(live, offsets[0, 0, 1, k] + across, 0), info)
    info = info.astype(jnp.float32)
    for end in (cols_a, cols_b, rows_a, rows_b):
        end[pl.ds(end.shape[0] - 8, 8), :] = info
    for copy in copies:
        copy.wait()
    low = lanes((tile, length)) < half
    to_left = jnp.where(low, tile_out[0, 0], swap(tile_out[1, 0], half))
    to_right = jnp.where(low, swap(tile_out[1, nb - 1], half), tile_out[0, nb - 1])
    cols_a[:tile], cols_b[:tile] = by_pairs("col", to_left, to_right)
    for part in (0, 1):
        for b in range(nb):
            at = pl.ds((part * nb + b) * half, half)
            rows_a[at, :], rows_b[at, :] = by_pairs(
                "row", tile_out[part, b, :half], tile_out[part, b, tile - half:])


def start_corners(cols_a, cols_b, after, corners_a, corners_b):
    length = cols_a.shape[1]
    half = length // 2
    tile = cols_a.shape[0] - 8
    low = lanes((tile, length)) < half
    left, right = by_side("col", cols_a[:tile], cols_b[:tile])
    for part in (0, 1):
        if part:
            left, right = swap(left, half), swap(right, half)
        value = jnp.where(low, right, left)
        at = pl.ds(part * half, half)
        corners_a[at, :], corners_b[at, :] = by_pairs("row", value[:half], value[tile - half:])
    first = lax.broadcasted_iota(jnp.int32, (8, length), 0) == 0
    info = jnp.where(first, cols_a[tile:], cols_b[tile:])
    corners_a[2 * half:] = info
    corners_b[2 * half:] = info


def fetch_pass(after, probe_from, amps_from, tables_from, probe, amps, tables, sems):
    copies = [
        pltpu.make_async_copy(source, target, sems.at[k])
        for k, (source, target) in enumerate(
            ((amps_from, amps), (tables_from, tables), (probe_from, probe)))
    ]
    for copy in copies:
        copy.start()
    for copy in copies:
        copy.wait()


def early_pass(offsets, counts, after, field, probe, amps, tables, acc, chosen):
    _, nb, tile, length = field.shape
    acc[...] = jnp.zeros_like(acc)
    found = jnp.minimum(choose(chosen, offsets, counts, tile, length, early), GROUP)
    add_gradients(field, acc, probe, amps, offsets, tables, chosen, found,
                  own_frame=True, own_acc=True)


def first_pass(offsets, counts, field, done, cols_a, cols_b, rows_a, rows_b, corners_a, corners_b,
               probe, amps, tables, frame, acc, tips_a, tips_b, sums_a, sums_b, edges_a, edges_b, chosen):
    _, nb, tile, length = field.shape
    half = length // 2
    rows = tile + 2 * half
    own = pl.ds(half, tile)
    left, right = by_side("col", cols_a[:tile], cols_b[:tile])
    top = pl.ds(0, half)
    bottom = pl.ds(half + tile, half)
    for part in (0, 1):
        for b in range(nb):
            frame[part, b + 1, own, :] = field[part, b]
            at = pl.ds((part * nb + b) * half, half)
            frame[part, b + 1, top, :], frame[part, b + 1, bottom, :] = by_side(
                "row", rows_a[at, :], rows_b[at, :])
        frame[part, 0, own, :] = swap(left, half) if part else left
        frame[part, nb + 1, own, :] = swap(right, half) if part else right
        at = pl.ds(part * half, half)
        ends = by_side("row", corners_a[at, :], corners_b[at, :])
        for block in (0, nb + 1):
            frame[part, block, top, :], frame[part, block, bottom, :] = ends
    empty = jnp.zeros((half, length), jnp.float32)
    for part in (0, 1):
        for b in range(nb + 2):
            acc[part, b, top, :] = empty
            acc[part, b, bottom, :] = empty
            acc[part, b, own, :] = (
                done[part, b - 1] if 0 < b <= nb else jnp.zeros((tile, length), jnp.float32))
    found = choose(
        chosen, offsets, counts, tile, length, touching, done_early=True)
    add_gradients(frame, acc, probe, amps, offsets, tables, chosen, found)
    low = lanes((rows, length)) < half
    for part in (0, 1):
        strip_a, strip_b = by_pairs(
            "col",
            jnp.where(low, acc[part, 1], acc[part, 0]),
            jnp.where(low, acc[part, nb + 1], acc[part, nb]),
        )
        for strip, tips, sums in ((strip_a, tips_a, sums_a), (strip_b, tips_b, sums_b)):
            tips[part, 0] = strip[:length]
            tips[part, 1] = strip[rows - length:]
            sums[part] = strip[length:rows - length]
    near = lanes((length, length)) < half
    for part in (0, 1):
        for b in range(nb - 1):
            ends = [
                acc[part, b + 2, at, :] if b < nb - 2
                else jnp.where(near, acc[part, nb, at, :], acc[part, 1, at, :])
                for at in (pl.ds(0, length), pl.ds(rows - length, length))
            ]
            edges_a[part, b], edges_b[part, b] = by_pairs("row", *ends)


def middle_corners(mine_a, mine_b, tips_a, tips_b, after, corners, *, odd_pairs):
    for part in (0, 1):
        up, down = [
            by_side("col", mine_a[part, k] + tips_a[part, k], mine_b[part, k] + tips_b[part, k])
            for k in (0, 1)
        ]
        for side in (0, 1):
            corners[part, side] = by_pairs("row", up[side], down[side])[0 if odd_pairs else 1]


def light_pass(mine, cols_a, cols_b, rows_a, rows_b, corners_a, corners_b, probe, after,
               inverse, light, power, places, listed, chosen, sem, *, npos):
    length = probe.shape[-1]
    half = length // 2
    blocks, rows, _ = inverse.shape
    nb = blocks - 2
    tile = nb * length
    my_row = lax.axis_index("row")
    my_col = lax.axis_index("col")
    sources = (mine, cols_a, cols_b, rows_a, rows_b, corners_a, corners_b)
    for k, source in enumerate(sources):
        given = source[source.shape[0] - 8:, :].astype(jnp.int32)
        col = pltpu.roll(given, length - npos, 1) - (my_col + 1) * tile + 2 * length
        row = given - (my_row + 1) * tile + half + length
        near = (given > 0) & (row > 0) & (row < rows + length)
        near = near & (col > length - half) & (col < 2 * length + tile + half)
        places[pl.ds(8 * k, 8), :] = jnp.where(near, row * 4 * tile + col, 0)
    copy = pltpu.make_async_copy(places, listed, sem)
    copy.start()
    for b in range(blocks):
        light[b + 1, pl.ds(length, rows), :] = jnp.zeros((rows, length), jnp.float32)
    power[...] = probe[0] * probe[0] + probe[1] * probe[1]
    lane = lanes((length, length))
    copy.wait()

    def look(index, found):
        line = jnp.where(index < len(sources), 8 * index, 8 * (index - 2) + 1)
        for slot in range(npos):
            place = listed[line, slot]
            chosen[found] = place
            found = found + jnp.where(place > 0, 1, 0)
        return found

    found = lax.fori_loop(0, len(sources) + 2, look, 0)

    def put(index, carry):
        place = chosen[index]
        start = lax.div(place, 4 * tile)
        col = lax.rem(place, 4 * tile)
        block = lax.div(col, length)
        shift = lax.rem(col, length)
        value = pltpu.roll(power[...], shift, 1)
        inside = lane >= shift
        light[block, pl.ds(start, length), :] += jnp.where(inside, value, 0.0)
        light[block + 1, pl.ds(start, length), :] += jnp.where(inside, 0.0, value)
        return carry

    lax.fori_loop(0, found, put, 0)
    spot = lax.broadcasted_iota(jnp.int32, (rows, length), 0)
    keep_from = jnp.where(my_row > 0, 0, half)
    keep_to = jnp.where(my_row < lax.axis_size("row") - 1, rows, rows - half)
    kept = (spot >= keep_from) & (spot < keep_to)
    for b in range(blocks):
        value = 1.0 / (light[b + 1, pl.ds(length, rows), :] + 1.0)
        keep = kept
        if b == 0:
            keep = keep & (my_col > 0)
        if b == nb + 1:
            keep = keep & (my_col < lax.axis_size("col") - 1)
        inverse[b] = jnp.where(keep, value, 0.0)


def update_pass(offsets, counts, frame, acc, inverse, tips_a, tips_b, sums_a, sums_b, probe, amps, tables,
                work, total, chosen):
    _, blocks, rows, length = frame.shape
    half = length // 2
    nb = blocks - 2
    work[...] = acc[...]
    found = choose(
        chosen, offsets, counts, nb * length, length,
        lambda mid_row, mid_col, **_: mid_col & mid_row)
    add_gradients(frame, work, probe, amps, offsets, tables, chosen, found)
    low = lanes((rows, length)) < half
    for part in (0, 1):
        left, right = by_side("col", *[
            above(above(tips[part, 0], sums[part]), tips[part, 1])
            for tips, sums in ((tips_a, sums_a), (tips_b, sums_b))
        ])
        for b in range(blocks):
            value = work[part, b]
            if b == 0:
                value = value + left
            if b == 1:
                value = value + jnp.where(low, left, 0.0)
            if b == nb:
                value = value + jnp.where(low, 0.0, right)
            if b == nb + 1:
                value = value + right
            work[part, b] = frame[part, b] + value * inverse[b]
    total[...] = jnp.zeros_like(total)
    found = choose(chosen, offsets, counts, nb * length, length, lambda mid_row, **_: mid_row)
    add_gradients(work, total, probe, amps, offsets, tables, chosen, found)


def second_pass(offsets, counts, work_from, total_from, inverse, edges_a, edges_b,
                corners_a, corners_b, probe, amps, tables,
                work, sums, tips_a, tips_b, cols_a, cols_b, rows_a, rows_b, total, chosen):
    _, blocks, rows, length = work.shape
    half = length // 2
    nb = blocks - 2
    tile = nb * length
    near = lanes((length, length)) < half
    middle = pl.ds(length, rows - 2 * length)
    for part in (0, 1):
        edges = [by_side("row", edges_a[part, b], edges_b[part, b]) for b in range(nb - 1)]
        corners = [by_side("row", corners_a[part, side], corners_b[part, side]) for side in (0, 1)]
        for k, at in enumerate((pl.ds(0, length), pl.ds(rows - length, length))):
            left, right, ends = corners[0][k], corners[1][k], edges[nb - 2][k]
            add = [left, jnp.where(near, left, ends)]
            add += [edges[b][k] for b in range(nb - 2)]
            add += [jnp.where(near, ends, right), right]
            for b in range(blocks):
                work[part, b, at, :] = work_from[part, b, at, :] + add[b] * inverse[b, at, :]
        for b in range(blocks):
            work[part, b, middle, :] = work_from[part, b, middle, :]
    total[...] = total_from[...]
    found = choose(
        chosen, offsets, counts, tile, length,
        lambda mid_row, cross_row, cross_col, **_: ~mid_row & (cross_row | cross_col))
    add_gradients(work, total, probe, amps, offsets, tables, chosen, found)
    low = lanes((rows, length)) < half
    strip_a, strip_b = by_pairs(
        "col",
        jnp.where(low, swap(total[1, 0], half), total[0, 0]),
        jnp.where(low, total[0, nb + 1], swap(total[1, nb + 1], half)),
    )
    for strip, tips, cols in ((strip_a, tips_a, cols_a), (strip_b, tips_b, cols_b)):
        tips[0] = strip[:half]
        tips[1] = strip[half + tile:]
        cols[...] = strip[half:half + tile]
    for part in (0, 1):
        for b in range(nb):
            sums[part, b] = total[part, b + 1, pl.ds(half, tile), :]
            rows_a[part * nb + b], rows_b[part * nb + b] = by_pairs(
                "row", total[part, b + 1, :half, :], total[part, b + 1, half + tile:, :])


def inner_pass(offsets, counts, work, probe, amps, tables, sums, chosen):
    _, nb, tile, length = sums.shape
    sums[...] = jnp.zeros_like(sums)
    found = choose(
        chosen, offsets, counts, tile, length,
        lambda mid_row, cross_row, cross_col, **_: ~mid_row & ~cross_row & ~cross_col)
    add_gradients(work, sums, probe, amps, offsets, tables, chosen, found, own_acc=True)


def end_rows(mine_a, mine_b, tips_a, tips_b, rows_a, rows_b):
    count = mine_a.shape[0]
    rows_a[:count] = mine_a[...]
    rows_b[:count] = mine_b[...]
    up, down = [by_side("col", tips_a[k], tips_b[k]) for k in (0, 1)]
    for side in (0, 1):
        rows_a[count + side], rows_b[count + side] = by_pairs("row", up[side], down[side])


def last_pass(work, sums, inner, inverse, cols_a, cols_b, rows_a, rows_b, out, result, sems):
    _, nb, tile, length = sums.shape
    half = length // 2
    low = lanes((tile, length)) < half
    own = pl.ds(half, tile)
    gap = jnp.zeros((tile - 2 * half, length), jnp.float32)
    sides = []
    for side, value in enumerate(by_side("col", cols_a[...], cols_b[...])):
        up, down = by_side("row", rows_a[2 * nb + side], rows_b[2 * nb + side])
        sides.append(value + above(above(up, gap), down))
    left, right = sides
    copies = []
    for part in (0, 1):
        if part:
            left, right = swap(left, half), swap(right, half)
        for b in range(nb):
            up, down = by_side("row", rows_a[part * nb + b], rows_b[part * nb + b])
            value = sums[part, b] + inner[part, b] + above(above(up, gap), down)
            if b == 0:
                value = value + jnp.where(low, left, 0.0)
            if b == nb - 1:
                value = value + jnp.where(low, 0.0, right)
            result[part, b] = work[part, b + 1, own, :] + value * inverse[b + 1, own, :]
            copy = pltpu.make_async_copy(
                result.at[part, b], out.at[part, :, b * length:(b + 1) * length],
                sems.at[part * nb + b])
            copy.start()
            copies.append(copy)
    for copy in copies:
        copy.wait()


def whole(memory_space=pltpu.VMEM):
    return pl.BlockSpec(memory_space=memory_space)


def call(body, shapes, places, scratch=(), cost=None):
    return pl.pallas_call(
        body,
        out_shape=[jax.ShapeDtypeStruct(shape, jnp.float32) for shape in shapes],
        in_specs=[whole({"s": pltpu.SMEM, "v": pltpu.VMEM, "a": pl.ANY, "h": pltpu.HBM}[p]) for p in places],
        out_specs=[whole()] * len(shapes),
        scratch_shapes=list(scratch),
        compiler_params=pltpu.CompilerParams(vmem_limit_bytes=VMEM_BYTES),
        cost_estimate=cost,
    )


def swap_pairs(first, second, axis):
    count = lax.axis_size(axis)
    got = []
    for value, start in ((first, 1), (second, 0)):
        pairs = [(i, i + 1) for i in range(start, count - 1, 2)]
        got.append(lax.ppermute(value, axis, pairs + [(b, a) for a, b in pairs]))
    return got


def shards(object_field, probe, amplitudes, offsets, counts):
    length = probe.shape[-1]
    half = length // 2
    tile = object_field.shape[1]
    npos = offsets.shape[2]
    nb = tile // length
    blocks = nb + 2
    rows = tile + 2 * half
    tables = jnp.asarray(dft_tables(length))
    offsets = jnp.swapaxes(offsets, 2, 3)

    def cost(positions):
        steps = 4 * 3 * 2 * length * (2 * length) ** 2
        return pl.CostEstimate(
            flops=positions * steps, bytes_accessed=8_000_000,
            transcendentals=positions * length * length)

    memory = pltpu.VMEM
    chosen = pltpu.SMEM((npos + GROUP,), jnp.int32)
    strip = (tile + 8, length)
    edge = (2 * nb * half + 8, length)
    def kept(array):
        return pltpu.with_memory_space_constraint(array, pltpu.HBM)

    field, cols_a, cols_b, rows_a, rows_b = call(
        start_pass, [(2, nb, tile, length), strip, strip, edge, edge], "hhs",
        [pltpu.SMEM((1, 1, 2, npos), jnp.int32), pltpu.SemaphoreType.DMA((nb + 1,))],
    )(kept(object_field), kept(offsets), counts)
    mine = cols_a
    probe, amplitudes, tables = pl.pallas_call(
        fetch_pass,
        out_shape=[
            jax.ShapeDtypeStruct(array.shape, array.dtype) for array in (probe, amplitudes, tables)],
        in_specs=[whole(pl.ANY)] + [whole(pltpu.HBM)] * 3,
        out_specs=[whole()] * 3,
        scratch_shapes=[pltpu.SemaphoreType.DMA((3,))],
        compiler_params=pltpu.CompilerParams(vmem_limit_bytes=VMEM_BYTES),
        cost_estimate=cost(1),
    )(cols_a, kept(probe), kept(amplitudes), kept(tables))
    cols_a, cols_b = swap_pairs(cols_a, cols_b, "col")
    rows_a, rows_b = swap_pairs(rows_a, rows_b, "row")
    corner = (2 * half + 8, length)
    corners_a, corners_b = call(start_corners, [corner, corner], "vva")(cols_a, cols_b, probe)
    (done,) = call(
        early_pass, [(2, nb, tile, length)], "ssavvvv", [chosen], cost(GROUP),
    )(offsets, counts, corners_b, field, probe, amplitudes, tables)
    corners_a, corners_b = swap_pairs(corners_a, corners_b, "row")

    full = (2, blocks, rows, length)
    strip = (2, rows, length)
    edge = (2, nb - 1, length, length)
    tip = (2, 2, length, length)
    strip = (2, rows - 2 * length, length)
    frame, acc, tips_a, tips_b, sums_a, sums_b, edges_a, edges_b = call(
        first_pass, [full, full, tip, tip, strip, strip, edge, edge], "ss" + 11 * "v", [chosen],
    )(offsets, counts, field, done, cols_a, cols_b, rows_a, rows_b, corners_a, corners_b,
      probe, amplitudes, tables)
    info = (mine, cols_a, cols_b, rows_a, rows_b, corners_a, corners_b)
    mine_a, mine_b = tips_a, tips_b
    tips_a, tips_b = swap_pairs(tips_a, tips_b, "col")
    edges_a, edges_b = swap_pairs(edges_a, edges_b, "row")
    sums_a, sums_b = swap_pairs(sums_a, sums_b, "col")
    (inverse,) = call(
        functools.partial(light_pass, npos=npos), [(blocks, rows, length)], 8 * "v" + "a",
        [memory((blocks + 2, rows + 2 * length, length), jnp.float32),
         memory((length, length), jnp.float32), memory((7 * 8, length), jnp.int32),
         pltpu.SMEM((7 * 8, length), jnp.int32), pltpu.SMEM((9 * npos + 1,), jnp.int32),
         pltpu.SemaphoreType.DMA],
        cost(npos // 2),
    )(*info, probe, acc)
    corners_a, corners_b = [
        call(functools.partial(middle_corners, odd_pairs=odd_pairs), [tip], "vvvva")(
            mine_a, mine_b, tips_a, tips_b, after)[0]
        for odd_pairs, after in ((True, acc), (False, inverse))
    ]
    corners_a, corners_b = swap_pairs(corners_a, corners_b, "row")

    work, total = call(update_pass, [full, full], "ss" + 10 * "v", [chosen], cost(npos // 2))(
        offsets, counts, frame, acc, inverse, tips_a, tips_b, sums_a, sums_b,
        probe, amplitudes, tables)
    own = (2, nb, tile, length)
    edge = (2 * nb, half, length)
    tip = (2, half, length)
    strip = (tile, length)
    work, sums, tips_a, tips_b, cols_a, cols_b, mine_a, mine_b = call(
        second_pass, [full, own, tip, tip, strip, strip, edge, edge], "ss" + 10 * "v",
        [memory(full, jnp.float32), chosen], cost(npos // 2),
    )(offsets, counts, work, total, inverse, edges_a, edges_b, corners_a, corners_b,
      probe, amplitudes, tables)
    tips_a, tips_b = swap_pairs(tips_a, tips_b, "col")
    cols_a, cols_b = swap_pairs(cols_a, cols_b, "col")
    edge = (2 * nb + 2, half, length)
    rows_a, rows_b = call(end_rows, [edge, edge], "vvvv")(mine_a, mine_b, tips_a, tips_b)
    rows_a, rows_b = swap_pairs(rows_a, rows_b, "row")
    (inner,) = call(inner_pass, [own], "ss" + 4 * "v", [chosen], cost(npos // 4))(
        offsets, counts, work, probe, amplitudes, tables)
    out = pl.pallas_call(
        last_pass,
        out_shape=jax.ShapeDtypeStruct((2, tile, tile), jnp.float32),
        in_specs=[whole()] * 8,
        out_specs=whole(pl.ANY),
        scratch_shapes=[memory(own, jnp.float32), pltpu.SemaphoreType.DMA((2 * nb,))],
        compiler_params=pltpu.CompilerParams(vmem_limit_bytes=VMEM_BYTES),
    )(work, sums, inner, inverse, cols_a, cols_b, rows_a, rows_b)
    return out


def solution(mesh):
    placed = (
        P(None, "row", "col"),
        P(),
        P("row", "col", None, None, None),
        P("row", "col", None, None),
        P("row", "col"),
    )
    return jax.shard_map(
        shards, mesh=mesh, in_specs=placed, out_specs=P(None, "row", "col"), check_vma=False
    )
```

```python
import functools
import math

import jax
import jax.numpy as jnp
import numpy as np
from jax import lax
from jax.experimental import pallas as pl
from jax.experimental.pallas import tpu as pltpu
from jax.sharding import PartitionSpec as P

ITERS = 2
FLOOR = 0.25
VMEM_BYTES = 16 * 1024 * 1024
GROUP = 4
CHAIN = 2


def split(value):
    high = value.astype(jnp.bfloat16)
    low = (value - high.astype(jnp.float32)).astype(jnp.bfloat16)
    return high, low


def dft_tables(length):
    index = np.arange(length)
    angle = (index[:, None] * index[None, :] % length) * (2.0 * math.pi / length)
    cosine = np.cos(angle) / math.sqrt(length)
    sine = np.sin(angle) / math.sqrt(length)
    ahead = np.block([[cosine, -sine], [sine, cosine]])
    parts = []
    for table in (ahead, ahead.T):
        high = table.astype(jnp.bfloat16)
        low = (table - high.astype(np.float64)).astype(jnp.bfloat16)
        parts += [high, low]
    return np.stack(parts)


def lanes(shape):
    return lax.broadcasted_iota(jnp.int32, shape, len(shape) - 1)


def swap(value, half):
    return pltpu.roll(value, half, value.ndim - 1)


def odd_place(axis):
    return lax.axis_index(axis) % 2 == 1


def by_pairs(axis, low, high):
    odd = odd_place(axis)
    return jnp.where(odd, high, low), jnp.where(odd, low, high)


def by_side(axis, first, second):
    odd = odd_place(axis)
    return jnp.where(odd, second, first), jnp.where(odd, first, second)


def times_right(rows, high, low):
    top, rest = split(rows)
    left = jnp.concatenate([top, top, rest], axis=1)
    right = jnp.concatenate([high, low, high], axis=0)
    return jnp.dot(left, right, preferred_element_type=jnp.float32)


def times_left(high, low, columns):
    top, rest = split(columns)
    left = jnp.concatenate([high, low, high], axis=1)
    right = jnp.concatenate([top, top, rest], axis=0)
    return jnp.dot(left, right, preferred_element_type=jnp.float32)


def beside(left, right):
    return jnp.concatenate([left, right], axis=1)


def above(top, bottom):
    return jnp.concatenate([top, bottom], axis=0)


def touching(mid_row, mid_col, **_):
    return ~(mid_row & mid_col)


def early(cross_row, cross_col, **spot):
    return touching(**spot) & ~cross_row & ~cross_col


def choose(chosen, offsets, counts, tile, length, wanted, done_early=False):
    last = tile - length
    half = length // 2

    def look(slot, carry):
        found, seen = carry
        row = offsets[0, 0, 0, slot]
        col = offsets[0, 0, 1, slot]
        spot = dict(
            mid_row=(row >= half) & (row <= last - half),
            mid_col=(col >= half) & (col <= last - half),
            cross_row=(row < 0) | (row > last),
            cross_col=(col < 0) | (col > last),
        )
        taken = wanted(**spot)
        if done_early:
            soon = early(**spot)
            taken = taken & ~(soon & (seen < GROUP))
            seen = seen + jnp.where(soon, 1, 0)
        chosen[found] = slot
        return found + jnp.where(taken, 1, 0), seen

    found, _ = lax.fori_loop(0, counts[0, 0], look, (0, 0))
    filler = chosen[0]
    for k in range(GROUP):
        chosen[found + k] = filler
    return found


def add_gradients(frame, acc, probe_ref, amps, offsets, tables, chosen, found, own_frame=False, own_acc=False):
    length = probe_ref.shape[-1]
    half = length // 2
    lane = lanes((length, length))

    def place(slot, ref, own):
        col = offsets[0, 0, 1, slot] + length
        block = lax.div(col, length)
        row = offsets[0, 0, 0, slot]
        if own:
            block = block - 1
        else:
            row = row + half
        after = jnp.minimum(block + 1, ref.shape[1] - 1)
        return pl.ds(row, length), block, after, lax.rem(col, length)

    def exit_wave(slot):
        at, block, after, shift = place(slot, frame, own_frame)
        inside = lane >= shift
        window = [
            jnp.where(inside, frame[part, block, at, :], frame[part, after, at, :])
            for part in (0, 1)
        ]
        probe = (pltpu.roll(probe_ref[0], shift, 1), pltpu.roll(probe_ref[1], shift, 1))
        wave = (probe[0] * window[0] - probe[1] * window[1],
                probe[0] * window[1] + probe[1] * window[0])
        return probe, wave

    def shrink(real, imag, slot):
        ratio = amps[0, 0, slot] * lax.rsqrt(real * real + imag * imag + FLOOR) - 1.0
        return real * ratio, imag * ratio

    def put(slot, live, probe, back_r, back_i):
        at, block, after, shift = place(slot, acc, own_acc)
        grads = (probe[0] * back_r + probe[1] * back_i, probe[0] * back_i - probe[1] * back_r)
        bound = jnp.where(live, shift, length)
        inside = lane >= bound
        beyond = lane < jnp.where(live, shift, 0)
        for part in (0, 1):
            acc[part, block, at, :] += jnp.where(inside, grads[part], 0.0)
            acc[part, after, at, :] += jnp.where(beyond, grads[part], 0.0)

    def work(slots):
        probes, waves = zip(*[exit_wave(slot) for slot in slots])
        rows = jnp.concatenate([beside(*wave) for wave in waves], axis=0)
        mid = times_right(rows, tables[0], tables[1])
        yield None
        mids = [mid[k * length:(k + 1) * length] for k in range(len(slots))]
        columns = above(
            jnp.concatenate([m[:, :length] for m in mids], axis=1),
            jnp.concatenate([m[:, length:] for m in mids], axis=1),
        )
        far = times_left(tables[2], tables[3], columns)
        yield None
        changes = [
            shrink(far[:length, k * length:(k + 1) * length],
                   far[length:, k * length:(k + 1) * length], slot)
            for k, slot in enumerate(slots)
        ]
        columns = above(
            jnp.concatenate([c[0] for c in changes], axis=1),
            jnp.concatenate([c[1] for c in changes], axis=1),
        )
        mid = times_left(tables[0], tables[1], columns)
        yield None
        rows = jnp.concatenate(
            [
                beside(mid[:length, k * length:(k + 1) * length],
                       mid[length:, k * length:(k + 1) * length])
                for k in range(len(slots))
            ],
            axis=0,
        )
        back = times_right(rows, tables[2], tables[3])
        yield None
        yield [
            (probes[k], back[k * length:(k + 1) * length, :length],
             back[k * length:(k + 1) * length, length:])
            for k in range(len(slots))
        ]

    def step(index, carry):
        places = [index * GROUP + k for k in range(GROUP)]
        slots = [chosen[at] for at in places]
        chains = [work(slots[k:k + CHAIN]) for k in range(0, GROUP, CHAIN)]
        gradients = [None]
        while gradients[0] is None:
            gradients = [next(chain) for chain in chains]
        gradients = [gradient for chain in gradients for gradient in chain]
        for at, slot, gradient in zip(places, slots, gradients):
            put(slot, at < found, *gradient)
        return carry

    lax.fori_loop(0, (found + GROUP - 1) // GROUP, step, 0)


def start_pass(field, offsets_from, counts, tile_out, cols_a, cols_b, rows_a, rows_b, offsets, sems):
    _, nb, tile, length = tile_out.shape
    half = length // 2
    npos = offsets.shape[3]
    listed = pltpu.make_async_copy(offsets_from, offsets, sems.at[nb])
    listed.start()
    copies = [
        pltpu.make_async_copy(
            field.at[:, :, b * length:(b + 1) * length], tile_out.at[:, b], sems.at[b])
        for b in range(nb)
    ]
    for copy in copies:
        copy.start()
    listed.wait()
    spot = lanes((8, length))
    info = jnp.zeros((8, length), jnp.int32)
    down = (lax.axis_index("row") + 1) * tile
    across = (lax.axis_index("col") + 1) * tile
    for k in range(npos):
        live = k < counts[0, 0]
        info = jnp.where(spot == k, jnp.where(live, offsets[0, 0, 0, k] + down, 0), info)
        info = jnp.where(spot == npos + k, jnp.where(live, offsets[0, 0, 1, k] + across, 0), info)
    info = info.astype(jnp.float32)
    for end in (cols_a, cols_b, rows_a, rows_b):
        end[pl.ds(end.shape[0] - 8, 8), :] = info
    for copy in copies:
        copy.wait()
    low = lanes((tile, length)) < half
    to_left = jnp.where(low, tile_out[0, 0], swap(tile_out[1, 0], half))
    to_right = jnp.where(low, swap(tile_out[1, nb - 1], half), tile_out[0, nb - 1])
    cols_a[:tile], cols_b[:tile] = by_pairs("col", to_left, to_right)
    for part in (0, 1):
        for b in range(nb):
            at = pl.ds((part * nb + b) * half, half)
            rows_a[at, :], rows_b[at, :] = by_pairs(
                "row", tile_out[part, b, :half], tile_out[part, b, tile - half:])


def start_corners(cols_a, cols_b, after, corners_a, corners_b):
    length = cols_a.shape[1]
    half = length // 2
    tile = cols_a.shape[0] - 8
    low = lanes((tile, length)) < half
    left, right = by_side("col", cols_a[:tile], cols_b[:tile])
    for part in (0, 1):
        if part:
            left, right = swap(left, half), swap(right, half)
        value = jnp.where(low, right, left)
        at = pl.ds(part * half, half)
        corners_a[at, :], corners_b[at, :] = by_pairs("row", value[:half], value[tile - half:])
    first = lax.broadcasted_iota(jnp.int32, (8, length), 0) == 0
    info = jnp.where(first, cols_a[tile:], cols_b[tile:])
    corners_a[2 * half:] = info
    corners_b[2 * half:] = info


def fetch_pass(after, probe_from, amps_from, tables_from, probe, amps, tables, sems):
    copies = [
        pltpu.make_async_copy(source, target, sems.at[k])
        for k, (source, target) in enumerate(
            ((amps_from, amps), (tables_from, tables), (probe_from, probe)))
    ]
    for copy in copies:
        copy.start()
    for copy in copies:
        copy.wait()


def early_pass(offsets, counts, after, field, probe, amps, tables, acc, chosen):
    _, nb, tile, length = field.shape
    acc[...] = jnp.zeros_like(acc)
    found = jnp.minimum(choose(chosen, offsets, counts, tile, length, early), GROUP)
    add_gradients(field, acc, probe, amps, offsets, tables, chosen, found,
                  own_frame=True, own_acc=True)


def first_pass(offsets, counts, field, done, cols_a, cols_b, rows_a, rows_b, corners_a, corners_b,
               probe, amps, tables, frame, acc, tips_a, tips_b, sums_a, sums_b, edges_a, edges_b, chosen):
    _, nb, tile, length = field.shape
    half = length // 2
    rows = tile + 2 * half
    own = pl.ds(half, tile)
    left, right = by_side("col", cols_a[:tile], cols_b[:tile])
    top = pl.ds(0, half)
    bottom = pl.ds(half + tile, half)
    for part in (0, 1):
        for b in range(nb):
            frame[part, b + 1, own, :] = field[part, b]
            at = pl.ds((part * nb + b) * half, half)
            frame[part, b + 1, top, :], frame[part, b + 1, bottom, :] = by_side(
                "row", rows_a[at, :], rows_b[at, :])
        frame[part, 0, own, :] = swap(left, half) if part else left
        frame[part, nb + 1, own, :] = swap(right, half) if part else right
        at = pl.ds(part * half, half)
        ends = by_side("row", corners_a[at, :], corners_b[at, :])
        for block in (0, nb + 1):
            frame[part, block, top, :], frame[part, block, bottom, :] = ends
    empty = jnp.zeros((half, length), jnp.float32)
    for part in (0, 1):
        for b in range(nb + 2):
            acc[part, b, top, :] = empty
            acc[part, b, bottom, :] = empty
            acc[part, b, own, :] = (
                done[part, b - 1] if 0 < b <= nb else jnp.zeros((tile, length), jnp.float32))
    found = choose(
        chosen, offsets, counts, tile, length, touching, done_early=True)
    add_gradients(frame, acc, probe, amps, offsets, tables, chosen, found)
    low = lanes((rows, length)) < half
    for part in (0, 1):
        strip_a, strip_b = by_pairs(
            "col",
            jnp.where(low, acc[part, 1], acc[part, 0]),
            jnp.where(low, acc[part, nb + 1], acc[part, nb]),
        )
        for strip, tips, sums in ((strip_a, tips_a, sums_a), (strip_b, tips_b, sums_b)):
            tips[part, 0] = strip[:length]
            tips[part, 1] = strip[rows - length:]
            sums[part] = strip[length:rows - length]
    near = lanes((length, length)) < half
    for part in (0, 1):
        for b in range(nb - 1):
            ends = [
                acc[part, b + 2, at, :] if b < nb - 2
                else jnp.where(near, acc[part, nb, at, :], acc[part, 1, at, :])
                for at in (pl.ds(0, length), pl.ds(rows - length, length))
            ]
            edges_a[part, b], edges_b[part, b] = by_pairs("row", *ends)


def middle_corners(mine_a, mine_b, tips_a, tips_b, after, corners, *, odd_pairs):
    for part in (0, 1):
        up, down = [
            by_side("col", mine_a[part, k] + tips_a[part, k], mine_b[part, k] + tips_b[part, k])
            for k in (0, 1)
        ]
        for side in (0, 1):
            corners[part, side] = by_pairs("row", up[side], down[side])[0 if odd_pairs else 1]


def light_pass(mine, cols_a, cols_b, rows_a, rows_b, corners_a, corners_b, probe, after,
               inverse, light, power, places, listed, chosen, sem, *, npos):
    length = probe.shape[-1]
    half = length // 2
    blocks, rows, _ = inverse.shape
    nb = blocks - 2
    tile = nb * length
    my_row = lax.axis_index("row")
    my_col = lax.axis_index("col")
    sources = (mine, cols_a, cols_b, rows_a, rows_b, corners_a, corners_b)
    for k, source in enumerate(sources):
        given = source[source.shape[0] - 8:, :].astype(jnp.int32)
        col = pltpu.roll(given, length - npos, 1) - (my_col + 1) * tile + 2 * length
        row = given - (my_row + 1) * tile + half + length
        near = (given > 0) & (row > 0) & (row < rows + length)
        near = near & (col > length - half) & (col < 2 * length + tile + half)
        places[pl.ds(8 * k, 8), :] = jnp.where(near, row * 4 * tile + col, 0)
    copy = pltpu.make_async_copy(places, listed, sem)
    copy.start()
    for b in range(blocks):
        light[b + 1, pl.ds(length, rows), :] = jnp.zeros((rows, length), jnp.float32)
    power[...] = probe[0] * probe[0] + probe[1] * probe[1]
    lane = lanes((length, length))
    copy.wait()

    def look(index, found):
        line = jnp.where(index < len(sources), 8 * index, 8 * (index - 2) + 1)
        for slot in range(npos):
            place = listed[line, slot]
            chosen[found] = place
            found = found + jnp.where(place > 0, 1, 0)
        return found

    found = lax.fori_loop(0, len(sources) + 2, look, 0)

    def put(index, carry):
        place = chosen[index]
        start = lax.div(place, 4 * tile)
        col = lax.rem(place, 4 * tile)
        block = lax.div(col, length)
        shift = lax.rem(col, length)
        value = pltpu.roll(power[...], shift, 1)
        inside = lane >= shift
        light[block, pl.ds(start, length), :] += jnp.where(inside, value, 0.0)
        light[block + 1, pl.ds(start, length), :] += jnp.where(inside, 0.0, value)
        return carry

    lax.fori_loop(0, found, put, 0)
    spot = lax.broadcasted_iota(jnp.int32, (rows, length), 0)
    keep_from = jnp.where(my_row > 0, 0, half)
    keep_to = jnp.where(my_row < lax.axis_size("row") - 1, rows, rows - half)
    kept = (spot >= keep_from) & (spot < keep_to)
    for b in range(blocks):
        value = 1.0 / (light[b + 1, pl.ds(length, rows), :] + 1.0)
        keep = kept
        if b == 0:
            keep = keep & (my_col > 0)
        if b == nb + 1:
            keep = keep & (my_col < lax.axis_size("col") - 1)
        inverse[b] = jnp.where(keep, value, 0.0)


def update_pass(offsets, counts, frame, acc, inverse, tips_a, tips_b, sums_a, sums_b, probe, amps, tables,
                work, total, chosen):
    _, blocks, rows, length = frame.shape
    half = length // 2
    nb = blocks - 2
    work[...] = acc[...]
    found = choose(
        chosen, offsets, counts, nb * length, length,
        lambda mid_row, mid_col, **_: mid_col & mid_row)
    add_gradients(frame, work, probe, amps, offsets, tables, chosen, found)
    low = lanes((rows, length)) < half
    for part in (0, 1):
        left, right = by_side("col", *[
            above(above(tips[part, 0], sums[part]), tips[part, 1])
            for tips, sums in ((tips_a, sums_a), (tips_b, sums_b))
        ])
        for b in range(blocks):
            value = work[part, b]
            if b == 0:
                value = value + left
            if b == 1:
                value = value + jnp.where(low, left, 0.0)
            if b == nb:
                value = value + jnp.where(low, 0.0, right)
            if b == nb + 1:
                value = value + right
            work[part, b] = frame[part, b] + value * inverse[b]
    total[...] = jnp.zeros_like(total)
    found = choose(chosen, offsets, counts, nb * length, length, lambda mid_row, **_: mid_row)
    add_gradients(work, total, probe, amps, offsets, tables, chosen, found)


def second_pass(offsets, counts, work_from, total_from, inverse, edges_a, edges_b,
                corners_a, corners_b, probe, amps, tables,
                work, sums, tips_a, tips_b, cols_a, cols_b, rows_a, rows_b, total, chosen):
    _, blocks, rows, length = work.shape
    half = length // 2
    nb = blocks - 2
    tile = nb * length
    near = lanes((length, length)) < half
    middle = pl.ds(length, rows - 2 * length)
    for part in (0, 1):
        edges = [by_side("row", edges_a[part, b], edges_b[part, b]) for b in range(nb - 1)]
        corners = [by_side("row", corners_a[part, side], corners_b[part, side]) for side in (0, 1)]
        for k, at in enumerate((pl.ds(0, length), pl.ds(rows - length, length))):
            left, right, ends = corners[0][k], corners[1][k], edges[nb - 2][k]
            add = [left, jnp.where(near, left, ends)]
            add += [edges[b][k] for b in range(nb - 2)]
            add += [jnp.where(near, ends, right), right]
            for b in range(blocks):
                work[part, b, at, :] = work_from[part, b, at, :] + add[b] * inverse[b, at, :]
        for b in range(blocks):
            work[part, b, middle, :] = work_from[part, b, middle, :]
    total[...] = total_from[...]
    found = choose(
        chosen, offsets, counts, tile, length,
        lambda mid_row, cross_row, cross_col, **_: ~mid_row & (cross_row | cross_col))
    add_gradients(work, total, probe, amps, offsets, tables, chosen, found)
    low = lanes((rows, length)) < half
    strip_a, strip_b = by_pairs(
        "col",
        jnp.where(low, swap(total[1, 0], half), total[0, 0]),
        jnp.where(low, total[0, nb + 1], swap(total[1, nb + 1], half)),
    )
    for strip, tips, cols in ((strip_a, tips_a, cols_a), (strip_b, tips_b, cols_b)):
        tips[0] = strip[:half]
        tips[1] = strip[half + tile:]
        cols[...] = strip
    for part in (0, 1):
        for b in range(nb):
            sums[part, b] = total[part, b + 1, pl.ds(half, tile), :]
            rows_a[part * nb + b], rows_b[part * nb + b] = by_pairs(
                "row", total[part, b + 1, :half, :], total[part, b + 1, half + tile:, :])


def inner_pass(offsets, counts, work, probe, amps, tables, sums, chosen):
    _, nb, tile, length = sums.shape
    sums[...] = jnp.zeros_like(sums)
    found = choose(
        chosen, offsets, counts, tile, length,
        lambda mid_row, cross_row, cross_col, **_: ~mid_row & ~cross_row & ~cross_col)
    add_gradients(work, sums, probe, amps, offsets, tables, chosen, found, own_acc=True)


def end_rows(mine_a, mine_b, tips_a, tips_b, rows_a, rows_b):
    count = mine_a.shape[0]
    rows_a[:count] = mine_a[...]
    rows_b[:count] = mine_b[...]
    up, down = [by_side("col", tips_a[k], tips_b[k]) for k in (0, 1)]
    for side in (0, 1):
        rows_a[count + side], rows_b[count + side] = by_pairs("row", up[side], down[side])


def last_pass(work, sums, inner, inverse, cols_a, cols_b, rows_a, rows_b, out, result, sems):
    _, nb, tile, length = sums.shape
    half = length // 2
    low = lanes((tile, length)) < half
    own = pl.ds(half, tile)
    gap = jnp.zeros((tile - 2 * half, length), jnp.float32)
    sides = []
    for side, value in enumerate(by_side("col", cols_a[own, :], cols_b[own, :])):
        up, down = by_side("row", rows_a[2 * nb + side], rows_b[2 * nb + side])
        sides.append(value + above(above(up, gap), down))
    left, right = sides
    copies = []
    for part in (0, 1):
        if part:
            left, right = swap(left, half), swap(right, half)
        for b in range(nb):
            up, down = by_side("row", rows_a[part * nb + b], rows_b[part * nb + b])
            value = sums[part, b] + inner[part, b] + above(above(up, gap), down)
            if b == 0:
                value = value + jnp.where(low, left, 0.0)
            if b == nb - 1:
                value = value + jnp.where(low, 0.0, right)
            result[part, b] = work[part, b + 1, own, :] + value * inverse[b + 1, own, :]
            copy = pltpu.make_async_copy(
                result.at[part, b], out.at[part, :, b * length:(b + 1) * length],
                sems.at[part * nb + b])
            copy.start()
            copies.append(copy)
    for copy in copies:
        copy.wait()


def whole(memory_space=pltpu.VMEM):
    return pl.BlockSpec(memory_space=memory_space)


def call(body, shapes, places, scratch=(), cost=None):
    return pl.pallas_call(
        body,
        out_shape=[jax.ShapeDtypeStruct(shape, jnp.float32) for shape in shapes],
        in_specs=[whole({"s": pltpu.SMEM, "v": pltpu.VMEM, "a": pl.ANY, "h": pltpu.HBM}[p]) for p in places],
        out_specs=[whole()] * len(shapes),
        scratch_shapes=list(scratch),
        compiler_params=pltpu.CompilerParams(vmem_limit_bytes=VMEM_BYTES),
        cost_estimate=cost,
    )


def swap_pairs(first, second, axis):
    count = lax.axis_size(axis)
    got = []
    for value, start in ((first, 1), (second, 0)):
        pairs = [(i, i + 1) for i in range(start, count - 1, 2)]
        got.append(lax.ppermute(value, axis, pairs + [(b, a) for a, b in pairs]))
    return got


def shards(object_field, probe, amplitudes, offsets, counts):
    length = probe.shape[-1]
    half = length // 2
    tile = object_field.shape[1]
    npos = offsets.shape[2]
    nb = tile // length
    blocks = nb + 2
    rows = tile + 2 * half
    tables = jnp.asarray(dft_tables(length))
    offsets = jnp.swapaxes(offsets, 2, 3)

    def cost(positions):
        steps = 4 * 3 * 2 * length * (2 * length) ** 2
        return pl.CostEstimate(
            flops=positions * steps, bytes_accessed=8_000_000,
            transcendentals=positions * length * length)

    memory = pltpu.VMEM
    chosen = pltpu.SMEM((npos + GROUP,), jnp.int32)
    strip = (tile + 8, length)
    edge = (2 * nb * half + 8, length)
    def kept(array):
        return pltpu.with_memory_space_constraint(array, pltpu.HBM)

    field, cols_a, cols_b, rows_a, rows_b = call(
        start_pass, [(2, nb, tile, length), strip, strip, edge, edge], "hhs",
        [pltpu.SMEM((1, 1, 2, npos), jnp.int32), pltpu.SemaphoreType.DMA((nb + 1,))],
    )(kept(object_field), kept(offsets), counts)
    mine = cols_a
    probe, amplitudes, tables = pl.pallas_call(
        fetch_pass,
        out_shape=[
            jax.ShapeDtypeStruct(array.shape, array.dtype) for array in (probe, amplitudes, tables)],
        in_specs=[whole(pl.ANY)] + [whole(pltpu.HBM)] * 3,
        out_specs=[whole()] * 3,
        scratch_shapes=[pltpu.SemaphoreType.DMA((3,))],
        compiler_params=pltpu.CompilerParams(vmem_limit_bytes=VMEM_BYTES),
        cost_estimate=cost(1),
    )(cols_a, kept(probe), kept(amplitudes), kept(tables))
    cols_a, cols_b = swap_pairs(cols_a, cols_b, "col")
    rows_a, rows_b = swap_pairs(rows_a, rows_b, "row")
    corner = (2 * half + 8, length)
    corners_a, corners_b = call(start_corners, [corner, corner], "vva")(cols_a, cols_b, probe)
    (done,) = call(
        early_pass, [(2, nb, tile, length)], "ssavvvv", [chosen], cost(GROUP),
    )(offsets, counts, corners_b, field, probe, amplitudes, tables)
    corners_a, corners_b = swap_pairs(corners_a, corners_b, "row")

    full = (2, blocks, rows, length)
    strip = (2, rows, length)
    edge = (2, nb - 1, length, length)
    tip = (2, 2, length, length)
    strip = (2, rows - 2 * length, length)
    frame, acc, tips_a, tips_b, sums_a, sums_b, edges_a, edges_b = call(
        first_pass, [full, full, tip, tip, strip, strip, edge, edge], "ss" + 11 * "v", [chosen],
    )(offsets, counts, field, done, cols_a, cols_b, rows_a, rows_b, corners_a, corners_b,
      probe, amplitudes, tables)
    info = (mine, cols_a, cols_b, rows_a, rows_b, corners_a, corners_b)
    mine_a, mine_b = tips_a, tips_b
    tips_a, tips_b = swap_pairs(tips_a, tips_b, "col")
    edges_a, edges_b = swap_pairs(edges_a, edges_b, "row")
    sums_a, sums_b = swap_pairs(sums_a, sums_b, "col")
    (inverse,) = call(
        functools.partial(light_pass, npos=npos), [(blocks, rows, length)], 8 * "v" + "a",
        [memory((blocks + 2, rows + 2 * length, length), jnp.float32),
         memory((length, length), jnp.float32), memory((7 * 8, length), jnp.int32),
         pltpu.SMEM((7 * 8, length), jnp.int32), pltpu.SMEM((9 * npos + 1,), jnp.int32),
         pltpu.SemaphoreType.DMA],
        cost(npos // 2),
    )(*info, probe, acc)
    corners_a, corners_b = [
        call(functools.partial(middle_corners, odd_pairs=odd_pairs), [tip], "vvvva")(
            mine_a, mine_b, tips_a, tips_b, after)[0]
        for odd_pairs, after in ((True, acc), (False, inverse))
    ]
    corners_a, corners_b = swap_pairs(corners_a, corners_b, "row")

    work, total = call(update_pass, [full, full], "ss" + 10 * "v", [chosen], cost(npos // 2))(
        offsets, counts, frame, acc, inverse, tips_a, tips_b, sums_a, sums_b,
        probe, amplitudes, tables)
    own = (2, nb, tile, length)
    edge = (2 * nb, half, length)
    tip = (2, half, length)
    strip = (rows, length)
    work, sums, tips_a, tips_b, cols_a, cols_b, mine_a, mine_b = call(
        second_pass, [full, own, tip, tip, strip, strip, edge, edge], "ss" + 10 * "v",
        [memory(full, jnp.float32), chosen], cost(npos // 2),
    )(offsets, counts, work, total, inverse, edges_a, edges_b, corners_a, corners_b,
      probe, amplitudes, tables)
    tips_a, tips_b = swap_pairs(tips_a, tips_b, "col")
    cols_a, cols_b = swap_pairs(cols_a, cols_b, "col")
    edge = (2 * nb + 2, half, length)
    rows_a, rows_b = call(end_rows, [edge, edge], "vvvv")(mine_a, mine_b, tips_a, tips_b)
    rows_a, rows_b = swap_pairs(rows_a, rows_b, "row")
    (inner,) = call(inner_pass, [own], "ss" + 4 * "v", [chosen], cost(npos // 4))(
        offsets, counts, work, probe, amplitudes, tables)
    out = pl.pallas_call(
        last_pass,
        out_shape=jax.ShapeDtypeStruct((2, tile, tile), jnp.float32),
        in_specs=[whole()] * 8,
        out_specs=whole(pl.ANY),
        scratch_shapes=[memory(own, jnp.float32), pltpu.SemaphoreType.DMA((2 * nb,))],
        compiler_params=pltpu.CompilerParams(vmem_limit_bytes=VMEM_BYTES),
    )(work, sums, inner, inverse, cols_a, cols_b, rows_a, rows_b)
    return out


def solution(mesh):
    placed = (
        P(None, "row", "col"),
        P(),
        P("row", "col", None, None, None),
        P("row", "col", None, None),
        P("row", "col"),
    )
    return jax.shard_map(
        shards, mesh=mesh, in_specs=placed, out_specs=P(None, "row", "col"), check_vma=False
    )
```

```python
import functools
import math

import jax
import jax.numpy as jnp
import numpy as np
from jax import lax
from jax.experimental import pallas as pl
from jax.experimental.pallas import tpu as pltpu
from jax.sharding import PartitionSpec as P

ITERS = 2
FLOOR = 0.25
VMEM_BYTES = 16 * 1024 * 1024
GROUP = 4
CHAIN = 2


def split(value):
    high = value.astype(jnp.bfloat16)
    low = (value - high.astype(jnp.float32)).astype(jnp.bfloat16)
    return high, low


def dft_tables(length):
    index = np.arange(length)
    angle = (index[:, None] * index[None, :] % length) * (2.0 * math.pi / length)
    cosine = np.cos(angle) / math.sqrt(length)
    sine = np.sin(angle) / math.sqrt(length)
    ahead = np.block([[cosine, -sine], [sine, cosine]])
    parts = []
    for table in (ahead, ahead.T):
        high = table.astype(jnp.bfloat16)
        low = (table - high.astype(np.float64)).astype(jnp.bfloat16)
        parts += [high, low]
    return np.stack(parts)


def lanes(shape):
    return lax.broadcasted_iota(jnp.int32, shape, len(shape) - 1)


def swap(value, half):
    return pltpu.roll(value, half, value.ndim - 1)


def odd_place(axis):
    return lax.axis_index(axis) % 2 == 1


def by_pairs(axis, low, high):
    odd = odd_place(axis)
    return jnp.where(odd, high, low), jnp.where(odd, low, high)


def by_side(axis, first, second):
    odd = odd_place(axis)
    return jnp.where(odd, second, first), jnp.where(odd, first, second)


def times_right(rows, high, low):
    top, rest = split(rows)
    left = jnp.concatenate([top, top, rest], axis=1)
    right = jnp.concatenate([high, low, high], axis=0)
    return jnp.dot(left, right, preferred_element_type=jnp.float32)


def times_left(high, low, columns):
    top, rest = split(columns)
    left = jnp.concatenate([high, low, high], axis=1)
    right = jnp.concatenate([top, top, rest], axis=0)
    return jnp.dot(left, right, preferred_element_type=jnp.float32)


def beside(left, right):
    return jnp.concatenate([left, right], axis=1)


def above(top, bottom):
    return jnp.concatenate([top, bottom], axis=0)


def touching(mid_row, mid_col, cross_row, cross_col):
    return ~(mid_row & mid_col) & (cross_row | cross_col)


def early(mid_row, mid_col, cross_row, cross_col):
    return ~(mid_row & mid_col) & ~(cross_row | cross_col)


def clear(mid_row, mid_col, cross_row, cross_col):
    return mid_row & mid_col


def collect(chosen, found, offsets, counts, tile, length, wanted, begin=0, end=None):
    last = tile - length
    half = length // 2

    def look(slot, carry):
        found, seen = carry
        row = offsets[0, 0, 0, slot]
        col = offsets[0, 0, 1, slot]
        taken = wanted(
            mid_row=(row >= half) & (row <= last - half),
            mid_col=(col >= half) & (col <= last - half),
            cross_row=(row < 0) | (row > last),
            cross_col=(col < 0) | (col > last),
        )
        listed = taken & (seen >= begin)
        if end is not None:
            listed = listed & (seen < end)
        chosen[found] = slot
        return found + jnp.where(listed, 1, 0), seen + jnp.where(taken, 1, 0)

    return lax.fori_loop(0, counts[0, 0], look, (found, 0))


def early_list(chosen, *place):
    found, known = collect(chosen, 0, *place, early, 0, GROUP)
    found, _ = collect(chosen, found, *place, clear, 0, GROUP - jnp.minimum(known, GROUP))
    return found


def first_list(chosen, *place):
    found, _ = collect(chosen, 0, *place, touching)
    found, known = collect(chosen, found, *place, early, GROUP)
    begin = GROUP - jnp.minimum(known, GROUP)
    end = begin + lax.rem(GROUP - lax.rem(found, GROUP), GROUP)
    found, _ = collect(chosen, found, *place, clear, begin, end)
    return found, end


def choose(chosen, *place):
    found, _ = collect(chosen, 0, *place)
    return found


def add_gradients(frame, acc, probe_ref, amps, offsets, tables, chosen, found, own_frame=False, own_acc=False):
    length = probe_ref.shape[-1]
    half = length // 2
    lane = lanes((length, length))

    def place(slot, ref, own):
        col = offsets[0, 0, 1, slot] + length
        block = lax.div(col, length)
        row = offsets[0, 0, 0, slot]
        if own:
            block = block - 1
        else:
            row = row + half
        after = jnp.minimum(block + 1, ref.shape[1] - 1)
        return pl.ds(row, length), block, after, lax.rem(col, length)

    def exit_wave(slot):
        at, block, after, shift = place(slot, frame, own_frame)
        inside = lane >= shift
        window = [
            jnp.where(inside, frame[part, block, at, :], frame[part, after, at, :])
            for part in (0, 1)
        ]
        probe = (pltpu.roll(probe_ref[0], shift, 1), pltpu.roll(probe_ref[1], shift, 1))
        wave = (probe[0] * window[0] - probe[1] * window[1],
                probe[0] * window[1] + probe[1] * window[0])
        return probe, wave

    def shrink(real, imag, slot):
        ratio = amps[0, 0, slot] * lax.rsqrt(real * real + imag * imag + FLOOR) - 1.0
        return real * ratio, imag * ratio

    def put(slot, live, probe, back_r, back_i):
        at, block, after, shift = place(slot, acc, own_acc)
        grads = (probe[0] * back_r + probe[1] * back_i, probe[0] * back_i - probe[1] * back_r)
        bound = jnp.where(live, shift, length)
        inside = lane >= bound
        beyond = lane < jnp.where(live, shift, 0)
        for part in (0, 1):
            acc[part, block, at, :] += jnp.where(inside, grads[part], 0.0)
            acc[part, after, at, :] += jnp.where(beyond, grads[part], 0.0)

    def work(slots):
        probes, waves = zip(*[exit_wave(slot) for slot in slots])
        rows = jnp.concatenate([beside(*wave) for wave in waves], axis=0)
        mid = times_right(rows, tables[0], tables[1])
        yield None
        mids = [mid[k * length:(k + 1) * length] for k in range(len(slots))]
        columns = above(
            jnp.concatenate([m[:, :length] for m in mids], axis=1),
            jnp.concatenate([m[:, length:] for m in mids], axis=1),
        )
        far = times_left(tables[2], tables[3], columns)
        yield None
        changes = [
            shrink(far[:length, k * length:(k + 1) * length],
                   far[length:, k * length:(k + 1) * length], slot)
            for k, slot in enumerate(slots)
        ]
        columns = above(
            jnp.concatenate([c[0] for c in changes], axis=1),
            jnp.concatenate([c[1] for c in changes], axis=1),
        )
        mid = times_left(tables[0], tables[1], columns)
        yield None
        rows = jnp.concatenate(
            [
                beside(mid[:length, k * length:(k + 1) * length],
                       mid[length:, k * length:(k + 1) * length])
                for k in range(len(slots))
            ],
            axis=0,
        )
        back = times_right(rows, tables[2], tables[3])
        yield None
        yield [
            (probes[k], back[k * length:(k + 1) * length, :length],
             back[k * length:(k + 1) * length, length:])
            for k in range(len(slots))
        ]

    def step(index, carry):
        places = [index * GROUP + k for k in range(GROUP)]
        slots = [chosen[jnp.where(at < found, at, 0)] for at in places]
        chains = [work(slots[k:k + CHAIN]) for k in range(0, GROUP, CHAIN)]
        gradients = [None]
        while gradients[0] is None:
            gradients = [next(chain) for chain in chains]
        gradients = [gradient for chain in gradients for gradient in chain]
        for at, slot, gradient in zip(places, slots, gradients):
            put(slot, at < found, *gradient)
        return carry

    lax.fori_loop(0, (found + GROUP - 1) // GROUP, step, 0)


def start_pass(field, offsets_from, counts, tile_out, cols_a, cols_b, rows_a, rows_b, offsets, sems):
    _, nb, tile, length = tile_out.shape
    half = length // 2
    npos = offsets.shape[3]
    listed = pltpu.make_async_copy(offsets_from, offsets, sems.at[nb])
    listed.start()
    copies = [
        pltpu.make_async_copy(
            field.at[:, :, b * length:(b + 1) * length], tile_out.at[:, b], sems.at[b])
        for b in range(nb)
    ]
    for copy in copies:
        copy.start()
    listed.wait()
    spot = lanes((8, length))
    info = jnp.zeros((8, length), jnp.int32)
    down = (lax.axis_index("row") + 1) * tile
    across = (lax.axis_index("col") + 1) * tile
    for k in range(npos):
        live = k < counts[0, 0]
        info = jnp.where(spot == k, jnp.where(live, offsets[0, 0, 0, k] + down, 0), info)
        info = jnp.where(spot == npos + k, jnp.where(live, offsets[0, 0, 1, k] + across, 0), info)
    info = info.astype(jnp.float32)
    for end in (cols_a, cols_b, rows_a, rows_b):
        end[pl.ds(end.shape[0] - 8, 8), :] = info
    for copy in copies:
        copy.wait()
    low = lanes((tile, length)) < half
    to_left = jnp.where(low, tile_out[0, 0], swap(tile_out[1, 0], half))
    to_right = jnp.where(low, swap(tile_out[1, nb - 1], half), tile_out[0, nb - 1])
    cols_a[:tile], cols_b[:tile] = by_pairs("col", to_left, to_right)
    for part in (0, 1):
        for b in range(nb):
            at = pl.ds((part * nb + b) * half, half)
            rows_a[at, :], rows_b[at, :] = by_pairs(
                "row", tile_out[part, b, :half], tile_out[part, b, tile - half:])


def start_corners(cols_a, cols_b, after, corners_a, corners_b):
    length = cols_a.shape[1]
    half = length // 2
    tile = cols_a.shape[0] - 8
    low = lanes((tile, length)) < half
    left, right = by_side("col", cols_a[:tile], cols_b[:tile])
    for part in (0, 1):
        if part:
            left, right = swap(left, half), swap(right, half)
        value = jnp.where(low, right, left)
        at = pl.ds(part * half, half)
        corners_a[at, :], corners_b[at, :] = by_pairs("row", value[:half], value[tile - half:])
    first = lax.broadcasted_iota(jnp.int32, (8, length), 0) == 0
    info = jnp.where(first, cols_a[tile:], cols_b[tile:])
    corners_a[2 * half:] = info
    corners_b[2 * half:] = info


def fetch_pass(after, probe_from, amps_from, tables_from, probe, amps, tables, sems):
    copies = [
        pltpu.make_async_copy(source, target, sems.at[k])
        for k, (source, target) in enumerate(
            ((amps_from, amps), (tables_from, tables), (probe_from, probe)))
    ]
    for copy in copies:
        copy.start()
    for copy in copies:
        copy.wait()


def early_pass(offsets, counts, after, field, probe, amps, tables, acc, chosen):
    _, nb, tile, length = field.shape
    acc[...] = jnp.zeros_like(acc)
    found = early_list(chosen, offsets, counts, tile, length)
    add_gradients(field, acc, probe, amps, offsets, tables, chosen, found,
                  own_frame=True, own_acc=True)


def first_pass(offsets, counts, field, done, cols_a, cols_b, rows_a, rows_b, corners_a, corners_b,
               probe, amps, tables, frame, acc, tips_a, tips_b, sums_a, sums_b, edges_a, edges_b, chosen):
    _, nb, tile, length = field.shape
    half = length // 2
    rows = tile + 2 * half
    own = pl.ds(half, tile)
    left, right = by_side("col", cols_a[:tile], cols_b[:tile])
    top = pl.ds(0, half)
    bottom = pl.ds(half + tile, half)
    for part in (0, 1):
        for b in range(nb):
            frame[part, b + 1, own, :] = field[part, b]
            at = pl.ds((part * nb + b) * half, half)
            frame[part, b + 1, top, :], frame[part, b + 1, bottom, :] = by_side(
                "row", rows_a[at, :], rows_b[at, :])
        frame[part, 0, own, :] = swap(left, half) if part else left
        frame[part, nb + 1, own, :] = swap(right, half) if part else right
        at = pl.ds(part * half, half)
        ends = by_side("row", corners_a[at, :], corners_b[at, :])
        for block in (0, nb + 1):
            frame[part, block, top, :], frame[part, block, bottom, :] = ends
    empty = jnp.zeros((half, length), jnp.float32)
    for part in (0, 1):
        for b in range(nb + 2):
            acc[part, b, top, :] = empty
            acc[part, b, bottom, :] = empty
            acc[part, b, own, :] = (
                done[part, b - 1] if 0 < b <= nb else jnp.zeros((tile, length), jnp.float32))
    found, _ = first_list(chosen, offsets, counts, tile, length)
    add_gradients(frame, acc, probe, amps, offsets, tables, chosen, found)
    low = lanes((rows, length)) < half
    for part in (0, 1):
        strip_a, strip_b = by_pairs(
            "col",
            jnp.where(low, acc[part, 1], acc[part, 0]),
            jnp.where(low, acc[part, nb + 1], acc[part, nb]),
        )
        for strip, tips, sums in ((strip_a, tips_a, sums_a), (strip_b, tips_b, sums_b)):
            tips[part, 0] = strip[:length]
            tips[part, 1] = strip[rows - length:]
            sums[part] = strip[length:rows - length]
    near = lanes((length, length)) < half
    for part in (0, 1):
        for b in range(nb - 1):
            ends = [
                acc[part, b + 2, at, :] if b < nb - 2
                else jnp.where(near, acc[part, nb, at, :], acc[part, 1, at, :])
                for at in (pl.ds(0, length), pl.ds(rows - length, length))
            ]
            edges_a[part, b], edges_b[part, b] = by_pairs("row", *ends)


def middle_corners(mine_a, mine_b, tips_a, tips_b, after, corners, *, odd_pairs):
    for part in (0, 1):
        up, down = [
            by_side("col", mine_a[part, k] + tips_a[part, k], mine_b[part, k] + tips_b[part, k])
            for k in (0, 1)
        ]
        for side in (0, 1):
            corners[part, side] = by_pairs("row", up[side], down[side])[0 if odd_pairs else 1]


def light_pass(mine, cols_a, cols_b, rows_a, rows_b, corners_a, corners_b, probe, after,
               inverse, light, power, places, listed, chosen, sem, *, npos):
    length = probe.shape[-1]
    half = length // 2
    blocks, rows, _ = inverse.shape
    nb = blocks - 2
    tile = nb * length
    my_row = lax.axis_index("row")
    my_col = lax.axis_index("col")
    sources = (mine, cols_a, cols_b, rows_a, rows_b, corners_a, corners_b)
    for k, source in enumerate(sources):
        given = source[source.shape[0] - 8:, :].astype(jnp.int32)
        col = pltpu.roll(given, length - npos, 1) - (my_col + 1) * tile + 2 * length
        row = given - (my_row + 1) * tile + half + length
        near = (given > 0) & (row > 0) & (row < rows + length)
        near = near & (col > length - half) & (col < 2 * length + tile + half)
        places[pl.ds(8 * k, 8), :] = jnp.where(near, row * 4 * tile + col, 0)
    copy = pltpu.make_async_copy(places, listed, sem)
    copy.start()
    for b in range(blocks):
        light[b + 1, pl.ds(length, rows), :] = jnp.zeros((rows, length), jnp.float32)
    power[...] = probe[0] * probe[0] + probe[1] * probe[1]
    lane = lanes((length, length))
    copy.wait()

    def look(index, found):
        line = jnp.where(index < len(sources), 8 * index, 8 * (index - 2) + 1)
        for slot in range(npos):
            place = listed[line, slot]
            chosen[found] = place
            found = found + jnp.where(place > 0, 1, 0)
        return found

    found = lax.fori_loop(0, len(sources) + 2, look, 0)

    def put(index, carry):
        place = chosen[index]
        start = lax.div(place, 4 * tile)
        col = lax.rem(place, 4 * tile)
        block = lax.div(col, length)
        shift = lax.rem(col, length)
        value = pltpu.roll(power[...], shift, 1)
        inside = lane >= shift
        light[block, pl.ds(start, length), :] += jnp.where(inside, value, 0.0)
        light[block + 1, pl.ds(start, length), :] += jnp.where(inside, 0.0, value)
        return carry

    lax.fori_loop(0, found, put, 0)
    spot = lax.broadcasted_iota(jnp.int32, (rows, length), 0)
    keep_from = jnp.where(my_row > 0, 0, half)
    keep_to = jnp.where(my_row < lax.axis_size("row") - 1, rows, rows - half)
    kept = (spot >= keep_from) & (spot < keep_to)
    for b in range(blocks):
        value = 1.0 / (light[b + 1, pl.ds(length, rows), :] + 1.0)
        keep = kept
        if b == 0:
            keep = keep & (my_col > 0)
        if b == nb + 1:
            keep = keep & (my_col < lax.axis_size("col") - 1)
        inverse[b] = jnp.where(keep, value, 0.0)


def update_pass(offsets, counts, frame, acc, inverse, tips_a, tips_b, sums_a, sums_b, probe, amps, tables,
                work, total, chosen):
    _, blocks, rows, length = frame.shape
    half = length // 2
    nb = blocks - 2
    work[...] = acc[...]
    _, done = first_list(chosen, offsets, counts, nb * length, length)
    found, _ = collect(chosen, 0, offsets, counts, nb * length, length, clear, done)
    add_gradients(frame, work, probe, amps, offsets, tables, chosen, found)
    low = lanes((rows, length)) < half
    for part in (0, 1):
        left, right = by_side("col", *[
            above(above(tips[part, 0], sums[part]), tips[part, 1])
            for tips, sums in ((tips_a, sums_a), (tips_b, sums_b))
        ])
        for b in range(blocks):
            value = work[part, b]
            if b == 0:
                value = value + left
            if b == 1:
                value = value + jnp.where(low, left, 0.0)
            if b == nb:
                value = value + jnp.where(low, 0.0, right)
            if b == nb + 1:
                value = value + right
            work[part, b] = frame[part, b] + value * inverse[b]
    total[...] = jnp.zeros_like(total)
    found = choose(chosen, offsets, counts, nb * length, length, lambda mid_row, **_: mid_row)
    add_gradients(work, total, probe, amps, offsets, tables, chosen, found)


def second_pass(offsets, counts, work_from, total_from, inverse, edges_a, edges_b,
                corners_a, corners_b, probe, amps, tables,
                work, sums, tips_a, tips_b, cols_a, cols_b, rows_a, rows_b, total, chosen):
    _, blocks, rows, length = work.shape
    half = length // 2
    nb = blocks - 2
    tile = nb * length
    near = lanes((length, length)) < half
    middle = pl.ds(length, rows - 2 * length)
    for part in (0, 1):
        edges = [by_side("row", edges_a[part, b], edges_b[part, b]) for b in range(nb - 1)]
        corners = [by_side("row", corners_a[part, side], corners_b[part, side]) for side in (0, 1)]
        for k, at in enumerate((pl.ds(0, length), pl.ds(rows - length, length))):
            left, right, ends = corners[0][k], corners[1][k], edges[nb - 2][k]
            add = [left, jnp.where(near, left, ends)]
            add += [edges[b][k] for b in range(nb - 2)]
            add += [jnp.where(near, ends, right), right]
            for b in range(blocks):
                work[part, b, at, :] = work_from[part, b, at, :] + add[b] * inverse[b, at, :]
        for b in range(blocks):
            work[part, b, middle, :] = work_from[part, b, middle, :]
    total[...] = total_from[...]
    found = choose(
        chosen, offsets, counts, tile, length,
        lambda mid_row, cross_row, cross_col, **_: ~mid_row & (cross_row | cross_col))
    add_gradients(work, total, probe, amps, offsets, tables, chosen, found)
    low = lanes((rows, length)) < half
    strip_a, strip_b = by_pairs(
        "col",
        jnp.where(low, swap(total[1, 0], half), total[0, 0]),
        jnp.where(low, total[0, nb + 1], swap(total[1, nb + 1], half)),
    )
    for strip, tips, cols in ((strip_a, tips_a, cols_a), (strip_b, tips_b, cols_b)):
        tips[0] = strip[:half]
        tips[1] = strip[half + tile:]
        cols[...] = strip
    for part in (0, 1):
        for b in range(nb):
            sums[part, b] = total[part, b + 1, pl.ds(half, tile), :]
            rows_a[part * nb + b], rows_b[part * nb + b] = by_pairs(
                "row", total[part, b + 1, :half, :], total[part, b + 1, half + tile:, :])


def inner_pass(offsets, counts, work, probe, amps, tables, sums, chosen):
    _, nb, tile, length = sums.shape
    sums[...] = jnp.zeros_like(sums)
    found = choose(
        chosen, offsets, counts, tile, length,
        lambda mid_row, cross_row, cross_col, **_: ~mid_row & ~cross_row & ~cross_col)
    add_gradients(work, sums, probe, amps, offsets, tables, chosen, found, own_acc=True)


def end_rows(mine_a, mine_b, tips_a, tips_b, rows_a, rows_b):
    count = mine_a.shape[0]
    rows_a[:count] = mine_a[...]
    rows_b[:count] = mine_b[...]
    up, down = [by_side("col", tips_a[k], tips_b[k]) for k in (0, 1)]
    for side in (0, 1):
        rows_a[count + side], rows_b[count + side] = by_pairs("row", up[side], down[side])


def last_pass(work, sums, inner, inverse, cols_a, cols_b, rows_a, rows_b, out, result, sems):
    _, nb, tile, length = sums.shape
    half = length // 2
    low = lanes((tile, length)) < half
    own = pl.ds(half, tile)
    gap = jnp.zeros((tile - 2 * half, length), jnp.float32)
    sides = []
    for side, value in enumerate(by_side("col", cols_a[own, :], cols_b[own, :])):
        up, down = by_side("row", rows_a[2 * nb + side], rows_b[2 * nb + side])
        sides.append(value + above(above(up, gap), down))
    left, right = sides
    copies = []
    for part in (0, 1):
        if part:
            left, right = swap(left, half), swap(right, half)
        for b in range(nb):
            up, down = by_side("row", rows_a[part * nb + b], rows_b[part * nb + b])
            value = sums[part, b] + inner[part, b] + above(above(up, gap), down)
            if b == 0:
                value = value + jnp.where(low, left, 0.0)
            if b == nb - 1:
                value = value + jnp.where(low, 0.0, right)
            result[part, b] = work[part, b + 1, own, :] + value * inverse[b + 1, own, :]
            copy = pltpu.make_async_copy(
                result.at[part, b], out.at[part, :, b * length:(b + 1) * length],
                sems.at[part * nb + b])
            copy.start()
            copies.append(copy)
    for copy in copies:
        copy.wait()


def whole(memory_space=pltpu.VMEM):
    return pl.BlockSpec(memory_space=memory_space)


def call(body, shapes, places, scratch=(), cost=None):
    return pl.pallas_call(
        body,
        out_shape=[jax.ShapeDtypeStruct(shape, jnp.float32) for shape in shapes],
        in_specs=[whole({"s": pltpu.SMEM, "v": pltpu.VMEM, "a": pl.ANY, "h": pltpu.HBM}[p]) for p in places],
        out_specs=[whole()] * len(shapes),
        scratch_shapes=list(scratch),
        compiler_params=pltpu.CompilerParams(vmem_limit_bytes=VMEM_BYTES),
        cost_estimate=cost,
    )


def swap_pairs(first, second, axis):
    count = lax.axis_size(axis)
    got = []
    for value, start in ((first, 1), (second, 0)):
        pairs = [(i, i + 1) for i in range(start, count - 1, 2)]
        got.append(lax.ppermute(value, axis, pairs + [(b, a) for a, b in pairs]))
    return got


def shards(object_field, probe, amplitudes, offsets, counts):
    length = probe.shape[-1]
    half = length // 2
    tile = object_field.shape[1]
    npos = offsets.shape[2]
    nb = tile // length
    blocks = nb + 2
    rows = tile + 2 * half
    tables = jnp.asarray(dft_tables(length))
    offsets = jnp.swapaxes(offsets, 2, 3)

    def cost(positions):
        steps = 4 * 3 * 2 * length * (2 * length) ** 2
        return pl.CostEstimate(
            flops=positions * steps, bytes_accessed=8_000_000,
            transcendentals=positions * length * length)

    memory = pltpu.VMEM
    chosen = pltpu.SMEM((npos + GROUP,), jnp.int32)
    strip = (tile + 8, length)
    edge = (2 * nb * half + 8, length)
    def kept(array):
        return pltpu.with_memory_space_constraint(array, pltpu.HBM)

    field, cols_a, cols_b, rows_a, rows_b = call(
        start_pass, [(2, nb, tile, length), strip, strip, edge, edge], "hhs",
        [pltpu.SMEM((1, 1, 2, npos), jnp.int32), pltpu.SemaphoreType.DMA((nb + 1,))],
    )(kept(object_field), kept(offsets), counts)
    mine = cols_a
    probe, amplitudes, tables = pl.pallas_call(
        fetch_pass,
        out_shape=[
            jax.ShapeDtypeStruct(array.shape, array.dtype) for array in (probe, amplitudes, tables)],
        in_specs=[whole(pl.ANY)] + [whole(pltpu.HBM)] * 3,
        out_specs=[whole()] * 3,
        scratch_shapes=[pltpu.SemaphoreType.DMA((3,))],
        compiler_params=pltpu.CompilerParams(vmem_limit_bytes=VMEM_BYTES),
        cost_estimate=cost(1),
    )(cols_a, kept(probe), kept(amplitudes), kept(tables))
    cols_a, cols_b = swap_pairs(cols_a, cols_b, "col")
    rows_a, rows_b = swap_pairs(rows_a, rows_b, "row")
    corner = (2 * half + 8, length)
    corners_a, corners_b = call(start_corners, [corner, corner], "vva")(cols_a, cols_b, probe)
    (done,) = call(
        early_pass, [(2, nb, tile, length)], "ssavvvv", [chosen], cost(GROUP),
    )(offsets, counts, corners_b, field, probe, amplitudes, tables)
    corners_a, corners_b = swap_pairs(corners_a, corners_b, "row")

    full = (2, blocks, rows, length)
    strip = (2, rows, length)
    edge = (2, nb - 1, length, length)
    tip = (2, 2, length, length)
    strip = (2, rows - 2 * length, length)
    frame, acc, tips_a, tips_b, sums_a, sums_b, edges_a, edges_b = call(
        first_pass, [full, full, tip, tip, strip, strip, edge, edge], "ss" + 11 * "v", [chosen],
    )(offsets, counts, field, done, cols_a, cols_b, rows_a, rows_b, corners_a, corners_b,
      probe, amplitudes, tables)
    info = (mine, cols_a, cols_b, rows_a, rows_b, corners_a, corners_b)
    mine_a, mine_b = tips_a, tips_b
    tips_a, tips_b = swap_pairs(tips_a, tips_b, "col")
    edges_a, edges_b = swap_pairs(edges_a, edges_b, "row")
    sums_a, sums_b = swap_pairs(sums_a, sums_b, "col")
    (inverse,) = call(
        functools.partial(light_pass, npos=npos), [(blocks, rows, length)], 8 * "v" + "a",
        [memory((blocks + 2, rows + 2 * length, length), jnp.float32),
         memory((length, length), jnp.float32), memory((7 * 8, length), jnp.int32),
         pltpu.SMEM((7 * 8, length), jnp.int32), pltpu.SMEM((9 * npos + 1,), jnp.int32),
         pltpu.SemaphoreType.DMA],
        cost(npos // 2),
    )(*info, probe, tips_b)
    corners_a, corners_b = [
        call(functools.partial(middle_corners, odd_pairs=odd_pairs), [tip], "vvvva")(
            mine_a, mine_b, tips_a, tips_b, after)[0]
        for odd_pairs, after in ((True, acc), (False, inverse))
    ]
    corners_a, corners_b = swap_pairs(corners_a, corners_b, "row")

    work, total = call(update_pass, [full, full], "ss" + 10 * "v", [chosen], cost(npos // 2))(
        offsets, counts, frame, acc, inverse, tips_a, tips_b, sums_a, sums_b,
        probe, amplitudes, tables)
    own = (2, nb, tile, length)
    edge = (2 * nb, half, length)
    tip = (2, half, length)
    strip = (rows, length)
    work, sums, tips_a, tips_b, cols_a, cols_b, mine_a, mine_b = call(
        second_pass, [full, own, tip, tip, strip, strip, edge, edge], "ss" + 10 * "v",
        [memory(full, jnp.float32), chosen], cost(npos // 2),
    )(offsets, counts, work, total, inverse, edges_a, edges_b, corners_a, corners_b,
      probe, amplitudes, tables)
    tips_a, tips_b = swap_pairs(tips_a, tips_b, "col")
    cols_a, cols_b = swap_pairs(cols_a, cols_b, "col")
    edge = (2 * nb + 2, half, length)
    rows_a, rows_b = call(end_rows, [edge, edge], "vvvv")(mine_a, mine_b, tips_a, tips_b)
    rows_a, rows_b = swap_pairs(rows_a, rows_b, "row")
    (inner,) = call(inner_pass, [own], "ss" + 4 * "v", [chosen], cost(npos // 4))(
        offsets, counts, work, probe, amplitudes, tables)
    out = pl.pallas_call(
        last_pass,
        out_shape=jax.ShapeDtypeStruct((2, tile, tile), jnp.float32),
        in_specs=[whole()] * 8,
        out_specs=whole(pl.ANY),
        scratch_shapes=[memory(own, jnp.float32), pltpu.SemaphoreType.DMA((2 * nb,))],
        compiler_params=pltpu.CompilerParams(vmem_limit_bytes=VMEM_BYTES),
    )(work, sums, inner, inverse, cols_a, cols_b, rows_a, rows_b)
    return out


def solution(mesh):
    placed = (
        P(None, "row", "col"),
        P(),
        P("row", "col", None, None, None),
        P("row", "col", None, None),
        P("row", "col"),
    )
    return jax.shard_map(
        shards, mesh=mesh, in_specs=placed, out_specs=P(None, "row", "col"), check_vma=False
    )
```

```python
import functools
import math

import jax
import jax.numpy as jnp
import numpy as np
from jax import lax
from jax.experimental import pallas as pl
from jax.experimental.pallas import tpu as pltpu
from jax.sharding import PartitionSpec as P

ITERS = 2
FLOOR = 0.25
VMEM_BYTES = 16 * 1024 * 1024
GROUP = 4
CHAIN = 2


def split(value):
    high = value.astype(jnp.bfloat16)
    low = (value - high.astype(jnp.float32)).astype(jnp.bfloat16)
    return high, low


def dft_tables(length):
    index = np.arange(length)
    angle = (index[:, None] * index[None, :] % length) * (2.0 * math.pi / length)
    cosine = np.cos(angle) / math.sqrt(length)
    sine = np.sin(angle) / math.sqrt(length)
    ahead = np.block([[cosine, -sine], [sine, cosine]])
    parts = []
    for table in (ahead, ahead.T):
        high = table.astype(jnp.bfloat16)
        low = (table - high.astype(np.float64)).astype(jnp.bfloat16)
        parts += [high, low]
    return np.stack(parts)


def lanes(shape):
    return lax.broadcasted_iota(jnp.int32, shape, len(shape) - 1)


def swap(value, half):
    return pltpu.roll(value, half, value.ndim - 1)


def odd_place(axis):
    return lax.axis_index(axis) % 2 == 1


def by_pairs(axis, low, high):
    odd = odd_place(axis)
    return jnp.where(odd, high, low), jnp.where(odd, low, high)


def by_side(axis, first, second):
    odd = odd_place(axis)
    return jnp.where(odd, second, first), jnp.where(odd, first, second)


def times_right(rows, high, low):
    top, rest = split(rows)
    left = jnp.concatenate([top, top, rest], axis=1)
    right = jnp.concatenate([high, low, high], axis=0)
    return jnp.dot(left, right, preferred_element_type=jnp.float32)


def times_left(high, low, columns):
    top, rest = split(columns)
    left = jnp.concatenate([high, low, high], axis=1)
    right = jnp.concatenate([top, top, rest], axis=0)
    return jnp.dot(left, right, preferred_element_type=jnp.float32)


def beside(left, right):
    return jnp.concatenate([left, right], axis=1)


def above(top, bottom):
    return jnp.concatenate([top, bottom], axis=0)


def touching(mid_row, mid_col, cross_row, cross_col):
    return ~(mid_row & mid_col) & (cross_row | cross_col)


def early(mid_row, mid_col, cross_row, cross_col):
    return ~(mid_row & mid_col) & ~(cross_row | cross_col)


def clear(mid_row, mid_col, cross_row, cross_col):
    return mid_row & mid_col


def collect(chosen, found, offsets, counts, tile, length, wanted, begin=0, end=None):
    last = tile - length
    half = length // 2

    def look(slot, carry):
        found, seen = carry
        row = offsets[0, 0, 0, slot]
        col = offsets[0, 0, 1, slot]
        taken = wanted(
            mid_row=(row >= half) & (row <= last - half),
            mid_col=(col >= half) & (col <= last - half),
            cross_row=(row < 0) | (row > last),
            cross_col=(col < 0) | (col > last),
        )
        listed = taken & (seen >= begin)
        if end is not None:
            listed = listed & (seen < end)
        chosen[found] = slot
        return found + jnp.where(listed, 1, 0), seen + jnp.where(taken, 1, 0)

    return lax.fori_loop(0, counts[0, 0], look, (found, 0))


def early_list(chosen, *place):
    found, known = collect(chosen, 0, *place, early, 0, GROUP)
    found, _ = collect(chosen, found, *place, clear, 0, GROUP - jnp.minimum(known, GROUP))
    return found


def first_list(chosen, *place):
    found, _ = collect(chosen, 0, *place, touching)
    found, known = collect(chosen, found, *place, early, GROUP)
    begin = GROUP - jnp.minimum(known, GROUP)
    end = begin + lax.rem(GROUP - lax.rem(found, GROUP), GROUP)
    found, _ = collect(chosen, found, *place, clear, begin, end)
    return found, end


def choose(chosen, *place):
    found, _ = collect(chosen, 0, *place)
    return found


def add_gradients(frame, acc, probe_ref, amps, offsets, tables, chosen, found, own_frame=False, own_acc=False):
    length = probe_ref.shape[-1]
    half = length // 2
    lane = lanes((length, length))

    def place(slot, ref, own):
        col = offsets[0, 0, 1, slot] + length
        block = lax.div(col, length)
        row = offsets[0, 0, 0, slot]
        if own:
            block = block - 1
        else:
            row = row + half
        after = jnp.minimum(block + 1, ref.shape[1] - 1)
        return pl.ds(row, length), block, after, lax.rem(col, length)

    def exit_wave(slot):
        at, block, after, shift = place(slot, frame, own_frame)
        inside = lane >= shift
        window = [
            jnp.where(inside, frame[part, block, at, :], frame[part, after, at, :])
            for part in (0, 1)
        ]
        probe = (pltpu.roll(probe_ref[0], shift, 1), pltpu.roll(probe_ref[1], shift, 1))
        wave = (probe[0] * window[0] - probe[1] * window[1],
                probe[0] * window[1] + probe[1] * window[0])
        return probe, wave

    def shrink(real, imag, slot):
        ratio = amps[0, 0, slot] * lax.rsqrt(real * real + imag * imag + FLOOR) - 1.0
        return real * ratio, imag * ratio

    def put(slot, live, probe, back_r, back_i):
        at, block, after, shift = place(slot, acc, own_acc)
        grads = (probe[0] * back_r + probe[1] * back_i, probe[0] * back_i - probe[1] * back_r)
        bound = jnp.where(live, shift, length)
        inside = lane >= bound
        beyond = lane < jnp.where(live, shift, 0)
        for part in (0, 1):
            acc[part, block, at, :] += jnp.where(inside, grads[part], 0.0)
            acc[part, after, at, :] += jnp.where(beyond, grads[part], 0.0)

    def work(slots):
        probes, waves = zip(*[exit_wave(slot) for slot in slots])
        rows = jnp.concatenate([beside(*wave) for wave in waves], axis=0)
        mid = times_right(rows, tables[0], tables[1])
        yield None
        mids = [mid[k * length:(k + 1) * length] for k in range(len(slots))]
        columns = above(
            jnp.concatenate([m[:, :length] for m in mids], axis=1),
            jnp.concatenate([m[:, length:] for m in mids], axis=1),
        )
        far = times_left(tables[2], tables[3], columns)
        yield None
        changes = [
            shrink(far[:length, k * length:(k + 1) * length],
                   far[length:, k * length:(k + 1) * length], slot)
            for k, slot in enumerate(slots)
        ]
        columns = above(
            jnp.concatenate([c[0] for c in changes], axis=1),
            jnp.concatenate([c[1] for c in changes], axis=1),
        )
        mid = times_left(tables[0], tables[1], columns)
        yield None
        rows = jnp.concatenate(
            [
                beside(mid[:length, k * length:(k + 1) * length],
                       mid[length:, k * length:(k + 1) * length])
                for k in range(len(slots))
            ],
            axis=0,
        )
        back = times_right(rows, tables[2], tables[3])
        yield None
        yield [
            (probes[k], back[k * length:(k + 1) * length, :length],
             back[k * length:(k + 1) * length, length:])
            for k in range(len(slots))
        ]

    def step(index, carry):
        places = [index * GROUP + k for k in range(GROUP)]
        slots = [chosen[jnp.where(at < found, at, 0)] for at in places]
        chains = [work(slots[k:k + CHAIN]) for k in range(0, GROUP, CHAIN)]
        gradients = [None]
        while gradients[0] is None:
            gradients = [next(chain) for chain in chains]
        gradients = [gradient for chain in gradients for gradient in chain]
        for at, slot, gradient in zip(places, slots, gradients):
            put(slot, at < found, *gradient)
        return carry

    lax.fori_loop(0, (found + GROUP - 1) // GROUP, step, 0)


def start_pass(field, offsets_from, counts, tile_out, cols_a, cols_b, rows_a, rows_b, offsets, sems):
    _, nb, tile, length = tile_out.shape
    half = length // 2
    npos = offsets.shape[3]
    listed = pltpu.make_async_copy(offsets_from, offsets, sems.at[nb])
    listed.start()
    copies = [
        pltpu.make_async_copy(
            field.at[:, :, b * length:(b + 1) * length], tile_out.at[:, b], sems.at[b])
        for b in range(nb)
    ]
    for copy in copies:
        copy.start()
    listed.wait()
    spot = lanes((8, length))
    info = jnp.zeros((8, length), jnp.int32)
    down = (lax.axis_index("row") + 1) * tile
    across = (lax.axis_index("col") + 1) * tile
    for k in range(npos):
        live = k < counts[0, 0]
        info = jnp.where(spot == k, jnp.where(live, offsets[0, 0, 0, k] + down, 0), info)
        info = jnp.where(spot == npos + k, jnp.where(live, offsets[0, 0, 1, k] + across, 0), info)
    info = info.astype(jnp.float32)
    for end in (cols_a, cols_b, rows_a, rows_b):
        end[pl.ds(end.shape[0] - 8, 8), :] = info
    for copy in copies:
        copy.wait()
    low = lanes((tile, length)) < half
    to_left = jnp.where(low, tile_out[0, 0], swap(tile_out[1, 0], half))
    to_right = jnp.where(low, swap(tile_out[1, nb - 1], half), tile_out[0, nb - 1])
    cols_a[:tile], cols_b[:tile] = by_pairs("col", to_left, to_right)
    for part in (0, 1):
        for b in range(nb):
            at = pl.ds((part * nb + b) * half, half)
            rows_a[at, :], rows_b[at, :] = by_pairs(
                "row", tile_out[part, b, :half], tile_out[part, b, tile - half:])


def start_corners(cols_a, cols_b, after, corners_a, corners_b):
    length = cols_a.shape[1]
    half = length // 2
    tile = cols_a.shape[0] - 8
    low = lanes((tile, length)) < half
    left, right = by_side("col", cols_a[:tile], cols_b[:tile])
    for part in (0, 1):
        if part:
            left, right = swap(left, half), swap(right, half)
        value = jnp.where(low, right, left)
        at = pl.ds(part * half, half)
        corners_a[at, :], corners_b[at, :] = by_pairs("row", value[:half], value[tile - half:])
    first = lax.broadcasted_iota(jnp.int32, (8, length), 0) == 0
    info = jnp.where(first, cols_a[tile:], cols_b[tile:])
    corners_a[2 * half:] = info
    corners_b[2 * half:] = info


def fetch_pass(after, probe_from, amps_from, tables_from, probe, amps, tables, sems):
    copies = [
        pltpu.make_async_copy(source, target, sems.at[k])
        for k, (source, target) in enumerate(
            ((amps_from, amps), (tables_from, tables), (probe_from, probe)))
    ]
    for copy in copies:
        copy.start()
    for copy in copies:
        copy.wait()


def early_pass(offsets, counts, after, field, probe, amps, tables, acc, chosen):
    _, nb, tile, length = field.shape
    acc[...] = jnp.zeros_like(acc)
    found = early_list(chosen, offsets, counts, tile, length)
    add_gradients(field, acc, probe, amps, offsets, tables, chosen, found,
                  own_frame=True, own_acc=True)


def first_pass(offsets, counts, field, done, cols_a, cols_b, rows_a, rows_b, corners_a, corners_b,
               probe, amps, tables, frame, acc, tips_a, tips_b, sums_a, sums_b, edges_a, edges_b, chosen):
    _, nb, tile, length = field.shape
    half = length // 2
    rows = tile + 2 * half
    own = pl.ds(half, tile)
    left, right = by_side("col", cols_a[:tile], cols_b[:tile])
    top = pl.ds(0, half)
    bottom = pl.ds(half + tile, half)
    for part in (0, 1):
        for b in range(nb):
            frame[part, b + 1, own, :] = field[part, b]
            at = pl.ds((part * nb + b) * half, half)
            frame[part, b + 1, top, :], frame[part, b + 1, bottom, :] = by_side(
                "row", rows_a[at, :], rows_b[at, :])
        frame[part, 0, own, :] = swap(left, half) if part else left
        frame[part, nb + 1, own, :] = swap(right, half) if part else right
        at = pl.ds(part * half, half)
        ends = by_side("row", corners_a[at, :], corners_b[at, :])
        for block in (0, nb + 1):
            frame[part, block, top, :], frame[part, block, bottom, :] = ends
    empty = jnp.zeros((half, length), jnp.float32)
    for part in (0, 1):
        for b in range(nb + 2):
            acc[part, b, top, :] = empty
            acc[part, b, bottom, :] = empty
            acc[part, b, own, :] = (
                done[part, b - 1] if 0 < b <= nb else jnp.zeros((tile, length), jnp.float32))
    found, _ = first_list(chosen, offsets, counts, tile, length)
    add_gradients(frame, acc, probe, amps, offsets, tables, chosen, found)
    low = lanes((rows, length)) < half
    for part in (0, 1):
        strip_a, strip_b = by_pairs(
            "col",
            jnp.where(low, acc[part, 1], acc[part, 0]),
            jnp.where(low, acc[part, nb + 1], acc[part, nb]),
        )
        for strip, tips, sums in ((strip_a, tips_a, sums_a), (strip_b, tips_b, sums_b)):
            tips[part, 0] = strip[:length]
            tips[part, 1] = strip[rows - length:]
            sums[part] = strip[length:rows - length]
    near = lanes((length, length)) < half
    for part in (0, 1):
        for b in range(nb - 1):
            ends = [
                acc[part, b + 2, at, :] if b < nb - 2
                else jnp.where(near, acc[part, nb, at, :], acc[part, 1, at, :])
                for at in (pl.ds(0, length), pl.ds(rows - length, length))
            ]
            edges_a[part, b], edges_b[part, b] = by_pairs("row", *ends)


def middle_corners(mine_a, mine_b, tips_a, tips_b, after, corners, *, odd_pairs):
    for part in (0, 1):
        up, down = [
            by_side("col", mine_a[part, k] + tips_a[part, k], mine_b[part, k] + tips_b[part, k])
            for k in (0, 1)
        ]
        for side in (0, 1):
            corners[part, side] = by_pairs("row", up[side], down[side])[0 if odd_pairs else 1]


def light_pass(mine, cols_a, cols_b, rows_a, rows_b, corners_a, corners_b, probe, after,
               inverse, light, power, places, listed, chosen, sem, *, npos):
    length = probe.shape[-1]
    half = length // 2
    blocks, rows, _ = inverse.shape
    nb = blocks - 2
    tile = nb * length
    my_row = lax.axis_index("row")
    my_col = lax.axis_index("col")
    sources = (mine, cols_a, cols_b, rows_a, rows_b, corners_a, corners_b)
    for k, source in enumerate(sources):
        given = source[source.shape[0] - 8:, :].astype(jnp.int32)
        col = pltpu.roll(given, length - npos, 1) - (my_col + 1) * tile + 2 * length
        row = given - (my_row + 1) * tile + half + length
        near = (given > 0) & (row > 0) & (row < rows + length)
        near = near & (col > length - half) & (col < 2 * length + tile + half)
        places[pl.ds(8 * k, 8), :] = jnp.where(near, row * 4 * tile + col, 0)
    copy = pltpu.make_async_copy(places, listed, sem)
    copy.start()
    for b in range(blocks):
        light[b + 1, pl.ds(length, rows), :] = jnp.zeros((rows, length), jnp.float32)
    power[...] = probe[0] * probe[0] + probe[1] * probe[1]
    lane = lanes((length, length))
    copy.wait()

    def look(index, found):
        line = jnp.where(index < len(sources), 8 * index, 8 * (index - 2) + 1)
        for slot in range(npos):
            place = listed[line, slot]
            chosen[found] = place
            found = found + jnp.where(place > 0, 1, 0)
        return found

    found = lax.fori_loop(0, len(sources) + 2, look, 0)

    def put(index, carry):
        place = chosen[index]
        start = lax.div(place, 4 * tile)
        col = lax.rem(place, 4 * tile)
        block = lax.div(col, length)
        shift = lax.rem(col, length)
        value = pltpu.roll(power[...], shift, 1)
        inside = lane >= shift
        light[block, pl.ds(start, length), :] += jnp.where(inside, value, 0.0)
        light[block + 1, pl.ds(start, length), :] += jnp.where(inside, 0.0, value)
        return carry

    lax.fori_loop(0, found, put, 0)
    spot = lax.broadcasted_iota(jnp.int32, (rows, length), 0)
    keep_from = jnp.where(my_row > 0, 0, half)
    keep_to = jnp.where(my_row < lax.axis_size("row") - 1, rows, rows - half)
    kept = (spot >= keep_from) & (spot < keep_to)
    for b in range(blocks):
        value = 1.0 / (light[b + 1, pl.ds(length, rows), :] + 1.0)
        keep = kept
        if b == 0:
            keep = keep & (my_col > 0)
        if b == nb + 1:
            keep = keep & (my_col < lax.axis_size("col") - 1)
        inverse[b] = jnp.where(keep, value, 0.0)


def update_pass(offsets, counts, after, frame, acc, inverse, tips_a, tips_b, sums_a, sums_b, probe, amps, tables,
                work, total, chosen):
    _, blocks, rows, length = frame.shape
    half = length // 2
    nb = blocks - 2
    work[...] = acc[...]
    _, done = first_list(chosen, offsets, counts, nb * length, length)
    found, _ = collect(chosen, 0, offsets, counts, nb * length, length, clear, done)
    add_gradients(frame, work, probe, amps, offsets, tables, chosen, found)
    low = lanes((rows, length)) < half
    for part in (0, 1):
        left, right = by_side("col", *[
            above(above(tips[part, 0], sums[part]), tips[part, 1])
            for tips, sums in ((tips_a, sums_a), (tips_b, sums_b))
        ])
        for b in range(blocks):
            value = work[part, b]
            if b == 0:
                value = value + left
            if b == 1:
                value = value + jnp.where(low, left, 0.0)
            if b == nb:
                value = value + jnp.where(low, 0.0, right)
            if b == nb + 1:
                value = value + right
            work[part, b] = frame[part, b] + value * inverse[b]
    total[...] = jnp.zeros_like(total)
    found = choose(chosen, offsets, counts, nb * length, length, lambda mid_row, **_: mid_row)
    add_gradients(work, total, probe, amps, offsets, tables, chosen, found)


def second_pass(offsets, counts, work_from, total_from, inverse, edges_a, edges_b,
                corners_a, corners_b, probe, amps, tables,
                work, sums, cols_a, cols_b, rows_a, rows_b, total, chosen):
    _, blocks, rows, length = work.shape
    half = length // 2
    nb = blocks - 2
    tile = nb * length
    near = lanes((length, length)) < half
    middle = pl.ds(length, rows - 2 * length)
    for part in (0, 1):
        edges = [by_side("row", edges_a[part, b], edges_b[part, b]) for b in range(nb - 1)]
        corners = [by_side("row", corners_a[part, side], corners_b[part, side]) for side in (0, 1)]
        for k, at in enumerate((pl.ds(0, length), pl.ds(rows - length, length))):
            left, right, ends = corners[0][k], corners[1][k], edges[nb - 2][k]
            add = [left, jnp.where(near, left, ends)]
            add += [edges[b][k] for b in range(nb - 2)]
            add += [jnp.where(near, ends, right), right]
            for b in range(blocks):
                work[part, b, at, :] = work_from[part, b, at, :] + add[b] * inverse[b, at, :]
        for b in range(blocks):
            work[part, b, middle, :] = work_from[part, b, middle, :]
    total[...] = total_from[...]
    found = choose(
        chosen, offsets, counts, tile, length,
        lambda mid_row, cross_row, cross_col, **_: ~mid_row & (cross_row | cross_col))
    add_gradients(work, total, probe, amps, offsets, tables, chosen, found)
    low = lanes((rows, length)) < half
    cols_a[...], cols_b[...] = by_pairs(
        "col",
        jnp.where(low, swap(total[1, 0], half), total[0, 0]),
        jnp.where(low, total[0, nb + 1], swap(total[1, nb + 1], half)),
    )
    for part in (0, 1):
        for b in range(nb):
            sums[part, b] = total[part, b + 1, pl.ds(half, tile), :]
            rows_a[part, b], rows_b[part, b] = by_pairs(
                "row", total[part, b + 1, :half, :], total[part, b + 1, half + tile:, :])


def inner_pass(offsets, counts, work, probe, amps, tables, sums, chosen):
    _, nb, tile, length = sums.shape
    sums[...] = jnp.zeros_like(sums)
    found = choose(
        chosen, offsets, counts, tile, length,
        lambda mid_row, cross_row, cross_col, **_: ~mid_row & ~cross_row & ~cross_col)
    add_gradients(work, sums, probe, amps, offsets, tables, chosen, found, own_acc=True)


def end_corners(cols_a, cols_b, corners_a, corners_b):
    rows, length = cols_a.shape
    half = length // 2
    for side, value in enumerate(by_side("col", cols_a[...], cols_b[...])):
        corners_a[side], corners_b[side] = by_pairs("row", value[:half], value[rows - half:])


def last_pass(work, sums, inner, inverse, cols_a, cols_b, rows_a, rows_b, corners_a, corners_b,
              out, result, sems):
    _, nb, tile, length = sums.shape
    half = length // 2
    low = lanes((tile, length)) < half
    own = pl.ds(half, tile)
    gap = jnp.zeros((tile - 2 * half, length), jnp.float32)
    sides = []
    for side, value in enumerate(by_side("col", cols_a[own, :], cols_b[own, :])):
        up, down = by_side("row", corners_a[side], corners_b[side])
        sides.append(value + above(above(up, gap), down))
    left, right = sides
    copies = []
    for part in (0, 1):
        if part:
            left, right = swap(left, half), swap(right, half)
        for b in range(nb):
            up, down = by_side("row", rows_a[part, b], rows_b[part, b])
            value = sums[part, b] + inner[part, b] + above(above(up, gap), down)
            if b == 0:
                value = value + jnp.where(low, left, 0.0)
            if b == nb - 1:
                value = value + jnp.where(low, 0.0, right)
            result[part, b] = work[part, b + 1, own, :] + value * inverse[b + 1, own, :]
            copy = pltpu.make_async_copy(
                result.at[part, b], out.at[part, :, b * length:(b + 1) * length],
                sems.at[part * nb + b])
            copy.start()
            copies.append(copy)
    for copy in copies:
        copy.wait()


def whole(memory_space=pltpu.VMEM):
    return pl.BlockSpec(memory_space=memory_space)


def call(body, shapes, places, scratch=(), cost=None):
    return pl.pallas_call(
        body,
        out_shape=[jax.ShapeDtypeStruct(shape, jnp.float32) for shape in shapes],
        in_specs=[whole({"s": pltpu.SMEM, "v": pltpu.VMEM, "a": pl.ANY, "h": pltpu.HBM}[p]) for p in places],
        out_specs=[whole()] * len(shapes),
        scratch_shapes=list(scratch),
        compiler_params=pltpu.CompilerParams(vmem_limit_bytes=VMEM_BYTES),
        cost_estimate=cost,
    )


def swap_pairs(first, second, axis):
    count = lax.axis_size(axis)
    got = []
    for value, start in ((first, 1), (second, 0)):
        pairs = [(i, i + 1) for i in range(start, count - 1, 2)]
        got.append(lax.ppermute(value, axis, pairs + [(b, a) for a, b in pairs]))
    return got


def shards(object_field, probe, amplitudes, offsets, counts):
    length = probe.shape[-1]
    half = length // 2
    tile = object_field.shape[1]
    npos = offsets.shape[2]
    nb = tile // length
    blocks = nb + 2
    rows = tile + 2 * half
    tables = jnp.asarray(dft_tables(length))
    offsets = jnp.swapaxes(offsets, 2, 3)

    def cost(positions):
        steps = 4 * 3 * 2 * length * (2 * length) ** 2
        return pl.CostEstimate(
            flops=positions * steps, bytes_accessed=8_000_000,
            transcendentals=positions * length * length)

    memory = pltpu.VMEM
    chosen = pltpu.SMEM((npos + GROUP,), jnp.int32)
    strip = (tile + 8, length)
    edge = (2 * nb * half + 8, length)
    def kept(array):
        return pltpu.with_memory_space_constraint(array, pltpu.HBM)

    field, cols_a, cols_b, rows_a, rows_b = call(
        start_pass, [(2, nb, tile, length), strip, strip, edge, edge], "hhs",
        [pltpu.SMEM((1, 1, 2, npos), jnp.int32), pltpu.SemaphoreType.DMA((nb + 1,))],
    )(kept(object_field), kept(offsets), counts)
    mine = cols_a
    probe, amplitudes, tables = pl.pallas_call(
        fetch_pass,
        out_shape=[
            jax.ShapeDtypeStruct(array.shape, array.dtype) for array in (probe, amplitudes, tables)],
        in_specs=[whole(pl.ANY)] + [whole(pltpu.HBM)] * 3,
        out_specs=[whole()] * 3,
        scratch_shapes=[pltpu.SemaphoreType.DMA((3,))],
        compiler_params=pltpu.CompilerParams(vmem_limit_bytes=VMEM_BYTES),
        cost_estimate=cost(1),
    )(cols_a, kept(probe), kept(amplitudes), kept(tables))
    cols_a, cols_b = swap_pairs(cols_a, cols_b, "col")
    rows_a, rows_b = swap_pairs(rows_a, rows_b, "row")
    corner = (2 * half + 8, length)
    corners_a, corners_b = call(start_corners, [corner, corner], "vva")(cols_a, cols_b, probe)
    (done,) = call(
        early_pass, [(2, nb, tile, length)], "ssavvvv", [chosen], cost(GROUP),
    )(offsets, counts, corners_b, field, probe, amplitudes, tables)
    corners_a, corners_b = swap_pairs(corners_a, corners_b, "row")

    full = (2, blocks, rows, length)
    strip = (2, rows, length)
    edge = (2, nb - 1, length, length)
    tip = (2, 2, length, length)
    strip = (2, rows - 2 * length, length)
    frame, acc, tips_a, tips_b, sums_a, sums_b, edges_a, edges_b = call(
        first_pass, [full, full, tip, tip, strip, strip, edge, edge], "ss" + 11 * "v", [chosen],
    )(offsets, counts, field, done, cols_a, cols_b, rows_a, rows_b, corners_a, corners_b,
      probe, amplitudes, tables)
    info = (mine, cols_a, cols_b, rows_a, rows_b, corners_a, corners_b)
    mine_a, mine_b = tips_a, tips_b
    tips_a, tips_b = swap_pairs(tips_a, tips_b, "col")
    edges_a, edges_b = swap_pairs(edges_a, edges_b, "row")
    sums_a, sums_b = swap_pairs(sums_a, sums_b, "col")
    (inverse,) = call(
        functools.partial(light_pass, npos=npos), [(blocks, rows, length)], 8 * "v" + "a",
        [memory((blocks + 2, rows + 2 * length, length), jnp.float32),
         memory((length, length), jnp.float32), memory((7 * 8, length), jnp.int32),
         pltpu.SMEM((7 * 8, length), jnp.int32), pltpu.SMEM((9 * npos + 1,), jnp.int32),
         pltpu.SemaphoreType.DMA],
        cost(npos // 2),
    )(*info, probe, tips_b)
    corners_a, corners_b = [
        call(functools.partial(middle_corners, odd_pairs=odd_pairs), [tip], "vvvva")(
            mine_a, mine_b, tips_a, tips_b, after)[0]
        for odd_pairs, after in ((True, acc), (False, inverse))
    ]
    corners_a, corners_b = swap_pairs(corners_a, corners_b, "row")

    work, total = call(update_pass, [full, full], "ssa" + 10 * "v", [chosen], cost(npos // 2))(
        offsets, counts, edges_a, frame, acc, inverse, tips_a, tips_b, sums_a, sums_b,
        probe, amplitudes, tables)
    strip = (rows, length)
    own = (2, nb, tile, length)
    edge = (2, nb, half, length)
    work, sums, cols_a, cols_b, rows_a, rows_b = call(
        second_pass, [full, own, strip, strip, edge, edge], "ss" + 10 * "v",
        [memory(full, jnp.float32), chosen], cost(npos // 2),
    )(offsets, counts, work, total, inverse, edges_a, edges_b, corners_a, corners_b,
      probe, amplitudes, tables)
    cols_a, cols_b = swap_pairs(cols_a, cols_b, "col")
    rows_a, rows_b = swap_pairs(rows_a, rows_b, "row")
    (inner,) = call(inner_pass, [own], "ss" + 4 * "v", [chosen], cost(npos // 4))(
        offsets, counts, work, probe, amplitudes, tables)
    corner = (2, half, length)
    corners_a, corners_b = call(end_corners, [corner, corner], "vv")(cols_a, cols_b)
    corners_a, corners_b = swap_pairs(corners_a, corners_b, "row")
    out = pl.pallas_call(
        last_pass,
        out_shape=jax.ShapeDtypeStruct((2, tile, tile), jnp.float32),
        in_specs=[whole()] * 10,
        out_specs=whole(pl.ANY),
        scratch_shapes=[memory(own, jnp.float32), pltpu.SemaphoreType.DMA((2 * nb,))],
        compiler_params=pltpu.CompilerParams(vmem_limit_bytes=VMEM_BYTES),
    )(work, sums, inner, inverse, cols_a, cols_b, rows_a, rows_b, corners_a, corners_b)
    return out


def solution(mesh):
    placed = (
        P(None, "row", "col"),
        P(),
        P("row", "col", None, None, None),
        P("row", "col", None, None),
        P("row", "col"),
    )
    return jax.shard_map(
        shards, mesh=mesh, in_specs=placed, out_specs=P(None, "row", "col"), check_vma=False
    )
```

```python
import functools
import math

import jax
import jax.numpy as jnp
import numpy as np
from jax import lax
from jax.experimental import pallas as pl
from jax.experimental.pallas import tpu as pltpu
from jax.sharding import PartitionSpec as P

ITERS = 2
FLOOR = 0.25
VMEM_BYTES = 16 * 1024 * 1024
GROUP = 4
CHAIN = 2


def split(value):
    high = value.astype(jnp.bfloat16)
    low = (value - high.astype(jnp.float32)).astype(jnp.bfloat16)
    return high, low


def dft_tables(length):
    index = np.arange(length)
    angle = (index[:, None] * index[None, :] % length) * (2.0 * math.pi / length)
    cosine = np.cos(angle) / math.sqrt(length)
    sine = np.sin(angle) / math.sqrt(length)
    ahead = np.block([[cosine, -sine], [sine, cosine]])
    parts = []
    for table in (ahead, ahead.T):
        high = table.astype(jnp.bfloat16)
        low = (table - high.astype(np.float64)).astype(jnp.bfloat16)
        parts += [high, low]
    return np.stack(parts)


def lanes(shape):
    return lax.broadcasted_iota(jnp.int32, shape, len(shape) - 1)


def swap(value, half):
    return pltpu.roll(value, half, value.ndim - 1)


def odd_place(axis):
    return lax.axis_index(axis) % 2 == 1


def by_pairs(axis, low, high):
    odd = odd_place(axis)
    return jnp.where(odd, high, low), jnp.where(odd, low, high)


def by_side(axis, first, second):
    odd = odd_place(axis)
    return jnp.where(odd, second, first), jnp.where(odd, first, second)


def times_right(rows, high, low):
    top, rest = split(rows)
    left = jnp.concatenate([top, top, rest], axis=1)
    right = jnp.concatenate([high, low, high], axis=0)
    return jnp.dot(left, right, preferred_element_type=jnp.float32)


def times_left(high, low, columns):
    top, rest = split(columns)
    left = jnp.concatenate([high, low, high], axis=1)
    right = jnp.concatenate([top, top, rest], axis=0)
    return jnp.dot(left, right, preferred_element_type=jnp.float32)


def beside(left, right):
    return jnp.concatenate([left, right], axis=1)


def above(top, bottom):
    return jnp.concatenate([top, bottom], axis=0)


def touching(mid_row, mid_col, cross_row, cross_col):
    return ~(mid_row & mid_col) & (cross_row | cross_col)


def early(mid_row, mid_col, cross_row, cross_col):
    return ~(mid_row & mid_col) & ~(cross_row | cross_col)


def clear(mid_row, mid_col, cross_row, cross_col):
    return mid_row & mid_col


def collect(chosen, found, offsets, counts, tile, length, wanted, begin=0, end=None):
    last = tile - length
    half = length // 2

    def look(slot, carry):
        found, seen = carry
        row = offsets[0, 0, 0, slot]
        col = offsets[0, 0, 1, slot]
        taken = wanted(
            mid_row=(row >= half) & (row <= last - half),
            mid_col=(col >= half) & (col <= last - half),
            cross_row=(row < 0) | (row > last),
            cross_col=(col < 0) | (col > last),
        )
        listed = taken & (seen >= begin)
        if end is not None:
            listed = listed & (seen < end)
        chosen[found] = slot
        return found + jnp.where(listed, 1, 0), seen + jnp.where(taken, 1, 0)

    return lax.fori_loop(0, counts[0, 0], look, (found, 0))


def early_list(chosen, *place):
    found, known = collect(chosen, 0, *place, early, 0, GROUP)
    found, _ = collect(chosen, found, *place, clear, 0, GROUP - jnp.minimum(known, GROUP))
    return found


def first_list(chosen, *place):
    found, _ = collect(chosen, 0, *place, touching)
    found, known = collect(chosen, found, *place, early, GROUP)
    begin = GROUP - jnp.minimum(known, GROUP)
    end = begin + lax.rem(CHAIN - lax.rem(found, CHAIN), CHAIN)
    found, _ = collect(chosen, found, *place, clear, begin, end)
    return found, end


def choose(chosen, *place):
    found, _ = collect(chosen, 0, *place)
    return found


def add_gradients(frame, acc, probe_ref, amps, offsets, tables, chosen, found, own_frame=False, own_acc=False):
    length = probe_ref.shape[-1]
    half = length // 2
    lane = lanes((length, length))

    def place(slot, ref, own):
        col = offsets[0, 0, 1, slot] + length
        block = lax.div(col, length)
        row = offsets[0, 0, 0, slot]
        if own:
            block = block - 1
        else:
            row = row + half
        after = jnp.minimum(block + 1, ref.shape[1] - 1)
        return pl.ds(row, length), block, after, lax.rem(col, length)

    def exit_wave(slot):
        at, block, after, shift = place(slot, frame, own_frame)
        inside = lane >= shift
        window = [
            jnp.where(inside, frame[part, block, at, :], frame[part, after, at, :])
            for part in (0, 1)
        ]
        probe = (pltpu.roll(probe_ref[0], shift, 1), pltpu.roll(probe_ref[1], shift, 1))
        wave = (probe[0] * window[0] - probe[1] * window[1],
                probe[0] * window[1] + probe[1] * window[0])
        return probe, wave

    def shrink(real, imag, slot):
        ratio = amps[0, 0, slot] * lax.rsqrt(real * real + imag * imag + FLOOR) - 1.0
        return real * ratio, imag * ratio

    def put(slot, live, probe, back_r, back_i):
        at, block, after, shift = place(slot, acc, own_acc)
        grads = (probe[0] * back_r + probe[1] * back_i, probe[0] * back_i - probe[1] * back_r)
        bound = jnp.where(live, shift, length)
        inside = lane >= bound
        beyond = lane < jnp.where(live, shift, 0)
        for part in (0, 1):
            acc[part, block, at, :] += jnp.where(inside, grads[part], 0.0)
            acc[part, after, at, :] += jnp.where(beyond, grads[part], 0.0)

    def work(slots):
        probes, waves = zip(*[exit_wave(slot) for slot in slots])
        rows = jnp.concatenate([beside(*wave) for wave in waves], axis=0)
        mid = times_right(rows, tables[0], tables[1])
        yield None
        mids = [mid[k * length:(k + 1) * length] for k in range(len(slots))]
        columns = above(
            jnp.concatenate([m[:, :length] for m in mids], axis=1),
            jnp.concatenate([m[:, length:] for m in mids], axis=1),
        )
        far = times_left(tables[2], tables[3], columns)
        yield None
        changes = [
            shrink(far[:length, k * length:(k + 1) * length],
                   far[length:, k * length:(k + 1) * length], slot)
            for k, slot in enumerate(slots)
        ]
        columns = above(
            jnp.concatenate([c[0] for c in changes], axis=1),
            jnp.concatenate([c[1] for c in changes], axis=1),
        )
        mid = times_left(tables[0], tables[1], columns)
        yield None
        rows = jnp.concatenate(
            [
                beside(mid[:length, k * length:(k + 1) * length],
                       mid[length:, k * length:(k + 1) * length])
                for k in range(len(slots))
            ],
            axis=0,
        )
        back = times_right(rows, tables[2], tables[3])
        yield None
        yield [
            (probes[k], back[k * length:(k + 1) * length, :length],
             back[k * length:(k + 1) * length, length:])
            for k in range(len(slots))
        ]

    def run(first, count):
        places = [first + k for k in range(count)]
        slots = [chosen[jnp.where(at < found, at, 0)] for at in places]
        chains = [work(slots[k:k + CHAIN]) for k in range(0, count, CHAIN)]
        gradients = [None]
        while gradients[0] is None:
            gradients = [next(chain) for chain in chains]
        gradients = [gradient for chain in gradients for gradient in chain]
        for at, slot, gradient in zip(places, slots, gradients):
            put(slot, at < found, *gradient)

    def step(index, carry):
        run(index * GROUP, GROUP)
        return carry

    steps = lax.div(found + GROUP - CHAIN - 1, GROUP)
    lax.fori_loop(0, steps, step, 0)

    @pl.when(found > steps * GROUP)
    def _():
        run(steps * GROUP, CHAIN)


def start_pass(field, offsets_from, counts, tile_out, cols_a, cols_b, rows_a, rows_b, offsets, sems):
    _, nb, tile, length = tile_out.shape
    half = length // 2
    npos = offsets.shape[3]
    listed = pltpu.make_async_copy(offsets_from, offsets, sems.at[nb])
    listed.start()
    copies = [
        pltpu.make_async_copy(
            field.at[:, :, b * length:(b + 1) * length], tile_out.at[:, b], sems.at[b])
        for b in range(nb)
    ]
    for copy in copies:
        copy.start()
    listed.wait()
    spot = lanes((8, length))
    info = jnp.zeros((8, length), jnp.int32)
    down = (lax.axis_index("row") + 1) * tile
    across = (lax.axis_index("col") + 1) * tile
    for k in range(npos):
        live = k < counts[0, 0]
        info = jnp.where(spot == k, jnp.where(live, offsets[0, 0, 0, k] + down, 0), info)
        info = jnp.where(spot == npos + k, jnp.where(live, offsets[0, 0, 1, k] + across, 0), info)
    info = info.astype(jnp.float32)
    for end in (cols_a, cols_b, rows_a, rows_b):
        end[pl.ds(end.shape[0] - 8, 8), :] = info
    for copy in copies:
        copy.wait()
    low = lanes((tile, length)) < half
    to_left = jnp.where(low, tile_out[0, 0], swap(tile_out[1, 0], half))
    to_right = jnp.where(low, swap(tile_out[1, nb - 1], half), tile_out[0, nb - 1])
    cols_a[:tile], cols_b[:tile] = by_pairs("col", to_left, to_right)
    for part in (0, 1):
        for b in range(nb):
            at = pl.ds((part * nb + b) * half, half)
            rows_a[at, :], rows_b[at, :] = by_pairs(
                "row", tile_out[part, b, :half], tile_out[part, b, tile - half:])


def start_corners(cols_a, cols_b, after, corners_a, corners_b):
    length = cols_a.shape[1]
    half = length // 2
    tile = cols_a.shape[0] - 8
    low = lanes((tile, length)) < half
    left, right = by_side("col", cols_a[:tile], cols_b[:tile])
    for part in (0, 1):
        if part:
            left, right = swap(left, half), swap(right, half)
        value = jnp.where(low, right, left)
        at = pl.ds(part * half, half)
        corners_a[at, :], corners_b[at, :] = by_pairs("row", value[:half], value[tile - half:])
    first = lax.broadcasted_iota(jnp.int32, (8, length), 0) == 0
    info = jnp.where(first, cols_a[tile:], cols_b[tile:])
    corners_a[2 * half:] = info
    corners_b[2 * half:] = info


def fetch_pass(after, probe_from, amps_from, tables_from, probe, amps, tables, sems):
    copies = [
        pltpu.make_async_copy(source, target, sems.at[k])
        for k, (source, target) in enumerate(
            ((amps_from, amps), (tables_from, tables), (probe_from, probe)))
    ]
    for copy in copies:
        copy.start()
    for copy in copies:
        copy.wait()


def early_pass(offsets, counts, after, field, probe, amps, tables, acc, chosen):
    _, nb, tile, length = field.shape
    acc[...] = jnp.zeros_like(acc)
    found = early_list(chosen, offsets, counts, tile, length)
    add_gradients(field, acc, probe, amps, offsets, tables, chosen, found,
                  own_frame=True, own_acc=True)


def first_pass(offsets, counts, field, done, cols_a, cols_b, rows_a, rows_b, corners_a, corners_b,
               probe, amps, tables, frame, acc, tips_a, tips_b, sums_a, sums_b, edges_a, edges_b, chosen):
    _, nb, tile, length = field.shape
    half = length // 2
    rows = tile + 2 * half
    own = pl.ds(half, tile)
    left, right = by_side("col", cols_a[:tile], cols_b[:tile])
    top = pl.ds(0, half)
    bottom = pl.ds(half + tile, half)
    for part in (0, 1):
        for b in range(nb):
            frame[part, b + 1, own, :] = field[part, b]
            at = pl.ds((part * nb + b) * half, half)
            frame[part, b + 1, top, :], frame[part, b + 1, bottom, :] = by_side(
                "row", rows_a[at, :], rows_b[at, :])
        frame[part, 0, own, :] = swap(left, half) if part else left
        frame[part, nb + 1, own, :] = swap(right, half) if part else right
        at = pl.ds(part * half, half)
        ends = by_side("row", corners_a[at, :], corners_b[at, :])
        for block in (0, nb + 1):
            frame[part, block, top, :], frame[part, block, bottom, :] = ends
    empty = jnp.zeros((half, length), jnp.float32)
    for part in (0, 1):
        for b in range(nb + 2):
            acc[part, b, top, :] = empty
            acc[part, b, bottom, :] = empty
            acc[part, b, own, :] = (
                done[part, b - 1] if 0 < b <= nb else jnp.zeros((tile, length), jnp.float32))
    found, _ = first_list(chosen, offsets, counts, tile, length)
    add_gradients(frame, acc, probe, amps, offsets, tables, chosen, found)
    low = lanes((rows, length)) < half
    for part in (0, 1):
        strip_a, strip_b = by_pairs(
            "col",
            jnp.where(low, acc[part, 1], acc[part, 0]),
            jnp.where(low, acc[part, nb + 1], acc[part, nb]),
        )
        for strip, tips, sums in ((strip_a, tips_a, sums_a), (strip_b, tips_b, sums_b)):
            tips[part, 0] = strip[:length]
            tips[part, 1] = strip[rows - length:]
            sums[part] = strip[length:rows - length]
    near = lanes((length, length)) < half
    for part in (0, 1):
        for b in range(nb - 1):
            ends = [
                acc[part, b + 2, at, :] if b < nb - 2
                else jnp.where(near, acc[part, nb, at, :], acc[part, 1, at, :])
                for at in (pl.ds(0, length), pl.ds(rows - length, length))
            ]
            edges_a[part, b], edges_b[part, b] = by_pairs("row", *ends)


def middle_corners(mine_a, mine_b, tips_a, tips_b, after, corners, *, odd_pairs):
    for part in (0, 1):
        up, down = [
            by_side("col", mine_a[part, k] + tips_a[part, k], mine_b[part, k] + tips_b[part, k])
            for k in (0, 1)
        ]
        for side in (0, 1):
            corners[part, side] = by_pairs("row", up[side], down[side])[0 if odd_pairs else 1]


def light_pass(mine, cols_a, cols_b, rows_a, rows_b, corners_a, corners_b, probe, after,
               inverse, light, power, places, listed, chosen, sem, *, npos):
    length = probe.shape[-1]
    half = length // 2
    blocks, rows, _ = inverse.shape
    nb = blocks - 2
    tile = nb * length
    my_row = lax.axis_index("row")
    my_col = lax.axis_index("col")
    sources = (mine, cols_a, cols_b, rows_a, rows_b, corners_a, corners_b)
    for k, source in enumerate(sources):
        given = source[source.shape[0] - 8:, :].astype(jnp.int32)
        col = pltpu.roll(given, length - npos, 1) - (my_col + 1) * tile + 2 * length
        row = given - (my_row + 1) * tile + half + length
        near = (given > 0) & (row > 0) & (row < rows + length)
        near = near & (col > length - half) & (col < 2 * length + tile + half)
        places[pl.ds(8 * k, 8), :] = jnp.where(near, row * 4 * tile + col, 0)
    copy = pltpu.make_async_copy(places, listed, sem)
    copy.start()
    for b in range(blocks):
        light[b + 1, pl.ds(length, rows), :] = jnp.zeros((rows, length), jnp.float32)
    power[...] = probe[0] * probe[0] + probe[1] * probe[1]
    lane = lanes((length, length))
    copy.wait()

    def look(index, found):
        line = jnp.where(index < len(sources), 8 * index, 8 * (index - 2) + 1)
        for slot in range(npos):
            place = listed[line, slot]
            chosen[found] = place
            found = found + jnp.where(place > 0, 1, 0)
        return found

    found = lax.fori_loop(0, len(sources) + 2, look, 0)

    def put(index, carry):
        place = chosen[index]
        start = lax.div(place, 4 * tile)
        col = lax.rem(place, 4 * tile)
        block = lax.div(col, length)
        shift = lax.rem(col, length)
        value = pltpu.roll(power[...], shift, 1)
        inside = lane >= shift
        light[block, pl.ds(start, length), :] += jnp.where(inside, value, 0.0)
        light[block + 1, pl.ds(start, length), :] += jnp.where(inside, 0.0, value)
        return carry

    lax.fori_loop(0, found, put, 0)
    spot = lax.broadcasted_iota(jnp.int32, (rows, length), 0)
    keep_from = jnp.where(my_row > 0, 0, half)
    keep_to = jnp.where(my_row < lax.axis_size("row") - 1, rows, rows - half)
    kept = (spot >= keep_from) & (spot < keep_to)
    for b in range(blocks):
        value = 1.0 / (light[b + 1, pl.ds(length, rows), :] + 1.0)
        keep = kept
        if b == 0:
            keep = keep & (my_col > 0)
        if b == nb + 1:
            keep = keep & (my_col < lax.axis_size("col") - 1)
        inverse[b] = jnp.where(keep, value, 0.0)


def update_pass(offsets, counts, after, frame, acc, inverse, tips_a, tips_b, sums_a, sums_b, probe, amps, tables,
                work, total, chosen):
    _, blocks, rows, length = frame.shape
    half = length // 2
    nb = blocks - 2
    work[...] = acc[...]
    _, done = first_list(chosen, offsets, counts, nb * length, length)
    found, _ = collect(chosen, 0, offsets, counts, nb * length, length, clear, done)
    add_gradients(frame, work, probe, amps, offsets, tables, chosen, found)
    low = lanes((rows, length)) < half
    for part in (0, 1):
        left, right = by_side("col", *[
            above(above(tips[part, 0], sums[part]), tips[part, 1])
            for tips, sums in ((tips_a, sums_a), (tips_b, sums_b))
        ])
        for b in range(blocks):
            value = work[part, b]
            if b == 0:
                value = value + left
            if b == 1:
                value = value + jnp.where(low, left, 0.0)
            if b == nb:
                value = value + jnp.where(low, 0.0, right)
            if b == nb + 1:
                value = value + right
            work[part, b] = frame[part, b] + value * inverse[b]
    total[...] = jnp.zeros_like(total)
    found = choose(chosen, offsets, counts, nb * length, length, lambda mid_row, **_: mid_row)
    add_gradients(work, total, probe, amps, offsets, tables, chosen, found)


def second_pass(offsets, counts, work_from, total_from, inverse, edges_a, edges_b,
                corners_a, corners_b, probe, amps, tables,
                work, total, cols_a, cols_b, rows_a, rows_b, chosen):
    _, blocks, rows, length = work.shape
    half = length // 2
    nb = blocks - 2
    tile = nb * length
    near = lanes((length, length)) < half
    middle = pl.ds(length, rows - 2 * length)
    for part in (0, 1):
        edges = [by_side("row", edges_a[part, b], edges_b[part, b]) for b in range(nb - 1)]
        corners = [by_side("row", corners_a[part, side], corners_b[part, side]) for side in (0, 1)]
        for k, at in enumerate((pl.ds(0, length), pl.ds(rows - length, length))):
            left, right, ends = corners[0][k], corners[1][k], edges[nb - 2][k]
            add = [left, jnp.where(near, left, ends)]
            add += [edges[b][k] for b in range(nb - 2)]
            add += [jnp.where(near, ends, right), right]
            for b in range(blocks):
                work[part, b, at, :] = work_from[part, b, at, :] + add[b] * inverse[b, at, :]
        for b in range(blocks):
            work[part, b, middle, :] = work_from[part, b, middle, :]
    total[...] = total_from[...]
    found = choose(
        chosen, offsets, counts, tile, length,
        lambda mid_row, cross_row, cross_col, **_: ~mid_row & (cross_row | cross_col))
    add_gradients(work, total, probe, amps, offsets, tables, chosen, found)
    low = lanes((rows, length)) < half
    cols_a[...], cols_b[...] = by_pairs(
        "col",
        jnp.where(low, swap(total[1, 0], half), total[0, 0]),
        jnp.where(low, total[0, nb + 1], swap(total[1, nb + 1], half)),
    )
    for part in (0, 1):
        for b in range(nb):
            rows_a[part, b], rows_b[part, b] = by_pairs(
                "row", total[part, b + 1, :half, :], total[part, b + 1, half + tile:, :])


def inner_pass(offsets, counts, work, probe, amps, tables, sums, chosen):
    _, nb, tile, length = sums.shape
    sums[...] = jnp.zeros_like(sums)
    found = choose(
        chosen, offsets, counts, tile, length,
        lambda mid_row, cross_row, cross_col, **_: ~mid_row & ~cross_row & ~cross_col)
    add_gradients(work, sums, probe, amps, offsets, tables, chosen, found, own_acc=True)


def end_corners(cols_a, cols_b, corners_a, corners_b):
    rows, length = cols_a.shape
    half = length // 2
    for side, value in enumerate(by_side("col", cols_a[...], cols_b[...])):
        corners_a[side], corners_b[side] = by_pairs("row", value[:half], value[rows - half:])


def last_pass(work, total, inner, inverse, cols_a, cols_b, rows_a, rows_b, corners_a, corners_b,
              out, result, sems):
    _, nb, tile, length = inner.shape
    half = length // 2
    low = lanes((tile, length)) < half
    own = pl.ds(half, tile)
    gap = jnp.zeros((tile - 2 * half, length), jnp.float32)
    sides = []
    for side, value in enumerate(by_side("col", cols_a[own, :], cols_b[own, :])):
        up, down = by_side("row", corners_a[side], corners_b[side])
        sides.append(value + above(above(up, gap), down))
    left, right = sides
    copies = []
    for part in (0, 1):
        if part:
            left, right = swap(left, half), swap(right, half)
        for b in range(nb):
            up, down = by_side("row", rows_a[part, b], rows_b[part, b])
            value = total[part, b + 1, own, :] + inner[part, b] + above(above(up, gap), down)
            if b == 0:
                value = value + jnp.where(low, left, 0.0)
            if b == nb - 1:
                value = value + jnp.where(low, 0.0, right)
            result[part, b] = work[part, b + 1, own, :] + value * inverse[b + 1, own, :]
            copy = pltpu.make_async_copy(
                result.at[part, b], out.at[part, :, b * length:(b + 1) * length],
                sems.at[part * nb + b])
            copy.start()
            copies.append(copy)
    for copy in copies:
        copy.wait()


def whole(memory_space=pltpu.VMEM):
    return pl.BlockSpec(memory_space=memory_space)


def call(body, shapes, places, scratch=(), cost=None):
    return pl.pallas_call(
        body,
        out_shape=[jax.ShapeDtypeStruct(shape, jnp.float32) for shape in shapes],
        in_specs=[whole({"s": pltpu.SMEM, "v": pltpu.VMEM, "a": pl.ANY, "h": pltpu.HBM}[p]) for p in places],
        out_specs=[whole()] * len(shapes),
        scratch_shapes=list(scratch),
        compiler_params=pltpu.CompilerParams(vmem_limit_bytes=VMEM_BYTES),
        cost_estimate=cost,
    )


def swap_pairs(first, second, axis):
    count = lax.axis_size(axis)
    got = []
    for value, start in ((first, 1), (second, 0)):
        pairs = [(i, i + 1) for i in range(start, count - 1, 2)]
        got.append(lax.ppermute(value, axis, pairs + [(b, a) for a, b in pairs]))
    return got


def shards(object_field, probe, amplitudes, offsets, counts):
    length = probe.shape[-1]
    half = length // 2
    tile = object_field.shape[1]
    npos = offsets.shape[2]
    nb = tile // length
    blocks = nb + 2
    rows = tile + 2 * half
    tables = jnp.asarray(dft_tables(length))
    offsets = jnp.swapaxes(offsets, 2, 3)

    def cost(positions):
        steps = 4 * 3 * 2 * length * (2 * length) ** 2
        return pl.CostEstimate(
            flops=positions * steps, bytes_accessed=8_000_000,
            transcendentals=positions * length * length)

    memory = pltpu.VMEM
    chosen = pltpu.SMEM((npos + GROUP,), jnp.int32)
    strip = (tile + 8, length)
    edge = (2 * nb * half + 8, length)
    def kept(array):
        return pltpu.with_memory_space_constraint(array, pltpu.HBM)

    field, cols_a, cols_b, rows_a, rows_b = call(
        start_pass, [(2, nb, tile, length), strip, strip, edge, edge], "hhs",
        [pltpu.SMEM((1, 1, 2, npos), jnp.int32), pltpu.SemaphoreType.DMA((nb + 1,))],
    )(kept(object_field), kept(offsets), counts)
    mine = cols_a
    probe, amplitudes, tables = pl.pallas_call(
        fetch_pass,
        out_shape=[
            jax.ShapeDtypeStruct(array.shape, array.dtype) for array in (probe, amplitudes, tables)],
        in_specs=[whole(pl.ANY)] + [whole(pltpu.HBM)] * 3,
        out_specs=[whole()] * 3,
        scratch_shapes=[pltpu.SemaphoreType.DMA((3,))],
        compiler_params=pltpu.CompilerParams(vmem_limit_bytes=VMEM_BYTES),
        cost_estimate=cost(1),
    )(cols_a, kept(probe), kept(amplitudes), kept(tables))
    cols_a, cols_b = swap_pairs(cols_a, cols_b, "col")
    rows_a, rows_b = swap_pairs(rows_a, rows_b, "row")
    corner = (2 * half + 8, length)
    corners_a, corners_b = call(start_corners, [corner, corner], "vva")(cols_a, cols_b, probe)
    (done,) = call(
        early_pass, [(2, nb, tile, length)], "ssavvvv", [chosen], cost(GROUP),
    )(offsets, counts, corners_b, field, probe, amplitudes, tables)
    corners_a, corners_b = swap_pairs(corners_a, corners_b, "row")

    full = (2, blocks, rows, length)
    strip = (2, rows, length)
    edge = (2, nb - 1, length, length)
    tip = (2, 2, length, length)
    strip = (2, rows - 2 * length, length)
    frame, acc, tips_a, tips_b, sums_a, sums_b, edges_a, edges_b = call(
        first_pass, [full, full, tip, tip, strip, strip, edge, edge], "ss" + 11 * "v", [chosen],
    )(offsets, counts, field, done, cols_a, cols_b, rows_a, rows_b, corners_a, corners_b,
      probe, amplitudes, tables)
    info = (mine, cols_a, cols_b, rows_a, rows_b, corners_a, corners_b)
    mine_a, mine_b = tips_a, tips_b
    tips_a, tips_b = swap_pairs(tips_a, tips_b, "col")
    edges_a, edges_b = swap_pairs(edges_a, edges_b, "row")
    sums_a, sums_b = swap_pairs(sums_a, sums_b, "col")
    (inverse,) = call(
        functools.partial(light_pass, npos=npos), [(blocks, rows, length)], 8 * "v" + "a",
        [memory((blocks + 2, rows + 2 * length, length), jnp.float32),
         memory((length, length), jnp.float32), memory((7 * 8, length), jnp.int32),
         pltpu.SMEM((7 * 8, length), jnp.int32), pltpu.SMEM((9 * npos + 1,), jnp.int32),
         pltpu.SemaphoreType.DMA],
        cost(npos // 2),
    )(*info, probe, tips_b)
    corners_a, corners_b = [
        call(functools.partial(middle_corners, odd_pairs=odd_pairs), [tip], "vvvva")(
            mine_a, mine_b, tips_a, tips_b, after)[0]
        for odd_pairs, after in ((True, acc), (False, inverse))
    ]
    corners_a, corners_b = swap_pairs(corners_a, corners_b, "row")

    work, total = call(update_pass, [full, full], "ssa" + 10 * "v", [chosen], cost(npos // 2))(
        offsets, counts, edges_a, frame, acc, inverse, tips_a, tips_b, sums_a, sums_b,
        probe, amplitudes, tables)
    strip = (rows, length)
    own = (2, nb, tile, length)
    edge = (2, nb, half, length)
    work, total, cols_a, cols_b, rows_a, rows_b = call(
        second_pass, [full, full, strip, strip, edge, edge], "ss" + 10 * "v",
        [chosen], cost(npos // 2),
    )(offsets, counts, work, total, inverse, edges_a, edges_b, corners_a, corners_b,
      probe, amplitudes, tables)
    cols_a, cols_b = swap_pairs(cols_a, cols_b, "col")
    rows_a, rows_b = swap_pairs(rows_a, rows_b, "row")
    (inner,) = call(inner_pass, [own], "ss" + 4 * "v", [chosen], cost(npos // 4))(
        offsets, counts, work, probe, amplitudes, tables)
    corner = (2, half, length)
    corners_a, corners_b = call(end_corners, [corner, corner], "vv")(cols_a, cols_b)
    corners_a, corners_b = swap_pairs(corners_a, corners_b, "row")
    out = pl.pallas_call(
        last_pass,
        out_shape=jax.ShapeDtypeStruct((2, tile, tile), jnp.float32),
        in_specs=[whole()] * 10,
        out_specs=whole(pl.ANY),
        scratch_shapes=[memory(own, jnp.float32), pltpu.SemaphoreType.DMA((2 * nb,))],
        compiler_params=pltpu.CompilerParams(vmem_limit_bytes=VMEM_BYTES),
    )(work, total, inner, inverse, cols_a, cols_b, rows_a, rows_b, corners_a, corners_b)
    return out


def solution(mesh):
    placed = (
        P(None, "row", "col"),
        P(),
        P("row", "col", None, None, None),
        P("row", "col", None, None),
        P("row", "col"),
    )
    return jax.shard_map(
        shards, mesh=mesh, in_specs=placed, out_specs=P(None, "row", "col"), check_vma=False
    )
```

```python
import functools
import math

import jax
import jax.numpy as jnp
import numpy as np
from jax import lax
from jax.experimental import pallas as pl
from jax.experimental.pallas import tpu as pltpu
from jax.sharding import PartitionSpec as P

ITERS = 2
FLOOR = 0.25
VMEM_BYTES = 16 * 1024 * 1024
GROUP = 4
CHAIN = 2


def split(value):
    high = value.astype(jnp.bfloat16)
    low = (value - high.astype(jnp.float32)).astype(jnp.bfloat16)
    return high, low


def dft_tables(length):
    index = np.arange(length)
    angle = (index[:, None] * index[None, :] % length) * (2.0 * math.pi / length)
    cosine = np.cos(angle) / math.sqrt(length)
    sine = np.sin(angle) / math.sqrt(length)
    ahead = np.block([[cosine, -sine], [sine, cosine]])
    parts = []
    for table in (ahead, ahead.T):
        high = table.astype(jnp.bfloat16)
        low = (table - high.astype(np.float64)).astype(jnp.bfloat16)
        parts += [high, low]
    return np.stack(parts)


def lanes(shape):
    return lax.broadcasted_iota(jnp.int32, shape, len(shape) - 1)


def swap(value, half):
    return pltpu.roll(value, half, value.ndim - 1)


def odd_place(axis):
    return lax.axis_index(axis) % 2 == 1


def by_pairs(axis, low, high):
    odd = odd_place(axis)
    return jnp.where(odd, high, low), jnp.where(odd, low, high)


def by_side(axis, first, second):
    odd = odd_place(axis)
    return jnp.where(odd, second, first), jnp.where(odd, first, second)


def times_right(rows, high, low):
    top, rest = split(rows)
    left = jnp.concatenate([top, top, rest], axis=1)
    right = jnp.concatenate([high, low, high], axis=0)
    return jnp.dot(left, right, preferred_element_type=jnp.float32)


def times_left(high, low, columns):
    top, rest = split(columns)
    left = jnp.concatenate([high, low, high], axis=1)
    right = jnp.concatenate([top, top, rest], axis=0)
    return jnp.dot(left, right, preferred_element_type=jnp.float32)


def beside(left, right):
    return jnp.concatenate([left, right], axis=1)


def above(top, bottom):
    return jnp.concatenate([top, bottom], axis=0)


def touching(mid_row, mid_col, cross_row, cross_col):
    return ~(mid_row & mid_col) & (cross_row | cross_col)


def early(mid_row, mid_col, cross_row, cross_col):
    return ~(mid_row & mid_col) & ~(cross_row | cross_col)


def clear(mid_row, mid_col, cross_row, cross_col):
    return mid_row & mid_col


def collect(chosen, found, offsets, counts, tile, length, wanted, begin=0, end=None):
    last = tile - length
    half = length // 2

    def look(slot, carry):
        found, seen = carry
        row = offsets[0, 0, 0, slot]
        col = offsets[0, 0, 1, slot]
        taken = wanted(
            mid_row=(row >= half) & (row <= last - half),
            mid_col=(col >= half) & (col <= last - half),
            cross_row=(row < 0) | (row > last),
            cross_col=(col < 0) | (col > last),
        )
        listed = taken & (seen >= begin)
        if end is not None:
            listed = listed & (seen < end)
        chosen[found] = slot
        return found + jnp.where(listed, 1, 0), seen + jnp.where(taken, 1, 0)

    return lax.fori_loop(0, counts[0, 0], look, (found, 0))


def early_list(chosen, *place):
    found, known = collect(chosen, 0, *place, early, 0, GROUP)
    found, _ = collect(chosen, found, *place, clear, 0, GROUP - jnp.minimum(known, GROUP))
    return found


def first_list(chosen, *place):
    found, _ = collect(chosen, 0, *place, touching)
    found, known = collect(chosen, found, *place, early, GROUP)
    begin = GROUP - jnp.minimum(known, GROUP)
    end = begin + lax.rem(GROUP - lax.rem(found, GROUP), GROUP)
    found, _ = collect(chosen, found, *place, clear, begin, end)
    return found, end


def choose(chosen, *place):
    found, _ = collect(chosen, 0, *place)
    return found


def add_gradients(frame, acc, probe_ref, amps, offsets, tables, chosen, found, own_frame=False, own_acc=False):
    length = probe_ref.shape[-1]
    half = length // 2
    lane = lanes((length, length))

    def place(slot, ref, own):
        col = offsets[0, 0, 1, slot] + length
        block = lax.div(col, length)
        row = offsets[0, 0, 0, slot]
        if own:
            block = block - 1
        else:
            row = row + half
        after = jnp.minimum(block + 1, ref.shape[1] - 1)
        return pl.ds(row, length), block, after, lax.rem(col, length)

    def exit_wave(slot):
        at, block, after, shift = place(slot, frame, own_frame)
        inside = lane >= shift
        window = [
            jnp.where(inside, frame[part, block, at, :], frame[part, after, at, :])
            for part in (0, 1)
        ]
        probe = (pltpu.roll(probe_ref[0], shift, 1), pltpu.roll(probe_ref[1], shift, 1))
        wave = (probe[0] * window[0] - probe[1] * window[1],
                probe[0] * window[1] + probe[1] * window[0])
        return probe, wave

    def shrink(real, imag, slot):
        ratio = amps[0, 0, slot] * lax.rsqrt(real * real + imag * imag + FLOOR) - 1.0
        return real * ratio, imag * ratio

    def put(slot, live, probe, back_r, back_i):
        at, block, after, shift = place(slot, acc, own_acc)
        grads = (probe[0] * back_r + probe[1] * back_i, probe[0] * back_i - probe[1] * back_r)
        bound = jnp.where(live, shift, length)
        inside = lane >= bound
        beyond = lane < jnp.where(live, shift, 0)
        for part in (0, 1):
            acc[part, block, at, :] += jnp.where(inside, grads[part], 0.0)
            acc[part, after, at, :] += jnp.where(beyond, grads[part], 0.0)

    def work(slots):
        probes, waves = zip(*[exit_wave(slot) for slot in slots])
        rows = jnp.concatenate([beside(*wave) for wave in waves], axis=0)
        mid = times_right(rows, tables[0], tables[1])
        yield None
        mids = [mid[k * length:(k + 1) * length] for k in range(len(slots))]
        columns = above(
            jnp.concatenate([m[:, :length] for m in mids], axis=1),
            jnp.concatenate([m[:, length:] for m in mids], axis=1),
        )
        far = times_left(tables[2], tables[3], columns)
        yield None
        changes = [
            shrink(far[:length, k * length:(k + 1) * length],
                   far[length:, k * length:(k + 1) * length], slot)
            for k, slot in enumerate(slots)
        ]
        columns = above(
            jnp.concatenate([c[0] for c in changes], axis=1),
            jnp.concatenate([c[1] for c in changes], axis=1),
        )
        mid = times_left(tables[0], tables[1], columns)
        yield None
        rows = jnp.concatenate(
            [
                beside(mid[:length, k * length:(k + 1) * length],
                       mid[length:, k * length:(k + 1) * length])
                for k in range(len(slots))
            ],
            axis=0,
        )
        back = times_right(rows, tables[2], tables[3])
        yield None
        yield [
            (probes[k], back[k * length:(k + 1) * length, :length],
             back[k * length:(k + 1) * length, length:])
            for k in range(len(slots))
        ]

    def run(first, count):
        places = [first + k for k in range(count)]
        slots = [chosen[jnp.where(at < found, at, 0)] for at in places]
        chains = [work(slots[k:k + CHAIN]) for k in range(0, count, CHAIN)]
        gradients = [None]
        while gradients[0] is None:
            gradients = [next(chain) for chain in chains]
        gradients = [gradient for chain in gradients for gradient in chain]
        for at, slot, gradient in zip(places, slots, gradients):
            put(slot, at < found, *gradient)

    def step(index, carry):
        run(index * GROUP, GROUP)
        return carry

    steps = lax.div(found + GROUP - CHAIN - 1, GROUP)
    lax.fori_loop(0, steps, step, 0)

    @pl.when(found > steps * GROUP)
    def _():
        run(steps * GROUP, CHAIN)


def start_pass(field, offsets_from, counts, tile_out, cols_a, cols_b, rows_a, rows_b, offsets, sems):
    _, nb, tile, length = tile_out.shape
    half = length // 2
    npos = offsets.shape[3]
    listed = pltpu.make_async_copy(offsets_from, offsets, sems.at[nb])
    listed.start()
    copies = [
        pltpu.make_async_copy(
            field.at[:, :, b * length:(b + 1) * length], tile_out.at[:, b], sems.at[b])
        for b in range(nb)
    ]
    for copy in copies:
        copy.start()
    listed.wait()
    spot = lanes((8, length))
    info = jnp.zeros((8, length), jnp.int32)
    down = (lax.axis_index("row") + 1) * tile
    across = (lax.axis_index("col") + 1) * tile
    for k in range(npos):
        live = k < counts[0, 0]
        info = jnp.where(spot == k, jnp.where(live, offsets[0, 0, 0, k] + down, 0), info)
        info = jnp.where(spot == npos + k, jnp.where(live, offsets[0, 0, 1, k] + across, 0), info)
    info = info.astype(jnp.float32)
    for end in (cols_a, cols_b, rows_a, rows_b):
        end[pl.ds(end.shape[0] - 8, 8), :] = info
    for copy in copies:
        copy.wait()
    low = lanes((tile, length)) < half
    to_left = jnp.where(low, tile_out[0, 0], swap(tile_out[1, 0], half))
    to_right = jnp.where(low, swap(tile_out[1, nb - 1], half), tile_out[0, nb - 1])
    cols_a[:tile], cols_b[:tile] = by_pairs("col", to_left, to_right)
    for part in (0, 1):
        for b in range(nb):
            at = pl.ds((part * nb + b) * half, half)
            rows_a[at, :], rows_b[at, :] = by_pairs(
                "row", tile_out[part, b, :half], tile_out[part, b, tile - half:])


def start_corners(cols_a, cols_b, after, corners_a, corners_b):
    length = cols_a.shape[1]
    half = length // 2
    tile = cols_a.shape[0] - 8
    low = lanes((tile, length)) < half
    left, right = by_side("col", cols_a[:tile], cols_b[:tile])
    for part in (0, 1):
        if part:
            left, right = swap(left, half), swap(right, half)
        value = jnp.where(low, right, left)
        at = pl.ds(part * half, half)
        corners_a[at, :], corners_b[at, :] = by_pairs("row", value[:half], value[tile - half:])
    first = lax.broadcasted_iota(jnp.int32, (8, length), 0) == 0
    info = jnp.where(first, cols_a[tile:], cols_b[tile:])
    corners_a[2 * half:] = info
    corners_b[2 * half:] = info


def fetch_pass(after, probe_from, amps_from, tables_from, probe, amps, tables, sems):
    copies = [
        pltpu.make_async_copy(source, target, sems.at[k])
        for k, (source, target) in enumerate(
            ((amps_from, amps), (tables_from, tables), (probe_from, probe)))
    ]
    for copy in copies:
        copy.start()
    for copy in copies:
        copy.wait()


def early_pass(offsets, counts, after, field, probe, amps, tables, acc, chosen):
    _, nb, tile, length = field.shape
    acc[...] = jnp.zeros_like(acc)
    found = early_list(chosen, offsets, counts, tile, length)
    add_gradients(field, acc, probe, amps, offsets, tables, chosen, found,
                  own_frame=True, own_acc=True)


def first_pass(offsets, counts, field, done, cols_a, cols_b, rows_a, rows_b, corners_a, corners_b,
               probe, amps, tables, frame, acc, tips_a, tips_b, sums_a, sums_b, edges_a, edges_b, chosen):
    _, nb, tile, length = field.shape
    half = length // 2
    rows = tile + 2 * half
    own = pl.ds(half, tile)
    left, right = by_side("col", cols_a[:tile], cols_b[:tile])
    top = pl.ds(0, half)
    bottom = pl.ds(half + tile, half)
    for part in (0, 1):
        for b in range(nb):
            frame[part, b + 1, own, :] = field[part, b]
            at = pl.ds((part * nb + b) * half, half)
            frame[part, b + 1, top, :], frame[part, b + 1, bottom, :] = by_side(
                "row", rows_a[at, :], rows_b[at, :])
        frame[part, 0, own, :] = swap(left, half) if part else left
        frame[part, nb + 1, own, :] = swap(right, half) if part else right
        at = pl.ds(part * half, half)
        ends = by_side("row", corners_a[at, :], corners_b[at, :])
        for block in (0, nb + 1):
            frame[part, block, top, :], frame[part, block, bottom, :] = ends
    empty = jnp.zeros((half, length), jnp.float32)
    for part in (0, 1):
        for b in range(nb + 2):
            acc[part, b, top, :] = empty
            acc[part, b, bottom, :] = empty
            acc[part, b, own, :] = (
                done[part, b - 1] if 0 < b <= nb else jnp.zeros((tile, length), jnp.float32))
    found, _ = first_list(chosen, offsets, counts, tile, length)
    add_gradients(frame, acc, probe, amps, offsets, tables, chosen, found)
    low = lanes((rows, length)) < half
    for part in (0, 1):
        strip_a, strip_b = by_pairs(
            "col",
            jnp.where(low, acc[part, 1], acc[part, 0]),
            jnp.where(low, acc[part, nb + 1], acc[part, nb]),
        )
        for strip, tips, sums in ((strip_a, tips_a, sums_a), (strip_b, tips_b, sums_b)):
            tips[part, 0] = strip[:length]
            tips[part, 1] = strip[rows - length:]
            sums[part] = strip[length:rows - length]
    near = lanes((length, length)) < half
    for part in (0, 1):
        for b in range(nb - 1):
            ends = [
                acc[part, b + 2, at, :] if b < nb - 2
                else jnp.where(near, acc[part, nb, at, :], acc[part, 1, at, :])
                for at in (pl.ds(0, length), pl.ds(rows - length, length))
            ]
            edges_a[part, b], edges_b[part, b] = by_pairs("row", *ends)


def middle_corners(mine_a, mine_b, tips_a, tips_b, after, corners, *, odd_pairs):
    for part in (0, 1):
        up, down = [
            by_side("col", mine_a[part, k] + tips_a[part, k], mine_b[part, k] + tips_b[part, k])
            for k in (0, 1)
        ]
        for side in (0, 1):
            corners[part, side] = by_pairs("row", up[side], down[side])[0 if odd_pairs else 1]


def light_pass(mine, cols_a, cols_b, rows_a, rows_b, corners_a, corners_b, probe, after,
               inverse, light, power, places, listed, chosen, sem, *, npos):
    length = probe.shape[-1]
    half = length // 2
    blocks, rows, _ = inverse.shape
    nb = blocks - 2
    tile = nb * length
    my_row = lax.axis_index("row")
    my_col = lax.axis_index("col")
    sources = (mine, cols_a, cols_b, rows_a, rows_b, corners_a, corners_b)
    for k, source in enumerate(sources):
        given = source[source.shape[0] - 8:, :].astype(jnp.int32)
        col = pltpu.roll(given, length - npos, 1) - (my_col + 1) * tile + 2 * length
        row = given - (my_row + 1) * tile + half + length
        near = (given > 0) & (row > 0) & (row < rows + length)
        near = near & (col > length - half) & (col < 2 * length + tile + half)
        places[pl.ds(8 * k, 8), :] = jnp.where(near, row * 4 * tile + col, 0)
    copy = pltpu.make_async_copy(places, listed, sem)
    copy.start()
    for b in range(blocks):
        light[b + 1, pl.ds(length, rows), :] = jnp.zeros((rows, length), jnp.float32)
    power[...] = probe[0] * probe[0] + probe[1] * probe[1]
    lane = lanes((length, length))
    copy.wait()

    def look(index, found):
        line = jnp.where(index < len(sources), 8 * index, 8 * (index - 2) + 1)
        for slot in range(npos):
            place = listed[line, slot]
            chosen[found] = place
            found = found + jnp.where(place > 0, 1, 0)
        return found

    found = lax.fori_loop(0, len(sources) + 2, look, 0)

    def put(index, carry):
        place = chosen[index]
        start = lax.div(place, 4 * tile)
        col = lax.rem(place, 4 * tile)
        block = lax.div(col, length)
        shift = lax.rem(col, length)
        value = pltpu.roll(power[...], shift, 1)
        inside = lane >= shift
        light[block, pl.ds(start, length), :] += jnp.where(inside, value, 0.0)
        light[block + 1, pl.ds(start, length), :] += jnp.where(inside, 0.0, value)
        return carry

    lax.fori_loop(0, found, put, 0)
    spot = lax.broadcasted_iota(jnp.int32, (rows, length), 0)
    keep_from = jnp.where(my_row > 0, 0, half)
    keep_to = jnp.where(my_row < lax.axis_size("row") - 1, rows, rows - half)
    kept = (spot >= keep_from) & (spot < keep_to)
    for b in range(blocks):
        value = 1.0 / (light[b + 1, pl.ds(length, rows), :] + 1.0)
        keep = kept
        if b == 0:
            keep = keep & (my_col > 0)
        if b == nb + 1:
            keep = keep & (my_col < lax.axis_size("col") - 1)
        inverse[b] = jnp.where(keep, value, 0.0)


def update_pass(offsets, counts, after, frame, acc, inverse, tips_a, tips_b, sums_a, sums_b, probe, amps, tables,
                work, total, chosen):
    _, blocks, rows, length = frame.shape
    half = length // 2
    nb = blocks - 2
    work[...] = acc[...]
    _, done = first_list(chosen, offsets, counts, nb * length, length)
    found, _ = collect(chosen, 0, offsets, counts, nb * length, length, clear, done)
    add_gradients(frame, work, probe, amps, offsets, tables, chosen, found)
    low = lanes((rows, length)) < half
    for part in (0, 1):
        left, right = by_side("col", *[
            above(above(tips[part, 0], sums[part]), tips[part, 1])
            for tips, sums in ((tips_a, sums_a), (tips_b, sums_b))
        ])
        for b in range(blocks):
            value = work[part, b]
            if b == 0:
                value = value + left
            if b == 1:
                value = value + jnp.where(low, left, 0.0)
            if b == nb:
                value = value + jnp.where(low, 0.0, right)
            if b == nb + 1:
                value = value + right
            work[part, b] = frame[part, b] + value * inverse[b]
    total[...] = jnp.zeros_like(total)
    found = choose(chosen, offsets, counts, nb * length, length, lambda mid_row, **_: mid_row)
    add_gradients(work, total, probe, amps, offsets, tables, chosen, found)


def second_pass(offsets, counts, work_from, total_from, inverse, edges_a, edges_b,
                corners_a, corners_b, probe, amps, tables,
                work, total, cols_a, cols_b, rows_a, rows_b, chosen):
    _, blocks, rows, length = work.shape
    half = length // 2
    nb = blocks - 2
    tile = nb * length
    near = lanes((length, length)) < half
    middle = pl.ds(length, rows - 2 * length)
    for part in (0, 1):
        edges = [by_side("row", edges_a[part, b], edges_b[part, b]) for b in range(nb - 1)]
        corners = [by_side("row", corners_a[part, side], corners_b[part, side]) for side in (0, 1)]
        for k, at in enumerate((pl.ds(0, length), pl.ds(rows - length, length))):
            left, right, ends = corners[0][k], corners[1][k], edges[nb - 2][k]
            add = [left, jnp.where(near, left, ends)]
            add += [edges[b][k] for b in range(nb - 2)]
            add += [jnp.where(near, ends, right), right]
            for b in range(blocks):
                work[part, b, at, :] = work_from[part, b, at, :] + add[b] * inverse[b, at, :]
        for b in range(blocks):
            work[part, b, middle, :] = work_from[part, b, middle, :]
    total[...] = total_from[...]
    found = choose(
        chosen, offsets, counts, tile, length,
        lambda mid_row, cross_row, cross_col, **_: ~mid_row & (cross_row | cross_col))
    add_gradients(work, total, probe, amps, offsets, tables, chosen, found)
    low = lanes((rows, length)) < half
    cols_a[...], cols_b[...] = by_pairs(
        "col",
        jnp.where(low, swap(total[1, 0], half), total[0, 0]),
        jnp.where(low, total[0, nb + 1], swap(total[1, nb + 1], half)),
    )
    for part in (0, 1):
        for b in range(nb):
            rows_a[part, b], rows_b[part, b] = by_pairs(
                "row", total[part, b + 1, :half, :], total[part, b + 1, half + tile:, :])


def inner_pass(offsets, counts, work, probe, amps, tables, sums, chosen):
    _, nb, tile, length = sums.shape
    sums[...] = jnp.zeros_like(sums)
    found = choose(
        chosen, offsets, counts, tile, length,
        lambda mid_row, cross_row, cross_col, **_: ~mid_row & ~cross_row & ~cross_col)
    add_gradients(work, sums, probe, amps, offsets, tables, chosen, found, own_acc=True)


def end_corners(cols_a, cols_b, corners_a, corners_b):
    rows, length = cols_a.shape
    half = length // 2
    for side, value in enumerate(by_side("col", cols_a[...], cols_b[...])):
        corners_a[side], corners_b[side] = by_pairs("row", value[:half], value[rows - half:])


def last_pass(work, total, inner, inverse, cols_a, cols_b, rows_a, rows_b, corners_a, corners_b,
              out, result, sems):
    _, nb, tile, length = inner.shape
    half = length // 2
    low = lanes((tile, length)) < half
    own = pl.ds(half, tile)
    gap = jnp.zeros((tile - 2 * half, length), jnp.float32)
    sides = []
    for side, value in enumerate(by_side("col", cols_a[own, :], cols_b[own, :])):
        up, down = by_side("row", corners_a[side], corners_b[side])
        sides.append(value + above(above(up, gap), down))
    left, right = sides
    copies = []
    for part in (0, 1):
        if part:
            left, right = swap(left, half), swap(right, half)
        for b in range(nb):
            up, down = by_side("row", rows_a[part, b], rows_b[part, b])
            value = total[part, b + 1, own, :] + inner[part, b] + above(above(up, gap), down)
            if b == 0:
                value = value + jnp.where(low, left, 0.0)
            if b == nb - 1:
                value = value + jnp.where(low, 0.0, right)
            result[part, b] = work[part, b + 1, own, :] + value * inverse[b + 1, own, :]
            copy = pltpu.make_async_copy(
                result.at[part, b], out.at[part, :, b * length:(b + 1) * length],
                sems.at[part * nb + b])
            copy.start()
            copies.append(copy)
    for copy in copies:
        copy.wait()


def whole(memory_space=pltpu.VMEM):
    return pl.BlockSpec(memory_space=memory_space)


def call(body, shapes, places, scratch=(), cost=None):
    return pl.pallas_call(
        body,
        out_shape=[jax.ShapeDtypeStruct(shape, jnp.float32) for shape in shapes],
        in_specs=[whole({"s": pltpu.SMEM, "v": pltpu.VMEM, "a": pl.ANY, "h": pltpu.HBM}[p]) for p in places],
        out_specs=[whole()] * len(shapes),
        scratch_shapes=list(scratch),
        compiler_params=pltpu.CompilerParams(vmem_limit_bytes=VMEM_BYTES),
        cost_estimate=cost,
    )


def swap_pairs(first, second, axis):
    count = lax.axis_size(axis)
    got = []
    for value, start in ((first, 1), (second, 0)):
        pairs = [(i, i + 1) for i in range(start, count - 1, 2)]
        got.append(lax.ppermute(value, axis, pairs + [(b, a) for a, b in pairs]))
    return got


def shards(object_field, probe, amplitudes, offsets, counts):
    length = probe.shape[-1]
    half = length // 2
    tile = object_field.shape[1]
    npos = offsets.shape[2]
    nb = tile // length
    blocks = nb + 2
    rows = tile + 2 * half
    tables = jnp.asarray(dft_tables(length))
    offsets = jnp.swapaxes(offsets, 2, 3)

    def cost(positions):
        steps = 4 * 3 * 2 * length * (2 * length) ** 2
        return pl.CostEstimate(
            flops=positions * steps, bytes_accessed=8_000_000,
            transcendentals=positions * length * length)

    memory = pltpu.VMEM
    chosen = pltpu.SMEM((npos + GROUP,), jnp.int32)
    strip = (tile + 8, length)
    edge = (2 * nb * half + 8, length)
    def kept(array):
        return pltpu.with_memory_space_constraint(array, pltpu.HBM)

    field, cols_a, cols_b, rows_a, rows_b = call(
        start_pass, [(2, nb, tile, length), strip, strip, edge, edge], "hhs",
        [pltpu.SMEM((1, 1, 2, npos), jnp.int32), pltpu.SemaphoreType.DMA((nb + 1,))],
    )(kept(object_field), kept(offsets), counts)
    mine = cols_a
    probe, amplitudes, tables = pl.pallas_call(
        fetch_pass,
        out_shape=[
            jax.ShapeDtypeStruct(array.shape, array.dtype) for array in (probe, amplitudes, tables)],
        in_specs=[whole(pl.ANY)] + [whole(pltpu.HBM)] * 3,
        out_specs=[whole()] * 3,
        scratch_shapes=[pltpu.SemaphoreType.DMA((3,))],
        compiler_params=pltpu.CompilerParams(vmem_limit_bytes=VMEM_BYTES),
        cost_estimate=cost(1),
    )(cols_a, kept(probe), kept(amplitudes), kept(tables))
    cols_a, cols_b = swap_pairs(cols_a, cols_b, "col")
    rows_a, rows_b = swap_pairs(rows_a, rows_b, "row")
    corner = (2 * half + 8, length)
    corners_a, corners_b = call(start_corners, [corner, corner], "vva")(cols_a, cols_b, probe)
    (done,) = call(
        early_pass, [(2, nb, tile, length)], "ssavvvv", [chosen], cost(GROUP),
    )(offsets, counts, corners_b, field, probe, amplitudes, tables)
    corners_a, corners_b = swap_pairs(corners_a, corners_b, "row")

    full = (2, blocks, rows, length)
    strip = (2, rows, length)
    edge = (2, nb - 1, length, length)
    tip = (2, 2, length, length)
    strip = (2, rows - 2 * length, length)
    frame, acc, tips_a, tips_b, sums_a, sums_b, edges_a, edges_b = call(
        first_pass, [full, full, tip, tip, strip, strip, edge, edge], "ss" + 11 * "v", [chosen],
    )(offsets, counts, field, done, cols_a, cols_b, rows_a, rows_b, corners_a, corners_b,
      probe, amplitudes, tables)
    info = (mine, cols_a, cols_b, rows_a, rows_b, corners_a, corners_b)
    mine_a, mine_b = tips_a, tips_b
    tips_a, tips_b = swap_pairs(tips_a, tips_b, "col")
    edges_a, edges_b = swap_pairs(edges_a, edges_b, "row")
    sums_a, sums_b = swap_pairs(sums_a, sums_b, "col")
    (inverse,) = call(
        functools.partial(light_pass, npos=npos), [(blocks, rows, length)], 8 * "v" + "a",
        [memory((blocks + 2, rows + 2 * length, length), jnp.float32),
         memory((length, length), jnp.float32), memory((7 * 8, length), jnp.int32),
         pltpu.SMEM((7 * 8, length), jnp.int32), pltpu.SMEM((9 * npos + 1,), jnp.int32),
         pltpu.SemaphoreType.DMA],
        cost(npos // 2),
    )(*info, probe, tips_b)
    corners_a, corners_b = [
        call(functools.partial(middle_corners, odd_pairs=odd_pairs), [tip], "vvvva")(
            mine_a, mine_b, tips_a, tips_b, after)[0]
        for odd_pairs, after in ((True, acc), (False, inverse))
    ]
    corners_a, corners_b = swap_pairs(corners_a, corners_b, "row")

    work, total = call(update_pass, [full, full], "ssa" + 10 * "v", [chosen], cost(npos // 2))(
        offsets, counts, edges_a, frame, acc, inverse, tips_a, tips_b, sums_a, sums_b,
        probe, amplitudes, tables)
    strip = (rows, length)
    own = (2, nb, tile, length)
    edge = (2, nb, half, length)
    work, total, cols_a, cols_b, rows_a, rows_b = call(
        second_pass, [full, full, strip, strip, edge, edge], "ss" + 10 * "v",
        [chosen], cost(npos // 2),
    )(offsets, counts, work, total, inverse, edges_a, edges_b, corners_a, corners_b,
      probe, amplitudes, tables)
    cols_a, cols_b = swap_pairs(cols_a, cols_b, "col")
    rows_a, rows_b = swap_pairs(rows_a, rows_b, "row")
    (inner,) = call(inner_pass, [own], "ss" + 4 * "v", [chosen], cost(npos // 4))(
        offsets, counts, work, probe, amplitudes, tables)
    corner = (2, half, length)
    corners_a, corners_b = call(end_corners, [corner, corner], "vv")(cols_a, cols_b)
    corners_a, corners_b = swap_pairs(corners_a, corners_b, "row")
    out = pl.pallas_call(
        last_pass,
        out_shape=jax.ShapeDtypeStruct((2, tile, tile), jnp.float32),
        in_specs=[whole()] * 10,
        out_specs=whole(pl.ANY),
        scratch_shapes=[memory(own, jnp.float32), pltpu.SemaphoreType.DMA((2 * nb,))],
        compiler_params=pltpu.CompilerParams(vmem_limit_bytes=VMEM_BYTES),
    )(work, total, inner, inverse, cols_a, cols_b, rows_a, rows_b, corners_a, corners_b)
    return out


def solution(mesh):
    placed = (
        P(None, "row", "col"),
        P(),
        P("row", "col", None, None, None),
        P("row", "col", None, None),
        P("row", "col"),
    )
    return jax.shard_map(
        shards, mesh=mesh, in_specs=placed, out_specs=P(None, "row", "col"), check_vma=False
    )
```
